128 devices in a mesh: ctx: 32 (over y, z, core), fsdp: 4 (over x).
Axes of the slice: x: 4, y: 4, z: 4, core: 2. Of those that a mesh axis runs over, the one named last changes fastest.
Arguments:
- tokens: bfloat16 [4, 4096, 768], P('fsdp', 'ctx'), may hold values from -6 to 6
- cotangent: bfloat16 [4, 4096, 768], P('fsdp', 'ctx'), may hold values from -6 to 6
- w_qkv: float32 [768, 2304], P(('ctx', 'fsdp')), may hold values from -0.3125 to 0.3125
- qkv_m: float32 [768, 2304], P(('ctx', 'fsdp')), may hold values from -40 to 40
- qkv_v: float32 [768, 2304], P(('ctx', 'fsdp')), may hold values from 2.048 to 32.768
- w_out: float32 [768, 768], P(('ctx', 'fsdp')), may hold values from -1.25 to 1.25
- out_m: float32 [768, 768], P(('ctx', 'fsdp')), may hold values from -40 to 40
- out_v: float32 [768, 768], P(('ctx', 'fsdp')), may hold values from 2.048 to 32.768
- w_fc: float32 [768, 3072], P(('ctx', 'fsdp')), may hold values from -0.21875 to 0.21875
- fc_m: float32 [768, 3072], P(('ctx', 'fsdp')), may hold values from -40 to 40
- fc_v: float32 [768, 3072], P(('ctx', 'fsdp')), may hold values from 2.048 to 32.768
- w_proj: float32 [3072, 768], P(('ctx', 'fsdp')), may hold values from -0.109375 to 0.109375
- proj_m: float32 [3072, 768], P(('ctx', 'fsdp')), may hold values from -40 to 40
- proj_v: float32 [3072, 768], P(('ctx', 'fsdp')), may hold values from 2.048 to 32.768
- vectors: float32 [768, 12], P(('ctx', 'fsdp')), may hold values from -0.6 to 1.3
- vec_m: float32 [768, 12], P(('ctx', 'fsdp')), may hold values from -80 to 80
- vec_v: float32 [768, 12], P(('ctx', 'fsdp')), may hold values from 8.192 to 131.072
Outputs:
- output: float32 [4, 4096, 768], P('fsdp', 'ctx')
- grad_tokens: float32 [4, 4096, 768], P('fsdp', 'ctx')
- new_w_qkv: float32 [768, 2304], P(('ctx', 'fsdp'))
- new_qkv_m: float32 [768, 2304], P(('ctx', 'fsdp'))
- new_qkv_v: float32 [768, 2304], P(('ctx', 'fsdp'))
- new_w_out: float32 [768, 768], P(('ctx', 'fsdp'))
- new_out_m: float32 [768, 768], P(('ctx', 'fsdp'))
- new_out_v: float32 [768, 768], P(('ctx', 'fsdp'))
- new_w_fc: float32 [768, 3072], P(('ctx', 'fsdp'))
- new_fc_m: float32 [768, 3072], P(('ctx', 'fsdp'))
- new_fc_v: float32 [768, 3072], P(('ctx', 'fsdp'))
- new_w_proj: float32 [3072, 768], P(('ctx', 'fsdp'))
- new_proj_m: float32 [3072, 768], P(('ctx', 'fsdp'))
- new_proj_v: float32 [3072, 768], P(('ctx', 'fsdp'))
- new_vectors: float32 [768, 12], P(('ctx', 'fsdp'))
- new_vec_m: float32 [768, 12], P(('ctx', 'fsdp'))
- new_vec_v: float32 [768, 12], P(('ctx', 'fsdp'))
The draws below stay inside these ranges and needn't reach their ends.
All inputs are finite; a program needn't handle non-finite values.
Results may differ from the reference program's by a relative error of at most 0.015.
The reference program's roundings to bfloat16 on the way count: a program that leaves them out, or rounds other values in their place, can miss the bound.
Values may be sent and summed in bfloat16 or wider, within the bound.
A program may use at most 192 MiB of HBM per device.

```python
import math
import jax
import jax.numpy as jnp
from jax import lax

D = 768
FF = 3072
H = 12
HD = 64
STEP = 10
NVEC = 12
L = 4096
SEQS = 4
TOKENS = 16384


def draw_vectors(key, part):
    key = jax.random.fold_in(key, 7)
    uniform_draw = jax.random.uniform(key, (D, NVEC), jnp.float32, -1.0, 1.0)
    column = jnp.arange(NVEC, dtype=jnp.int32)[None, :]
    is_gain = (column == 0) | (column == 5)
    return jnp.where(is_gain, 1.0 + 0.3 * uniform_draw, 0.6 * uniform_draw)


def block_levels(key, extent, split, smallest, largest):
    level, own = 1.0, jax.random.fold_in(key, 6)
    for axis_at, parts in split:
        draws = jnp.exp(jax.random.uniform(jax.random.fold_in(own, axis_at), (parts,), jnp.float32, smallest / len(split), largest / len(split)))
        level = level * jnp.repeat(draws, extent[axis_at] // parts).reshape([-1 if axis == axis_at else 1 for axis in range(len(extent))])
    return level


def normal_values(stream_key, extent, spread, limit, pieces=(), kind=jnp.bfloat16):
    array = jax.random.normal(stream_key, extent, jnp.float32) * spread
    if len(pieces) > 0:
        array = block_levels(stream_key, extent, pieces, -0.22, 0.18) * array
    return jnp.clip(array, min=-limit, max=limit).astype(kind)


def setup_inputs(seed: int = 0) -> dict:
    arg_keys = jax.random.split(jax.random.key(seed), 18)
    tokens = normal_values(arg_keys[0], (SEQS, L, D), 1.0, 6.0, ((0, 4), (1, 32)))
    cotangent = normal_values(arg_keys[1], (SEQS, L, D), 1.0, 6.0, ((0, 4), (1, 32)))
    w_qkv = normal_values(arg_keys[2], (D, 3 * D), (D // 2) ** -0.5, 0.3125, ((0, 128),), jnp.float32)
    qkv_m = normal_values(arg_keys[3], (D, 3 * D), (0.055 * TOKENS ** 0.5), 40.0, ((0, 128),), jnp.float32)
    qkv_v = jnp.clip(jnp.exp(math.log(32.768) - 2.7725887 * jax.random.uniform(arg_keys[4], (D, 3 * D), jnp.float32) ** block_levels(arg_keys[4], (D, 3 * D), ((0, 128),), -0.2, 0.2)), 2.048, 32.768)
    w_out = normal_values(arg_keys[5], (D, D), (D // 32) ** -0.5, 1.25, ((0, 128),), jnp.float32)
    out_m = normal_values(arg_keys[6], (D, D), (0.055 * TOKENS ** 0.5), 40.0, ((0, 128),), jnp.float32)
    out_v = jnp.clip(jnp.exp(math.log(32.768) - 2.7725887 * jax.random.uniform(arg_keys[7], (D, D), jnp.float32) ** block_levels(arg_keys[7], (D, D), ((0, 128),), -0.2, 0.2)), 2.048, 32.768)
    w_fc = normal_values(arg_keys[8], (D, FF), D ** -0.5, 0.21875, ((0, 128),), jnp.float32)
    fc_m = normal_values(arg_keys[9], (D, FF), (0.055 * TOKENS ** 0.5), 40.0, ((0, 128),), jnp.float32)
    fc_v = jnp.clip(jnp.exp(math.log(32.768) - 2.7725887 * jax.random.uniform(arg_keys[10], (D, FF), jnp.float32) ** block_levels(arg_keys[10], (D, FF), ((0, 128),), -0.2, 0.2)), 2.048, 32.768)
    w_proj = normal_values(arg_keys[11], (FF, D), FF ** -0.5, 0.109375, ((0, 128),), jnp.float32)
    proj_m = normal_values(arg_keys[12], (FF, D), (0.055 * TOKENS ** 0.5), 40.0, ((0, 128),), jnp.float32)
    proj_v = jnp.clip(jnp.exp(math.log(32.768) - 2.7725887 * jax.random.uniform(arg_keys[13], (FF, D), jnp.float32) ** block_levels(arg_keys[13], (FF, D), ((0, 128),), -0.2, 0.2)), 2.048, 32.768)
    vectors = draw_vectors(jax.random.fold_in(arg_keys[17], 71), 0)
    vec_m = normal_values(arg_keys[15], (D, NVEC), (0.11 * TOKENS ** 0.5), 80.0, ((0, 128),), jnp.float32)
    vec_v = jnp.clip(jnp.exp(math.log(131.072) - 2.7725887 * jax.random.uniform(arg_keys[16], (D, NVEC), jnp.float32) ** block_levels(arg_keys[16], (D, NVEC), ((0, 128),), -0.2, 0.2)), 8.192, 131.072)
    return dict(tokens=tokens, cotangent=cotangent, w_qkv=w_qkv, qkv_m=qkv_m, qkv_v=qkv_v, w_out=w_out, out_m=out_m, out_v=out_v, w_fc=w_fc, fc_m=fc_m, fc_v=fc_v, w_proj=w_proj, proj_m=proj_m, proj_v=proj_v, vectors=vectors, vec_m=vec_m, vec_v=vec_v)


@jax.custom_vjp
def low(v):
    return lax.optimization_barrier(v.astype(jnp.bfloat16)).astype(jnp.float32)

@jax.custom_vjp
def low_back(v):
    return v

def low_keep(v):
    return (low(v), None)

def low_pass(kept, grad):
    return (grad,)

def back_keep(v):
    return (v, None)

def back_low(kept, grad):
    return (low(grad),)
low.defvjp(low_keep, low_pass)
low_back.defvjp(back_keep, back_low)
EPSILON = 1e-05
BETA_ONE = 0.9
BETA_TWO = 0.999
ADAM_EPSILON = 1e-08
HIGHEST = lax.Precision.HIGHEST

def layer_norm(inputs, gain, shift):
    row_mean = lax.optimization_barrier(jnp.mean(inputs, -1, keepdims=True))
    centered = inputs - row_mean
    variance = lax.optimization_barrier(jnp.mean(centered * centered, -1, keepdims=True))
    return centered * lax.rsqrt(variance + EPSILON) * gain + shift

def gelu_tanh(values):
    return 0.5 * values * (1.0 + jnp.tanh(0.7978845608028654 * (values + 0.044715 * values * values * values)))

def attend(query, key_rows, value_rows):
    length = query.shape[0]
    block = min(512, length)
    count = length // block
    query_heads = query.reshape(count, block, H, HD).transpose(0, 2, 1, 3)
    key_heads = key_rows.reshape(length, H, HD).transpose(1, 0, 2)
    value_heads = value_rows.reshape(length, H, HD).transpose(1, 0, 2)
    starts = jnp.arange(count, dtype=jnp.int32) * block
    key_pos = jnp.arange(length, dtype=jnp.int32)

    def one_block(operands):
        query_blk, start = operands
        raw = jnp.einsum('hqd,hkd->hqk', query_blk, key_heads, precision=HIGHEST) * 0.125
        query_pos = start + jnp.arange(block, dtype=jnp.int32)
        scores = jnp.where(query_pos[:, None] >= key_pos[None, :], low_back(raw), -1000000000.0)
        row_max = lax.optimization_barrier(jnp.max(scores, -1, keepdims=True))
        exponent = jnp.exp(scores - row_max)
        attn_prob = exponent / lax.optimization_barrier(jnp.sum(exponent, -1, keepdims=True))
        return jnp.einsum('hqk,hkd->hqd', low(attn_prob), value_heads, precision=HIGHEST)
    blocks = lax.map(jax.checkpoint(one_block), (query_heads, starts))
    return blocks.transpose(0, 2, 1, 3).reshape(length, H * HD)

def layer(params, inputs):
    w_qkv, w_out, w_fc, w_proj, vectors = params
    width = inputs.shape[1]
    gain_one = vectors[:, 0]
    shift_one = vectors[:, 1]
    q_bias = vectors[:, 2]
    v_bias = vectors[:, 3]
    out_bias = vectors[:, 4]
    gain_two = vectors[:, 5]
    shift_two = vectors[:, 6]
    proj_bias = vectors[:, 7]
    fc_bias = vectors[:, 8:].T.reshape(-1)
    act_one = low(layer_norm(inputs, gain_one, shift_one))
    mixed = jnp.dot(act_one, w_qkv, precision=HIGHEST)
    query = low_back(low(mixed[:, :width] + q_bias))
    key_rows = low_back(low(mixed[:, width:2 * width]))
    value_rows = low_back(low(mixed[:, 2 * width:] + v_bias))
    heads = low_back(low(attend(query, key_rows, value_rows)))
    x_two = inputs + low_back(jnp.dot(heads, w_out, precision=HIGHEST) + out_bias)
    act_two = low(layer_norm(x_two, gain_two, shift_two))
    hidden = low_back(jnp.dot(act_two, w_fc, precision=HIGHEST) + fc_bias)
    act_three = low(gelu_tanh(hidden))
    return x_two + jnp.dot(act_three, w_proj, precision=HIGHEST) + proj_bias

def adam_update(weight, moment_one, moment_two, gradient, rate, decay):
    new_one = BETA_ONE * moment_one + (1.0 - BETA_ONE) * gradient
    new_two = BETA_TWO * moment_two + (1.0 - BETA_TWO) * gradient * gradient
    fix_one = 1.0 - BETA_ONE ** STEP
    fix_two = 1.0 - BETA_TWO ** STEP
    direction = new_one / fix_one / (jnp.sqrt(new_two / fix_two) + ADAM_EPSILON)
    return (weight - rate * (direction + decay * weight), new_one, new_two)

def reference(tokens, cotangent, w_qkv, qkv_m, qkv_v, w_out, out_m, out_v, w_fc, fc_m, fc_v, w_proj, proj_m, proj_v, vectors, vec_m, vec_v):
    inputs = tokens.astype(jnp.float32)

    def forward(inputs_all, weight_a, weight_b, weight_c, weight_d, weight_e):
        params = (low(weight_a), low(weight_b), low(weight_c), low(weight_d), low(weight_e))

        def one_sequence(sequence):
            return layer(params, sequence)
        return lax.map(one_sequence, inputs_all)
    output, backward = jax.vjp(forward, inputs, w_qkv, w_out, w_fc, w_proj, vectors)
    grads = backward(cotangent.astype(jnp.float32))
    new_qkv = adam_update(w_qkv, qkv_m, qkv_v, grads[1], 0.1, 0.1)
    new_out = adam_update(w_out, out_m, out_v, grads[2], 0.3, 0.1)
    new_fc = adam_update(w_fc, fc_m, fc_v, grads[3], 0.05, 0.1)
    new_proj = adam_update(w_proj, proj_m, proj_v, grads[4], 0.03, 0.1)
    new_vec = adam_update(vectors, vec_m, vec_v, grads[5], 0.5, 0.0)
    return (output, grads[0], new_qkv[0], new_qkv[1], new_qkv[2], new_out[0], new_out[1], new_out[2], new_fc[0], new_fc[1], new_fc[2], new_proj[0], new_proj[1], new_proj[2], new_vec[0], new_vec[1], new_vec[2])
```

```python
import jax
import jax.numpy as jnp
from jax import lax
from jax.experimental import pallas as pl
from jax.experimental.pallas import tpu as pltpu
from jax.sharding import PartitionSpec as P

STEP = 10
EPSILON = 1e-05
BETA_ONE = 0.9
BETA_TWO = 0.999
ADAM_EPSILON = 1e-08
MESH = pl.DeviceIdType.MESH
BF = jnp.bfloat16
F32 = jnp.float32
ANY = pl.BlockSpec(memory_space=pl.ANY)
VMEM = pl.BlockSpec(memory_space=pltpu.VMEM)
LIMIT = 56 * 1024 * 1024


def coords():
    c = lax.axis_index("ctx")
    return c // 8, (c // 2) % 4, c % 2, lax.axis_index("fsdp")


def device(y, z, k, x):
    return ((y * 4 + z) * 2 + k, x)


def ring(v, step):
    return lax.rem(v + step, 4)


def greet(devices):
    barrier = pltpu.get_barrier_semaphore()
    for one in devices:
        pl.semaphore_signal(barrier, inc=1, device_id=one, device_id_type=MESH)
    pl.semaphore_wait(barrier, len(devices))


def remote(src, dst, send, recv, to):
    return pltpu.make_async_remote_copy(
        src, dst, send, recv, device_id=to, device_id_type=MESH
    )


def comm(kernel, outs, cid, sems, args, scratch=(), spaces=None, name=None):
    return pl.pallas_call(
        kernel,
        out_shape=outs,
        in_specs=[ANY] * len(args) if spaces is None else spaces[0],
        out_specs=[ANY] * len(outs) if spaces is None else spaces[1],
        scratch_shapes=list(scratch) + [pltpu.SemaphoreType.DMA((n,)) for n in sems],
        compiler_params=pltpu.CompilerParams(
            collective_id=cid, has_side_effects=True, vmem_limit_bytes=LIMIT
        ),
        name=name,
    )(*args)


def first_gather(w_qkv, w_fc, w_out, w_proj, vectors, rows):
    width = 4736

    def kernel(
        wq_ref, wf_ref, wo_ref, wp_ref, wv_ref, r_ref,
        q_out, f_out, o_out, p_out, ro_ref,
        wide, packed, got, fc48, qkv48, out48, proj_wide, q_send, f_send, o_send, p_send,
        ms, mr, fs, fr, s1, r1, s2, r2, ps, pr, xs_s, xs_r, xf_s, xf_r, rs, rr, cs, cr, loc,
    ):
        y, z, k, x = coords()
        me = y * 4 + z
        sib = device(y, z, 1 - k, x)
        steps = (1, 2, 3)
        greet(
            [sib]
            + [device(y, z, k, ring(x, d)) for d in steps]
            + [
                device(ring(y, a), ring(z, b), k, x)
                for a in range(4)
                for b in range(4)
                if (a, b) != (0, 0)
            ]
        )
        own_r = pltpu.make_async_copy(r_ref, ro_ref.at[k, z], loc.at[0])
        own_r.start()
        row_copies = []
        for d in steps:
            c = remote(
                r_ref, ro_ref.at[k, z], rs.at[d], rr.at[d], device(y, ring(z, d), k, x)
            )
            row_copies.append(c)
        wide[...] = jnp.zeros_like(wide)
        wide[0:6, 0:3072] = wf_ref[...]
        wide[6:12, 0:2304] = wq_ref[...]
        wide[6:12, 2304:3072] = wo_ref[...]
        wide[0:12, 3072:3840] = wp_ref[0:12]
        wide[0:12, 3840:4608] = wp_ref[12:24]
        wide[0:6, 4608:4620] = wv_ref[...]
        t = k * 4 + x
        packed[...] = wide[...].astype(BF)
        got[t] = packed[...]
        message = []
        for d in steps:
            c = remote(packed, got.at[t], ms.at[d], mr.at[d], device(y, z, k, ring(x, d)))
            c.start()
            message.append(c)
        c = remote(packed, got.at[t], fs.at[0], fr.at[0], sib)
        c.start()
        forward = [c]
        for c in row_copies:
            c.start()
        c = remote(r_ref, ro_ref.at[k, z], cs.at[0], cr.at[0], sib)
        c.start()
        row_forward = [c]
        for d in steps:
            message[d - 1].wait_recv()
            src = k * 4 + ring(x, 4 - d)
            f = remote(got.at[src], got.at[src], fs.at[d], fr.at[d], sib)
            f.start()
            forward.append(f)
        for f in forward:
            f.wait_recv()
        for i in range(8):
            piece = got[i].astype(F32)
            at = slice(6 * i, 6 * i + 6)
            fc48[at] = piece[0:6, 0:3072]
            qkv48[at] = piece[6:12, 0:2304]
            out48[at, 0:768] = piece[6:12, 2304:3072]
            out48[at, 768:896] = piece[0:6, 4608:4736]
            proj_wide[24 * i : 24 * i + 12] = piece[0:12, 3072:3840]
            proj_wide[24 * i + 12 : 24 * i + 24] = piece[0:12, 3840:4608]
        for j in range(4):
            q_send[j, :, 0:192] = qkv48[:, 192 * j : 192 * j + 192].astype(BF)
            q_send[j, :, 192:384] = qkv48[:, 768 + 192 * j : 960 + 192 * j].astype(BF)
            q_send[j, :, 384:576] = qkv48[:, 1536 + 192 * j : 1728 + 192 * j].astype(BF)
            q_send[j, :, 576:640] = out48[:, 768:832].astype(BF)
        for j in range(8):
            f_send[j] = fc48[:, 384 * j : 384 * j + 384].astype(BF)
        o_send[0] = out48[:, 0:384].astype(BF)
        o_send[1] = out48[:, 384:768].astype(BF)
        p_send[...] = proj_wide[...].astype(BF)

        group = pl.ds(pl.multiple_of(16 * jnp.minimum(x, 2), 16), 16)

        def to_of(m):
            return ring(y, m // 4), ring(z, m % 4)

        def q_copy(m):
            ty, tz = to_of(m)
            return remote(
                q_send.at[tz, group], q_out.at[me, group], s1.at[m], r1.at[m],
                device(ty, tz, k, x),
            )

        def f_copy(m):
            ty, tz = to_of(m)
            return remote(
                f_send.at[tz * 2 + k], f_out.at[me], s2.at[m], r2.at[m], device(ty, tz, k, x)
            )

        def o_copy(m):
            ty, tz = to_of(m)
            return remote(o_send.at[k], o_out.at[me], s2.at[m], r2.at[m], device(ty, tz, k, x))

        def p_copy(a):
            return remote(
                p_send, p_out.at[z % 2], ps.at[a], pr.at[z % 2], device(ring(y, a), y, k, x)
            )

        def each(copy, what):
            def step(m, carry):
                what(copy(m))
                return carry

            lax.fori_loop(1, 16, step, 0)

        start = lambda c: c.start()
        finish = lambda c: c.wait()

        @pl.when(x < 3)
        def _():
            each(q_copy, start)
            c = pltpu.make_async_copy(q_send.at[z, group], q_out.at[me, group], loc.at[1])
            c.start()
            c.wait()

        @pl.when(x == 1)
        def _():
            each(f_copy, start)
            c = pltpu.make_async_copy(f_send.at[z * 2 + k], f_out.at[me], loc.at[2])
            c.start()
            c.wait()

        @pl.when(x == 2)
        def _():
            each(o_copy, start)
            c = pltpu.make_async_copy(o_send.at[k], o_out.at[me], loc.at[2])
            c.start()
            c.wait()

        @pl.when((x == 3) & (k == z // 2))
        def _():
            for a in range(1, 4):
                p_copy(a).start()

            @pl.when(z != y)
            def _():
                p_copy(0).start()

            @pl.when(z == y)
            def _():
                c = pltpu.make_async_copy(p_send, p_out.at[z % 2], loc.at[2])
                c.start()
                c.wait()

        half = pl.ds(8 * k, 8)
        other_half = pl.ds(8 * (1 - k), 8)

        def rows_of(plane):
            return pl.ds(pl.multiple_of(16 * plane, 16), 16)

        @pl.when(x < 3)
        def _():
            each(q_copy, finish)
            for d in steps:
                remote(
                    q_out.at[half, group], q_out.at[half, group], xs_s.at[d], xs_r.at[x],
                    device(y, z, k, ring(x, d)),
                ).start()

        def pass_on(a):
            return remote(
                q_out.at[half, rows_of(a)], q_out.at[half, rows_of(a)], xf_s.at[a], xf_r.at[a], sib
            )

        for a in range(3):

            @pl.when(x != a)
            def _():
                remote(
                    q_out.at[half, rows_of(a)], q_out.at[half, rows_of(a)], xs_s.at[0],
                    xs_r.at[a], sib,
                ).wait_recv()
                pass_on(a).start()

        for d in steps:
            row_copies[d - 1].wait_recv()
            src = ring(z, 4 - d)
            f = remote(ro_ref.at[k, src], ro_ref.at[k, src], cs.at[d], cr.at[d], sib)
            f.start()
            row_forward.append(f)

        @pl.when(x == 1)
        def _():
            each(f_copy, finish)

        @pl.when(x == 2)
        def _():
            each(o_copy, finish)

        @pl.when((x == 3) & (k == z // 2))
        def _():
            for a in range(1, 4):
                p_copy(a).wait_send()

            @pl.when(z != y)
            def _():
                p_copy(0).wait_send()

        for j in range(2):
            @pl.when((x == 3) & jnp.logical_not((y == z) & (z == 2 * k + j)))
            def _():
                remote(p_send, p_out.at[j], ps.at[0], pr.at[j], sib).wait_recv()

        @pl.when(x < 3)
        def _():
            for d in steps:
                remote(
                    q_out.at[half, group], q_out.at[half, group], xs_s.at[d], xs_r.at[x],
                    device(y, z, k, ring(x, d)),
                ).wait_send()

        for a in range(3):

            @pl.when(x != a)
            def _():
                pass_on(a).wait_send()
                remote(
                    q_out.at[other_half, rows_of(a)], q_out.at[other_half, rows_of(a)],
                    xf_s.at[a], xf_r.at[a], sib,
                ).wait_recv()

        for c in message + row_copies + forward:
            c.wait_send()
        for c in row_forward:
            c.wait()
        own_r.wait()

    return comm(
        kernel,
        [
            jax.ShapeDtypeStruct((16, 48, 640), BF),
            jax.ShapeDtypeStruct((16, 48, 384), BF),
            jax.ShapeDtypeStruct((16, 48, 384), BF),
            jax.ShapeDtypeStruct((2, 192, 768), BF),
            jax.ShapeDtypeStruct((2, 4) + rows.shape, BF),
        ],
        0,
        (4, 4, 4, 4, 16, 16, 16, 16, 4, 2, 4, 4, 4, 4, 4, 4, 4, 4, 3),
        (w_qkv, w_fc, w_out, w_proj, vectors, rows),
        scratch=[
            pltpu.VMEM((16, width), F32),
            pltpu.VMEM((16, width), BF),
            pltpu.VMEM((8, 16, width), BF),
            pltpu.VMEM((48, 3072), F32),
            pltpu.VMEM((48, 2304), F32),
            pltpu.VMEM((48, 896), F32),
            pltpu.VMEM((192, 768), F32),
            pltpu.VMEM((4, 48, 640), BF),
            pltpu.VMEM((8, 48, 384), BF),
            pltpu.VMEM((2, 48, 384), BF),
            pltpu.VMEM((192, 768), BF),
        ],
        spaces=([VMEM] * 5 + [ANY], [ANY] * 5),
        name="first_gather",
    )


def kv_gather(kv, rows, fc, out, proj):
    def kernel(
        v_ref, r_ref, f_ref, o_ref, p_ref, vo_ref, ro_ref, fo_ref, oo_ref, po_ref,
        vs, vr, rs, rr, cs, cr, ds, dr, ws, wr, os, orr, loc,
    ):
        y, z, k, x = coords()
        sib = device(y, z, 1 - k, x)
        ys = [(d, ring(y, d)) for d in (1, 2, 3)]
        zs = [(d, ring(z, d)) for d in (1, 2, 3)]
        greet(
            [sib]
            + [device(b, z, k, x) for _, b in ys]
            + [device(y, b, k, x) for _, b in zs]
            + [device(y, z, k, ring(x, d)) for d in (1, 2, 3)]
        )
        own = [
            pltpu.make_async_copy(v_ref, vo_ref.at[y, k], loc.at[0]),
            pltpu.make_async_copy(r_ref, ro_ref.at[k, z], loc.at[1]),
        ]
        for c in own:
            c.start()
        kv_copies, row_copies, forward = [], [], []
        for d, b in ys:
            c = remote(v_ref, vo_ref.at[y, k], vs.at[d], vr.at[d], device(b, z, k, x))
            c.start()
            kv_copies.append(c)
        for d, b in zs:
            c = remote(r_ref, ro_ref.at[k, z], rs.at[d], rr.at[d], device(y, b, k, x))
            c.start()
            row_copies.append(c)

        weights = ((1, f_ref, fo_ref), (2, o_ref, oo_ref.at[k]), (3, p_ref, po_ref))

        def weight_copy(a, d):
            _, src, dst = weights[a - 1]
            return remote(src, dst, ws.at[d], wr.at[a], device(y, z, k, ring(x, d)))

        for a in (1, 2, 3):

            @pl.when(x == a)
            def _():
                for d in (1, 2, 3):
                    weight_copy(a, d).start()
                _, src, dst = weights[a - 1]
                c = pltpu.make_async_copy(src, dst, loc.at[2])
                c.start()
                c.wait()

        c = remote(v_ref, vo_ref.at[y, k], cs.at[0], cr.at[0], sib)
        c.start()
        forward.append(c)
        c = remote(r_ref, ro_ref.at[k, z], ds.at[0], dr.at[0], sib)
        c.start()
        forward.append(c)
        for c, (d, b) in zip(row_copies, zs):
            c.wait_recv()
            src = ring(z, 4 - d)
            f = remote(ro_ref.at[k, src], ro_ref.at[k, src], ds.at[d], dr.at[d], sib)
            f.start()
            forward.append(f)
        for c, (d, b) in zip(kv_copies, ys):
            c.wait_recv()
            src = ring(y, 4 - d)
            f = remote(vo_ref.at[src, k], vo_ref.at[src, k], cs.at[d], cr.at[d], sib)
            f.start()
            forward.append(f)
        for a in (2, 1, 3):

            @pl.when(x != a)
            def _():
                weight_copy(a, 1).wait_recv()

            if a == 2:
                c = remote(oo_ref.at[k], oo_ref.at[k], os.at[0], orr.at[0], sib)
                c.start()
                forward.append(c)
        for a in (1, 2, 3):

            @pl.when(x == a)
            def _():
                for d in (1, 2, 3):
                    weight_copy(a, d).wait_send()

        for c in kv_copies + row_copies:
            c.wait_send()
        for c in forward:
            c.wait()
        for c in own:
            c.wait()

    return comm(
        kernel,
        [
            jax.ShapeDtypeStruct((4, 2) + kv.shape, BF),
            jax.ShapeDtypeStruct((2, 4) + rows.shape, BF),
            jax.ShapeDtypeStruct((16, 48, 384), BF),
            jax.ShapeDtypeStruct((2, 16, 48, 384), BF),
            jax.ShapeDtypeStruct((2, 192, 768), BF),
        ],
        2,
        (4, 4, 4, 4, 4, 4, 4, 4, 4, 4, 1, 1, 3),
        (kv, rows, fc, out, proj),
        name="kv_gather",
    )


def heads_gather(heads):
    def kernel(h_ref, ho_ref, hs, hr, cs, cr, loc):
        y, z, k, x = coords()
        sib = device(y, z, 1 - k, x)
        zs = [(d, ring(z, d)) for d in (1, 2, 3)]
        greet([sib] + [device(y, b, k, x) for _, b in zs])
        own = pltpu.make_async_copy(h_ref, ho_ref.at[z, k], loc.at[0])
        own.start()
        copies = []
        for d, b in zs:
            c = remote(h_ref, ho_ref.at[z, k], hs.at[d], hr.at[d], device(y, b, k, x))
            c.start()
            copies.append(c)
        c = remote(h_ref, ho_ref.at[z, k], cs.at[0], cr.at[0], sib)
        c.start()
        forward = [c]
        for c, (d, b) in zip(copies, zs):
            c.wait_recv()
            src = ring(z, 4 - d)
            f = remote(ho_ref.at[src, k], ho_ref.at[src, k], cs.at[d], cr.at[d], sib)
            f.start()
            forward.append(f)
        for c in copies:
            c.wait_send()
        for c in forward:
            c.wait()
        own.wait()

    return comm(
        kernel,
        [jax.ShapeDtypeStruct((4, 2) + heads.shape, BF)],
        3,
        (4, 4, 4, 4, 1),
        (heads,),
        name="heads_gather",
    )[0]


def z_gather(rows):
    def kernel(r_ref, ro_ref, rs, rr, loc):
        y, z, k, x = coords()
        zs = [(d, ring(z, d)) for d in (1, 2, 3)]
        greet([device(y, b, k, x) for _, b in zs])
        own = pltpu.make_async_copy(r_ref, ro_ref.at[z], loc.at[0])
        own.start()
        copies = []
        for d, b in zs:
            c = remote(r_ref, ro_ref.at[z], rs.at[d], rr.at[d], device(y, b, k, x))
            c.start()
            copies.append(c)
        for c in copies:
            c.wait()
        own.wait()

    return comm(
        kernel,
        [jax.ShapeDtypeStruct((4,) + rows.shape, BF)],
        4,
        (4, 4, 1),
        (rows,),
        name="z_gather",
    )[0]


def group_sum(parts, cid, name):
    n = parts.shape[0]
    rows, cols = parts.shape[3:]

    def kernel(p_ref, o_ref, got, mine, far, cs, cr, zs, zr):
        y, z, k, x = coords()
        sib = device(y, z, 1 - k, x)
        ring_z = [(d, ring(z, d)) for d in (1, 2, 3)]
        greet([sib] + [device(y, b, k, x) for _, b in ring_z])
        order = ring_z + [(0, z)]
        pairs = []
        for i in range(n):
            for d, b in order:
                c = remote(
                    p_ref.at[i, 1 - k, b], got.at[i, b], cs.at[4 * i + d], cr.at[4 * i + d], sib
                )
                c.start()
                pairs.append(c)
        copies = []
        for i in range(n):
            for d, b in order:
                pairs[4 * i + (d - 1) % 4].wait_recv()
                total = p_ref[i, k, b].astype(F32) + got[i, b].astype(F32)
                if d == 0:
                    o_ref[i] = total
                else:
                    mine[i, d - 1] = total.astype(BF)
                    c = remote(
                        mine.at[i, d - 1],
                        far.at[i, d - 1],
                        zs.at[3 * i + d - 1],
                        zr.at[3 * i + d - 1],
                        device(y, b, k, x),
                    )
                    c.start()
                    copies.append(c)
        for i in range(n):
            for d in range(3):
                copies[3 * i + d].wait_recv()
            o_ref[i] = (
                o_ref[i] + far[i, 0].astype(F32) + far[i, 1].astype(F32) + far[i, 2].astype(F32)
            )
        for c in copies:
            c.wait_send()
        for c in pairs:
            c.wait_send()

    return comm(
        kernel,
        [jax.ShapeDtypeStruct((n, rows, cols), F32)],
        cid,
        (4 * n, 4 * n, 3 * n, 3 * n),
        (parts,),
        scratch=[
            pltpu.VMEM((n, 4, rows, cols), BF),
            pltpu.VMEM((n, 3, rows, cols), BF),
            pltpu.VMEM((n, 3, rows, cols), BF),
        ],
        spaces=([VMEM], [VMEM]),
        name=name,
    )[0]


def kv_sum(parts, fc, proj):
    rows, cols = parts.shape[2:]

    def kernel(
        p_ref, f_ref, w_ref, o_ref, fo_ref, wo_ref, got, mine, far, f_far, w_far,
        cs, cr, ys, yr, fs, fr, ws, wr,
    ):
        y, z, k, x = coords()
        sib = device(y, z, 1 - k, x)
        ring_y = [(d, ring(y, d)) for d in (1, 2, 3)]
        greet(
            [sib]
            + [device(b, z, k, x) for _, b in ring_y]
            + [device(y, z, k, ring(x, d)) for d in (1, 2, 3)]
        )
        order = ring_y + [(0, y)]
        pairs = []
        for d, b in order:
            c = remote(p_ref.at[b, 1 - k], got.at[b], cs.at[d], cr.at[b], sib)
            c.start()
            pairs.append(c)
        weights = []
        for d in (1, 2, 3):
            b = ring(x, d)
            to = device(y, z, k, b)
            weights.append(
                remote(f_ref.at[:, b], f_far.at[d - 1], fs.at[d - 1], fr.at[d - 1], to)
            )
            weights.append(
                remote(w_ref.at[:, b], w_far.at[d - 1], ws.at[d - 1], wr.at[d - 1], to)
            )
        for c in weights:
            c.start()
        copies = []
        for i, (d, b) in enumerate(order):
            pairs[i].wait_recv()
            total = p_ref[b, k].astype(F32) + got[b].astype(F32)
            if d == 0:
                o_ref[...] = total
            else:
                mine[d - 1] = total.astype(BF)
                c = remote(
                    mine.at[d - 1], far.at[d - 1], ys.at[d - 1], yr.at[d - 1], device(b, z, k, x)
                )
                c.start()
                copies.append(c)
        for c in weights:
            c.wait()
        fo_ref[...] = (
            f_ref[:, x].astype(F32)
            + f_far[0].astype(F32)
            + f_far[1].astype(F32)
            + f_far[2].astype(F32)
        ).astype(BF)
        wo_ref[...] = (
            w_ref[:, x].astype(F32)
            + w_far[0].astype(F32)
            + w_far[1].astype(F32)
            + w_far[2].astype(F32)
        ).astype(BF)
        for c in copies:
            c.wait_recv()
        o_ref[...] = (
            o_ref[...] + far[0].astype(F32) + far[1].astype(F32) + far[2].astype(F32)
        )
        for c in copies:
            c.wait_send()
        for c in pairs:
            c.wait_send()

    return comm(
        kernel,
        [
            jax.ShapeDtypeStruct((rows, cols), F32),
            jax.ShapeDtypeStruct((4, 48, 384), BF),
            jax.ShapeDtypeStruct((2, 48, 768), BF),
        ],
        5,
        (4, 4, 3, 3, 3, 3, 3, 3),
        (parts, fc, proj),
        scratch=[
            pltpu.VMEM((4, rows, cols), BF),
            pltpu.VMEM((3, rows, cols), BF),
            pltpu.VMEM((3, rows, cols), BF),
            pltpu.VMEM((3, 4, 48, 384), BF),
            pltpu.VMEM((3, 2, 48, 768), BF),
        ],
        spaces=([VMEM] * 3, [VMEM] * 3),
        name="kv_sum",
    )


def last_sums(one, mix, vec, fc, proj):
    wide = 3200

    def kernel(
        one_ref, mix_ref, vec_ref, fc_ref, proj_ref, one_out, rows_out, proj_out,
        one_far, mix_got, mix_sum, mix_far, vec_far, mix_mine, vec_mine,
        mix_all, fc_all, vec_all, proj_all, proj_sum, out_send,
        zs, zr, cs, cr, s1, r1, s2, r2, s3, r3, s4, r4, s5, r5, s6, r6, s7, r7, s8, r8, loc,
    ):
        y, z, k, x = coords()
        me = y * 4 + z
        sib = device(y, z, 1 - k, x)
        steps = (1, 2, 3)
        greet(
            [sib]
            + [device(y, z, j, ring(x, d)) for d in steps for j in (k, 1 - k)]
            + [
                device(ring(y, a), ring(z, b), k, x)
                for a in range(4)
                for b in range(4)
                if (a, b) != (0, 0)
            ]
        )
        mine_at = pl.ds(pl.multiple_of(384 * k, 128), 384)
        other_at = pl.ds(pl.multiple_of(384 * (1 - k), 128), 384)
        swap = []
        for d in (1, 2, 3, 0):
            b = ring(x, d)
            c = remote(mix_ref.at[:, b, :, other_at], mix_got.at[b], cs.at[d], cr.at[d], sib)
            c.start()
            swap.append(c)
        along = []
        for d in steps:
            b = ring(x, d)
            to = device(y, z, k, b)
            c = remote(vec_ref.at[:, b], vec_far.at[d - 1], s2.at[d - 1], r2.at[d - 1], to)
            c.start()
            along.append(c)
            swap[d - 1].wait_recv()
            mix_sum[d] = (
                mix_ref[:, b, :, mine_at].astype(F32) + mix_got[b].astype(F32)
            ).astype(BF)
            c = remote(mix_sum.at[d], mix_far.at[d - 1], s1.at[d - 1], r1.at[d - 1], to)
            c.start()
            along.append(c)
        ones = []
        for d in steps:
            c = remote(
                one_ref.at[ring(z, d)], one_far.at[d - 1], zs.at[d - 1], zr.at[d - 1],
                device(y, ring(z, d), k, x),
            )
            c.start()
            ones.append(c)

        def plane(src, dst, send, recv, a):
            return remote(src.at[a], dst.at[me], send.at[a], recv.at[me], device(a, x, k, x))

        def all_start(src, dst, send, recv):
            for a in range(4):
                here = (a == y) & (z == x)

                @pl.when(jnp.logical_not(here))
                def _():
                    plane(src, dst, send, recv, a).start()

                @pl.when(here)
                def _():
                    c = pltpu.make_async_copy(src.at[a], dst.at[me], loc.at[0])
                    c.start()
                    c.wait()

        def all_finish(src, dst, send, recv):
            for a in range(4):

                @pl.when(jnp.logical_not((a == y) & (z == x)))
                def _():
                    plane(src, dst, send, recv, a).wait_send()

        def all_receive(src, dst, send, recv):
            def step(i, carry):
                @pl.when(i != me)
                def _():
                    remote(src.at[0], dst.at[i], send.at[0], recv.at[i], sib).wait_recv()

                return carry

            lax.fori_loop(0, 16, step, 0)

        all_start(fc_ref, fc_all, s4, r4)

        def proj_copy(j):
            return remote(
                proj_ref.at[j], proj_all.at[y], s6.at[j], r6.at[y], device(z, 2 * k + j, k, x)
            )

        for j in range(2):
            here = (y == z) & (z == 2 * k + j)

            @pl.when(jnp.logical_not(here))
            def _():
                proj_copy(j).start()

            @pl.when(here)
            def _():
                c = pltpu.make_async_copy(proj_ref.at[j], proj_all.at[y], loc.at[1])
                c.start()
                c.wait()

        swap[3].wait_recv()
        for c in along:
            c.wait_recv()
        mix_mine[...] = (
            mix_ref[:, x, :, mine_at].astype(F32)
            + mix_got[x].astype(F32)
            + mix_far[0].astype(F32)
            + mix_far[1].astype(F32)
            + mix_far[2].astype(F32)
        ).astype(BF)
        vec_mine[...] = (
            vec_ref[:, x].astype(F32)
            + vec_far[0].astype(F32)
            + vec_far[1].astype(F32)
            + vec_far[2].astype(F32)
        ).astype(BF)
        all_start(mix_mine, mix_all, s3, r3)
        all_start(vec_mine, vec_all, s5, r5)
        for c in ones:
            c.wait_recv()
        one_out[...] = (
            one_ref[z].astype(F32)
            + one_far[0].astype(F32)
            + one_far[1].astype(F32)
            + one_far[2].astype(F32)
        )

        def proj_last(i):
            return remote(
                proj_sum.at[i], proj_out, s8.at[i], r8.at[0],
                device(y, z, x // 2, lax.rem(2 * x + i, 4)),
            )

        def proj_here(i):
            return (k == x // 2) & (x == lax.rem(2 * x + i, 4))

        holder = k == z // 2
        for a in range(4):

            @pl.when(holder & jnp.logical_not((a == y) & (z == y)))
            def _():
                remote(proj_ref.at[0], proj_all.at[a], s6.at[0], r6.at[a], sib).wait_recv()

        @pl.when(holder)
        def _():
            total = (
                proj_all[0].astype(F32)
                + proj_all[1].astype(F32)
                + proj_all[2].astype(F32)
                + proj_all[3].astype(F32)
            )
            for i in range(2):
                proj_sum[i] = total[24 * i : 24 * i + 24]

                @pl.when(jnp.logical_not(proj_here(i)))
                def _():
                    proj_last(i).start()

                @pl.when(proj_here(i))
                def _():
                    c = pltpu.make_async_copy(proj_sum.at[i], proj_out, loc.at[2])
                    c.start()
                    c.wait()

        def last_copy(i):
            return remote(
                out_send.at[i], rows_out.at[k], s7.at[i], r7.at[k], device(y, z, i // 4, i % 4)
            )

        def last_here(i):
            return k * 4 + x == i

        @pl.when(z == x)
        def _():
            all_receive(fc_ref, fc_all, s4, r4)
            all_receive(mix_mine, mix_all, s3, r3)
            all_receive(vec_mine, vec_all, s5, r5)

            def four(ref, b):
                return (
                    ref[b].astype(F32)
                    + ref[4 + b].astype(F32)
                    + ref[8 + b].astype(F32)
                    + ref[12 + b].astype(F32)
                )

            for b in range(4):
                m, f = four(mix_all, b), four(fc_all, b)
                for i in range(8):
                    rows = slice(6 * i, 6 * i + 6)
                    out_send[i, 0:6, 384 * b : 384 * b + 384] = m[rows]
                    out_send[i, 0:6, 1536 + 384 * b : 1920 + 384 * b] = f[rows]
            v = four(vec_all, 0) + four(vec_all, 1) + four(vec_all, 2) + four(vec_all, 3)
            for i in range(8):
                out_send[i, 0:6, 3072:3200] = v[6 * i : 6 * i + 6]
                out_send[i, 6:8, :] = jnp.zeros((2, wide), F32)
            for i in range(8):

                @pl.when(jnp.logical_not(last_here(i)))
                def _():
                    last_copy(i).start()

                @pl.when(last_here(i))
                def _():
                    c = pltpu.make_async_copy(out_send.at[i], rows_out.at[k], loc.at[3])
                    c.start()
                    c.wait()

        for j in range(2):

            @pl.when(jnp.logical_not((z == x) & (k == j)))
            def _():
                remote(out_send.at[0], rows_out.at[j], s7.at[0], r7.at[j], sib).wait_recv()

        @pl.when(jnp.logical_not((k == z // 2) & (x == (4 * k + x) // 2)))
        def _():
            remote(proj_sum.at[0], proj_out, s8.at[0], r8.at[0], sib).wait_recv()

        @pl.when(z == x)
        def _():
            for i in range(8):

                @pl.when(jnp.logical_not(last_here(i)))
                def _():
                    last_copy(i).wait_send()

        for i in range(2):

            @pl.when(holder & jnp.logical_not(proj_here(i)))
            def _():
                proj_last(i).wait_send()

        for j in range(2):

            @pl.when(jnp.logical_not((y == z) & (z == 2 * k + j)))
            def _():
                proj_copy(j).wait_send()

        all_finish(fc_ref, fc_all, s4, r4)
        all_finish(mix_mine, mix_all, s3, r3)
        all_finish(vec_mine, vec_all, s5, r5)
        for c in swap + along + ones:
            c.wait_send()

    return comm(
        kernel,
        [
            jax.ShapeDtypeStruct((128, 768), F32),
            jax.ShapeDtypeStruct((2, 8, wide), F32),
            jax.ShapeDtypeStruct((24, 768), F32),
        ],
        6,
        (3, 3, 4, 4, 3, 3, 3, 3, 4, 16, 4, 16, 4, 16, 2, 4, 8, 2, 2, 1, 4),
        (one, mix, vec, fc, proj),
        scratch=[
            pltpu.VMEM((3, 128, 768), BF),
            pltpu.VMEM((4, 4, 48, 384), BF),
            pltpu.VMEM((4, 4, 48, 384), BF),
            pltpu.VMEM((3, 4, 48, 384), BF),
            pltpu.VMEM((3, 4, 48, 128), BF),
            pltpu.VMEM((4, 48, 384), BF),
            pltpu.VMEM((4, 48, 128), BF),
            pltpu.VMEM((16, 48, 384), BF),
            pltpu.VMEM((16, 48, 384), BF),
            pltpu.VMEM((16, 48, 128), BF),
            pltpu.VMEM((4, 48, 768), BF),
            pltpu.VMEM((2, 24, 768), F32),
            pltpu.VMEM((8, 8, wide), F32),
        ],
        spaces=([VMEM] * 5, [VMEM] * 3),
        name="last_sums",
    )


def head_rows(matrix, head):
    row = lax.broadcasted_iota(jnp.int32, matrix.shape, 0)
    keep = (row >= 64 * head) & (row < 64 * head + 64)
    return jnp.where(keep, matrix, jnp.zeros_like(matrix))


def head_cols(matrix, head):
    col = lax.broadcasted_iota(jnp.int32, matrix.shape, 1)
    keep = (col >= 64 * head) & (col < 64 * head + 64)
    return jnp.where(keep, matrix, jnp.zeros_like(matrix))


def place(index):
    return (index // 128) * 256 + index % 128


def dot(a, b):
    return jnp.dot(a, b, preferred_element_type=F32)


def attend(query, kv_all):
    def kernel(q_ref, kv_ref, h_ref, ot_ref, lse_ref, qt, m_ref, l_ref):
        y, z, k, x = coords()
        q_t = q_ref[...].T
        for head in range(3):
            qt[head] = head_rows(q_t, head)
        m_ref[...] = jnp.full_like(m_ref, -1e30)
        l_ref[...] = jnp.zeros_like(l_ref)
        ot_ref[...] = jnp.zeros_like(ot_ref)

        def block(by, bk, masked):
            keys = kv_ref[by, bk, :, :192]
            values_t = kv_ref[by, bk, :, 192:].T
            if masked:
                key_at = place(lax.broadcasted_iota(jnp.int32, (512, 512), 0)) + 128 * bk
                query_at = place(lax.broadcasted_iota(jnp.int32, (512, 512), 1)) + 128 * k
                visible = query_at >= key_at
            for head in range(3):
                s = dot(keys, qt[head])
                if masked:
                    s = jnp.where(visible, s, -1e9)
                old = m_ref[head : head + 1]
                new = jnp.maximum(old, jnp.max(s, 0, keepdims=True))
                e = jnp.exp(s - new)
                scale = jnp.exp(old - new)
                m_ref[head : head + 1] = new
                l_ref[head : head + 1] = l_ref[head : head + 1] * scale + jnp.sum(
                    e, 0, keepdims=True
                )
                rows = slice(64 * head, 64 * head + 64)
                ot_ref[rows] = ot_ref[rows] * scale + dot(values_t[rows], e.astype(BF))

        def step(j, carry):
            block(j // 2, j % 2, False)
            return carry

        lax.fori_loop(0, 2 * y, step, 0)
        block(y, 0, True)
        block(y, 1, True)
        for head in range(3):
            rows = slice(64 * head, 64 * head + 64)
            total = l_ref[head : head + 1]
            ot_ref[rows] = ot_ref[rows] / total
            lse_ref[head : head + 1] = m_ref[head : head + 1] + jnp.log(total)
        h_ref[...] = ot_ref[...].T.astype(BF)

    return pl.pallas_call(
        kernel,
        out_shape=[
            jax.ShapeDtypeStruct((512, 192), BF),
            jax.ShapeDtypeStruct((192, 512), F32),
            jax.ShapeDtypeStruct((8, 512), F32),
        ],
        in_specs=[VMEM] * 2,
        out_specs=[VMEM] * 3,
        scratch_shapes=[
            pltpu.VMEM((3, 192, 512), BF),
            pltpu.VMEM((8, 512), F32),
            pltpu.VMEM((8, 512), F32),
        ],
        compiler_params=pltpu.CompilerParams(vmem_limit_bytes=LIMIT),
        name="attend",
    )(query, kv_all)


def attend_back(query, grad_heads, kv_all, out_t, lse):
    def kernel(q_ref, g_ref, kv_ref, ot_ref, lse_ref, dq_ref, dkv_ref, qt, gt, qm, gm, delta, dqt):
        y, z, k, x = coords()
        query_blk, grad_blk = q_ref[...], g_ref[...]
        q_t, g_t = query_blk.T, grad_blk.T
        for head in range(3):
            rows = slice(64 * head, 64 * head + 64)
            qt[head] = head_rows(q_t, head)
            gt[head] = head_rows(g_t, head)
            qm[head] = head_cols(query_blk, head)
            gm[head] = head_cols(grad_blk, head)
            delta[head : head + 1] = jnp.sum(
                g_t[rows].astype(F32) * ot_ref[rows], 0, keepdims=True
            )
        dqt[...] = jnp.zeros_like(dqt)

        def block(by, bk, masked):
            keys = kv_ref[by, bk, :, :192]
            values = kv_ref[by, bk, :, 192:]
            keys_t = keys.T
            if masked:
                key_at = place(lax.broadcasted_iota(jnp.int32, (512, 512), 0)) + 128 * bk
                query_at = place(lax.broadcasted_iota(jnp.int32, (512, 512), 1)) + 128 * k
                visible = query_at >= key_at
            dk = dv = None
            for head in range(3):
                s = dot(keys, qt[head])
                p = jnp.exp(s - lse_ref[head : head + 1])
                if masked:
                    p = jnp.where(visible, p, 0.0)
                dp = dot(values, gt[head])
                ds = (p * (dp - delta[head : head + 1])).astype(BF)
                pv = dot(p.astype(BF), gm[head])
                pk = dot(ds, qm[head])
                dv = pv if dv is None else dv + pv
                dk = pk if dk is None else dk + pk
                rows = slice(64 * head, 64 * head + 64)
                dqt[rows] += dot(keys_t[rows], ds)
            dkv_ref[by, bk, :, :192] = dk.astype(BF)
            dkv_ref[by, bk, :, 192:] = dv.astype(BF)

        def step(j, carry):
            block(j // 2, j % 2, False)
            return carry

        def clear(j, carry):
            dkv_ref[j // 2, j % 2] = jnp.zeros((512, 384), BF)
            return carry

        lax.fori_loop(0, 2 * y, step, 0)
        block(y, 0, True)
        block(y, 1, True)
        lax.fori_loop(2 * y + 2, 8, clear, 0)
        dq_ref[...] = (dqt[...].T * 0.125).astype(BF)

    return pl.pallas_call(
        kernel,
        out_shape=[
            jax.ShapeDtypeStruct((512, 192), BF),
            jax.ShapeDtypeStruct((4, 2, 512, 384), BF),
        ],
        in_specs=[VMEM] * 5,
        out_specs=[VMEM] * 2,
        scratch_shapes=[
            pltpu.VMEM((3, 192, 512), BF),
            pltpu.VMEM((3, 192, 512), BF),
            pltpu.VMEM((3, 512, 192), BF),
            pltpu.VMEM((3, 512, 192), BF),
            pltpu.VMEM((8, 512), F32),
            pltpu.VMEM((192, 512), F32),
        ],
        compiler_params=pltpu.CompilerParams(vmem_limit_bytes=LIMIT),
        name="attend_back",
    )(query, grad_heads, kv_all, out_t, lse)


def normalize(rows):
    centered = rows - jnp.mean(rows, -1, keepdims=True)
    inverse = lax.rsqrt(jnp.mean(centered * centered, -1, keepdims=True) + EPSILON)
    return centered * inverse, inverse


def normalize_back(normed, inverse, gain, grad):
    scaled = grad * gain
    return inverse * (
        scaled
        - jnp.mean(scaled, -1, keepdims=True)
        - normed * jnp.mean(scaled * normed, -1, keepdims=True)
    )


def gelu_tanh(values):
    return (
        0.5
        * values
        * (1.0 + jnp.tanh(0.7978845608028654 * (values + 0.044715 * values * values * values)))
    )


def adam_update(weight, moment_one, moment_two, gradient, rate, decay):
    new_one = BETA_ONE * moment_one + (1.0 - BETA_ONE) * gradient
    new_two = BETA_TWO * moment_two + (1.0 - BETA_TWO) * gradient * gradient
    fix_one = 1.0 - BETA_ONE**STEP
    fix_two = 1.0 - BETA_TWO**STEP
    direction = new_one / fix_one / (jnp.sqrt(new_two / fix_two) + ADAM_EPSILON)
    return (weight - rate * (direction + decay * weight), new_one, new_two)


def shards(
    tokens,
    cotangent,
    w_qkv,
    qkv_m,
    qkv_v,
    w_out,
    out_m,
    out_v,
    w_fc,
    fc_m,
    fc_v,
    w_proj,
    proj_m,
    proj_v,
    vectors,
    vec_m,
    vec_v,
):
    y, z, k, x = coords()
    wq, fc_part, out_part, proj_part, x_group = first_gather(
        w_qkv, w_fc, w_out, w_proj, vectors, tokens[0]
    )
    wq = wq.reshape(768, 640)
    vec = wq[:, 576:588].astype(F32)
    wq = wq[:, :576]
    gain_one, shift_one, q_bias, v_bias = vec[:, 0], vec[:, 1], vec[:, 2], vec[:, 3]
    out_bias, gain_two, shift_two, proj_bias = vec[:, 4], vec[:, 5], vec[:, 6], vec[:, 7]
    fc_bias = lax.dynamic_slice(vec[:, 8:].T.reshape(-1), ((2 * z + k) * 384,), (384,))
    bias = jnp.concatenate(
        [
            lax.dynamic_slice(q_bias, (192 * z,), (192,)),
            jnp.zeros((192,), F32),
            lax.dynamic_slice(v_bias, (192 * z,), (192,)),
        ]
    )
    x_core = lax.dynamic_index_in_dim(x_group, k, 0, False).reshape(512, 768).astype(F32)
    normed_core, _ = normalize(x_core)
    act_one = (normed_core * gain_one + shift_one).astype(BF)
    mixed = (dot(act_one, wq) + bias).astype(BF)
    query = mixed[:, :192] * jnp.asarray(0.125, BF)
    kv_all, dy_group, wf, wo, wp = kv_gather(
        mixed[:, 192:], cotangent[0], fc_part, out_part, proj_part
    )
    wf = wf.reshape(768, 384)
    wo = jnp.concatenate([wo[0].reshape(768, 384), wo[1].reshape(768, 384)], 1)
    wp = wp.reshape(384, 768)
    heads, out_t, lse = attend(query, kv_all)
    heads_all = heads_gather(heads)
    heads_all = jnp.concatenate([heads_all[i].reshape(1024, 192) for i in range(4)], 1)
    x_two = x_group.reshape(1024, 768).astype(F32) + dot(heads_all, wo) + out_bias
    normed_two, inverse_two = normalize(x_two)
    act_two = (normed_two * gain_two + shift_two).astype(BF)
    hidden = dot(act_two, wf) + fc_bias
    gelu_out, gelu_back = jax.vjp(gelu_tanh, hidden)
    act_three = gelu_out.astype(BF)
    dy = dy_group.reshape(1024, 768)
    result_part = dot(act_three, wp).astype(BF)
    grad_w_proj = dot(act_three.T, dy)
    grad_hidden = gelu_back(dot(dy, wp.T))[0].astype(BF)
    grad_w_fc = dot(act_two.T, grad_hidden)
    grad_fc_bias = jnp.sum(grad_hidden.astype(F32), 0)
    norm_part = dot(grad_hidden, wf.T).astype(BF)
    sums = group_sum(
        jnp.stack([norm_part, result_part]).reshape(2, 2, 4, 128, 768), 8, "ffn_sum"
    )

    def own(group):
        return lax.dynamic_slice(group, ((k * 4 + z) * 128, 0), (128, group.shape[1]))

    own_x_two = own(x_two)
    output = own_x_two + sums[1] + proj_bias
    own_normed, own_inverse = normalize(own_x_two)
    grad_output = cotangent[0].astype(F32)
    grad_norm_two = sums[0]
    grad_x_two = grad_output + normalize_back(own_normed, own_inverse, gain_two, grad_norm_two)
    grad_branch = grad_x_two.astype(BF)
    branch_core = z_gather(grad_branch).reshape(512, 768)
    wo_rows = lax.dynamic_slice(wo, (192 * z, 0), (192, 768))
    grad_heads = dot(branch_core, wo_rows.T).astype(BF)
    grad_query, kv_parts = attend_back(query, grad_heads, kv_all, out_t, lse)
    grad_kv, fc_sum, proj_sum = kv_sum(
        kv_parts,
        grad_w_fc.astype(BF).reshape(4, 4, 48, 384),
        grad_w_proj.astype(BF).reshape(2, 4, 48, 768),
    )
    grad_mixed = jnp.concatenate([grad_query, grad_kv.astype(BF)], 1)
    branch_cols = lax.dynamic_slice(branch_core, (0, 192 * z), (512, 192))
    heads_core = lax.dynamic_index_in_dim(heads_all.reshape(2, 512, 768), k, 0, False)
    left = jnp.concatenate([act_one, heads_core], 0)
    gap = jnp.zeros((512, 96), BF)
    room = jnp.zeros((512, 288), BF)
    right = jnp.concatenate(
        [
            jnp.concatenate([grad_mixed[:, :288], gap, grad_mixed[:, 288:], gap], 1),
            jnp.concatenate([room, branch_cols[:, :96], room, branch_cols[:, 96:]], 1),
        ],
        0,
    )
    grad_mix = dot(left.T, right).astype(BF)
    one_part = dot(grad_mixed, wq.T)

    def spread(piece, at, size):
        return lax.dynamic_update_slice(jnp.zeros((size,), F32), piece, (at,))

    mixed_sums = jnp.sum(grad_mixed.astype(F32), 0)
    columns = jnp.stack(
        [
            jnp.sum(one_part * normed_core, 0),
            jnp.sum(one_part, 0),
            spread(mixed_sums[:192], 192 * z, 768),
            spread(mixed_sums[384:], 192 * z, 768),
            jnp.sum(grad_branch.astype(F32), 0),
            jnp.sum(grad_norm_two * own_normed, 0),
            jnp.sum(grad_norm_two, 0),
            jnp.sum(grad_output, 0),
        ]
        + list(spread(grad_fc_bias, (2 * z + k) * 384, 3072).reshape(4, 768)),
        1,
    )
    grad_vec = jnp.pad(columns, ((0, 0), (0, 116))).astype(BF)
    grad_norm_one, last_rows, sum_proj = last_sums(
        one_part.astype(BF).reshape(4, 128, 768),
        grad_mix.reshape(4, 4, 48, 768),
        grad_vec.reshape(4, 4, 48, 128),
        fc_sum,
        proj_sum,
    )
    normed_one, inverse_one = normalize(tokens[0].astype(F32))
    grad_inputs = grad_x_two + normalize_back(normed_one, inverse_one, gain_one, grad_norm_one)
    last_rows = last_rows[:, :6]
    mix_rows = last_rows[:, :, :1536].reshape(2, 6, 4, 384)
    sum_qkv = (
        mix_rows[..., :288]
        .transpose(1, 2, 0, 3)
        .reshape(6, 4, 3, 192)
        .transpose(0, 2, 1, 3)
        .reshape(6, 2304)
    )
    sum_out = mix_rows[..., 288:].transpose(1, 2, 0, 3).reshape(6, 768)
    sum_fc = last_rows[:, :, 1536:3072].reshape(2, 6, 4, 384).transpose(1, 2, 0, 3).reshape(6, 3072)
    sum_vec = last_rows[0, :, 3072:3084] + last_rows[1, :, 3072:3084]
    new_qkv = adam_update(w_qkv, qkv_m, qkv_v, sum_qkv, 0.1, 0.1)
    new_out = adam_update(w_out, out_m, out_v, sum_out, 0.3, 0.1)
    new_fc = adam_update(w_fc, fc_m, fc_v, sum_fc, 0.05, 0.1)
    new_proj = adam_update(w_proj, proj_m, proj_v, sum_proj, 0.03, 0.1)
    new_vec = adam_update(vectors, vec_m, vec_v, sum_vec, 0.5, 0.0)
    return (output[None], grad_inputs[None], *new_qkv, *new_out, *new_fc, *new_proj, *new_vec)


def solution(mesh):
    split = P("fsdp", "ctx", None)
    rows = P(("ctx", "fsdp"), None)
    return jax.shard_map(
        shards,
        mesh=mesh,
        in_specs=(split, split) + (rows,) * 15,
        out_specs=(split, split) + (rows,) * 15,
        check_vma=False,
    )
```

```python
import jax
import jax.numpy as jnp
from jax import lax
from jax.experimental import pallas as pl
from jax.experimental.pallas import tpu as pltpu
from jax.sharding import PartitionSpec as P

STEP = 10
EPSILON = 1e-05
BETA_ONE = 0.9
BETA_TWO = 0.999
ADAM_EPSILON = 1e-08
MESH = pl.DeviceIdType.MESH
BF = jnp.bfloat16
F32 = jnp.float32
ANY = pl.BlockSpec(memory_space=pl.ANY)
VMEM = pl.BlockSpec(memory_space=pltpu.VMEM)
LIMIT = 56 * 1024 * 1024


def coords():
    c = lax.axis_index("ctx")
    return c // 8, (c // 2) % 4, c % 2, lax.axis_index("fsdp")


def device(y, z, k, x):
    return ((y * 4 + z) * 2 + k, x)


def ring(v, step):
    return lax.rem(v + step, 4)


def greet(devices):
    barrier = pltpu.get_barrier_semaphore()
    for one in devices:
        pl.semaphore_signal(barrier, inc=1, device_id=one, device_id_type=MESH)
    pl.semaphore_wait(barrier, len(devices))


def remote(src, dst, send, recv, to):
    return pltpu.make_async_remote_copy(
        src, dst, send, recv, device_id=to, device_id_type=MESH
    )


def comm(kernel, outs, cid, sems, args, scratch=(), spaces=None, name=None):
    return pl.pallas_call(
        kernel,
        out_shape=outs,
        in_specs=[ANY] * len(args) if spaces is None else spaces[0],
        out_specs=[ANY] * len(outs) if spaces is None else spaces[1],
        scratch_shapes=list(scratch) + [pltpu.SemaphoreType.DMA((n,)) for n in sems],
        compiler_params=pltpu.CompilerParams(
            collective_id=cid, has_side_effects=True, vmem_limit_bytes=LIMIT
        ),
        name=name,
    )(*args)


def first_gather(w_qkv, w_fc, w_out, w_proj, vectors, rows):
    width = 4736

    def kernel(
        wq_ref, wf_ref, wo_ref, wp_ref, wv_ref, r_ref,
        q_out, f_out, o_out, p_out, ro_ref,
        wide, packed, got, fc48, qkv48, out48, proj_wide, q_send, f_send, o_send, p_send,
        ms, mr, fs, fr, s1, r1, s2, r2, ps, pr, xs_s, xs_r, xf_s, xf_r, rs, rr, cs, cr, loc,
    ):
        y, z, k, x = coords()
        me = y * 4 + z
        sib = device(y, z, 1 - k, x)
        steps = (1, 2, 3)
        greet(
            [sib]
            + [device(y, z, k, ring(x, d)) for d in steps]
            + [
                device(ring(y, a), ring(z, b), k, x)
                for a in range(4)
                for b in range(4)
                if (a, b) != (0, 0)
            ]
        )
        own_r = pltpu.make_async_copy(r_ref, ro_ref.at[k, z], loc.at[0])
        own_r.start()
        row_copies = []
        for d in steps:
            c = remote(
                r_ref, ro_ref.at[k, z], rs.at[d], rr.at[d], device(y, ring(z, d), k, x)
            )
            row_copies.append(c)
        wide[...] = jnp.zeros_like(wide)
        wide[0:6, 0:3072] = wf_ref[...]
        wide[6:12, 0:2304] = wq_ref[...]
        wide[6:12, 2304:3072] = wo_ref[...]
        wide[0:12, 3072:3840] = wp_ref[0:12]
        wide[0:12, 3840:4608] = wp_ref[12:24]
        wide[0:6, 4608:4620] = wv_ref[...]
        t = k * 4 + x
        packed[...] = wide[...].astype(BF)
        got[t] = packed[...]
        message = []
        for d in steps:
            c = remote(packed, got.at[t], ms.at[d], mr.at[d], device(y, z, k, ring(x, d)))
            c.start()
            message.append(c)
        c = remote(packed, got.at[t], fs.at[0], fr.at[0], sib)
        c.start()
        forward = [c]
        for c in row_copies:
            c.start()
        c = remote(r_ref, ro_ref.at[k, z], cs.at[0], cr.at[0], sib)
        c.start()
        row_forward = [c]
        for d in steps:
            message[d - 1].wait_recv()
            src = k * 4 + ring(x, 4 - d)
            f = remote(got.at[src], got.at[src], fs.at[d], fr.at[d], sib)
            f.start()
            forward.append(f)
        for f in forward:
            f.wait_recv()
        for i in range(8):
            piece = got[i].astype(F32)
            at = slice(6 * i, 6 * i + 6)
            fc48[at] = piece[0:6, 0:3072]
            qkv48[at] = piece[6:12, 0:2304]
            out48[at, 0:768] = piece[6:12, 2304:3072]
            out48[at, 768:896] = piece[0:6, 4608:4736]
            proj_wide[24 * i : 24 * i + 12] = piece[0:12, 3072:3840]
            proj_wide[24 * i + 12 : 24 * i + 24] = piece[0:12, 3840:4608]
        for j in range(4):
            q_send[j, :, 0:192] = qkv48[:, 192 * j : 192 * j + 192].astype(BF)
            q_send[j, :, 192:384] = qkv48[:, 768 + 192 * j : 960 + 192 * j].astype(BF)
            q_send[j, :, 384:576] = qkv48[:, 1536 + 192 * j : 1728 + 192 * j].astype(BF)
            q_send[j, :, 576:640] = out48[:, 768:832].astype(BF)
        for j in range(8):
            f_send[j] = fc48[:, 384 * j : 384 * j + 384].astype(BF)
        o_send[0] = out48[:, 0:384].astype(BF)
        o_send[1] = out48[:, 384:768].astype(BF)
        p_send[...] = proj_wide[...].astype(BF)

        group = pl.ds(pl.multiple_of(16 * jnp.minimum(x, 2), 16), 16)

        def to_of(m):
            return ring(y, m // 4), ring(z, m % 4)

        def q_copy(m):
            ty, tz = to_of(m)
            return remote(
                q_send.at[tz, group], q_out.at[me, group], s1.at[m], r1.at[m],
                device(ty, tz, k, x),
            )

        def f_copy(m):
            ty, tz = to_of(m)
            return remote(
                f_send.at[tz * 2 + k], f_out.at[me], s2.at[m], r2.at[m], device(ty, tz, k, x)
            )

        def o_copy(m):
            ty, tz = to_of(m)
            return remote(o_send.at[k], o_out.at[me], s2.at[m], r2.at[m], device(ty, tz, k, x))

        def p_copy(a):
            return remote(
                p_send, p_out.at[z % 2], ps.at[a], pr.at[z % 2], device(ring(y, a), y, k, x)
            )

        def each(copy, what):
            def step(m, carry):
                what(copy(m))
                return carry

            lax.fori_loop(1, 16, step, 0)

        start = lambda c: c.start()
        finish = lambda c: c.wait()

        @pl.when(x < 3)
        def _():
            each(q_copy, start)
            c = pltpu.make_async_copy(q_send.at[z, group], q_out.at[me, group], loc.at[1])
            c.start()
            c.wait()

        @pl.when(x == 1)
        def _():
            each(f_copy, start)
            c = pltpu.make_async_copy(f_send.at[z * 2 + k], f_out.at[me], loc.at[2])
            c.start()
            c.wait()

        @pl.when(x == 2)
        def _():
            each(o_copy, start)
            c = pltpu.make_async_copy(o_send.at[k], o_out.at[me], loc.at[2])
            c.start()
            c.wait()

        @pl.when((x == 3) & (k == z // 2))
        def _():
            for a in range(1, 4):
                p_copy(a).start()

            @pl.when(z != y)
            def _():
                p_copy(0).start()

            @pl.when(z == y)
            def _():
                c = pltpu.make_async_copy(p_send, p_out.at[z % 2], loc.at[2])
                c.start()
                c.wait()

        half = pl.ds(8 * k, 8)
        other_half = pl.ds(8 * (1 - k), 8)

        def rows_of(plane):
            return pl.ds(pl.multiple_of(16 * plane, 16), 16)

        @pl.when(x < 3)
        def _():
            each(q_copy, finish)
            for d in steps:
                remote(
                    q_out.at[half, group], q_out.at[half, group], xs_s.at[d], xs_r.at[x],
                    device(y, z, k, ring(x, d)),
                ).start()

        def pass_on(a):
            return remote(
                q_out.at[half, rows_of(a)], q_out.at[half, rows_of(a)], xf_s.at[a], xf_r.at[a], sib
            )

        for a in range(3):

            @pl.when(x != a)
            def _():
                remote(
                    q_out.at[half, rows_of(a)], q_out.at[half, rows_of(a)], xs_s.at[0],
                    xs_r.at[a], sib,
                ).wait_recv()
                pass_on(a).start()

        for d in steps:
            row_copies[d - 1].wait_recv()
            src = ring(z, 4 - d)
            f = remote(ro_ref.at[k, src], ro_ref.at[k, src], cs.at[d], cr.at[d], sib)
            f.start()
            row_forward.append(f)

        @pl.when(x == 1)
        def _():
            each(f_copy, finish)

        @pl.when(x == 2)
        def _():
            each(o_copy, finish)

        @pl.when((x == 3) & (k == z // 2))
        def _():
            for a in range(1, 4):
                p_copy(a).wait_send()

            @pl.when(z != y)
            def _():
                p_copy(0).wait_send()

        for j in range(2):
            @pl.when((x == 3) & jnp.logical_not((y == z) & (z == 2 * k + j)))
            def _():
                remote(p_send, p_out.at[j], ps.at[0], pr.at[j], sib).wait_recv()

        @pl.when(x < 3)
        def _():
            for d in steps:
                remote(
                    q_out.at[half, group], q_out.at[half, group], xs_s.at[d], xs_r.at[x],
                    device(y, z, k, ring(x, d)),
                ).wait_send()

        for a in range(3):

            @pl.when(x != a)
            def _():
                pass_on(a).wait_send()
                remote(
                    q_out.at[other_half, rows_of(a)], q_out.at[other_half, rows_of(a)],
                    xf_s.at[a], xf_r.at[a], sib,
                ).wait_recv()

        for c in message + row_copies + forward:
            c.wait_send()
        for c in row_forward:
            c.wait()
        own_r.wait()

    return comm(
        kernel,
        [
            jax.ShapeDtypeStruct((16, 48, 640), BF),
            jax.ShapeDtypeStruct((16, 48, 384), BF),
            jax.ShapeDtypeStruct((16, 48, 384), BF),
            jax.ShapeDtypeStruct((2, 192, 768), BF),
            jax.ShapeDtypeStruct((2, 4) + rows.shape, BF),
        ],
        0,
        (4, 4, 4, 4, 16, 16, 16, 16, 4, 2, 4, 4, 4, 4, 4, 4, 4, 4, 3),
        (w_qkv, w_fc, w_out, w_proj, vectors, rows),
        scratch=[
            pltpu.VMEM((16, width), F32),
            pltpu.VMEM((16, width), BF),
            pltpu.VMEM((8, 16, width), BF),
            pltpu.VMEM((48, 3072), F32),
            pltpu.VMEM((48, 2304), F32),
            pltpu.VMEM((48, 896), F32),
            pltpu.VMEM((192, 768), F32),
            pltpu.VMEM((4, 48, 640), BF),
            pltpu.VMEM((8, 48, 384), BF),
            pltpu.VMEM((2, 48, 384), BF),
            pltpu.VMEM((192, 768), BF),
        ],
        spaces=([VMEM] * 5 + [ANY], [ANY] * 5),
        name="first_gather",
    )


def group_sum(parts, cid, name):
    n = parts.shape[0]
    rows, cols = parts.shape[3:]

    def kernel(p_ref, o_ref, got, mine, far, cs, cr, zs, zr):
        y, z, k, x = coords()
        sib = device(y, z, 1 - k, x)
        ring_z = [(d, ring(z, d)) for d in (1, 2, 3)]
        greet([sib] + [device(y, b, k, x) for _, b in ring_z])
        order = ring_z + [(0, z)]
        pairs = []
        for i in range(n):
            for d, b in order:
                c = remote(
                    p_ref.at[i, 1 - k, b], got.at[i, b], cs.at[4 * i + d], cr.at[4 * i + d], sib
                )
                c.start()
                pairs.append(c)
        copies = []
        for i in range(n):
            for d, b in order:
                pairs[4 * i + (d - 1) % 4].wait_recv()
                total = p_ref[i, k, b].astype(F32) + got[i, b].astype(F32)
                if d == 0:
                    o_ref[i] = total
                else:
                    mine[i, d - 1] = total.astype(BF)
                    c = remote(
                        mine.at[i, d - 1],
                        far.at[i, d - 1],
                        zs.at[3 * i + d - 1],
                        zr.at[3 * i + d - 1],
                        device(y, b, k, x),
                    )
                    c.start()
                    copies.append(c)
        for i in range(n):
            for d in range(3):
                copies[3 * i + d].wait_recv()
            o_ref[i] = (
                o_ref[i] + far[i, 0].astype(F32) + far[i, 1].astype(F32) + far[i, 2].astype(F32)
            )
        for c in copies:
            c.wait_send()
        for c in pairs:
            c.wait_send()

    return comm(
        kernel,
        [jax.ShapeDtypeStruct((n, rows, cols), F32)],
        cid,
        (4 * n, 4 * n, 3 * n, 3 * n),
        (parts,),
        scratch=[
            pltpu.VMEM((n, 4, rows, cols), BF),
            pltpu.VMEM((n, 3, rows, cols), BF),
            pltpu.VMEM((n, 3, rows, cols), BF),
        ],
        spaces=([VMEM], [VMEM]),
        name=name,
    )[0]


def last_sums(one, mix, vec, fc, proj):
    wide = 3200

    def kernel(
        one_ref, mix_ref, vec_ref, fc_ref, proj_ref, one_out, rows_out, proj_out,
        one_far, mix_got, mix_sum, mix_far, vec_far, mix_mine, vec_mine,
        mix_all, fc_all, vec_all, proj_all, proj_sum, out_send,
        zs, zr, cs, cr, s1, r1, s2, r2, s3, r3, s4, r4, s5, r5, s6, r6, s7, r7, s8, r8, loc,
    ):
        y, z, k, x = coords()
        me = y * 4 + z
        sib = device(y, z, 1 - k, x)
        steps = (1, 2, 3)
        greet(
            [sib]
            + [device(y, z, j, ring(x, d)) for d in steps for j in (k, 1 - k)]
            + [
                device(ring(y, a), ring(z, b), k, x)
                for a in range(4)
                for b in range(4)
                if (a, b) != (0, 0)
            ]
        )
        mine_at = pl.ds(pl.multiple_of(384 * k, 128), 384)
        other_at = pl.ds(pl.multiple_of(384 * (1 - k), 128), 384)
        swap = []
        for d in (1, 2, 3, 0):
            b = ring(x, d)
            c = remote(mix_ref.at[:, b, :, other_at], mix_got.at[b], cs.at[d], cr.at[d], sib)
            c.start()
            swap.append(c)
        along = []
        for d in steps:
            b = ring(x, d)
            to = device(y, z, k, b)
            c = remote(vec_ref.at[:, b], vec_far.at[d - 1], s2.at[d - 1], r2.at[d - 1], to)
            c.start()
            along.append(c)
            swap[d - 1].wait_recv()
            mix_sum[d] = (
                mix_ref[:, b, :, mine_at].astype(F32) + mix_got[b].astype(F32)
            ).astype(BF)
            c = remote(mix_sum.at[d], mix_far.at[d - 1], s1.at[d - 1], r1.at[d - 1], to)
            c.start()
            along.append(c)
        ones = []
        for d in steps:
            c = remote(
                one_ref.at[ring(z, d)], one_far.at[d - 1], zs.at[d - 1], zr.at[d - 1],
                device(y, ring(z, d), k, x),
            )
            c.start()
            ones.append(c)

        def plane(src, dst, send, recv, a):
            return remote(src.at[a], dst.at[me], send.at[a], recv.at[me], device(a, x, k, x))

        def all_start(src, dst, send, recv):
            for a in range(4):
                here = (a == y) & (z == x)

                @pl.when(jnp.logical_not(here))
                def _():
                    plane(src, dst, send, recv, a).start()

                @pl.when(here)
                def _():
                    c = pltpu.make_async_copy(src.at[a], dst.at[me], loc.at[0])
                    c.start()
                    c.wait()

        def all_finish(src, dst, send, recv):
            for a in range(4):

                @pl.when(jnp.logical_not((a == y) & (z == x)))
                def _():
                    plane(src, dst, send, recv, a).wait_send()

        def all_receive(src, dst, send, recv):
            def step(i, carry):
                @pl.when(i != me)
                def _():
                    remote(src.at[0], dst.at[i], send.at[0], recv.at[i], sib).wait_recv()

                return carry

            lax.fori_loop(0, 16, step, 0)

        all_start(fc_ref, fc_all, s4, r4)

        def proj_copy(j):
            return remote(
                proj_ref.at[j], proj_all.at[y], s6.at[j], r6.at[y], device(z, 2 * k + j, k, x)
            )

        for j in range(2):
            here = (y == z) & (z == 2 * k + j)

            @pl.when(jnp.logical_not(here))
            def _():
                proj_copy(j).start()

            @pl.when(here)
            def _():
                c = pltpu.make_async_copy(proj_ref.at[j], proj_all.at[y], loc.at[1])
                c.start()
                c.wait()

        swap[3].wait_recv()
        for c in along:
            c.wait_recv()
        mix_mine[...] = (
            mix_ref[:, x, :, mine_at].astype(F32)
            + mix_got[x].astype(F32)
            + mix_far[0].astype(F32)
            + mix_far[1].astype(F32)
            + mix_far[2].astype(F32)
        ).astype(BF)
        vec_mine[...] = (
            vec_ref[:, x].astype(F32)
            + vec_far[0].astype(F32)
            + vec_far[1].astype(F32)
            + vec_far[2].astype(F32)
        ).astype(BF)
        all_start(mix_mine, mix_all, s3, r3)
        all_start(vec_mine, vec_all, s5, r5)
        for c in ones:
            c.wait_recv()
        one_out[...] = (
            one_ref[z].astype(F32)
            + one_far[0].astype(F32)
            + one_far[1].astype(F32)
            + one_far[2].astype(F32)
        )

        def proj_last(i):
            return remote(
                proj_sum.at[i], proj_out, s8.at[i], r8.at[0],
                device(y, z, x // 2, lax.rem(2 * x + i, 4)),
            )

        def proj_here(i):
            return (k == x // 2) & (x == lax.rem(2 * x + i, 4))

        holder = k == z // 2
        for a in range(4):

            @pl.when(holder & jnp.logical_not((a == y) & (z == y)))
            def _():
                remote(proj_ref.at[0], proj_all.at[a], s6.at[0], r6.at[a], sib).wait_recv()

        @pl.when(holder)
        def _():
            total = (
                proj_all[0].astype(F32)
                + proj_all[1].astype(F32)
                + proj_all[2].astype(F32)
                + proj_all[3].astype(F32)
            )
            for i in range(2):
                proj_sum[i] = total[24 * i : 24 * i + 24]

                @pl.when(jnp.logical_not(proj_here(i)))
                def _():
                    proj_last(i).start()

                @pl.when(proj_here(i))
                def _():
                    c = pltpu.make_async_copy(proj_sum.at[i], proj_out, loc.at[2])
                    c.start()
                    c.wait()

        def last_copy(i):
            return remote(
                out_send.at[i], rows_out.at[k], s7.at[i], r7.at[k], device(y, z, i // 4, i % 4)
            )

        def last_here(i):
            return k * 4 + x == i

        @pl.when(z == x)
        def _():
            all_receive(fc_ref, fc_all, s4, r4)
            all_receive(mix_mine, mix_all, s3, r3)
            all_receive(vec_mine, vec_all, s5, r5)

            def four(ref, b):
                return (
                    ref[b].astype(F32)
                    + ref[4 + b].astype(F32)
                    + ref[8 + b].astype(F32)
                    + ref[12 + b].astype(F32)
                )

            for b in range(4):
                m, f = four(mix_all, b), four(fc_all, b)
                for i in range(8):
                    rows = slice(6 * i, 6 * i + 6)
                    out_send[i, 0:6, 384 * b : 384 * b + 384] = m[rows]
                    out_send[i, 0:6, 1536 + 384 * b : 1920 + 384 * b] = f[rows]
            v = four(vec_all, 0) + four(vec_all, 1) + four(vec_all, 2) + four(vec_all, 3)
            for i in range(8):
                out_send[i, 0:6, 3072:3200] = v[6 * i : 6 * i + 6]
                out_send[i, 6:8, :] = jnp.zeros((2, wide), F32)
            for i in range(8):

                @pl.when(jnp.logical_not(last_here(i)))
                def _():
                    last_copy(i).start()

                @pl.when(last_here(i))
                def _():
                    c = pltpu.make_async_copy(out_send.at[i], rows_out.at[k], loc.at[3])
                    c.start()
                    c.wait()

        for j in range(2):

            @pl.when(jnp.logical_not((z == x) & (k == j)))
            def _():
                remote(out_send.at[0], rows_out.at[j], s7.at[0], r7.at[j], sib).wait_recv()

        @pl.when(jnp.logical_not((k == z // 2) & (x == (4 * k + x) // 2)))
        def _():
            remote(proj_sum.at[0], proj_out, s8.at[0], r8.at[0], sib).wait_recv()

        @pl.when(z == x)
        def _():
            for i in range(8):

                @pl.when(jnp.logical_not(last_here(i)))
                def _():
                    last_copy(i).wait_send()

        for i in range(2):

            @pl.when(holder & jnp.logical_not(proj_here(i)))
            def _():
                proj_last(i).wait_send()

        for j in range(2):

            @pl.when(jnp.logical_not((y == z) & (z == 2 * k + j)))
            def _():
                proj_copy(j).wait_send()

        all_finish(fc_ref, fc_all, s4, r4)
        all_finish(mix_mine, mix_all, s3, r3)
        all_finish(vec_mine, vec_all, s5, r5)
        for c in swap + along + ones:
            c.wait_send()

    return comm(
        kernel,
        [
            jax.ShapeDtypeStruct((128, 768), F32),
            jax.ShapeDtypeStruct((2, 8, wide), F32),
            jax.ShapeDtypeStruct((24, 768), F32),
        ],
        6,
        (3, 3, 4, 4, 3, 3, 3, 3, 4, 16, 4, 16, 4, 16, 2, 4, 8, 2, 2, 1, 4),
        (one, mix, vec, fc, proj),
        scratch=[
            pltpu.VMEM((3, 128, 768), BF),
            pltpu.VMEM((4, 4, 48, 384), BF),
            pltpu.VMEM((4, 4, 48, 384), BF),
            pltpu.VMEM((3, 4, 48, 384), BF),
            pltpu.VMEM((3, 4, 48, 128), BF),
            pltpu.VMEM((4, 48, 384), BF),
            pltpu.VMEM((4, 48, 128), BF),
            pltpu.VMEM((16, 48, 384), BF),
            pltpu.VMEM((16, 48, 384), BF),
            pltpu.VMEM((16, 48, 128), BF),
            pltpu.VMEM((4, 48, 768), BF),
            pltpu.VMEM((2, 24, 768), F32),
            pltpu.VMEM((8, 8, wide), F32),
        ],
        spaces=([VMEM] * 5, [VMEM] * 3),
        name="last_sums",
    )


def head_rows(matrix, head):
    row = lax.broadcasted_iota(jnp.int32, matrix.shape, 0)
    keep = (row >= 64 * head) & (row < 64 * head + 64)
    return jnp.where(keep, matrix, jnp.zeros_like(matrix))


def head_cols(matrix, head):
    col = lax.broadcasted_iota(jnp.int32, matrix.shape, 1)
    keep = (col >= 64 * head) & (col < 64 * head + 64)
    return jnp.where(keep, matrix, jnp.zeros_like(matrix))


def place(index):
    return (index // 128) * 256 + index % 128


def dot(a, b):
    return jnp.dot(a, b, preferred_element_type=F32)


def attend(query, kv, rows, fc, out, proj):
    def kernel(
        q_ref, v_ref, r_ref, f_ref, o_ref, p_ref,
        ho_ref, ot_ref, lse_ref, vo_ref, ro_ref, fo_ref, oo_ref, po_ref,
        qt, m_ref, l_ref, h_buf,
        vs, vr, rs, rr, cs, cr, ds, dr, ws, wr, os, orr, hs, hr, gs, gr, loc,
    ):
        y, z, k, x = coords()
        sib = device(y, z, 1 - k, x)
        steps = (1, 2, 3)
        greet(
            [sib]
            + [device(ring(y, d), z, k, x) for d in steps]
            + [device(y, ring(z, d), k, x) for d in steps]
            + [device(y, z, k, ring(x, d)) for d in steps]
        )

        def kv_copy(d):
            return remote(
                v_ref, vo_ref.at[y, k], vs.at[d], vr.at[d], device(ring(y, d), z, k, x)
            )

        for d in steps:

            @pl.when(y + d < 4)
            def _():
                kv_copy(d).start()

        swap = remote(v_ref, vo_ref.at[y, k], cs.at[0], cr.at[0], sib)
        swap.start()
        vo_ref[y, k] = v_ref[...]
        own_r = pltpu.make_async_copy(r_ref, ro_ref.at[k, z], loc.at[0])
        own_r.start()
        row_copies = []
        for d in steps:
            c = remote(
                r_ref, ro_ref.at[k, z], rs.at[d], rr.at[d], device(y, ring(z, d), k, x)
            )
            c.start()
            row_copies.append(c)
        row_first = remote(r_ref, ro_ref.at[k, z], ds.at[0], dr.at[0], sib)
        row_first.start()

        weights = ((1, f_ref, fo_ref), (2, o_ref, oo_ref.at[k]), (3, p_ref, po_ref))

        def weight_copy(a, d):
            _, src, dst = weights[a - 1]
            return remote(src, dst, ws.at[d], wr.at[a], device(y, z, k, ring(x, d)))

        def weight_own(a):
            _, src, dst = weights[a - 1]
            return pltpu.make_async_copy(src, dst, loc.at[1])

        for a in steps:

            @pl.when(x == a)
            def _():
                for d in steps:
                    weight_copy(a, d).start()
                weight_own(a).start()

        q_t = q_ref[...].T
        for head in range(3):
            qt[head] = head_rows(q_t, head)
        m_ref[...] = jnp.full_like(m_ref, -1e30)
        l_ref[...] = jnp.zeros_like(l_ref)
        ot_ref[...] = jnp.zeros_like(ot_ref)

        def block(by, bk, masked):
            keys = vo_ref[by, bk, :, :192]
            values_t = vo_ref[by, bk, :, 192:].T
            if masked:
                key_at = place(lax.broadcasted_iota(jnp.int32, (512, 512), 0)) + 128 * bk
                query_at = place(lax.broadcasted_iota(jnp.int32, (512, 512), 1)) + 128 * k
                visible = query_at >= key_at
            for head in range(3):
                s = dot(keys, qt[head])
                if masked:
                    s = jnp.where(visible, s, -1e9)
                old = m_ref[head : head + 1]
                new = jnp.maximum(old, jnp.max(s, 0, keepdims=True))
                e = jnp.exp(s - new)
                scale = jnp.exp(old - new)
                m_ref[head : head + 1] = new
                l_ref[head : head + 1] = l_ref[head : head + 1] * scale + jnp.sum(
                    e, 0, keepdims=True
                )
                at = slice(64 * head, 64 * head + 64)
                ot_ref[at] = ot_ref[at] * scale + dot(values_t[at], e.astype(BF))

        def diagonal(j, carry):
            @pl.when(j == 1)
            def _():
                remote(v_ref, vo_ref.at[y, 1 - k], cs.at[0], cr.at[0], sib).wait_recv()

            block(y, lax.rem(k + j, 2), True)
            return carry

        lax.fori_loop(0, 2, diagonal, 0)

        def pass_on(d):
            return remote(
                vo_ref.at[y - d, k], vo_ref.at[y - d, k], cs.at[d], cr.at[d], sib
            )

        def earlier(i, carry):
            d, j = i // 2 + 1, i % 2

            @pl.when(j == 0)
            def _():
                remote(v_ref, vo_ref.at[y - d, k], vs.at[d], vr.at[d], sib).wait_recv()
                pass_on(d).start()

            @pl.when(j == 1)
            def _():
                remote(v_ref, vo_ref.at[y - d, 1 - k], cs.at[d], cr.at[d], sib).wait_recv()

            block(y - d, lax.rem(k + j, 2), False)
            return carry

        lax.fori_loop(0, 2 * y, earlier, 0)
        for head in range(3):
            at = slice(64 * head, 64 * head + 64)
            total = l_ref[head : head + 1]
            ot_ref[at] = ot_ref[at] / total
            lse_ref[head : head + 1] = m_ref[head : head + 1] + jnp.log(total)
        h_buf[...] = ot_ref[...].T.astype(BF)
        heads_copies = []
        for d in steps:
            c = remote(
                h_buf, ho_ref.at[z, k], hs.at[d], hr.at[d], device(y, ring(z, d), k, x)
            )
            c.start()
            heads_copies.append(c)
        c = remote(h_buf, ho_ref.at[z, k], gs.at[0], gr.at[0], sib)
        c.start()
        forward = [c, row_first]
        own_h = pltpu.make_async_copy(h_buf, ho_ref.at[z, k], loc.at[2])
        own_h.start()
        for d in steps:
            row_copies[d - 1].wait_recv()
            src = ring(z, 4 - d)
            c = remote(ro_ref.at[k, src], ro_ref.at[k, src], ds.at[d], dr.at[d], sib)
            c.start()
            forward.append(c)
        for a in steps:

            @pl.when(x == a)
            def _():
                weight_own(a).wait()

            @pl.when(x != a)
            def _():
                weight_copy(a, 1).wait_recv()

        c = remote(oo_ref.at[k], oo_ref.at[k], os.at[0], orr.at[0], sib)
        c.start()
        forward.append(c)
        for d in steps:
            heads_copies[d - 1].wait_recv()
            src = ring(z, 4 - d)
            c = remote(ho_ref.at[src, k], ho_ref.at[src, k], gs.at[d], gr.at[d], sib)
            c.start()
            forward.append(c)
        for c in forward:
            c.wait()
        for c in row_copies + heads_copies + [swap]:
            c.wait_send()
        for d in steps:

            @pl.when(y + d < 4)
            def _():
                kv_copy(d).wait_send()

            @pl.when(y >= d)
            def _():
                pass_on(d).wait_send()

        for a in steps:

            @pl.when(x == a)
            def _():
                for d in steps:
                    weight_copy(a, d).wait_send()

        own_r.wait()
        own_h.wait()

    return comm(
        kernel,
        [
            jax.ShapeDtypeStruct((4, 2, 512, 192), BF),
            jax.ShapeDtypeStruct((192, 512), F32),
            jax.ShapeDtypeStruct((8, 512), F32),
            jax.ShapeDtypeStruct((4, 2, 512, 384), BF),
            jax.ShapeDtypeStruct((2, 4, 128, 768), BF),
            jax.ShapeDtypeStruct((16, 48, 384), BF),
            jax.ShapeDtypeStruct((2, 16, 48, 384), BF),
            jax.ShapeDtypeStruct((2, 192, 768), BF),
        ],
        2,
        (4, 4, 4, 4, 4, 4, 4, 4, 4, 4, 1, 1, 4, 4, 4, 4, 3),
        (query, kv, rows, fc, out, proj),
        scratch=[
            pltpu.VMEM((3, 192, 512), BF),
            pltpu.VMEM((8, 512), F32),
            pltpu.VMEM((8, 512), F32),
            pltpu.VMEM((512, 192), BF),
        ],
        spaces=(
            [VMEM, VMEM, ANY, ANY, ANY, ANY],
            [ANY, VMEM, VMEM, VMEM, ANY, ANY, ANY, ANY],
        ),
        name="attend",
    )


def attend_back(query, branch, wo_rows, kv_all, out_t, lse, fc, proj):
    def kernel(
        q_ref, b_ref, w_ref, kv_ref, ot_ref, lse_ref, f_ref, p_ref,
        dq_ref, dkv_ref, bo_ref, fo_ref, po_ref,
        qt, gt, qm, gm, delta, dqt, out_buf, keep, got, far, f_far, p_far,
        bs, br, cs, cr, ys, yr, fs, fr, ps, pr,
    ):
        y, z, k, x = coords()
        sib = device(y, z, 1 - k, x)
        steps = (1, 2, 3)
        greet(
            [sib]
            + [device(ring(y, d), z, k, x) for d in steps]
            + [device(y, ring(z, d), k, x) for d in steps]
            + [device(y, z, k, ring(x, d)) for d in steps]
        )
        branches = []
        for d in steps:
            c = remote(b_ref, bo_ref.at[z], bs.at[d], br.at[d], device(y, ring(z, d), k, x))
            c.start()
            branches.append(c)
        weights = []
        for d in steps:
            b = ring(x, d)
            to = device(y, z, k, b)
            weights.append(
                remote(f_ref.at[:, b], f_far.at[d - 1], fs.at[d - 1], fr.at[d - 1], to)
            )
            weights.append(
                remote(p_ref.at[:, b], p_far.at[d - 1], ps.at[d - 1], pr.at[d - 1], to)
            )
        for c in weights:
            c.start()
        bo_ref[z] = b_ref[...]
        query_blk = q_ref[...]
        q_t = query_blk.T
        for head in range(3):
            qt[head] = head_rows(q_t, head)
            qm[head] = head_cols(query_blk, head)
        dqt[...] = jnp.zeros_like(dqt)
        for c in branches:
            c.wait_recv()
        grad_blk = lax.dot_general(
            bo_ref[...].reshape(512, 768),
            w_ref[...],
            (((1,), (1,)), ((), ())),
            preferred_element_type=F32,
        ).astype(BF)
        g_t = grad_blk.T
        for head in range(3):
            at = slice(64 * head, 64 * head + 64)
            gt[head] = head_rows(g_t, head)
            gm[head] = head_cols(grad_blk, head)
            delta[head : head + 1] = jnp.sum(g_t[at].astype(F32) * ot_ref[at], 0, keepdims=True)

        def block(by, bk, masked, to_ref, to):
            keys = kv_ref[by, bk, :, :192]
            values = kv_ref[by, bk, :, 192:]
            keys_t = keys.T
            if masked:
                key_at = place(lax.broadcasted_iota(jnp.int32, (512, 512), 0)) + 128 * bk
                query_at = place(lax.broadcasted_iota(jnp.int32, (512, 512), 1)) + 128 * k
                visible = query_at >= key_at
            dk = dv = None
            for head in range(3):
                s = dot(keys, qt[head])
                p = jnp.exp(s - lse_ref[head : head + 1])
                if masked:
                    p = jnp.where(visible, p, 0.0)
                dp = dot(values, gt[head])
                ds = (p * (dp - delta[head : head + 1])).astype(BF)
                pv = dot(p.astype(BF), gm[head])
                pk = dot(ds, qm[head])
                dv = pv if dv is None else dv + pv
                dk = pk if dk is None else dk + pk
                at = slice(64 * head, 64 * head + 64)
                dqt[at] += dot(keys_t[at], ds)
            to_ref[to, :, :192] = dk.astype(BF)
            to_ref[to, :, 192:] = dv.astype(BF)

        def cross(d):
            return remote(out_buf.at[d], got.at[d], cs.at[d], cr.at[d], sib)

        def up(d):
            return remote(keep.at[d], far.at[d], ys.at[d], yr.at[d], device(y - d, z, k, x))

        def earlier(i, carry):
            d = y - i
            block(y - d, 1 - k, False, out_buf, d)
            cross(d).start()
            block(y - d, k, False, keep, d)
            cross(d).wait_recv()
            keep[d] = (keep[d].astype(F32) + got[d].astype(F32)).astype(BF)
            up(d).start()
            return carry

        lax.fori_loop(0, y, earlier, 0)
        block(y, 1 - k, True, out_buf, 0)
        cross(0).start()
        block(y, k, True, keep, 0)
        dq_ref[...] = (dqt[...].T * 0.125).astype(BF)
        cross(0).wait_recv()
        for c in weights:
            c.wait()
        fo_ref[...] = (
            f_ref[:, x].astype(F32)
            + f_far[0].astype(F32)
            + f_far[1].astype(F32)
            + f_far[2].astype(F32)
        ).astype(BF)
        po_ref[...] = (
            p_ref[:, x].astype(F32)
            + p_far[0].astype(F32)
            + p_far[1].astype(F32)
            + p_far[2].astype(F32)
        ).astype(BF)
        dkv_ref[...] = keep[0].astype(F32) + got[0].astype(F32)
        for d in (1, 2, 3):

            @pl.when(y + d < 4)
            def _():
                remote(keep.at[d], far.at[d], ys.at[d], yr.at[d], sib).wait_recv()
                dkv_ref[...] += far[d].astype(F32)

        for c in branches:
            c.wait_send()
        cross(0).wait_send()
        for d in (1, 2, 3):

            @pl.when(y >= d)
            def _():
                cross(d).wait_send()
                up(d).wait_send()

    return comm(
        kernel,
        [
            jax.ShapeDtypeStruct((512, 192), BF),
            jax.ShapeDtypeStruct((512, 384), F32),
            jax.ShapeDtypeStruct((4, 128, 768), BF),
            jax.ShapeDtypeStruct((4, 48, 384), BF),
            jax.ShapeDtypeStruct((2, 48, 768), BF),
        ],
        5,
        (4, 4, 4, 4, 4, 4, 3, 3, 3, 3),
        (query, branch, wo_rows, kv_all, out_t, lse, fc, proj),
        scratch=[
            pltpu.VMEM((3, 192, 512), BF),
            pltpu.VMEM((3, 192, 512), BF),
            pltpu.VMEM((3, 512, 192), BF),
            pltpu.VMEM((3, 512, 192), BF),
            pltpu.VMEM((8, 512), F32),
            pltpu.VMEM((192, 512), F32),
            pltpu.VMEM((4, 512, 384), BF),
            pltpu.VMEM((4, 512, 384), BF),
            pltpu.VMEM((4, 512, 384), BF),
            pltpu.VMEM((4, 512, 384), BF),
            pltpu.VMEM((3, 4, 48, 384), BF),
            pltpu.VMEM((3, 2, 48, 768), BF),
        ],
        spaces=([VMEM] * 8, [VMEM] * 5),
        name="attend_back",
    )


def normalize(rows):
    centered = rows - jnp.mean(rows, -1, keepdims=True)
    inverse = lax.rsqrt(jnp.mean(centered * centered, -1, keepdims=True) + EPSILON)
    return centered * inverse, inverse


def normalize_back(normed, inverse, gain, grad):
    scaled = grad * gain
    return inverse * (
        scaled
        - jnp.mean(scaled, -1, keepdims=True)
        - normed * jnp.mean(scaled * normed, -1, keepdims=True)
    )


def gelu_tanh(values):
    return (
        0.5
        * values
        * (1.0 + jnp.tanh(0.7978845608028654 * (values + 0.044715 * values * values * values)))
    )


def adam_update(weight, moment_one, moment_two, gradient, rate, decay):
    new_one = BETA_ONE * moment_one + (1.0 - BETA_ONE) * gradient
    new_two = BETA_TWO * moment_two + (1.0 - BETA_TWO) * gradient * gradient
    fix_one = 1.0 - BETA_ONE**STEP
    fix_two = 1.0 - BETA_TWO**STEP
    direction = new_one / fix_one / (jnp.sqrt(new_two / fix_two) + ADAM_EPSILON)
    return (weight - rate * (direction + decay * weight), new_one, new_two)


def shards(
    tokens,
    cotangent,
    w_qkv,
    qkv_m,
    qkv_v,
    w_out,
    out_m,
    out_v,
    w_fc,
    fc_m,
    fc_v,
    w_proj,
    proj_m,
    proj_v,
    vectors,
    vec_m,
    vec_v,
):
    y, z, k, x = coords()
    wq, fc_part, out_part, proj_part, x_group = first_gather(
        w_qkv, w_fc, w_out, w_proj, vectors, tokens[0]
    )
    wq = wq.reshape(768, 640)
    vec = wq[:, 576:588].astype(F32)
    wq = wq[:, :576]
    gain_one, shift_one, q_bias, v_bias = vec[:, 0], vec[:, 1], vec[:, 2], vec[:, 3]
    out_bias, gain_two, shift_two, proj_bias = vec[:, 4], vec[:, 5], vec[:, 6], vec[:, 7]
    fc_bias = lax.dynamic_slice(vec[:, 8:].T.reshape(-1), ((2 * z + k) * 384,), (384,))
    bias = jnp.concatenate(
        [
            lax.dynamic_slice(q_bias, (192 * z,), (192,)),
            jnp.zeros((192,), F32),
            lax.dynamic_slice(v_bias, (192 * z,), (192,)),
        ]
    )
    x_core = lax.dynamic_index_in_dim(x_group, k, 0, False).reshape(512, 768).astype(F32)
    normed_core, _ = normalize(x_core)
    act_one = (normed_core * gain_one + shift_one).astype(BF)
    mixed = (dot(act_one, wq) + bias).astype(BF)
    query = mixed[:, :192] * jnp.asarray(0.125, BF)
    heads_all, out_t, lse, kv_all, dy_group, wf, wo, wp = attend(
        query, mixed[:, 192:], cotangent[0], fc_part, out_part, proj_part
    )
    wf = wf.reshape(768, 384)
    wo = jnp.concatenate([wo[0].reshape(768, 384), wo[1].reshape(768, 384)], 1)
    wp = wp.reshape(384, 768)
    heads_all = jnp.concatenate([heads_all[i].reshape(1024, 192) for i in range(4)], 1)
    x_two = x_group.reshape(1024, 768).astype(F32) + dot(heads_all, wo) + out_bias
    normed_two, inverse_two = normalize(x_two)
    act_two = (normed_two * gain_two + shift_two).astype(BF)
    hidden = dot(act_two, wf) + fc_bias
    gelu_out, gelu_back = jax.vjp(gelu_tanh, hidden)
    act_three = gelu_out.astype(BF)
    dy = dy_group.reshape(1024, 768)
    result_part = dot(act_three, wp).astype(BF)
    grad_w_proj = dot(act_three.T, dy)
    grad_hidden = gelu_back(dot(dy, wp.T))[0].astype(BF)
    grad_w_fc = dot(act_two.T, grad_hidden)
    grad_fc_bias = jnp.sum(grad_hidden.astype(F32), 0)
    norm_part = dot(grad_hidden, wf.T).astype(BF)
    sums = group_sum(
        jnp.stack([norm_part, result_part]).reshape(2, 2, 4, 128, 768), 8, "ffn_sum"
    )

    def own(group):
        return lax.dynamic_slice(group, ((k * 4 + z) * 128, 0), (128, group.shape[1]))

    own_x_two = own(x_two)
    output = own_x_two + sums[1] + proj_bias
    own_normed, own_inverse = normalize(own_x_two)
    grad_output = cotangent[0].astype(F32)
    grad_norm_two = sums[0]
    grad_x_two = grad_output + normalize_back(own_normed, own_inverse, gain_two, grad_norm_two)
    grad_branch = grad_x_two.astype(BF)
    wo_rows = lax.dynamic_slice(wo, (192 * z, 0), (192, 768))
    grad_query, grad_kv, branch_core, fc_sum, proj_sum = attend_back(
        query,
        grad_branch,
        wo_rows,
        kv_all,
        out_t,
        lse,
        grad_w_fc.astype(BF).reshape(4, 4, 48, 384),
        grad_w_proj.astype(BF).reshape(2, 4, 48, 768),
    )
    branch_core = branch_core.reshape(512, 768)
    grad_mixed = jnp.concatenate([grad_query, grad_kv.astype(BF)], 1)
    branch_cols = lax.dynamic_slice(branch_core, (0, 192 * z), (512, 192))
    heads_core = lax.dynamic_index_in_dim(heads_all.reshape(2, 512, 768), k, 0, False)
    left = jnp.concatenate([act_one, heads_core], 0)
    gap = jnp.zeros((512, 96), BF)
    room = jnp.zeros((512, 288), BF)
    right = jnp.concatenate(
        [
            jnp.concatenate([grad_mixed[:, :288], gap, grad_mixed[:, 288:], gap], 1),
            jnp.concatenate([room, branch_cols[:, :96], room, branch_cols[:, 96:]], 1),
        ],
        0,
    )
    grad_mix = dot(left.T, right).astype(BF)
    one_part = dot(grad_mixed, wq.T)

    def spread(piece, at, size):
        return lax.dynamic_update_slice(jnp.zeros((size,), F32), piece, (at,))

    mixed_sums = jnp.sum(grad_mixed.astype(F32), 0)
    columns = jnp.stack(
        [
            jnp.sum(one_part * normed_core, 0),
            jnp.sum(one_part, 0),
            spread(mixed_sums[:192], 192 * z, 768),
            spread(mixed_sums[384:], 192 * z, 768),
            jnp.sum(grad_branch.astype(F32), 0),
            jnp.sum(grad_norm_two * own_normed, 0),
            jnp.sum(grad_norm_two, 0),
            jnp.sum(grad_output, 0),
        ]
        + list(spread(grad_fc_bias, (2 * z + k) * 384, 3072).reshape(4, 768)),
        1,
    )
    grad_vec = jnp.pad(columns, ((0, 0), (0, 116))).astype(BF)
    grad_norm_one, last_rows, sum_proj = last_sums(
        one_part.astype(BF).reshape(4, 128, 768),
        grad_mix.reshape(4, 4, 48, 768),
        grad_vec.reshape(4, 4, 48, 128),
        fc_sum,
        proj_sum,
    )
    normed_one, inverse_one = normalize(tokens[0].astype(F32))
    grad_inputs = grad_x_two + normalize_back(normed_one, inverse_one, gain_one, grad_norm_one)
    last_rows = last_rows[:, :6]
    mix_rows = last_rows[:, :, :1536].reshape(2, 6, 4, 384)
    sum_qkv = (
        mix_rows[..., :288]
        .transpose(1, 2, 0, 3)
        .reshape(6, 4, 3, 192)
        .transpose(0, 2, 1, 3)
        .reshape(6, 2304)
    )
    sum_out = mix_rows[..., 288:].transpose(1, 2, 0, 3).reshape(6, 768)
    sum_fc = last_rows[:, :, 1536:3072].reshape(2, 6, 4, 384).transpose(1, 2, 0, 3).reshape(6, 3072)
    sum_vec = last_rows[0, :, 3072:3084] + last_rows[1, :, 3072:3084]
    new_qkv = adam_update(w_qkv, qkv_m, qkv_v, sum_qkv, 0.1, 0.1)
    new_out = adam_update(w_out, out_m, out_v, sum_out, 0.3, 0.1)
    new_fc = adam_update(w_fc, fc_m, fc_v, sum_fc, 0.05, 0.1)
    new_proj = adam_update(w_proj, proj_m, proj_v, sum_proj, 0.03, 0.1)
    new_vec = adam_update(vectors, vec_m, vec_v, sum_vec, 0.5, 0.0)
    return (output[None], grad_inputs[None], *new_qkv, *new_out, *new_fc, *new_proj, *new_vec)


def solution(mesh):
    split = P("fsdp", "ctx", None)
    rows = P(("ctx", "fsdp"), None)
    return jax.shard_map(
        shards,
        mesh=mesh,
        in_specs=(split, split) + (rows,) * 15,
        out_specs=(split, split) + (rows,) * 15,
        check_vma=False,
    )
```

```python
import jax
import jax.numpy as jnp
from jax import lax
from jax.experimental import pallas as pl
from jax.experimental.pallas import tpu as pltpu
from jax.sharding import PartitionSpec as P

STEP = 10
EPSILON = 1e-05
BETA_ONE = 0.9
BETA_TWO = 0.999
ADAM_EPSILON = 1e-08
MESH = pl.DeviceIdType.MESH
BF = jnp.bfloat16
F32 = jnp.float32
ANY = pl.BlockSpec(memory_space=pl.ANY)
VMEM = pl.BlockSpec(memory_space=pltpu.VMEM)
LIMIT = 56 * 1024 * 1024


def coords():
    c = lax.axis_index("ctx")
    return c // 8, (c // 2) % 4, c % 2, lax.axis_index("fsdp")


def device(y, z, k, x):
    return ((y * 4 + z) * 2 + k, x)


def ring(v, step):
    return lax.rem(v + step, 4)


def greet(devices):
    barrier = pltpu.get_barrier_semaphore()
    for one in devices:
        pl.semaphore_signal(barrier, inc=1, device_id=one, device_id_type=MESH)
    pl.semaphore_wait(barrier, len(devices))


def remote(src, dst, send, recv, to):
    return pltpu.make_async_remote_copy(
        src, dst, send, recv, device_id=to, device_id_type=MESH
    )


def comm(kernel, outs, cid, sems, args, scratch=(), spaces=None, name=None):
    return pl.pallas_call(
        kernel,
        out_shape=outs,
        in_specs=[ANY] * len(args) if spaces is None else spaces[0],
        out_specs=[ANY] * len(outs) if spaces is None else spaces[1],
        scratch_shapes=list(scratch) + [pltpu.SemaphoreType.DMA((n,)) for n in sems],
        compiler_params=pltpu.CompilerParams(
            collective_id=cid, has_side_effects=True, vmem_limit_bytes=LIMIT
        ),
        name=name,
    )(*args)


def first_gather(w_qkv, w_fc, w_out, w_proj, vectors, rows):
    width = 4736

    def kernel(
        wq_ref, wf_ref, wo_ref, wp_ref, wv_ref, r_ref,
        q_out, f_out, o_out, p_out, ro_ref,
        wide, packed, got, fc48, qkv48, out48, proj_wide, q_send, f_send, o_send, p_send,
        ms, mr, fs, fr, s1, r1, s2, r2, ps, pr, xs_s, xs_r, xf_s, xf_r, rs, rr, cs, cr, loc,
    ):
        y, z, k, x = coords()
        me = y * 4 + z
        sib = device(y, z, 1 - k, x)
        steps = (1, 2, 3)
        greet(
            [sib]
            + [device(y, z, k, ring(x, d)) for d in steps]
            + [
                device(ring(y, a), ring(z, b), k, x)
                for a in range(4)
                for b in range(4)
                if (a, b) != (0, 0)
            ]
        )
        own_r = pltpu.make_async_copy(r_ref, ro_ref.at[k, z], loc.at[0])
        own_r.start()
        row_copies = []
        for d in steps:
            c = remote(
                r_ref, ro_ref.at[k, z], rs.at[d], rr.at[d], device(y, ring(z, d), k, x)
            )
            row_copies.append(c)
        wide[...] = jnp.zeros_like(wide)
        wide[0:6, 0:3072] = wf_ref[...]
        wide[6:12, 0:2304] = wq_ref[...]
        wide[6:12, 2304:3072] = wo_ref[...]
        wide[0:12, 3072:3840] = wp_ref[0:12]
        wide[0:12, 3840:4608] = wp_ref[12:24]
        wide[0:6, 4608:4620] = wv_ref[...]
        t = k * 4 + x
        packed[...] = wide[...].astype(BF)
        got[t] = packed[...]
        message = []
        for d in steps:
            c = remote(packed, got.at[t], ms.at[d], mr.at[d], device(y, z, k, ring(x, d)))
            c.start()
            message.append(c)
        c = remote(packed, got.at[t], fs.at[0], fr.at[0], sib)
        c.start()
        forward = [c]
        for c in row_copies:
            c.start()
        c = remote(r_ref, ro_ref.at[k, z], cs.at[0], cr.at[0], sib)
        c.start()
        row_forward = [c]
        for d in steps:
            message[d - 1].wait_recv()
            src = k * 4 + ring(x, 4 - d)
            f = remote(got.at[src], got.at[src], fs.at[d], fr.at[d], sib)
            f.start()
            forward.append(f)
        for f in forward:
            f.wait_recv()
        for i in range(8):
            piece = got[i].astype(F32)
            at = slice(6 * i, 6 * i + 6)
            fc48[at] = piece[0:6, 0:3072]
            qkv48[at] = piece[6:12, 0:2304]
            out48[at, 0:768] = piece[6:12, 2304:3072]
            out48[at, 768:896] = piece[0:6, 4608:4736]
            proj_wide[24 * i : 24 * i + 12] = piece[0:12, 3072:3840]
            proj_wide[24 * i + 12 : 24 * i + 24] = piece[0:12, 3840:4608]
        for j in range(4):
            q_send[j, :, 0:192] = qkv48[:, 192 * j : 192 * j + 192].astype(BF)
            q_send[j, :, 192:384] = qkv48[:, 768 + 192 * j : 960 + 192 * j].astype(BF)
            q_send[j, :, 384:576] = qkv48[:, 1536 + 192 * j : 1728 + 192 * j].astype(BF)
            q_send[j, :, 576:640] = out48[:, 768:832].astype(BF)
        for j in range(8):
            f_send[j] = fc48[:, 384 * j : 384 * j + 384].astype(BF)
        o_send[0] = out48[:, 0:384].astype(BF)
        o_send[1] = out48[:, 384:768].astype(BF)
        p_send[...] = proj_wide[...].astype(BF)

        group = pl.ds(pl.multiple_of(16 * jnp.minimum(x, 2), 16), 16)

        def to_of(m):
            return ring(y, m // 4), ring(z, m % 4)

        def q_copy(m):
            ty, tz = to_of(m)
            return remote(
                q_send.at[tz, group], q_out.at[me, group], s1.at[m], r1.at[m],
                device(ty, tz, k, x),
            )

        def f_copy(m):
            ty, tz = to_of(m)
            return remote(
                f_send.at[tz * 2 + k], f_out.at[me], s2.at[m], r2.at[m], device(ty, tz, k, x)
            )

        def o_copy(m):
            ty, tz = to_of(m)
            return remote(o_send.at[k], o_out.at[me], s2.at[m], r2.at[m], device(ty, tz, k, x))

        def p_copy(a):
            return remote(
                p_send, p_out.at[z % 2], ps.at[a], pr.at[z % 2], device(ring(y, a), y, k, x)
            )

        def each(copy, what):
            def step(m, carry):
                what(copy(m))
                return carry

            lax.fori_loop(1, 16, step, 0)

        start = lambda c: c.start()
        finish = lambda c: c.wait()

        @pl.when(x < 3)
        def _():
            each(q_copy, start)
            c = pltpu.make_async_copy(q_send.at[z, group], q_out.at[me, group], loc.at[1])
            c.start()
            c.wait()

        @pl.when(x == 1)
        def _():
            each(f_copy, start)
            c = pltpu.make_async_copy(f_send.at[z * 2 + k], f_out.at[me], loc.at[2])
            c.start()
            c.wait()

        @pl.when(x == 2)
        def _():
            each(o_copy, start)
            c = pltpu.make_async_copy(o_send.at[k], o_out.at[me], loc.at[2])
            c.start()
            c.wait()

        @pl.when((x == 3) & (k == z // 2))
        def _():
            for a in range(1, 4):
                p_copy(a).start()

            @pl.when(z != y)
            def _():
                p_copy(0).start()

            @pl.when(z == y)
            def _():
                c = pltpu.make_async_copy(p_send, p_out.at[z % 2], loc.at[2])
                c.start()
                c.wait()

        half = pl.ds(8 * k, 8)
        other_half = pl.ds(8 * (1 - k), 8)

        def rows_of(plane):
            return pl.ds(pl.multiple_of(16 * plane, 16), 16)

        @pl.when(x < 3)
        def _():
            each(q_copy, finish)
            for d in steps:
                remote(
                    q_out.at[half, group], q_out.at[half, group], xs_s.at[d], xs_r.at[x],
                    device(y, z, k, ring(x, d)),
                ).start()

        def pass_on(a):
            return remote(
                q_out.at[half, rows_of(a)], q_out.at[half, rows_of(a)], xf_s.at[a], xf_r.at[a], sib
            )

        for a in range(3):

            @pl.when(x != a)
            def _():
                remote(
                    q_out.at[half, rows_of(a)], q_out.at[half, rows_of(a)], xs_s.at[0],
                    xs_r.at[a], sib,
                ).wait_recv()
                pass_on(a).start()

        for d in steps:
            row_copies[d - 1].wait_recv()
            src = ring(z, 4 - d)
            f = remote(ro_ref.at[k, src], ro_ref.at[k, src], cs.at[d], cr.at[d], sib)
            f.start()
            row_forward.append(f)

        @pl.when(x == 1)
        def _():
            each(f_copy, finish)

        @pl.when(x == 2)
        def _():
            each(o_copy, finish)

        @pl.when((x == 3) & (k == z // 2))
        def _():
            for a in range(1, 4):
                p_copy(a).wait_send()

            @pl.when(z != y)
            def _():
                p_copy(0).wait_send()

        for j in range(2):
            @pl.when((x == 3) & jnp.logical_not((y == z) & (z == 2 * k + j)))
            def _():
                remote(p_send, p_out.at[j], ps.at[0], pr.at[j], sib).wait_recv()

        @pl.when(x < 3)
        def _():
            for d in steps:
                remote(
                    q_out.at[half, group], q_out.at[half, group], xs_s.at[d], xs_r.at[x],
                    device(y, z, k, ring(x, d)),
                ).wait_send()

        for a in range(3):

            @pl.when(x != a)
            def _():
                pass_on(a).wait_send()
                remote(
                    q_out.at[other_half, rows_of(a)], q_out.at[other_half, rows_of(a)],
                    xf_s.at[a], xf_r.at[a], sib,
                ).wait_recv()

        for c in message + row_copies + forward:
            c.wait_send()
        for c in row_forward:
            c.wait()
        own_r.wait()

    return comm(
        kernel,
        [
            jax.ShapeDtypeStruct((16, 48, 640), BF),
            jax.ShapeDtypeStruct((16, 48, 384), BF),
            jax.ShapeDtypeStruct((16, 48, 384), BF),
            jax.ShapeDtypeStruct((2, 192, 768), BF),
            jax.ShapeDtypeStruct((2, 4) + rows.shape, BF),
        ],
        0,
        (4, 4, 4, 4, 16, 16, 16, 16, 4, 2, 4, 4, 4, 4, 4, 4, 4, 4, 3),
        (w_qkv, w_fc, w_out, w_proj, vectors, rows),
        scratch=[
            pltpu.VMEM((16, width), F32),
            pltpu.VMEM((16, width), BF),
            pltpu.VMEM((8, 16, width), BF),
            pltpu.VMEM((48, 3072), F32),
            pltpu.VMEM((48, 2304), F32),
            pltpu.VMEM((48, 896), F32),
            pltpu.VMEM((192, 768), F32),
            pltpu.VMEM((4, 48, 640), BF),
            pltpu.VMEM((8, 48, 384), BF),
            pltpu.VMEM((2, 48, 384), BF),
            pltpu.VMEM((192, 768), BF),
        ],
        spaces=([VMEM] * 5 + [ANY], [ANY] * 5),
        name="first_gather",
    )


def last_sums(one, mix, vec, fc, proj):
    wide = 3200

    def kernel(
        one_ref, mix_ref, vec_ref, fc_ref, proj_ref, one_out, rows_out, proj_out,
        one_far, mix_got, mix_sum, mix_far, vec_far, mix_mine, vec_mine,
        mix_all, fc_all, vec_all, proj_all, proj_sum, out_send,
        zs, zr, cs, cr, s1, r1, s2, r2, s3, r3, s4, r4, s5, r5, s6, r6, s7, r7, s8, r8, loc,
    ):
        y, z, k, x = coords()
        me = y * 4 + z
        sib = device(y, z, 1 - k, x)
        steps = (1, 2, 3)
        greet(
            [sib]
            + [device(y, z, j, ring(x, d)) for d in steps for j in (k, 1 - k)]
            + [
                device(ring(y, a), ring(z, b), k, x)
                for a in range(4)
                for b in range(4)
                if (a, b) != (0, 0)
            ]
        )
        mine_at = pl.ds(pl.multiple_of(384 * k, 128), 384)
        other_at = pl.ds(pl.multiple_of(384 * (1 - k), 128), 384)
        swap = []
        for d in (1, 2, 3, 0):
            b = ring(x, d)
            c = remote(mix_ref.at[:, b, :, other_at], mix_got.at[b], cs.at[d], cr.at[d], sib)
            c.start()
            swap.append(c)
        along = []
        for d in steps:
            b = ring(x, d)
            to = device(y, z, k, b)
            c = remote(vec_ref.at[:, b], vec_far.at[d - 1], s2.at[d - 1], r2.at[d - 1], to)
            c.start()
            along.append(c)
            swap[d - 1].wait_recv()
            mix_sum[d] = (
                mix_ref[:, b, :, mine_at].astype(F32) + mix_got[b].astype(F32)
            ).astype(BF)
            c = remote(mix_sum.at[d], mix_far.at[d - 1], s1.at[d - 1], r1.at[d - 1], to)
            c.start()
            along.append(c)
        ones = []
        for d in steps:
            c = remote(
                one_ref.at[ring(z, d)], one_far.at[d - 1], zs.at[d - 1], zr.at[d - 1],
                device(y, ring(z, d), k, x),
            )
            c.start()
            ones.append(c)

        def plane(src, dst, send, recv, a):
            return remote(src.at[a], dst.at[me], send.at[a], recv.at[me], device(a, x, k, x))

        def all_start(src, dst, send, recv):
            for a in range(4):
                here = (a == y) & (z == x)

                @pl.when(jnp.logical_not(here))
                def _():
                    plane(src, dst, send, recv, a).start()

                @pl.when(here)
                def _():
                    c = pltpu.make_async_copy(src.at[a], dst.at[me], loc.at[0])
                    c.start()
                    c.wait()

        def all_finish(src, dst, send, recv):
            for a in range(4):

                @pl.when(jnp.logical_not((a == y) & (z == x)))
                def _():
                    plane(src, dst, send, recv, a).wait_send()

        def all_receive(src, dst, send, recv):
            def step(i, carry):
                @pl.when(i != me)
                def _():
                    remote(src.at[0], dst.at[i], send.at[0], recv.at[i], sib).wait_recv()

                return carry

            lax.fori_loop(0, 16, step, 0)

        all_start(fc_ref, fc_all, s4, r4)

        def proj_copy(j):
            return remote(
                proj_ref.at[j], proj_all.at[y], s6.at[j], r6.at[y], device(z, 2 * k + j, k, x)
            )

        for j in range(2):
            here = (y == z) & (z == 2 * k + j)

            @pl.when(jnp.logical_not(here))
            def _():
                proj_copy(j).start()

            @pl.when(here)
            def _():
                c = pltpu.make_async_copy(proj_ref.at[j], proj_all.at[y], loc.at[1])
                c.start()
                c.wait()

        swap[3].wait_recv()
        for c in along:
            c.wait_recv()
        mix_mine[...] = (
            mix_ref[:, x, :, mine_at].astype(F32)
            + mix_got[x].astype(F32)
            + mix_far[0].astype(F32)
            + mix_far[1].astype(F32)
            + mix_far[2].astype(F32)
        ).astype(BF)
        vec_mine[...] = (
            vec_ref[:, x].astype(F32)
            + vec_far[0].astype(F32)
            + vec_far[1].astype(F32)
            + vec_far[2].astype(F32)
        ).astype(BF)
        all_start(mix_mine, mix_all, s3, r3)
        all_start(vec_mine, vec_all, s5, r5)
        for c in ones:
            c.wait_recv()
        one_out[...] = (
            one_ref[z].astype(F32)
            + one_far[0].astype(F32)
            + one_far[1].astype(F32)
            + one_far[2].astype(F32)
        )

        def proj_last(i):
            return remote(
                proj_sum.at[i], proj_out, s8.at[i], r8.at[0],
                device(y, z, x // 2, lax.rem(2 * x + i, 4)),
            )

        def proj_here(i):
            return (k == x // 2) & (x == lax.rem(2 * x + i, 4))

        holder = k == z // 2
        for a in range(4):

            @pl.when(holder & jnp.logical_not((a == y) & (z == y)))
            def _():
                remote(proj_ref.at[0], proj_all.at[a], s6.at[0], r6.at[a], sib).wait_recv()

        @pl.when(holder)
        def _():
            total = (
                proj_all[0].astype(F32)
                + proj_all[1].astype(F32)
                + proj_all[2].astype(F32)
                + proj_all[3].astype(F32)
            )
            for i in range(2):
                proj_sum[i] = total[24 * i : 24 * i + 24]

                @pl.when(jnp.logical_not(proj_here(i)))
                def _():
                    proj_last(i).start()

                @pl.when(proj_here(i))
                def _():
                    c = pltpu.make_async_copy(proj_sum.at[i], proj_out, loc.at[2])
                    c.start()
                    c.wait()

        def last_copy(i):
            return remote(
                out_send.at[i], rows_out.at[k], s7.at[i], r7.at[k], device(y, z, i // 4, i % 4)
            )

        def last_here(i):
            return k * 4 + x == i

        @pl.when(z == x)
        def _():
            all_receive(fc_ref, fc_all, s4, r4)
            all_receive(mix_mine, mix_all, s3, r3)
            all_receive(vec_mine, vec_all, s5, r5)

            def four(ref, b):
                return (
                    ref[b].astype(F32)
                    + ref[4 + b].astype(F32)
                    + ref[8 + b].astype(F32)
                    + ref[12 + b].astype(F32)
                )

            for b in range(4):
                m, f = four(mix_all, b), four(fc_all, b)
                for i in range(8):
                    rows = slice(6 * i, 6 * i + 6)
                    out_send[i, 0:6, 384 * b : 384 * b + 384] = m[rows]
                    out_send[i, 0:6, 1536 + 384 * b : 1920 + 384 * b] = f[rows]
            v = four(vec_all, 0) + four(vec_all, 1) + four(vec_all, 2) + four(vec_all, 3)
            for i in range(8):
                out_send[i, 0:6, 3072:3200] = v[6 * i : 6 * i + 6]
                out_send[i, 6:8, :] = jnp.zeros((2, wide), F32)
            for i in range(8):

                @pl.when(jnp.logical_not(last_here(i)))
                def _():
                    last_copy(i).start()

                @pl.when(last_here(i))
                def _():
                    c = pltpu.make_async_copy(out_send.at[i], rows_out.at[k], loc.at[3])
                    c.start()
                    c.wait()

        for j in range(2):

            @pl.when(jnp.logical_not((z == x) & (k == j)))
            def _():
                remote(out_send.at[0], rows_out.at[j], s7.at[0], r7.at[j], sib).wait_recv()

        @pl.when(jnp.logical_not((k == z // 2) & (x == (4 * k + x) // 2)))
        def _():
            remote(proj_sum.at[0], proj_out, s8.at[0], r8.at[0], sib).wait_recv()

        @pl.when(z == x)
        def _():
            for i in range(8):

                @pl.when(jnp.logical_not(last_here(i)))
                def _():
                    last_copy(i).wait_send()

        for i in range(2):

            @pl.when(holder & jnp.logical_not(proj_here(i)))
            def _():
                proj_last(i).wait_send()

        for j in range(2):

            @pl.when(jnp.logical_not((y == z) & (z == 2 * k + j)))
            def _():
                proj_copy(j).wait_send()

        all_finish(fc_ref, fc_all, s4, r4)
        all_finish(mix_mine, mix_all, s3, r3)
        all_finish(vec_mine, vec_all, s5, r5)
        for c in swap + along + ones:
            c.wait_send()

    return comm(
        kernel,
        [
            jax.ShapeDtypeStruct((128, 768), F32),
            jax.ShapeDtypeStruct((2, 8, wide), F32),
            jax.ShapeDtypeStruct((24, 768), F32),
        ],
        6,
        (3, 3, 4, 4, 3, 3, 3, 3, 4, 16, 4, 16, 4, 16, 2, 4, 8, 2, 2, 1, 4),
        (one, mix, vec, fc, proj),
        scratch=[
            pltpu.VMEM((3, 128, 768), BF),
            pltpu.VMEM((4, 4, 48, 384), BF),
            pltpu.VMEM((4, 4, 48, 384), BF),
            pltpu.VMEM((3, 4, 48, 384), BF),
            pltpu.VMEM((3, 4, 48, 128), BF),
            pltpu.VMEM((4, 48, 384), BF),
            pltpu.VMEM((4, 48, 128), BF),
            pltpu.VMEM((16, 48, 384), BF),
            pltpu.VMEM((16, 48, 384), BF),
            pltpu.VMEM((16, 48, 128), BF),
            pltpu.VMEM((4, 48, 768), BF),
            pltpu.VMEM((2, 24, 768), F32),
            pltpu.VMEM((8, 8, wide), F32),
        ],
        spaces=([VMEM] * 5, [VMEM] * 3),
        name="last_sums",
    )


def head_rows(matrix, head):
    row = lax.broadcasted_iota(jnp.int32, matrix.shape, 0)
    keep = (row >= 64 * head) & (row < 64 * head + 64)
    return jnp.where(keep, matrix, jnp.zeros_like(matrix))


def head_cols(matrix, head):
    col = lax.broadcasted_iota(jnp.int32, matrix.shape, 1)
    keep = (col >= 64 * head) & (col < 64 * head + 64)
    return jnp.where(keep, matrix, jnp.zeros_like(matrix))


def place(index):
    return (index // 128) * 256 + index % 128


def dot(a, b):
    return jnp.dot(a, b, preferred_element_type=F32)


def attend(tokens, wq, bias, rows768, rows, fc, out, proj):
    def kernel(
        x_ref, wq_ref, b_ref, g_ref, r_ref, f_ref, o_ref, p_ref,
        ho_ref, ot_ref, lse_ref, vo_ref, ro_ref, fo_ref, oo_ref, po_ref, q_ref, a_ref, n_ref,
        qt, m_ref, l_ref, h_buf, v_ref,
        vs, vr, rs, rr, cs, cr, ds, dr, ws, wr, os, orr, hs, hr, gs, gr, loc,
    ):
        y, z, k, x = coords()
        sib = device(y, z, 1 - k, x)
        steps = (1, 2, 3)
        greet(
            [sib]
            + [device(ring(y, d), z, k, x) for d in steps]
            + [device(y, ring(z, d), k, x) for d in steps]
            + [device(y, z, k, ring(x, d)) for d in steps]
        )

        own_r = pltpu.make_async_copy(r_ref, ro_ref.at[k, z], loc.at[0])
        own_r.start()
        row_copies = []
        for d in steps:
            c = remote(
                r_ref, ro_ref.at[k, z], rs.at[d], rr.at[d], device(y, ring(z, d), k, x)
            )
            c.start()
            row_copies.append(c)
        row_first = remote(r_ref, ro_ref.at[k, z], ds.at[0], dr.at[0], sib)
        row_first.start()

        weights = ((1, f_ref, fo_ref), (2, o_ref, oo_ref.at[k]), (3, p_ref, po_ref))

        def weight_copy(a, d):
            _, src, dst = weights[a - 1]
            return remote(src, dst, ws.at[d], wr.at[a], device(y, z, k, ring(x, d)))

        def weight_own(a):
            _, src, dst = weights[a - 1]
            return pltpu.make_async_copy(src, dst, loc.at[1])

        for a in steps:

            @pl.when(x == a)
            def _():
                for d in steps:
                    weight_copy(a, d).start()
                weight_own(a).start()

        normed, _ = normalize(x_ref[k].reshape(512, 768).astype(F32))
        n_ref[...] = normed.astype(BF)
        act = (normed * g_ref[0:1] + g_ref[1:2]).astype(BF)
        a_ref[...] = act
        mixed = dot(act, wq_ref[...]) + b_ref[...]
        v_ref[...] = mixed[:, 192:576].astype(BF)

        def kv_copy(d):
            return remote(
                v_ref, vo_ref.at[y, k], vs.at[d], vr.at[d], device(ring(y, d), z, k, x)
            )

        for d in steps:

            @pl.when(y + d < 4)
            def _():
                kv_copy(d).start()

        swap = remote(v_ref, vo_ref.at[y, k], cs.at[0], cr.at[0], sib)
        swap.start()
        vo_ref[y, k] = v_ref[...]
        query = mixed[:, :192].astype(BF) * jnp.asarray(0.125, BF)
        q_ref[...] = query
        q_t = query.T
        for head in range(3):
            qt[head] = head_rows(q_t, head)
        m_ref[...] = jnp.full_like(m_ref, -1e30)
        l_ref[...] = jnp.zeros_like(l_ref)
        ot_ref[...] = jnp.zeros_like(ot_ref)

        def block(by, bk, masked):
            keys = vo_ref[by, bk, :, :192]
            values_t = vo_ref[by, bk, :, 192:].T
            if masked:
                key_at = place(lax.broadcasted_iota(jnp.int32, (512, 512), 0)) + 128 * bk
                query_at = place(lax.broadcasted_iota(jnp.int32, (512, 512), 1)) + 128 * k
                visible = query_at >= key_at
            for head in range(3):
                s = dot(keys, qt[head])
                if masked:
                    s = jnp.where(visible, s, -1e9)
                old = m_ref[head : head + 1]
                new = jnp.maximum(old, jnp.max(s, 0, keepdims=True))
                e = jnp.exp(s - new)
                scale = jnp.exp(old - new)
                m_ref[head : head + 1] = new
                l_ref[head : head + 1] = l_ref[head : head + 1] * scale + jnp.sum(
                    e, 0, keepdims=True
                )
                at = slice(64 * head, 64 * head + 64)
                ot_ref[at] = ot_ref[at] * scale + dot(values_t[at], e.astype(BF))

        def diagonal(j, carry):
            @pl.when(j == 1)
            def _():
                remote(v_ref, vo_ref.at[y, 1 - k], cs.at[0], cr.at[0], sib).wait_recv()

            block(y, lax.rem(k + j, 2), True)
            return carry

        lax.fori_loop(0, 2, diagonal, 0)

        def pass_on(d):
            return remote(
                vo_ref.at[y - d, k], vo_ref.at[y - d, k], cs.at[d], cr.at[d], sib
            )

        def earlier(i, carry):
            d, j = i // 2 + 1, i % 2

            @pl.when(j == 0)
            def _():
                remote(v_ref, vo_ref.at[y - d, k], vs.at[d], vr.at[d], sib).wait_recv()
                pass_on(d).start()

            @pl.when(j == 1)
            def _():
                remote(v_ref, vo_ref.at[y - d, 1 - k], cs.at[d], cr.at[d], sib).wait_recv()

            block(y - d, lax.rem(k + j, 2), False)
            return carry

        lax.fori_loop(0, 2 * y, earlier, 0)
        for head in range(3):
            at = slice(64 * head, 64 * head + 64)
            total = l_ref[head : head + 1]
            ot_ref[at] = ot_ref[at] / total
            lse_ref[head : head + 1] = m_ref[head : head + 1] + jnp.log(total)
        h_buf[...] = ot_ref[...].T.astype(BF)
        heads_copies = []
        for d in steps:
            c = remote(
                h_buf, ho_ref.at[z, k], hs.at[d], hr.at[d], device(y, ring(z, d), k, x)
            )
            c.start()
            heads_copies.append(c)
        c = remote(h_buf, ho_ref.at[z, k], gs.at[0], gr.at[0], sib)
        c.start()
        forward = [c, row_first]
        own_h = pltpu.make_async_copy(h_buf, ho_ref.at[z, k], loc.at[2])
        own_h.start()
        for d in steps:
            row_copies[d - 1].wait_recv()
            src = ring(z, 4 - d)
            c = remote(ro_ref.at[k, src], ro_ref.at[k, src], ds.at[d], dr.at[d], sib)
            c.start()
            forward.append(c)
        for a in steps:

            @pl.when(x == a)
            def _():
                weight_own(a).wait()

            @pl.when(x != a)
            def _():
                weight_copy(a, 1).wait_recv()

        c = remote(oo_ref.at[k], oo_ref.at[k], os.at[0], orr.at[0], sib)
        c.start()
        forward.append(c)
        for d in steps:
            heads_copies[d - 1].wait_recv()
            src = ring(z, 4 - d)
            c = remote(ho_ref.at[src, k], ho_ref.at[src, k], gs.at[d], gr.at[d], sib)
            c.start()
            forward.append(c)
        for c in forward:
            c.wait()
        for c in row_copies + heads_copies + [swap]:
            c.wait_send()
        for d in steps:

            @pl.when(y + d < 4)
            def _():
                kv_copy(d).wait_send()

            @pl.when(y >= d)
            def _():
                pass_on(d).wait_send()

        for a in steps:

            @pl.when(x == a)
            def _():
                for d in steps:
                    weight_copy(a, d).wait_send()

        own_r.wait()
        own_h.wait()

    return comm(
        kernel,
        [
            jax.ShapeDtypeStruct((4, 2, 512, 192), BF),
            jax.ShapeDtypeStruct((192, 512), F32),
            jax.ShapeDtypeStruct((8, 512), F32),
            jax.ShapeDtypeStruct((4, 2, 512, 384), BF),
            jax.ShapeDtypeStruct((2, 4, 128, 768), BF),
            jax.ShapeDtypeStruct((16, 48, 384), BF),
            jax.ShapeDtypeStruct((2, 16, 48, 384), BF),
            jax.ShapeDtypeStruct((2, 192, 768), BF),
            jax.ShapeDtypeStruct((512, 192), BF),
            jax.ShapeDtypeStruct((512, 768), BF),
            jax.ShapeDtypeStruct((512, 768), BF),
        ],
        2,
        (4, 4, 4, 4, 4, 4, 4, 4, 4, 4, 1, 1, 4, 4, 4, 4, 3),
        (tokens, wq, bias, rows768, rows, fc, out, proj),
        scratch=[
            pltpu.VMEM((3, 192, 512), BF),
            pltpu.VMEM((8, 512), F32),
            pltpu.VMEM((8, 512), F32),
            pltpu.VMEM((512, 192), BF),
            pltpu.VMEM((512, 384), BF),
        ],
        spaces=(
            [VMEM, VMEM, VMEM, VMEM, ANY, ANY, ANY, ANY],
            [ANY, VMEM, VMEM, VMEM, ANY, ANY, ANY, ANY, VMEM, VMEM, VMEM],
        ),
        name="attend",
    )


def attend_back(query, branch, wo, kv_all, out_t, lse, fc, proj):
    def kernel(
        q_ref, b_ref, w_ref, kv_ref, ot_ref, lse_ref, f_ref, p_ref,
        dq_ref, dkv_ref, fo_ref, po_ref,
        qt, gt, qm, gm, delta, dqt, out_buf, keep, got, far, f_far, p_far,
        cs, cr, ys, yr, fs, fr, ps, pr,
    ):
        y, z, k, x = coords()
        sib = device(y, z, 1 - k, x)
        steps = (1, 2, 3)
        greet(
            [sib]
            + [device(ring(y, d), z, k, x) for d in steps]
            + [device(y, z, k, ring(x, d)) for d in steps]
        )
        weights = []
        for d in steps:
            b = ring(x, d)
            to = device(y, z, k, b)
            weights.append(
                remote(f_ref.at[:, b], f_far.at[d - 1], fs.at[d - 1], fr.at[d - 1], to)
            )
            weights.append(
                remote(p_ref.at[:, b], p_far.at[d - 1], ps.at[d - 1], pr.at[d - 1], to)
            )
        for c in weights:
            c.start()
        query_blk = q_ref[...]
        q_t = query_blk.T
        for head in range(3):
            qt[head] = head_rows(q_t, head)
            qm[head] = head_cols(query_blk, head)
        dqt[...] = jnp.zeros_like(dqt)
        nt = (((1,), (1,)), ((), ()))
        own_heads = pl.ds(pl.multiple_of(192 * z, 64), 192)
        grad_blk = lax.dot_general(
            b_ref[:, :384], w_ref[0, own_heads], nt, preferred_element_type=F32
        )
        grad_blk += lax.dot_general(
            b_ref[:, 384:], w_ref[1, own_heads], nt, preferred_element_type=F32
        )
        grad_blk = grad_blk.astype(BF)
        g_t = grad_blk.T
        for head in range(3):
            at = slice(64 * head, 64 * head + 64)
            gt[head] = head_rows(g_t, head)
            gm[head] = head_cols(grad_blk, head)
            delta[head : head + 1] = jnp.sum(g_t[at].astype(F32) * ot_ref[at], 0, keepdims=True)

        def block(by, bk, masked, to_ref, to):
            keys = kv_ref[by, bk, :, :192]
            values = kv_ref[by, bk, :, 192:]
            keys_t = keys.T
            if masked:
                key_at = place(lax.broadcasted_iota(jnp.int32, (512, 512), 0)) + 128 * bk
                query_at = place(lax.broadcasted_iota(jnp.int32, (512, 512), 1)) + 128 * k
                visible = query_at >= key_at
            dk = dv = None
            for head in range(3):
                s = dot(keys, qt[head])
                p = jnp.exp(s - lse_ref[head : head + 1])
                if masked:
                    p = jnp.where(visible, p, 0.0)
                dp = dot(values, gt[head])
                ds = (p * (dp - delta[head : head + 1])).astype(BF)
                pv = dot(p.astype(BF), gm[head])
                pk = dot(ds, qm[head])
                dv = pv if dv is None else dv + pv
                dk = pk if dk is None else dk + pk
                at = slice(64 * head, 64 * head + 64)
                dqt[at] += dot(keys_t[at], ds)
            to_ref[to, :, :192] = dk.astype(BF)
            to_ref[to, :, 192:] = dv.astype(BF)

        def cross(d):
            return remote(out_buf.at[d], got.at[d], cs.at[d], cr.at[d], sib)

        def up(d):
            return remote(keep.at[d], far.at[d], ys.at[d], yr.at[d], device(y - d, z, k, x))

        def earlier(i, carry):
            d = y - i
            block(y - d, 1 - k, False, out_buf, d)
            cross(d).start()
            block(y - d, k, False, keep, d)
            cross(d).wait_recv()
            keep[d] = (keep[d].astype(F32) + got[d].astype(F32)).astype(BF)
            up(d).start()
            return carry

        lax.fori_loop(0, y, earlier, 0)
        block(y, 1 - k, True, out_buf, 0)
        cross(0).start()
        block(y, k, True, keep, 0)
        dq_ref[...] = (dqt[...].T * 0.125).astype(BF)
        cross(0).wait_recv()
        for c in weights:
            c.wait()
        fo_ref[...] = (
            f_ref[:, x].astype(F32)
            + f_far[0].astype(F32)
            + f_far[1].astype(F32)
            + f_far[2].astype(F32)
        ).astype(BF)
        po_ref[...] = (
            p_ref[:, x].astype(F32)
            + p_far[0].astype(F32)
            + p_far[1].astype(F32)
            + p_far[2].astype(F32)
        ).astype(BF)
        dkv_ref[...] = keep[0].astype(F32) + got[0].astype(F32)
        for d in (1, 2, 3):

            @pl.when(y + d < 4)
            def _():
                remote(keep.at[d], far.at[d], ys.at[d], yr.at[d], sib).wait_recv()
                dkv_ref[...] += far[d].astype(F32)

        cross(0).wait_send()
        for d in (1, 2, 3):

            @pl.when(y >= d)
            def _():
                cross(d).wait_send()
                up(d).wait_send()

    return comm(
        kernel,
        [
            jax.ShapeDtypeStruct((512, 192), BF),
            jax.ShapeDtypeStruct((512, 384), F32),
            jax.ShapeDtypeStruct((4, 48, 384), BF),
            jax.ShapeDtypeStruct((2, 48, 768), BF),
        ],
        5,
        (4, 4, 4, 4, 3, 3, 3, 3),
        (query, branch, wo, kv_all, out_t, lse, fc, proj),
        scratch=[
            pltpu.VMEM((3, 192, 512), BF),
            pltpu.VMEM((3, 192, 512), BF),
            pltpu.VMEM((3, 512, 192), BF),
            pltpu.VMEM((3, 512, 192), BF),
            pltpu.VMEM((8, 512), F32),
            pltpu.VMEM((192, 512), F32),
            pltpu.VMEM((4, 512, 384), BF),
            pltpu.VMEM((4, 512, 384), BF),
            pltpu.VMEM((4, 512, 384), BF),
            pltpu.VMEM((4, 512, 384), BF),
            pltpu.VMEM((3, 4, 48, 384), BF),
            pltpu.VMEM((3, 2, 48, 768), BF),
        ],
        spaces=([VMEM] * 8, [VMEM] * 4),
        name="attend_back",
    )


def normalize(rows):
    centered = rows - jnp.mean(rows, -1, keepdims=True)
    inverse = lax.rsqrt(jnp.mean(centered * centered, -1, keepdims=True) + EPSILON)
    return centered * inverse, inverse


def normalize_back(normed, inverse, gain, grad):
    scaled = grad * gain
    return inverse * (
        scaled
        - jnp.mean(scaled, -1, keepdims=True)
        - normed * jnp.mean(scaled * normed, -1, keepdims=True)
    )


def feed_forward(heads_all, x_group, dy_group, wo, wf, wp, rows768, fc_bias):
    def kernel(
        h_ref, x_ref, dy_ref, wo_ref, wf_ref, wp_ref, v_ref, fb_ref,
        out_ref, gx_ref, bo_ref, gwf_ref, gwp_ref, gfb_ref, gv_ref,
        a2, act, df, x_two, normed, inverse, norm_other, norm_mine, res_other, res_mine,
        norm_got, res_got, norm_far, res_far, branch,
        cs, cr, es, er, zs, zr, ws, wr, bs, br,
    ):
        y, z, k, x = coords()
        sib = device(y, z, 1 - k, x)
        steps = (1, 2, 3)
        greet([sib] + [device(y, ring(z, d), k, x) for d in steps])
        out_bias, gain, shift, proj_bias = (v_ref[i : i + 1] for i in range(4))

        def half(kk, norm_ref, res_ref):
            two = x_ref[kk].reshape(512, 768).astype(F32) + out_bias
            for g in range(4):
                h = h_ref[g, kk]
                at = slice(192 * g, 192 * g + 192)
                part = jnp.concatenate([dot(h, wo_ref[0, at]), dot(h, wo_ref[1, at])], 1)
                two = two + part
            x_two[...] = two
            n, inv = normalize(two)
            normed[...] = n
            inverse[...] = jnp.broadcast_to(inv, (512, 128))
            a = (n * gain + shift).astype(BF)
            a2[kk] = a
            hidden = dot(a, wf_ref[...]) + fb_ref[...]
            square = hidden * hidden
            t = jnp.tanh(0.7978845608028654 * (hidden + 0.044715 * square * hidden))
            act_blk = (0.5 * hidden * (1.0 + t)).astype(BF)
            act[kk] = act_blk
            slope = 0.5 * (1.0 + t) + 0.5 * hidden * (1.0 - t * t) * (
                0.7978845608028654 * (1.0 + 3 * 0.044715 * square)
            )
            dy = dy_ref[kk].reshape(512, 768)
            back = lax.dot_general(
                dy, wp_ref[...], (((1,), (1,)), ((), ())), preferred_element_type=F32
            )
            df_blk = (back * slope).astype(BF)
            df[kk] = df_blk
            norm_part = lax.dot_general(
                df_blk, wf_ref[...], (((1,), (1,)), ((), ())), preferred_element_type=F32
            )
            norm_ref[...] = norm_part.astype(BF).reshape(4, 128, 768)
            res_ref[...] = dot(act_blk, wp_ref[...]).astype(BF).reshape(4, 128, 768)

        half(1 - k, norm_other, res_other)
        swaps = []
        for d in (1, 2, 3, 0):
            b = ring(z, d)
            c = remote(norm_other.at[b], norm_got.at[b], cs.at[d], cr.at[d], sib)
            c.start()
            swaps.append(c)
        for d in (1, 2, 3, 0):
            b = ring(z, d)
            c = remote(res_other.at[b], res_got.at[b], es.at[d], er.at[d], sib)
            c.start()
            swaps.append(c)
        half(k, norm_mine, res_mine)
        sends = []
        for i, (mine, got, far, s, r) in enumerate(
            ((norm_mine, norm_got, norm_far, zs, zr), (res_mine, res_got, res_far, ws, wr))
        ):
            for d in steps:
                b = ring(z, d)
                swaps[4 * i + d - 1].wait_recv()
                mine[b] = (mine[b].astype(F32) + got[b].astype(F32)).astype(BF)
                c = remote(
                    mine.at[b], far.at[d - 1], s.at[d - 1], r.at[d - 1], device(y, b, k, x)
                )
                c.start()
                sends.append(c)
        tn = (((0,), (0,)), ((), ()))
        gwf = lax.dot_general(a2[0], df[0], tn, preferred_element_type=F32)
        gwf += lax.dot_general(a2[1], df[1], tn, preferred_element_type=F32)
        gwf_ref[...] = gwf.astype(BF)
        own_rows = pl.ds(pl.multiple_of(128 * z, 128), 128)
        swaps[3].wait_recv()
        for c in sends[:3]:
            c.wait_recv()
        da = (
            norm_mine[z].astype(F32)
            + norm_got[z].astype(F32)
            + norm_far[0].astype(F32)
            + norm_far[1].astype(F32)
            + norm_far[2].astype(F32)
        )
        n = normed[own_rows]
        dy = dy_ref[k, z].astype(F32)
        gx = dy + normalize_back(n, inverse[own_rows, 0:1], gain, da)
        gx_ref[...] = gx
        low = gx.astype(BF)
        branch[...] = low
        bo_ref[z] = low
        branches = []
        for d in steps:
            c = remote(
                branch, bo_ref.at[z], bs.at[d - 1], br.at[d - 1], device(y, ring(z, d), k, x)
            )
            c.start()
            branches.append(c)
        gwp = lax.dot_general(
            act[0], dy_ref[0].reshape(512, 768), tn, preferred_element_type=F32
        )
        gwp += lax.dot_general(
            act[1], dy_ref[1].reshape(512, 768), tn, preferred_element_type=F32
        )
        gwp_ref[...] = gwp.astype(BF)
        gfb_ref[...] = jnp.sum(df[0].astype(F32), 0, keepdims=True) + jnp.sum(
            df[1].astype(F32), 0, keepdims=True
        )
        gv_ref[0:1] = jnp.sum(low.astype(F32), 0, keepdims=True)
        gv_ref[1:2] = jnp.sum(da * n, 0, keepdims=True)
        gv_ref[2:3] = jnp.sum(da, 0, keepdims=True)
        gv_ref[3:4] = jnp.sum(dy, 0, keepdims=True)
        swaps[7].wait_recv()
        for c in sends[3:]:
            c.wait_recv()
        out_ref[...] = (
            x_two[own_rows]
            + proj_bias
            + res_mine[z].astype(F32)
            + res_got[z].astype(F32)
            + res_far[0].astype(F32)
            + res_far[1].astype(F32)
            + res_far[2].astype(F32)
        )
        for c in branches:
            c.wait()
        for c in swaps + sends:
            c.wait_send()

    return comm(
        kernel,
        [
            jax.ShapeDtypeStruct((128, 768), F32),
            jax.ShapeDtypeStruct((128, 768), F32),
            jax.ShapeDtypeStruct((4, 128, 768), BF),
            jax.ShapeDtypeStruct((768, 384), BF),
            jax.ShapeDtypeStruct((384, 768), BF),
            jax.ShapeDtypeStruct((1, 384), F32),
            jax.ShapeDtypeStruct((4, 768), F32),
        ],
        3,
        (4, 4, 4, 4, 3, 3, 3, 3, 3, 3),
        (heads_all, x_group, dy_group, wo, wf, wp, rows768, fc_bias),
        scratch=[
            pltpu.VMEM((2, 512, 768), BF),
            pltpu.VMEM((2, 512, 384), BF),
            pltpu.VMEM((2, 512, 384), BF),
            pltpu.VMEM((512, 768), F32),
            pltpu.VMEM((512, 768), F32),
            pltpu.VMEM((512, 128), F32),
        ]
        + [pltpu.VMEM((4, 128, 768), BF)] * 6
        + [pltpu.VMEM((3, 128, 768), BF)] * 2
        + [pltpu.VMEM((128, 768), BF)],
        spaces=([VMEM] * 8, [VMEM] * 7),
        name="feed_forward",
    )


def adam_update(weight, moment_one, moment_two, gradient, rate, decay):
    new_one = BETA_ONE * moment_one + (1.0 - BETA_ONE) * gradient
    new_two = BETA_TWO * moment_two + (1.0 - BETA_TWO) * gradient * gradient
    fix_one = 1.0 - BETA_ONE**STEP
    fix_two = 1.0 - BETA_TWO**STEP
    direction = new_one / fix_one / (jnp.sqrt(new_two / fix_two) + ADAM_EPSILON)
    return (weight - rate * (direction + decay * weight), new_one, new_two)


def shards(
    tokens,
    cotangent,
    w_qkv,
    qkv_m,
    qkv_v,
    w_out,
    out_m,
    out_v,
    w_fc,
    fc_m,
    fc_v,
    w_proj,
    proj_m,
    proj_v,
    vectors,
    vec_m,
    vec_v,
):
    y, z, k, x = coords()
    wq, fc_part, out_part, proj_part, x_group = first_gather(
        w_qkv, w_fc, w_out, w_proj, vectors, tokens[0]
    )
    wq = wq.reshape(768, 640)
    vec_rows = wq[:, 576:592].astype(F32).T
    gain_one = vec_rows[0]
    bias = jnp.concatenate(
        [
            lax.dynamic_slice(vec_rows, (2, 192 * z), (1, 192)),
            jnp.zeros((1, 192), F32),
            lax.dynamic_slice(vec_rows, (3, 192 * z), (1, 192)),
            jnp.zeros((1, 64), F32),
        ],
        1,
    )
    fc_bias = lax.dynamic_slice(vec_rows[8:12].reshape(1, 3072), (0, (2 * z + k) * 384), (1, 384))
    heads_all, out_t, lse, kv_all, dy_group, wf, wo, wp, query, act_one, normed_core = attend(
        x_group, wq, bias, vec_rows[0:2], cotangent[0], fc_part, out_part, proj_part
    )
    wo = wo.reshape(2, 768, 384)
    output, grad_x_two, branch_core, grad_w_fc, grad_w_proj, grad_fc_bias, vec_sums = feed_forward(
        heads_all,
        x_group,
        dy_group,
        wo,
        wf.reshape(768, 384),
        wp.reshape(384, 768),
        vec_rows[4:8],
        fc_bias,
    )
    branch_core = branch_core.reshape(512, 768)
    grad_query, grad_kv, fc_sum, proj_sum = attend_back(
        query,
        branch_core,
        wo,
        kv_all,
        out_t,
        lse,
        grad_w_fc.reshape(4, 4, 48, 384),
        grad_w_proj.reshape(2, 4, 48, 768),
    )
    grad_mixed = jnp.concatenate([grad_query, grad_kv.astype(BF)], 1)
    branch_cols = lax.dynamic_slice(branch_core, (0, 192 * z), (512, 192))
    heads_core = lax.dynamic_index_in_dim(heads_all, k, 1, False)
    heads_core = jnp.concatenate([heads_core[i] for i in range(4)], 1)
    left = jnp.concatenate([act_one, heads_core], 0)
    gap = jnp.zeros((512, 96), BF)
    room = jnp.zeros((512, 288), BF)
    right = jnp.concatenate(
        [
            jnp.concatenate([grad_mixed[:, :288], gap, grad_mixed[:, 288:], gap], 1),
            jnp.concatenate([room, branch_cols[:, :96], room, branch_cols[:, 96:]], 1),
        ],
        0,
    )
    grad_mix = dot(left.T, right).astype(BF)
    one_part = dot(grad_mixed, wq[:, :576].T)

    def spread(piece, at, size):
        return lax.dynamic_update_slice(jnp.zeros((size,), F32), piece, (at,))

    mixed_sums = jnp.sum(grad_mixed.astype(F32), 0)
    columns = jnp.stack(
        [
            jnp.sum(one_part * normed_core.astype(F32), 0),
            jnp.sum(one_part, 0),
            spread(mixed_sums[:192], 192 * z, 768),
            spread(mixed_sums[384:], 192 * z, 768),
            vec_sums[0],
            vec_sums[1],
            vec_sums[2],
            vec_sums[3],
        ]
        + list(spread(grad_fc_bias[0], (2 * z + k) * 384, 3072).reshape(4, 768)),
        1,
    )
    grad_vec = jnp.pad(columns, ((0, 0), (0, 116))).astype(BF)
    grad_norm_one, last_rows, sum_proj = last_sums(
        one_part.astype(BF).reshape(4, 128, 768),
        grad_mix.reshape(4, 4, 48, 768),
        grad_vec.reshape(4, 4, 48, 128),
        fc_sum,
        proj_sum,
    )
    normed_one, inverse_one = normalize(tokens[0].astype(F32))
    grad_inputs = grad_x_two + normalize_back(normed_one, inverse_one, gain_one, grad_norm_one)
    last_rows = last_rows[:, :6]
    mix_rows = last_rows[:, :, :1536].reshape(2, 6, 4, 384)
    sum_qkv = (
        mix_rows[..., :288]
        .transpose(1, 2, 0, 3)
        .reshape(6, 4, 3, 192)
        .transpose(0, 2, 1, 3)
        .reshape(6, 2304)
    )
    sum_out = mix_rows[..., 288:].transpose(1, 2, 0, 3).reshape(6, 768)
    sum_fc = last_rows[:, :, 1536:3072].reshape(2, 6, 4, 384).transpose(1, 2, 0, 3).reshape(6, 3072)
    sum_vec = last_rows[0, :, 3072:3084] + last_rows[1, :, 3072:3084]
    new_qkv = adam_update(w_qkv, qkv_m, qkv_v, sum_qkv, 0.1, 0.1)
    new_out = adam_update(w_out, out_m, out_v, sum_out, 0.3, 0.1)
    new_fc = adam_update(w_fc, fc_m, fc_v, sum_fc, 0.05, 0.1)
    new_proj = adam_update(w_proj, proj_m, proj_v, sum_proj, 0.03, 0.1)
    new_vec = adam_update(vectors, vec_m, vec_v, sum_vec, 0.5, 0.0)
    return (output[None], grad_inputs[None], *new_qkv, *new_out, *new_fc, *new_proj, *new_vec)


def solution(mesh):
    split = P("fsdp", "ctx", None)
    rows = P(("ctx", "fsdp"), None)
    return jax.shard_map(
        shards,
        mesh=mesh,
        in_specs=(split, split) + (rows,) * 15,
        out_specs=(split, split) + (rows,) * 15,
        check_vma=False,
    )
```

```python
import jax
import jax.numpy as jnp
from jax import lax
from jax.experimental import pallas as pl
from jax.experimental.pallas import tpu as pltpu
from jax.sharding import PartitionSpec as P

STEP = 10
EPSILON = 1e-05
BETA_ONE = 0.9
BETA_TWO = 0.999
ADAM_EPSILON = 1e-08
MESH = pl.DeviceIdType.MESH
BF = jnp.bfloat16
F32 = jnp.float32
ANY = pl.BlockSpec(memory_space=pl.ANY)
VMEM = pl.BlockSpec(memory_space=pltpu.VMEM)
LIMIT = 56 * 1024 * 1024


def coords():
    c = lax.axis_index("ctx")
    return c // 8, (c // 2) % 4, c % 2, lax.axis_index("fsdp")


def device(y, z, k, x):
    return ((y * 4 + z) * 2 + k, x)


def ring(v, step):
    return lax.rem(v + step, 4)


def greet(devices):
    barrier = pltpu.get_barrier_semaphore()
    for one in devices:
        pl.semaphore_signal(barrier, inc=1, device_id=one, device_id_type=MESH)
    pl.semaphore_wait(barrier, len(devices))


def remote(src, dst, send, recv, to):
    return pltpu.make_async_remote_copy(
        src, dst, send, recv, device_id=to, device_id_type=MESH
    )


def comm(kernel, outs, cid, sems, args, scratch=(), spaces=None, name=None):
    return pl.pallas_call(
        kernel,
        out_shape=outs,
        in_specs=[ANY] * len(args) if spaces is None else spaces[0],
        out_specs=[ANY] * len(outs) if spaces is None else spaces[1],
        scratch_shapes=list(scratch) + [pltpu.SemaphoreType.DMA((n,)) for n in sems],
        compiler_params=pltpu.CompilerParams(
            collective_id=cid, has_side_effects=True, vmem_limit_bytes=LIMIT
        ),
        name=name,
    )(*args)


def first_gather(w_qkv, w_fc, w_out, w_proj, vectors, rows):
    width = 4736

    def kernel(
        wq_ref, wf_ref, wo_ref, wp_ref, wv_ref, r_ref,
        q_out, f_out, o_out, p_out, ro_ref,
        wide, packed, got, fc48, qkv48, out48, proj_wide, q_send, f_send, o_send, p_send,
        ms, mr, fs, fr, s1, r1, s2, r2, ps, pr, xs_s, xs_r, xf_s, xf_r, rs, rr, cs, cr, loc,
    ):
        y, z, k, x = coords()
        me = y * 4 + z
        sib = device(y, z, 1 - k, x)
        steps = (1, 2, 3)
        greet(
            [sib]
            + [device(y, z, k, ring(x, d)) for d in steps]
            + [
                device(ring(y, a), ring(z, b), k, x)
                for a in range(4)
                for b in range(4)
                if (a, b) != (0, 0)
            ]
        )
        own_r = pltpu.make_async_copy(r_ref, ro_ref.at[k, z], loc.at[0])
        own_r.start()
        row_copies = []
        for d in steps:
            c = remote(
                r_ref, ro_ref.at[k, z], rs.at[d], rr.at[d], device(y, ring(z, d), k, x)
            )
            row_copies.append(c)
        wide[...] = jnp.zeros_like(wide)
        wide[0:6, 0:3072] = wf_ref[...]
        wide[6:12, 0:2304] = wq_ref[...]
        wide[6:12, 2304:3072] = wo_ref[...]
        wide[0:12, 3072:3840] = wp_ref[0:12]
        wide[0:12, 3840:4608] = wp_ref[12:24]
        wide[0:6, 4608:4620] = wv_ref[...]
        t = k * 4 + x
        packed[...] = wide[...].astype(BF)
        got[t] = packed[...]
        message = []
        for d in steps:
            c = remote(packed, got.at[t], ms.at[d], mr.at[d], device(y, z, k, ring(x, d)))
            c.start()
            message.append(c)
        c = remote(packed, got.at[t], fs.at[0], fr.at[0], sib)
        c.start()
        forward = [c]
        for c in row_copies:
            c.start()
        c = remote(r_ref, ro_ref.at[k, z], cs.at[0], cr.at[0], sib)
        c.start()
        row_forward = [c]
        for d in steps:
            message[d - 1].wait_recv()
            src = k * 4 + ring(x, 4 - d)
            f = remote(got.at[src], got.at[src], fs.at[d], fr.at[d], sib)
            f.start()
            forward.append(f)
        for f in forward:
            f.wait_recv()
        for i in range(8):
            piece = got[i].astype(F32)
            at = slice(6 * i, 6 * i + 6)
            fc48[at] = piece[0:6, 0:3072]
            qkv48[at] = piece[6:12, 0:2304]
            out48[at, 0:768] = piece[6:12, 2304:3072]
            out48[at, 768:896] = piece[0:6, 4608:4736]
            proj_wide[24 * i : 24 * i + 12] = piece[0:12, 3072:3840]
            proj_wide[24 * i + 12 : 24 * i + 24] = piece[0:12, 3840:4608]
        for j in range(4):
            q_send[j, :, 0:192] = qkv48[:, 192 * j : 192 * j + 192].astype(BF)
            q_send[j, :, 192:384] = qkv48[:, 768 + 192 * j : 960 + 192 * j].astype(BF)
            q_send[j, :, 384:576] = qkv48[:, 1536 + 192 * j : 1728 + 192 * j].astype(BF)
            q_send[j, :, 576:640] = out48[:, 768:832].astype(BF)
        for j in range(8):
            f_send[j] = fc48[:, 384 * j : 384 * j + 384].astype(BF)
        o_send[0] = out48[:, 0:384].astype(BF)
        o_send[1] = out48[:, 384:768].astype(BF)
        p_send[...] = proj_wide[...].astype(BF)

        group = pl.ds(pl.multiple_of(16 * jnp.minimum(x, 2), 16), 16)

        def to_of(m):
            return ring(y, m // 4), ring(z, m % 4)

        def q_copy(m):
            ty, tz = to_of(m)
            return remote(
                q_send.at[tz, group], q_out.at[me, group], s1.at[m], r1.at[m],
                device(ty, tz, k, x),
            )

        def f_copy(m):
            ty, tz = to_of(m)
            return remote(
                f_send.at[tz * 2 + k], f_out.at[me], s2.at[m], r2.at[m], device(ty, tz, k, x)
            )

        def o_copy(m):
            ty, tz = to_of(m)
            return remote(o_send.at[k], o_out.at[me], s2.at[m], r2.at[m], device(ty, tz, k, x))

        def p_copy(a):
            return remote(
                p_send, p_out.at[z % 2], ps.at[a], pr.at[z % 2], device(ring(y, a), y, k, x)
            )

        def each(copy, what):
            def step(m, carry):
                what(copy(m))
                return carry

            lax.fori_loop(1, 16, step, 0)

        start = lambda c: c.start()
        finish = lambda c: c.wait()

        @pl.when(x < 3)
        def _():
            each(q_copy, start)
            c = pltpu.make_async_copy(q_send.at[z, group], q_out.at[me, group], loc.at[1])
            c.start()
            c.wait()

        @pl.when(x == 1)
        def _():
            each(f_copy, start)
            c = pltpu.make_async_copy(f_send.at[z * 2 + k], f_out.at[me], loc.at[2])
            c.start()
            c.wait()

        @pl.when(x == 2)
        def _():
            each(o_copy, start)
            c = pltpu.make_async_copy(o_send.at[k], o_out.at[me], loc.at[2])
            c.start()
            c.wait()

        @pl.when((x == 3) & (k == z // 2))
        def _():
            for a in range(1, 4):
                p_copy(a).start()

            @pl.when(z != y)
            def _():
                p_copy(0).start()

            @pl.when(z == y)
            def _():
                c = pltpu.make_async_copy(p_send, p_out.at[z % 2], loc.at[2])
                c.start()
                c.wait()

        half = pl.ds(8 * k, 8)
        other_half = pl.ds(8 * (1 - k), 8)

        def rows_of(plane):
            return pl.ds(pl.multiple_of(16 * plane, 16), 16)

        @pl.when(x < 3)
        def _():
            each(q_copy, finish)
            for d in steps:
                remote(
                    q_out.at[half, group], q_out.at[half, group], xs_s.at[d], xs_r.at[x],
                    device(y, z, k, ring(x, d)),
                ).start()

        def pass_on(a):
            return remote(
                q_out.at[half, rows_of(a)], q_out.at[half, rows_of(a)], xf_s.at[a], xf_r.at[a], sib
            )

        for a in range(3):

            @pl.when(x != a)
            def _():
                remote(
                    q_out.at[half, rows_of(a)], q_out.at[half, rows_of(a)], xs_s.at[0],
                    xs_r.at[a], sib,
                ).wait_recv()
                pass_on(a).start()

        for d in steps:
            row_copies[d - 1].wait_recv()
            src = ring(z, 4 - d)
            f = remote(ro_ref.at[k, src], ro_ref.at[k, src], cs.at[d], cr.at[d], sib)
            f.start()
            row_forward.append(f)

        @pl.when(x == 1)
        def _():
            each(f_copy, finish)

        @pl.when(x == 2)
        def _():
            each(o_copy, finish)

        @pl.when((x == 3) & (k == z // 2))
        def _():
            for a in range(1, 4):
                p_copy(a).wait_send()

            @pl.when(z != y)
            def _():
                p_copy(0).wait_send()

        for j in range(2):
            @pl.when((x == 3) & jnp.logical_not((y == z) & (z == 2 * k + j)))
            def _():
                remote(p_send, p_out.at[j], ps.at[0], pr.at[j], sib).wait_recv()

        @pl.when(x < 3)
        def _():
            for d in steps:
                remote(
                    q_out.at[half, group], q_out.at[half, group], xs_s.at[d], xs_r.at[x],
                    device(y, z, k, ring(x, d)),
                ).wait_send()

        for a in range(3):

            @pl.when(x != a)
            def _():
                pass_on(a).wait_send()
                remote(
                    q_out.at[other_half, rows_of(a)], q_out.at[other_half, rows_of(a)],
                    xf_s.at[a], xf_r.at[a], sib,
                ).wait_recv()

        for c in message + row_copies + forward:
            c.wait_send()
        for c in row_forward:
            c.wait()
        own_r.wait()

    return comm(
        kernel,
        [
            jax.ShapeDtypeStruct((16, 48, 640), BF),
            jax.ShapeDtypeStruct((16, 48, 384), BF),
            jax.ShapeDtypeStruct((16, 48, 384), BF),
            jax.ShapeDtypeStruct((2, 192, 768), BF),
            jax.ShapeDtypeStruct((2, 4) + rows.shape, BF),
        ],
        0,
        (4, 4, 4, 4, 16, 16, 16, 16, 4, 2, 4, 4, 4, 4, 4, 4, 4, 4, 3),
        (w_qkv, w_fc, w_out, w_proj, vectors, rows),
        scratch=[
            pltpu.VMEM((16, width), F32),
            pltpu.VMEM((16, width), BF),
            pltpu.VMEM((8, 16, width), BF),
            pltpu.VMEM((48, 3072), F32),
            pltpu.VMEM((48, 2304), F32),
            pltpu.VMEM((48, 896), F32),
            pltpu.VMEM((192, 768), F32),
            pltpu.VMEM((4, 48, 640), BF),
            pltpu.VMEM((8, 48, 384), BF),
            pltpu.VMEM((2, 48, 384), BF),
            pltpu.VMEM((192, 768), BF),
        ],
        spaces=([VMEM] * 5 + [ANY], [ANY] * 5),
        name="first_gather",
    )


def last_sums(pieces, fc, proj, state):
    wide = 3200

    def kernel(*refs):
        (
            act_ref, n_ref, h_ref, gq_ref, gkv_ref, br_ref, wq_ref, vs_ref, fb_ref,
            tok_ref, gx_ref, gain_ref, fc_ref, proj_ref,
        ) = refs[:14]
        state_ref = refs[14:29]
        gin_ref = refs[29]
        new_ref = refs[30:45]
        (
            one_far, mix_got, mix_sum, mix_far, vec_far, mix_mine, vec_mine,
            mix_all, fc_all, vec_all, proj_all, proj_sum, out_send,
            one_ref, mix_other, mix_ref, vec_ref, rows_out, proj_out,
            act_t, heads, heads_t, d_ref, right_one, right_two, vec_rows, g_qkv, g_out, g_fc,
        ) = refs[45:74]
        (
        zs, zr, cs, cr, s1, r1, s2, r2, s3, r3, s4, r4, s5, r5, s6, r6, s7, r7, s8, r8, loc,
        ) = refs[74:]
        y, z, k, x = coords()
        me = y * 4 + z
        sib = device(y, z, 1 - k, x)
        steps = (1, 2, 3)
        greet(
            [sib]
            + [device(y, z, j, ring(x, d)) for d in steps for j in (k, 1 - k)]
            + [
                device(ring(y, a), ring(z, b), k, x)
                for a in range(4)
                for b in range(4)
                if (a, b) != (0, 0)
            ]
        )
        d_ref[:, 0:192] = gq_ref[...]
        d_ref[:, 192:576] = gkv_ref[...].astype(BF)
        d_ref[:, 576:640] = jnp.zeros((512, 64), BF)
        right_one[...] = jnp.zeros_like(right_one)
        right_one[:, 0:288] = d_ref[:, 0:288]
        right_one[:, 384:672] = d_ref[:, 288:576]
        right_two[...] = jnp.zeros_like(right_two)
        vec_rows[...] = jnp.zeros_like(vec_rows)
        sums = jnp.sum(d_ref[...].astype(F32), 0, keepdims=True)
        at_half = pl.ds(pl.multiple_of(384 * k, 128), 384)
        for b in range(4):
            heads[:, 192 * b : 192 * b + 192] = h_ref[b, k]

            @pl.when(z == b)
            def _():
                right_two[:, 288:384] = br_ref[:, 192 * b : 192 * b + 96]
                right_two[:, 672:768] = br_ref[:, 192 * b + 96 : 192 * b + 192]
                vec_rows[2:3, 192 * b : 192 * b + 192] = sums[:, 0:192]
                vec_rows[3:4, 192 * b : 192 * b + 192] = sums[:, 384:576]
                vec_rows[8 + b : 9 + b, at_half] = fb_ref[...]

        vec_rows[4:8] = vs_ref[...]
        act_t[...] = act_ref[...].T
        heads_t[...] = heads[...].T

        def product(h):
            at = pl.ds(pl.multiple_of(384 * h, 128), 384)
            total = dot(act_t[...], right_one[:, at]) + dot(heads_t[...], right_two[:, at])
            return total.reshape(4, 4, 48, 384)

        mix_other[...] = product(1 - k).astype(BF)
        swap = []
        for d in (1, 2, 3, 0):
            b = ring(x, d)
            c = remote(mix_other.at[:, b], mix_got.at[b], cs.at[d], cr.at[d], sib)
            c.start()
            swap.append(c)
        mix_ref[...] = product(k).astype(BF)
        one = lax.dot_general(
            d_ref[...], wq_ref[...], (((1,), (1,)), ((), ())), preferred_element_type=F32
        )
        one_ref[...] = one.astype(BF).reshape(4, 128, 768)
        vec_rows[0:1] = jnp.sum(one * n_ref[...].astype(F32), 0, keepdims=True)
        vec_rows[1:2] = jnp.sum(one, 0, keepdims=True)
        vec_ref[...] = vec_rows[...].T.astype(BF).reshape(4, 4, 48, 128)
        along = []
        for d in steps:
            b = ring(x, d)
            to = device(y, z, k, b)
            swap[d - 1].wait_recv()
            mix_sum[d] = (mix_ref[:, b].astype(F32) + mix_got[b].astype(F32)).astype(BF)
            c = remote(mix_sum.at[d], mix_far.at[d - 1], s1.at[d - 1], r1.at[d - 1], to)
            c.start()
            along.append(c)
            c = remote(vec_ref.at[:, b], vec_far.at[d - 1], s2.at[d - 1], r2.at[d - 1], to)
            c.start()
            along.append(c)
        ones = []
        for d in steps:
            c = remote(
                one_ref.at[ring(z, d)], one_far.at[d - 1], zs.at[d - 1], zr.at[d - 1],
                device(y, ring(z, d), k, x),
            )
            c.start()
            ones.append(c)

        def plane(src, dst, send, recv, a):
            return remote(src.at[a], dst.at[me], send.at[a], recv.at[me], device(a, x, k, x))

        def all_start(src, dst, send, recv):
            for a in range(4):
                here = (a == y) & (z == x)

                @pl.when(jnp.logical_not(here))
                def _():
                    plane(src, dst, send, recv, a).start()

                @pl.when(here)
                def _():
                    c = pltpu.make_async_copy(src.at[a], dst.at[me], loc.at[0])
                    c.start()
                    c.wait()

        def all_finish(src, dst, send, recv):
            for a in range(4):

                @pl.when(jnp.logical_not((a == y) & (z == x)))
                def _():
                    plane(src, dst, send, recv, a).wait_send()

        def all_receive(src, dst, send, recv):
            def step(i, carry):
                @pl.when(i != me)
                def _():
                    remote(src.at[0], dst.at[i], send.at[0], recv.at[i], sib).wait_recv()

                return carry

            lax.fori_loop(0, 16, step, 0)

        all_start(fc_ref, fc_all, s4, r4)

        def proj_copy(j):
            return remote(
                proj_ref.at[j], proj_all.at[y], s6.at[j], r6.at[y], device(z, 2 * k + j, k, x)
            )

        for j in range(2):
            here = (y == z) & (z == 2 * k + j)

            @pl.when(jnp.logical_not(here))
            def _():
                proj_copy(j).start()

            @pl.when(here)
            def _():
                c = pltpu.make_async_copy(proj_ref.at[j], proj_all.at[y], loc.at[1])
                c.start()
                c.wait()

        swap[3].wait_recv()
        for c in along:
            c.wait_recv()
        mix_mine[...] = (
            mix_ref[:, x].astype(F32)
            + mix_got[x].astype(F32)
            + mix_far[0].astype(F32)
            + mix_far[1].astype(F32)
            + mix_far[2].astype(F32)
        ).astype(BF)
        vec_mine[...] = (
            vec_ref[:, x].astype(F32)
            + vec_far[0].astype(F32)
            + vec_far[1].astype(F32)
            + vec_far[2].astype(F32)
        ).astype(BF)
        all_start(mix_mine, mix_all, s3, r3)
        all_start(vec_mine, vec_all, s5, r5)
        for c in ones:
            c.wait_recv()
        grad = (
            one_ref[z].astype(F32)
            + one_far[0].astype(F32)
            + one_far[1].astype(F32)
            + one_far[2].astype(F32)
        )
        normed, inverse = normalize(tok_ref[...].astype(F32))
        gin_ref[...] = gx_ref[...] + normalize_back(normed, inverse, gain_ref[...], grad)

        def proj_last(i):
            return remote(
                proj_sum.at[i], proj_out, s8.at[i], r8.at[0],
                device(y, z, x // 2, lax.rem(2 * x + i, 4)),
            )

        def proj_here(i):
            return (k == x // 2) & (x == lax.rem(2 * x + i, 4))

        holder = k == z // 2
        for a in range(4):

            @pl.when(holder & jnp.logical_not((a == y) & (z == y)))
            def _():
                remote(proj_ref.at[0], proj_all.at[a], s6.at[0], r6.at[a], sib).wait_recv()

        @pl.when(holder)
        def _():
            total = (
                proj_all[0].astype(F32)
                + proj_all[1].astype(F32)
                + proj_all[2].astype(F32)
                + proj_all[3].astype(F32)
            )
            for i in range(2):
                proj_sum[i] = total[24 * i : 24 * i + 24]

                @pl.when(jnp.logical_not(proj_here(i)))
                def _():
                    proj_last(i).start()

                @pl.when(proj_here(i))
                def _():
                    c = pltpu.make_async_copy(proj_sum.at[i], proj_out, loc.at[2])
                    c.start()
                    c.wait()

        def last_copy(i):
            return remote(
                out_send.at[i], rows_out.at[k], s7.at[i], r7.at[k], device(y, z, i // 4, i % 4)
            )

        def last_here(i):
            return k * 4 + x == i

        @pl.when(z == x)
        def _():
            all_receive(fc_ref, fc_all, s4, r4)
            all_receive(mix_mine, mix_all, s3, r3)
            all_receive(vec_mine, vec_all, s5, r5)

            def four(ref, b):
                return (
                    ref[b].astype(F32)
                    + ref[4 + b].astype(F32)
                    + ref[8 + b].astype(F32)
                    + ref[12 + b].astype(F32)
                )

            for b in range(4):
                m, f = four(mix_all, b), four(fc_all, b)
                for i in range(8):
                    rows = slice(6 * i, 6 * i + 6)
                    out_send[i, 0:6, 384 * b : 384 * b + 384] = m[rows]
                    out_send[i, 0:6, 1536 + 384 * b : 1920 + 384 * b] = f[rows]
            v = four(vec_all, 0) + four(vec_all, 1) + four(vec_all, 2) + four(vec_all, 3)
            for i in range(8):
                out_send[i, 0:6, 3072:3200] = v[6 * i : 6 * i + 6]
                out_send[i, 6:8, :] = jnp.zeros((2, wide), F32)
            for i in range(8):

                @pl.when(jnp.logical_not(last_here(i)))
                def _():
                    last_copy(i).start()

                @pl.when(last_here(i))
                def _():
                    c = pltpu.make_async_copy(out_send.at[i], rows_out.at[k], loc.at[3])
                    c.start()
                    c.wait()

        for j in range(2):

            @pl.when(jnp.logical_not((z == x) & (k == j)))
            def _():
                remote(out_send.at[0], rows_out.at[j], s7.at[0], r7.at[j], sib).wait_recv()

        @pl.when(jnp.logical_not((k == z // 2) & (x == (4 * k + x) // 2)))
        def _():
            remote(proj_sum.at[0], proj_out, s8.at[0], r8.at[0], sib).wait_recv()

        for b in range(4):
            one_half = rows_out[0, 0:6, 384 * b : 384 * b + 384]
            two_half = rows_out[1, 0:6, 384 * b : 384 * b + 384]
            q = 192 * b
            g_qkv[:, q : q + 192] = one_half[:, 0:192]
            g_qkv[:, 768 + q : 864 + q] = one_half[:, 192:288]
            g_qkv[:, 864 + q : 960 + q] = two_half[:, 0:96]
            g_qkv[:, 1536 + q : 1728 + q] = two_half[:, 96:288]
            g_out[:, q : q + 96] = one_half[:, 288:384]
            g_out[:, q + 96 : q + 192] = two_half[:, 288:384]
            for j in range(2):
                at = 384 * (2 * b + j)
                g_fc[:, at : at + 384] = rows_out[j, 0:6, 1536 + 384 * b : 1920 + 384 * b]
        g_vec = rows_out[0, 0:6, 3072:3084] + rows_out[1, 0:6, 3072:3084]
        for i, (gradient, rate, decay) in enumerate(
            (
                (g_qkv[...], 0.1, 0.1),
                (g_out[...], 0.3, 0.1),
                (g_fc[...], 0.05, 0.1),
                (proj_out[...], 0.03, 0.1),
                (g_vec, 0.5, 0.0),
            )
        ):
            w, m, v = state_ref[3 * i : 3 * i + 3]
            results = adam_update(w[...], m[...], v[...], gradient, rate, decay)
            for j in range(3):
                new_ref[3 * i + j][...] = results[j]

        @pl.when(z == x)
        def _():
            for i in range(8):

                @pl.when(jnp.logical_not(last_here(i)))
                def _():
                    last_copy(i).wait_send()

        for i in range(2):

            @pl.when(holder & jnp.logical_not(proj_here(i)))
            def _():
                proj_last(i).wait_send()

        for j in range(2):

            @pl.when(jnp.logical_not((y == z) & (z == 2 * k + j)))
            def _():
                proj_copy(j).wait_send()

        all_finish(fc_ref, fc_all, s4, r4)
        all_finish(mix_mine, mix_all, s3, r3)
        all_finish(vec_mine, vec_all, s5, r5)
        for c in swap + along + ones:
            c.wait_send()

    return comm(
        kernel,
        [
            jax.ShapeDtypeStruct((128, 768), F32),
        ]
        + [jax.ShapeDtypeStruct(one.shape, F32) for one in state],
        6,
        (3, 3, 4, 4, 3, 3, 3, 3, 4, 16, 4, 16, 4, 16, 2, 4, 8, 2, 2, 1, 4),
        (*pieces, fc, proj, *state),
        scratch=[
            pltpu.VMEM((3, 128, 768), BF),
            pltpu.VMEM((4, 4, 48, 384), BF),
            pltpu.VMEM((4, 4, 48, 384), BF),
            pltpu.VMEM((3, 4, 48, 384), BF),
            pltpu.VMEM((3, 4, 48, 128), BF),
            pltpu.VMEM((4, 48, 384), BF),
            pltpu.VMEM((4, 48, 128), BF),
            pltpu.VMEM((16, 48, 384), BF),
            pltpu.VMEM((16, 48, 384), BF),
            pltpu.VMEM((16, 48, 128), BF),
            pltpu.VMEM((4, 48, 768), BF),
            pltpu.VMEM((2, 24, 768), F32),
            pltpu.VMEM((8, 8, wide), F32),
            pltpu.VMEM((4, 128, 768), BF),
            pltpu.VMEM((4, 4, 48, 384), BF),
            pltpu.VMEM((4, 4, 48, 384), BF),
            pltpu.VMEM((4, 4, 48, 128), BF),
            pltpu.VMEM((2, 8, wide), F32),
            pltpu.VMEM((24, 768), F32),
            pltpu.VMEM((768, 512), BF),
            pltpu.VMEM((512, 768), BF),
            pltpu.VMEM((768, 512), BF),
            pltpu.VMEM((512, 640), BF),
            pltpu.VMEM((512, 768), BF),
            pltpu.VMEM((512, 768), BF),
            pltpu.VMEM((128, 768), F32),
            pltpu.VMEM((6, 2304), F32),
            pltpu.VMEM((6, 768), F32),
            pltpu.VMEM((6, 3072), F32),
        ],
        spaces=([VMEM] * 29, [VMEM] * 16),
        name="last_sums",
    )


def head_rows(matrix, head):
    row = lax.broadcasted_iota(jnp.int32, matrix.shape, 0)
    keep = (row >= 64 * head) & (row < 64 * head + 64)
    return jnp.where(keep, matrix, jnp.zeros_like(matrix))


def head_cols(matrix, head):
    col = lax.broadcasted_iota(jnp.int32, matrix.shape, 1)
    keep = (col >= 64 * head) & (col < 64 * head + 64)
    return jnp.where(keep, matrix, jnp.zeros_like(matrix))


def place(index):
    return (index // 128) * 256 + index % 128


def dot(a, b):
    return jnp.dot(a, b, preferred_element_type=F32)


def attend(tokens, wq, bias, rows768, rows, fc, out, proj):
    def kernel(
        x_ref, wq_ref, b_ref, g_ref, r_ref, f_ref, o_ref, p_ref,
        ho_ref, ot_ref, lse_ref, vo_ref, ro_ref, fo_ref, oo_ref, po_ref, q_ref, a_ref, n_ref,
        qt, m_ref, l_ref, h_buf, v_ref,
        vs, vr, rs, rr, cs, cr, ds, dr, ws, wr, os, orr, hs, hr, gs, gr, loc,
    ):
        y, z, k, x = coords()
        sib = device(y, z, 1 - k, x)
        steps = (1, 2, 3)
        greet(
            [sib]
            + [device(ring(y, d), z, k, x) for d in steps]
            + [device(y, ring(z, d), k, x) for d in steps]
            + [device(y, z, k, ring(x, d)) for d in steps]
        )

        own_r = pltpu.make_async_copy(r_ref, ro_ref.at[k, z], loc.at[0])
        own_r.start()
        row_copies = []
        for d in steps:
            c = remote(
                r_ref, ro_ref.at[k, z], rs.at[d], rr.at[d], device(y, ring(z, d), k, x)
            )
            c.start()
            row_copies.append(c)
        row_first = remote(r_ref, ro_ref.at[k, z], ds.at[0], dr.at[0], sib)
        row_first.start()

        weights = ((1, f_ref, fo_ref), (2, o_ref, oo_ref.at[k]), (3, p_ref, po_ref))

        def weight_copy(a, d):
            _, src, dst = weights[a - 1]
            return remote(src, dst, ws.at[d], wr.at[a], device(y, z, k, ring(x, d)))

        def weight_own(a):
            _, src, dst = weights[a - 1]
            return pltpu.make_async_copy(src, dst, loc.at[1])

        for a in steps:

            @pl.when(x == a)
            def _():
                for d in steps:
                    weight_copy(a, d).start()
                weight_own(a).start()

        normed, _ = normalize(x_ref[k].reshape(512, 768).astype(F32))
        n_ref[...] = normed.astype(BF)
        act = (normed * g_ref[0:1] + g_ref[1:2]).astype(BF)
        a_ref[...] = act
        mixed = dot(act, wq_ref[...]) + b_ref[...]
        v_ref[...] = mixed[:, 192:576].astype(BF)

        def kv_copy(d):
            return remote(
                v_ref, vo_ref.at[y, k], vs.at[d], vr.at[d], device(ring(y, d), z, k, x)
            )

        for d in steps:

            @pl.when(y + d < 4)
            def _():
                kv_copy(d).start()

        swap = remote(v_ref, vo_ref.at[y, k], cs.at[0], cr.at[0], sib)
        swap.start()
        vo_ref[y, k] = v_ref[...]
        query = mixed[:, :192].astype(BF) * jnp.asarray(0.125, BF)
        q_ref[...] = query
        q_t = query.T
        for head in range(3):
            qt[head] = head_rows(q_t, head)
        m_ref[...] = jnp.full_like(m_ref, -1e30)
        l_ref[...] = jnp.zeros_like(l_ref)
        ot_ref[...] = jnp.zeros_like(ot_ref)

        def block(by, bk, masked):
            keys = vo_ref[by, bk, :, :192]
            values_t = vo_ref[by, bk, :, 192:].T
            if masked:
                key_at = place(lax.broadcasted_iota(jnp.int32, (512, 512), 0)) + 128 * bk
                query_at = place(lax.broadcasted_iota(jnp.int32, (512, 512), 1)) + 128 * k
                visible = query_at >= key_at
            for head in range(3):
                s = dot(keys, qt[head])
                if masked:
                    s = jnp.where(visible, s, -1e9)
                old = m_ref[head : head + 1]
                new = jnp.maximum(old, jnp.max(s, 0, keepdims=True))
                e = jnp.exp(s - new)
                scale = jnp.exp(old - new)
                m_ref[head : head + 1] = new
                l_ref[head : head + 1] = l_ref[head : head + 1] * scale + jnp.sum(
                    e, 0, keepdims=True
                )
                at = slice(64 * head, 64 * head + 64)
                ot_ref[at] = ot_ref[at] * scale + dot(values_t[at], e.astype(BF))

        def diagonal(j, carry):
            @pl.when(j == 1)
            def _():
                remote(v_ref, vo_ref.at[y, 1 - k], cs.at[0], cr.at[0], sib).wait_recv()

            block(y, lax.rem(k + j, 2), True)
            return carry

        lax.fori_loop(0, 2, diagonal, 0)

        def pass_on(d):
            return remote(
                vo_ref.at[y - d, k], vo_ref.at[y - d, k], cs.at[d], cr.at[d], sib
            )

        def earlier(i, carry):
            d, j = i // 2 + 1, i % 2

            @pl.when(j == 0)
            def _():
                remote(v_ref, vo_ref.at[y - d, k], vs.at[d], vr.at[d], sib).wait_recv()
                pass_on(d).start()

            @pl.when(j == 1)
            def _():
                remote(v_ref, vo_ref.at[y - d, 1 - k], cs.at[d], cr.at[d], sib).wait_recv()

            block(y - d, lax.rem(k + j, 2), False)
            return carry

        lax.fori_loop(0, 2 * y, earlier, 0)
        for head in range(3):
            at = slice(64 * head, 64 * head + 64)
            total = l_ref[head : head + 1]
            ot_ref[at] = ot_ref[at] / total
            lse_ref[head : head + 1] = m_ref[head : head + 1] + jnp.log(total)
        h_buf[...] = ot_ref[...].T.astype(BF)
        heads_copies = []
        for d in steps:
            c = remote(
                h_buf, ho_ref.at[z, k], hs.at[d], hr.at[d], device(y, ring(z, d), k, x)
            )
            c.start()
            heads_copies.append(c)
        c = remote(h_buf, ho_ref.at[z, k], gs.at[0], gr.at[0], sib)
        c.start()
        forward = [c, row_first]
        own_h = pltpu.make_async_copy(h_buf, ho_ref.at[z, k], loc.at[2])
        own_h.start()
        for d in steps:
            row_copies[d - 1].wait_recv()
            src = ring(z, 4 - d)
            c = remote(ro_ref.at[k, src], ro_ref.at[k, src], ds.at[d], dr.at[d], sib)
            c.start()
            forward.append(c)
        for a in steps:

            @pl.when(x == a)
            def _():
                weight_own(a).wait()

            @pl.when(x != a)
            def _():
                weight_copy(a, 1).wait_recv()

        c = remote(oo_ref.at[k], oo_ref.at[k], os.at[0], orr.at[0], sib)
        c.start()
        forward.append(c)
        for d in steps:
            heads_copies[d - 1].wait_recv()
            src = ring(z, 4 - d)
            c = remote(ho_ref.at[src, k], ho_ref.at[src, k], gs.at[d], gr.at[d], sib)
            c.start()
            forward.append(c)
        for c in forward:
            c.wait()
        for c in row_copies + heads_copies + [swap]:
            c.wait_send()
        for d in steps:

            @pl.when(y + d < 4)
            def _():
                kv_copy(d).wait_send()

            @pl.when(y >= d)
            def _():
                pass_on(d).wait_send()

        for a in steps:

            @pl.when(x == a)
            def _():
                for d in steps:
                    weight_copy(a, d).wait_send()

        own_r.wait()
        own_h.wait()

    return comm(
        kernel,
        [
            jax.ShapeDtypeStruct((4, 2, 512, 192), BF),
            jax.ShapeDtypeStruct((192, 512), F32),
            jax.ShapeDtypeStruct((8, 512), F32),
            jax.ShapeDtypeStruct((4, 2, 512, 384), BF),
            jax.ShapeDtypeStruct((2, 4, 128, 768), BF),
            jax.ShapeDtypeStruct((16, 48, 384), BF),
            jax.ShapeDtypeStruct((2, 16, 48, 384), BF),
            jax.ShapeDtypeStruct((2, 192, 768), BF),
            jax.ShapeDtypeStruct((512, 192), BF),
            jax.ShapeDtypeStruct((512, 768), BF),
            jax.ShapeDtypeStruct((512, 768), BF),
        ],
        2,
        (4, 4, 4, 4, 4, 4, 4, 4, 4, 4, 1, 1, 4, 4, 4, 4, 3),
        (tokens, wq, bias, rows768, rows, fc, out, proj),
        scratch=[
            pltpu.VMEM((3, 192, 512), BF),
            pltpu.VMEM((8, 512), F32),
            pltpu.VMEM((8, 512), F32),
            pltpu.VMEM((512, 192), BF),
            pltpu.VMEM((512, 384), BF),
        ],
        spaces=(
            [VMEM, VMEM, VMEM, VMEM, ANY, ANY, ANY, ANY],
            [ANY, VMEM, VMEM, VMEM, ANY, ANY, ANY, ANY, VMEM, VMEM, VMEM],
        ),
        name="attend",
    )


def attend_back(query, branch, wo, kv_all, out_t, lse, fc, proj):
    def kernel(
        q_ref, b_ref, w_ref, kv_ref, ot_ref, lse_ref, f_ref, p_ref,
        dq_ref, dkv_ref, fo_ref, po_ref,
        qt, gt, qm, gm, delta, dqt, out_buf, keep, got, far, f_far, p_far,
        cs, cr, ys, yr, fs, fr, ps, pr,
    ):
        y, z, k, x = coords()
        sib = device(y, z, 1 - k, x)
        steps = (1, 2, 3)
        greet(
            [sib]
            + [device(ring(y, d), z, k, x) for d in steps]
            + [device(y, z, k, ring(x, d)) for d in steps]
        )
        weights = []
        for d in steps:
            b = ring(x, d)
            to = device(y, z, k, b)
            weights.append(
                remote(f_ref.at[:, b], f_far.at[d - 1], fs.at[d - 1], fr.at[d - 1], to)
            )
            weights.append(
                remote(p_ref.at[:, b], p_far.at[d - 1], ps.at[d - 1], pr.at[d - 1], to)
            )
        for c in weights:
            c.start()
        query_blk = q_ref[...]
        q_t = query_blk.T
        for head in range(3):
            qt[head] = head_rows(q_t, head)
            qm[head] = head_cols(query_blk, head)
        dqt[...] = jnp.zeros_like(dqt)
        nt = (((1,), (1,)), ((), ()))
        own_heads = pl.ds(pl.multiple_of(192 * z, 64), 192)
        grad_blk = lax.dot_general(
            b_ref[:, :384], w_ref[0, own_heads], nt, preferred_element_type=F32
        )
        grad_blk += lax.dot_general(
            b_ref[:, 384:], w_ref[1, own_heads], nt, preferred_element_type=F32
        )
        grad_blk = grad_blk.astype(BF)
        g_t = grad_blk.T
        for head in range(3):
            at = slice(64 * head, 64 * head + 64)
            gt[head] = head_rows(g_t, head)
            gm[head] = head_cols(grad_blk, head)
            delta[head : head + 1] = jnp.sum(g_t[at].astype(F32) * ot_ref[at], 0, keepdims=True)

        def block(by, bk, masked, to_ref, to):
            keys = kv_ref[by, bk, :, :192]
            values = kv_ref[by, bk, :, 192:]
            keys_t = keys.T
            if masked:
                key_at = place(lax.broadcasted_iota(jnp.int32, (512, 512), 0)) + 128 * bk
                query_at = place(lax.broadcasted_iota(jnp.int32, (512, 512), 1)) + 128 * k
                visible = query_at >= key_at
            dk = dv = None
            for head in range(3):
                s = dot(keys, qt[head])
                p = jnp.exp(s - lse_ref[head : head + 1])
                if masked:
                    p = jnp.where(visible, p, 0.0)
                dp = dot(values, gt[head])
                ds = (p * (dp - delta[head : head + 1])).astype(BF)
                pv = dot(p.astype(BF), gm[head])
                pk = dot(ds, qm[head])
                dv = pv if dv is None else dv + pv
                dk = pk if dk is None else dk + pk
                at = slice(64 * head, 64 * head + 64)
                dqt[at] += dot(keys_t[at], ds)
            to_ref[to, :, :192] = dk.astype(BF)
            to_ref[to, :, 192:] = dv.astype(BF)

        def cross(d):
            return remote(out_buf.at[d], got.at[d], cs.at[d], cr.at[d], sib)

        def up(d):
            return remote(keep.at[d], far.at[d], ys.at[d], yr.at[d], device(y - d, z, k, x))

        def earlier(i, carry):
            d = y - i
            block(y - d, 1 - k, False, out_buf, d)
            cross(d).start()
            block(y - d, k, False, keep, d)
            cross(d).wait_recv()
            keep[d] = (keep[d].astype(F32) + got[d].astype(F32)).astype(BF)
            up(d).start()
            return carry

        lax.fori_loop(0, y, earlier, 0)
        block(y, 1 - k, True, out_buf, 0)
        cross(0).start()
        block(y, k, True, keep, 0)
        dq_ref[...] = (dqt[...].T * 0.125).astype(BF)
        cross(0).wait_recv()
        for c in weights:
            c.wait()
        fo_ref[...] = (
            f_ref[:, x].astype(F32)
            + f_far[0].astype(F32)
            + f_far[1].astype(F32)
            + f_far[2].astype(F32)
        ).astype(BF)
        po_ref[...] = (
            p_ref[:, x].astype(F32)
            + p_far[0].astype(F32)
            + p_far[1].astype(F32)
            + p_far[2].astype(F32)
        ).astype(BF)
        dkv_ref[...] = keep[0].astype(F32) + got[0].astype(F32)
        for d in (1, 2, 3):

            @pl.when(y + d < 4)
            def _():
                remote(keep.at[d], far.at[d], ys.at[d], yr.at[d], sib).wait_recv()
                dkv_ref[...] += far[d].astype(F32)

        cross(0).wait_send()
        for d in (1, 2, 3):

            @pl.when(y >= d)
            def _():
                cross(d).wait_send()
                up(d).wait_send()

    return comm(
        kernel,
        [
            jax.ShapeDtypeStruct((512, 192), BF),
            jax.ShapeDtypeStruct((512, 384), F32),
            jax.ShapeDtypeStruct((4, 48, 384), BF),
            jax.ShapeDtypeStruct((2, 48, 768), BF),
        ],
        5,
        (4, 4, 4, 4, 3, 3, 3, 3),
        (query, branch, wo, kv_all, out_t, lse, fc, proj),
        scratch=[
            pltpu.VMEM((3, 192, 512), BF),
            pltpu.VMEM((3, 192, 512), BF),
            pltpu.VMEM((3, 512, 192), BF),
            pltpu.VMEM((3, 512, 192), BF),
            pltpu.VMEM((8, 512), F32),
            pltpu.VMEM((192, 512), F32),
            pltpu.VMEM((4, 512, 384), BF),
            pltpu.VMEM((4, 512, 384), BF),
            pltpu.VMEM((4, 512, 384), BF),
            pltpu.VMEM((4, 512, 384), BF),
            pltpu.VMEM((3, 4, 48, 384), BF),
            pltpu.VMEM((3, 2, 48, 768), BF),
        ],
        spaces=([VMEM] * 8, [VMEM] * 4),
        name="attend_back",
    )


def normalize(rows):
    centered = rows - jnp.mean(rows, -1, keepdims=True)
    inverse = lax.rsqrt(jnp.mean(centered * centered, -1, keepdims=True) + EPSILON)
    return centered * inverse, inverse


def normalize_back(normed, inverse, gain, grad):
    scaled = grad * gain
    return inverse * (
        scaled
        - jnp.mean(scaled, -1, keepdims=True)
        - normed * jnp.mean(scaled * normed, -1, keepdims=True)
    )


def feed_forward(heads_all, x_group, dy_group, wo, wf, wp, rows768, fc_bias):
    def kernel(
        h_ref, x_ref, dy_ref, wo_ref, wf_ref, wp_ref, v_ref, fb_ref,
        out_ref, gx_ref, bo_ref, gwf_ref, gwp_ref, gfb_ref, gv_ref,
        a2, act, df, x_two, normed, inverse, norm_other, norm_mine, res_other, res_mine,
        norm_got, res_got, norm_far, res_far, branch,
        cs, cr, es, er, zs, zr, ws, wr, bs, br,
    ):
        y, z, k, x = coords()
        sib = device(y, z, 1 - k, x)
        steps = (1, 2, 3)
        greet([sib] + [device(y, ring(z, d), k, x) for d in steps])
        out_bias, gain, shift, proj_bias = (v_ref[i : i + 1] for i in range(4))

        def half(kk, norm_ref, res_ref):
            two = x_ref[kk].reshape(512, 768).astype(F32) + out_bias
            for g in range(4):
                h = h_ref[g, kk]
                at = slice(192 * g, 192 * g + 192)
                part = jnp.concatenate([dot(h, wo_ref[0, at]), dot(h, wo_ref[1, at])], 1)
                two = two + part
            x_two[...] = two
            n, inv = normalize(two)
            normed[...] = n
            inverse[...] = jnp.broadcast_to(inv, (512, 128))
            a = (n * gain + shift).astype(BF)
            a2[kk] = a
            hidden = dot(a, wf_ref[...]) + fb_ref[...]
            square = hidden * hidden
            t = jnp.tanh(0.7978845608028654 * (hidden + 0.044715 * square * hidden))
            act_blk = (0.5 * hidden * (1.0 + t)).astype(BF)
            act[kk] = act_blk
            slope = 0.5 * (1.0 + t) + 0.5 * hidden * (1.0 - t * t) * (
                0.7978845608028654 * (1.0 + 3 * 0.044715 * square)
            )
            dy = dy_ref[kk].reshape(512, 768)
            back = lax.dot_general(
                dy, wp_ref[...], (((1,), (1,)), ((), ())), preferred_element_type=F32
            )
            df_blk = (back * slope).astype(BF)
            df[kk] = df_blk
            norm_part = lax.dot_general(
                df_blk, wf_ref[...], (((1,), (1,)), ((), ())), preferred_element_type=F32
            )
            norm_ref[...] = norm_part.astype(BF).reshape(4, 128, 768)
            res_ref[...] = dot(act_blk, wp_ref[...]).astype(BF).reshape(4, 128, 768)

        half(1 - k, norm_other, res_other)
        swaps = []
        for d in (1, 2, 3, 0):
            b = ring(z, d)
            c = remote(norm_other.at[b], norm_got.at[b], cs.at[d], cr.at[d], sib)
            c.start()
            swaps.append(c)
        for d in (1, 2, 3, 0):
            b = ring(z, d)
            c = remote(res_other.at[b], res_got.at[b], es.at[d], er.at[d], sib)
            c.start()
            swaps.append(c)
        half(k, norm_mine, res_mine)
        sends = []
        for i, (mine, got, far, s, r) in enumerate(
            ((norm_mine, norm_got, norm_far, zs, zr), (res_mine, res_got, res_far, ws, wr))
        ):
            for d in steps:
                b = ring(z, d)
                swaps[4 * i + d - 1].wait_recv()
                mine[b] = (mine[b].astype(F32) + got[b].astype(F32)).astype(BF)
                c = remote(
                    mine.at[b], far.at[d - 1], s.at[d - 1], r.at[d - 1], device(y, b, k, x)
                )
                c.start()
                sends.append(c)
        tn = (((0,), (0,)), ((), ()))
        gwf = lax.dot_general(a2[0], df[0], tn, preferred_element_type=F32)
        gwf += lax.dot_general(a2[1], df[1], tn, preferred_element_type=F32)
        gwf_ref[...] = gwf.astype(BF)
        own_rows = pl.ds(pl.multiple_of(128 * z, 128), 128)
        swaps[3].wait_recv()
        for c in sends[:3]:
            c.wait_recv()
        da = (
            norm_mine[z].astype(F32)
            + norm_got[z].astype(F32)
            + norm_far[0].astype(F32)
            + norm_far[1].astype(F32)
            + norm_far[2].astype(F32)
        )
        n = normed[own_rows]
        dy = dy_ref[k, z].astype(F32)
        gx = dy + normalize_back(n, inverse[own_rows, 0:1], gain, da)
        gx_ref[...] = gx
        low = gx.astype(BF)
        branch[...] = low
        bo_ref[z] = low
        branches = []
        for d in steps:
            c = remote(
                branch, bo_ref.at[z], bs.at[d - 1], br.at[d - 1], device(y, ring(z, d), k, x)
            )
            c.start()
            branches.append(c)
        gwp = lax.dot_general(
            act[0], dy_ref[0].reshape(512, 768), tn, preferred_element_type=F32
        )
        gwp += lax.dot_general(
            act[1], dy_ref[1].reshape(512, 768), tn, preferred_element_type=F32
        )
        gwp_ref[...] = gwp.astype(BF)
        gfb_ref[...] = jnp.sum(df[0].astype(F32), 0, keepdims=True) + jnp.sum(
            df[1].astype(F32), 0, keepdims=True
        )
        gv_ref[0:1] = jnp.sum(low.astype(F32), 0, keepdims=True)
        gv_ref[1:2] = jnp.sum(da * n, 0, keepdims=True)
        gv_ref[2:3] = jnp.sum(da, 0, keepdims=True)
        gv_ref[3:4] = jnp.sum(dy, 0, keepdims=True)
        swaps[7].wait_recv()
        for c in sends[3:]:
            c.wait_recv()
        out_ref[...] = (
            x_two[own_rows]
            + proj_bias
            + res_mine[z].astype(F32)
            + res_got[z].astype(F32)
            + res_far[0].astype(F32)
            + res_far[1].astype(F32)
            + res_far[2].astype(F32)
        )
        for c in branches:
            c.wait()
        for c in swaps + sends:
            c.wait_send()

    return comm(
        kernel,
        [
            jax.ShapeDtypeStruct((128, 768), F32),
            jax.ShapeDtypeStruct((128, 768), F32),
            jax.ShapeDtypeStruct((4, 128, 768), BF),
            jax.ShapeDtypeStruct((768, 384), BF),
            jax.ShapeDtypeStruct((384, 768), BF),
            jax.ShapeDtypeStruct((1, 384), F32),
            jax.ShapeDtypeStruct((4, 768), F32),
        ],
        3,
        (4, 4, 4, 4, 3, 3, 3, 3, 3, 3),
        (heads_all, x_group, dy_group, wo, wf, wp, rows768, fc_bias),
        scratch=[
            pltpu.VMEM((2, 512, 768), BF),
            pltpu.VMEM((2, 512, 384), BF),
            pltpu.VMEM((2, 512, 384), BF),
            pltpu.VMEM((512, 768), F32),
            pltpu.VMEM((512, 768), F32),
            pltpu.VMEM((512, 128), F32),
        ]
        + [pltpu.VMEM((4, 128, 768), BF)] * 6
        + [pltpu.VMEM((3, 128, 768), BF)] * 2
        + [pltpu.VMEM((128, 768), BF)],
        spaces=([VMEM] * 8, [VMEM] * 7),
        name="feed_forward",
    )


def adam_update(weight, moment_one, moment_two, gradient, rate, decay):
    new_one = BETA_ONE * moment_one + (1.0 - BETA_ONE) * gradient
    new_two = BETA_TWO * moment_two + (1.0 - BETA_TWO) * gradient * gradient
    fix_one = 1.0 - BETA_ONE**STEP
    fix_two = 1.0 - BETA_TWO**STEP
    direction = new_one / fix_one / (jnp.sqrt(new_two / fix_two) + ADAM_EPSILON)
    return (weight - rate * (direction + decay * weight), new_one, new_two)


def shards(
    tokens,
    cotangent,
    w_qkv,
    qkv_m,
    qkv_v,
    w_out,
    out_m,
    out_v,
    w_fc,
    fc_m,
    fc_v,
    w_proj,
    proj_m,
    proj_v,
    vectors,
    vec_m,
    vec_v,
):
    y, z, k, x = coords()
    state = (
        w_qkv, qkv_m, qkv_v, w_out, out_m, out_v, w_fc, fc_m, fc_v, w_proj, proj_m, proj_v,
        vectors, vec_m, vec_v,
    )
    wq, fc_part, out_part, proj_part, x_group = first_gather(
        w_qkv, w_fc, w_out, w_proj, vectors, tokens[0]
    )
    wq = wq.reshape(768, 640)
    vec_rows = wq[:, 576:592].astype(F32).T
    bias = jnp.concatenate(
        [
            lax.dynamic_slice(vec_rows, (2, 192 * z), (1, 192)),
            jnp.zeros((1, 192), F32),
            lax.dynamic_slice(vec_rows, (3, 192 * z), (1, 192)),
            jnp.zeros((1, 64), F32),
        ],
        1,
    )
    fc_bias = lax.dynamic_slice(vec_rows[8:12].reshape(1, 3072), (0, (2 * z + k) * 384), (1, 384))
    heads_all, out_t, lse, kv_all, dy_group, wf, wo, wp, query, act_one, normed_core = attend(
        x_group, wq, bias, vec_rows[0:2], cotangent[0], fc_part, out_part, proj_part
    )
    wo = wo.reshape(2, 768, 384)
    output, grad_x_two, branch_core, grad_w_fc, grad_w_proj, grad_fc_bias, vec_sums = feed_forward(
        heads_all,
        x_group,
        dy_group,
        wo,
        wf.reshape(768, 384),
        wp.reshape(384, 768),
        vec_rows[4:8],
        fc_bias,
    )
    branch_core = branch_core.reshape(512, 768)
    grad_query, grad_kv, fc_sum, proj_sum = attend_back(
        query,
        branch_core,
        wo,
        kv_all,
        out_t,
        lse,
        grad_w_fc.reshape(4, 4, 48, 384),
        grad_w_proj.reshape(2, 4, 48, 768),
    )
    grad_inputs, *new_state = last_sums(
        (
            act_one,
            normed_core,
            heads_all,
            grad_query,
            grad_kv,
            branch_core,
            wq,
            vec_sums,
            grad_fc_bias,
            tokens[0],
            grad_x_two,
            vec_rows[0:1],
        ),
        fc_sum,
        proj_sum,
        state,
    )
    return (output[None], grad_inputs[None], *new_state)


def solution(mesh):
    split = P("fsdp", "ctx", None)
    rows = P(("ctx", "fsdp"), None)
    return jax.shard_map(
        shards,
        mesh=mesh,
        in_specs=(split, split) + (rows,) * 15,
        out_specs=(split, split) + (rows,) * 15,
        check_vma=False,
    )
```

```python
import jax
import jax.numpy as jnp
from jax import lax
from jax.experimental import pallas as pl
from jax.experimental.pallas import tpu as pltpu
from jax.sharding import PartitionSpec as P

STEP = 10
EPSILON = 1e-05
BETA_ONE = 0.9
BETA_TWO = 0.999
ADAM_EPSILON = 1e-08
MESH = pl.DeviceIdType.MESH
BF = jnp.bfloat16
F32 = jnp.float32
ANY = pl.BlockSpec(memory_space=pl.ANY)
VMEM = pl.BlockSpec(memory_space=pltpu.VMEM)
LIMIT = 56 * 1024 * 1024


def coords():
    c = lax.axis_index("ctx")
    return c // 8, (c // 2) % 4, c % 2, lax.axis_index("fsdp")


def device(y, z, k, x):
    return ((y * 4 + z) * 2 + k, x)


def ring(v, step):
    return lax.rem(v + step, 4)


def greet(devices):
    barrier = pltpu.get_barrier_semaphore()
    for one in devices:
        pl.semaphore_signal(barrier, inc=1, device_id=one, device_id_type=MESH)
    pl.semaphore_wait(barrier, len(devices))


def remote(src, dst, send, recv, to):
    return pltpu.make_async_remote_copy(
        src, dst, send, recv, device_id=to, device_id_type=MESH
    )


def comm(kernel, outs, cid, sems, args, scratch=(), spaces=None, name=None):
    return pl.pallas_call(
        kernel,
        out_shape=outs,
        in_specs=[ANY] * len(args) if spaces is None else spaces[0],
        out_specs=[ANY] * len(outs) if spaces is None else spaces[1],
        scratch_shapes=list(scratch) + [pltpu.SemaphoreType.DMA((n,)) for n in sems],
        compiler_params=pltpu.CompilerParams(
            collective_id=cid, has_side_effects=True, vmem_limit_bytes=LIMIT
        ),
        name=name,
    )(*args)


def last_sums(pieces, fc, proj):
    wide = 3200

    def kernel(*refs):
        (
            act_ref, n_ref, h_ref, gq_ref, gkv_ref, br_ref, wq_ref, vs_ref, fb_ref,
            fc_ref, proj_ref,
        ) = refs[:11]
        one_out, rows_out, proj_out = refs[11:14]
        (
            one_far, mix_got, mix_sum, mix_far, vec_far, mix_mine, vec_mine,
            mix_all, fc_all, vec_all, proj_all, proj_sum, out_send,
            one_ref, mix_other, mix_ref, vec_ref,
            act_t, heads, heads_t, d_ref, right_one, right_two, vec_rows,
        ) = refs[14:38]
        (
        zs, zr, cs, cr, s1, r1, s2, r2, s3, r3, s4, r4, s5, r5, s6, r6, s7, r7, s8, r8, loc,
        ) = refs[38:]
        y, z, k, x = coords()
        me = y * 4 + z
        sib = device(y, z, 1 - k, x)
        steps = (1, 2, 3)
        greet(
            [sib]
            + [device(y, z, j, ring(x, d)) for d in steps for j in (k, 1 - k)]
            + [
                device(ring(y, a), ring(z, b), k, x)
                for a in range(4)
                for b in range(4)
                if (a, b) != (0, 0)
            ]
        )
        d_ref[:, 0:192] = gq_ref[...]
        d_ref[:, 192:576] = gkv_ref[...].astype(BF)
        d_ref[:, 576:640] = jnp.zeros((512, 64), BF)
        right_one[...] = jnp.zeros_like(right_one)
        right_one[:, 0:288] = d_ref[:, 0:288]
        right_one[:, 384:672] = d_ref[:, 288:576]
        right_two[...] = jnp.zeros_like(right_two)
        vec_rows[...] = jnp.zeros_like(vec_rows)
        sums = jnp.sum(d_ref[...].astype(F32), 0, keepdims=True)
        at_half = pl.ds(pl.multiple_of(384 * k, 128), 384)
        for b in range(4):
            heads[:, 192 * b : 192 * b + 192] = h_ref[b, k]

            @pl.when(z == b)
            def _():
                right_two[:, 288:384] = br_ref[:, 192 * b : 192 * b + 96]
                right_two[:, 672:768] = br_ref[:, 192 * b + 96 : 192 * b + 192]
                vec_rows[2:3, 192 * b : 192 * b + 192] = sums[:, 0:192]
                vec_rows[3:4, 192 * b : 192 * b + 192] = sums[:, 384:576]
                vec_rows[8 + b : 9 + b, at_half] = fb_ref[...]

        vec_rows[4:8] = vs_ref[...]
        act_t[...] = act_ref[...].T
        heads_t[...] = heads[...].T

        def product(h):
            at = pl.ds(pl.multiple_of(384 * h, 128), 384)
            total = dot(act_t[...], right_one[:, at]) + dot(heads_t[...], right_two[:, at])
            return total.reshape(4, 4, 48, 384)

        mix_other[...] = product(1 - k).astype(BF)
        swap = []
        for d in (1, 2, 3, 0):
            b = ring(x, d)
            c = remote(mix_other.at[:, b], mix_got.at[b], cs.at[d], cr.at[d], sib)
            c.start()
            swap.append(c)
        mix_ref[...] = product(k).astype(BF)
        one = lax.dot_general(
            d_ref[...], wq_ref[...], (((1,), (1,)), ((), ())), preferred_element_type=F32
        )
        one_ref[...] = one.astype(BF).reshape(4, 128, 768)
        vec_rows[0:1] = jnp.sum(one * n_ref[...].astype(F32), 0, keepdims=True)
        vec_rows[1:2] = jnp.sum(one, 0, keepdims=True)
        vec_ref[...] = vec_rows[...].T.astype(BF).reshape(4, 4, 48, 128)
        along = []
        for d in steps:
            b = ring(x, d)
            to = device(y, z, k, b)
            swap[d - 1].wait_recv()
            mix_sum[d] = (mix_ref[:, b].astype(F32) + mix_got[b].astype(F32)).astype(BF)
            c = remote(mix_sum.at[d], mix_far.at[d - 1], s1.at[d - 1], r1.at[d - 1], to)
            c.start()
            along.append(c)
            c = remote(vec_ref.at[:, b], vec_far.at[d - 1], s2.at[d - 1], r2.at[d - 1], to)
            c.start()
            along.append(c)
        ones = []
        for d in steps:
            c = remote(
                one_ref.at[ring(z, d)], one_far.at[d - 1], zs.at[d - 1], zr.at[d - 1],
                device(y, ring(z, d), k, x),
            )
            c.start()
            ones.append(c)

        def plane(src, dst, send, recv, a):
            return remote(src.at[a], dst.at[me], send.at[a], recv.at[me], device(a, x, k, x))

        def all_start(src, dst, send, recv):
            for a in range(4):
                here = (a == y) & (z == x)

                @pl.when(jnp.logical_not(here))
                def _():
                    plane(src, dst, send, recv, a).start()

                @pl.when(here)
                def _():
                    c = pltpu.make_async_copy(src.at[a], dst.at[me], loc.at[0])
                    c.start()
                    c.wait()

        def all_finish(src, dst, send, recv):
            for a in range(4):

                @pl.when(jnp.logical_not((a == y) & (z == x)))
                def _():
                    plane(src, dst, send, recv, a).wait_send()

        def all_receive(src, dst, send, recv):
            def step(i, carry):
                @pl.when(i != me)
                def _():
                    remote(src.at[0], dst.at[i], send.at[0], recv.at[i], sib).wait_recv()

                return carry

            lax.fori_loop(0, 16, step, 0)

        all_start(fc_ref, fc_all, s4, r4)

        def proj_copy(j):
            return remote(
                proj_ref.at[j], proj_all.at[y], s6.at[j], r6.at[y], device(z, 2 * k + j, k, x)
            )

        for j in range(2):
            here = (y == z) & (z == 2 * k + j)

            @pl.when(jnp.logical_not(here))
            def _():
                proj_copy(j).start()

            @pl.when(here)
            def _():
                c = pltpu.make_async_copy(proj_ref.at[j], proj_all.at[y], loc.at[1])
                c.start()
                c.wait()

        swap[3].wait_recv()
        for c in along:
            c.wait_recv()
        mix_mine[...] = (
            mix_ref[:, x].astype(F32)
            + mix_got[x].astype(F32)
            + mix_far[0].astype(F32)
            + mix_far[1].astype(F32)
            + mix_far[2].astype(F32)
        ).astype(BF)
        vec_mine[...] = (
            vec_ref[:, x].astype(F32)
            + vec_far[0].astype(F32)
            + vec_far[1].astype(F32)
            + vec_far[2].astype(F32)
        ).astype(BF)
        all_start(mix_mine, mix_all, s3, r3)
        all_start(vec_mine, vec_all, s5, r5)
        for c in ones:
            c.wait_recv()
        one_out[...] = (
            one_ref[z].astype(F32)
            + one_far[0].astype(F32)
            + one_far[1].astype(F32)
            + one_far[2].astype(F32)
        )

        def proj_last(i):
            return remote(
                proj_sum.at[i], proj_out, s8.at[i], r8.at[0],
                device(y, z, x // 2, lax.rem(2 * x + i, 4)),
            )

        def proj_here(i):
            return (k == x // 2) & (x == lax.rem(2 * x + i, 4))

        holder = k == z // 2
        for a in range(4):

            @pl.when(holder & jnp.logical_not((a == y) & (z == y)))
            def _():
                remote(proj_ref.at[0], proj_all.at[a], s6.at[0], r6.at[a], sib).wait_recv()

        @pl.when(holder)
        def _():
            total = (
                proj_all[0].astype(F32)
                + proj_all[1].astype(F32)
                + proj_all[2].astype(F32)
                + proj_all[3].astype(F32)
            )
            for i in range(2):
                proj_sum[i] = total[24 * i : 24 * i + 24]

                @pl.when(jnp.logical_not(proj_here(i)))
                def _():
                    proj_last(i).start()

                @pl.when(proj_here(i))
                def _():
                    c = pltpu.make_async_copy(proj_sum.at[i], proj_out, loc.at[2])
                    c.start()
                    c.wait()

        def last_copy(i):
            return remote(
                out_send.at[i], rows_out.at[k], s7.at[i], r7.at[k], device(y, z, i // 4, i % 4)
            )

        def last_here(i):
            return k * 4 + x == i

        @pl.when(z == x)
        def _():
            all_receive(fc_ref, fc_all, s4, r4)
            all_receive(mix_mine, mix_all, s3, r3)
            all_receive(vec_mine, vec_all, s5, r5)

            def four(ref, b):
                return (
                    ref[b].astype(F32)
                    + ref[4 + b].astype(F32)
                    + ref[8 + b].astype(F32)
                    + ref[12 + b].astype(F32)
                )

            for b in range(4):
                m, f = four(mix_all, b), four(fc_all, b)
                for i in range(8):
                    rows = slice(6 * i, 6 * i + 6)
                    out_send[i, 0:6, 384 * b : 384 * b + 384] = m[rows]
                    out_send[i, 0:6, 1536 + 384 * b : 1920 + 384 * b] = f[rows]
            v = four(vec_all, 0) + four(vec_all, 1) + four(vec_all, 2) + four(vec_all, 3)
            for i in range(8):
                out_send[i, 0:6, 3072:3200] = v[6 * i : 6 * i + 6]
                out_send[i, 6:8, :] = jnp.zeros((2, wide), F32)
            for i in range(8):

                @pl.when(jnp.logical_not(last_here(i)))
                def _():
                    last_copy(i).start()

                @pl.when(last_here(i))
                def _():
                    c = pltpu.make_async_copy(out_send.at[i], rows_out.at[k], loc.at[3])
                    c.start()
                    c.wait()

        for j in range(2):

            @pl.when(jnp.logical_not((z == x) & (k == j)))
            def _():
                remote(out_send.at[0], rows_out.at[j], s7.at[0], r7.at[j], sib).wait_recv()

        @pl.when(jnp.logical_not((k == z // 2) & (x == (4 * k + x) // 2)))
        def _():
            remote(proj_sum.at[0], proj_out, s8.at[0], r8.at[0], sib).wait_recv()

        @pl.when(z == x)
        def _():
            for i in range(8):

                @pl.when(jnp.logical_not(last_here(i)))
                def _():
                    last_copy(i).wait_send()

        for i in range(2):

            @pl.when(holder & jnp.logical_not(proj_here(i)))
            def _():
                proj_last(i).wait_send()

        for j in range(2):

            @pl.when(jnp.logical_not((y == z) & (z == 2 * k + j)))
            def _():
                proj_copy(j).wait_send()

        all_finish(fc_ref, fc_all, s4, r4)
        all_finish(mix_mine, mix_all, s3, r3)
        all_finish(vec_mine, vec_all, s5, r5)
        for c in swap + along + ones:
            c.wait_send()

    return comm(
        kernel,
        [
            jax.ShapeDtypeStruct((128, 768), F32),
            jax.ShapeDtypeStruct((2, 8, wide), F32),
            jax.ShapeDtypeStruct((24, 768), F32),
        ],
        6,
        (3, 3, 4, 4, 3, 3, 3, 3, 4, 16, 4, 16, 4, 16, 2, 4, 8, 2, 2, 1, 4),
        (*pieces, fc, proj),
        scratch=[
            pltpu.VMEM((3, 128, 768), BF),
            pltpu.VMEM((4, 4, 48, 384), BF),
            pltpu.VMEM((4, 4, 48, 384), BF),
            pltpu.VMEM((3, 4, 48, 384), BF),
            pltpu.VMEM((3, 4, 48, 128), BF),
            pltpu.VMEM((4, 48, 384), BF),
            pltpu.VMEM((4, 48, 128), BF),
            pltpu.VMEM((16, 48, 384), BF),
            pltpu.VMEM((16, 48, 384), BF),
            pltpu.VMEM((16, 48, 128), BF),
            pltpu.VMEM((4, 48, 768), BF),
            pltpu.VMEM((2, 24, 768), F32),
            pltpu.VMEM((8, 8, wide), F32),
            pltpu.VMEM((4, 128, 768), BF),
            pltpu.VMEM((4, 4, 48, 384), BF),
            pltpu.VMEM((4, 4, 48, 384), BF),
            pltpu.VMEM((4, 4, 48, 128), BF),
            pltpu.VMEM((768, 512), BF),
            pltpu.VMEM((512, 768), BF),
            pltpu.VMEM((768, 512), BF),
            pltpu.VMEM((512, 640), BF),
            pltpu.VMEM((512, 768), BF),
            pltpu.VMEM((512, 768), BF),
            pltpu.VMEM((128, 768), F32),
        ],
        spaces=([VMEM] * 11, [VMEM] * 3),
        name="last_sums",
    )


def finish(grad_one, grad_x_two, tokens, vec_rows, rows, proj_rows, result, state):
    def kernel(*refs):
        one_ref, gx_ref, t_ref, v_ref, rows_ref, p_ref, res_ref = refs[:7]
        state_ref = refs[7:22]
        out_ref, gin_ref = refs[22:24]
        new_ref = refs[24:39]
        g_qkv, g_out, g_fc = refs[39:]
        out_ref[...] = res_ref[...]
        normed, inverse = normalize(t_ref[...].astype(F32))
        gin_ref[...] = gx_ref[...] + normalize_back(normed, inverse, v_ref[0:1], one_ref[...])
        for b in range(4):
            one_half = rows_ref[0, 0:6, 384 * b : 384 * b + 384]
            two_half = rows_ref[1, 0:6, 384 * b : 384 * b + 384]
            q = 192 * b
            g_qkv[:, q : q + 192] = one_half[:, 0:192]
            g_qkv[:, 768 + q : 864 + q] = one_half[:, 192:288]
            g_qkv[:, 864 + q : 960 + q] = two_half[:, 0:96]
            g_qkv[:, 1536 + q : 1728 + q] = two_half[:, 96:288]
            g_out[:, q : q + 96] = one_half[:, 288:384]
            g_out[:, q + 96 : q + 192] = two_half[:, 288:384]
            for j in range(2):
                at = 384 * (2 * b + j)
                g_fc[:, at : at + 384] = rows_ref[j, 0:6, 1536 + 384 * b : 1920 + 384 * b]
        g_vec = rows_ref[0, 0:6, 3072:3084] + rows_ref[1, 0:6, 3072:3084]
        for i, (gradient, rate, decay) in enumerate(
            (
                (g_qkv[...], 0.1, 0.1),
                (g_out[...], 0.3, 0.1),
                (g_fc[...], 0.05, 0.1),
                (p_ref[...], 0.03, 0.1),
                (g_vec, 0.5, 0.0),
            )
        ):
            w, m, v = state_ref[3 * i : 3 * i + 3]
            results = adam_update(w[...], m[...], v[...], gradient, rate, decay)
            for j in range(3):
                new_ref[3 * i + j][...] = results[j]

    return pl.pallas_call(
        kernel,
        out_shape=[jax.ShapeDtypeStruct((128, 768), F32)] * 2
        + [jax.ShapeDtypeStruct(one.shape, F32) for one in state],
        in_specs=[VMEM] * 22,
        out_specs=[VMEM] * 17,
        scratch_shapes=[
            pltpu.VMEM((6, 2304), F32),
            pltpu.VMEM((6, 768), F32),
            pltpu.VMEM((6, 3072), F32),
        ],
        compiler_params=pltpu.CompilerParams(vmem_limit_bytes=LIMIT),
        name="finish",
    )(grad_one, grad_x_two, tokens, vec_rows, rows, proj_rows, result, *state)


def head_rows(matrix, head):
    row = lax.broadcasted_iota(jnp.int32, matrix.shape, 0)
    keep = (row >= 64 * head) & (row < 64 * head + 64)
    return jnp.where(keep, matrix, jnp.zeros_like(matrix))


def head_cols(matrix, head):
    col = lax.broadcasted_iota(jnp.int32, matrix.shape, 1)
    keep = (col >= 64 * head) & (col < 64 * head + 64)
    return jnp.where(keep, matrix, jnp.zeros_like(matrix))


def place(index):
    return (index // 128) * 256 + index % 128


def dot(a, b):
    return jnp.dot(a, b, preferred_element_type=F32)


def forward(w_qkv, w_fc, w_out, w_proj, vectors, tokens, cotangent):
    wide_q, wide_r = 1280, 3456

    def kernel(
        wq_ref, wf_ref, wo_ref, wp_ref, wv_ref, t_ref, r_ref,
        ho_ref, ot_ref, lse_ref, vo_ref, ro_ref, fo_ref, oo_ref, po_ref, q_ref, a_ref, n_ref,
        q_out, x_ref, vec_ref,
        wide_one, wide_two, packed_q, packed_r, got_q, got_r,
        fc48, qkv48, out48, proj_wide, q_send, f_send, o_send, p_send, f_mid, o_mid, p_mid,
        bias, qt, m_ref, l_ref, h_buf, v_ref,
        mq_s, mq_r, fq_s, fq_r, mr_s, mr_r, fr_s, fr_r, s1, r1, s2, r2, ps, pr,
        xs_s, xs_r, xf_s, xf_r, ts, tr, us, ur,
        vs, vr, rs, rr, cs, cr, ds, dr, ws, wr, os, orr, hs, hr, gs, gr, loc,
    ):
        y, z, k, x = coords()
        me = y * 4 + z
        t = k * 4 + x
        sib = device(y, z, 1 - k, x)
        steps = (1, 2, 3)
        greet(
            [sib]
            + [device(y, z, k, ring(x, d)) for d in steps]
            + [
                device(ring(y, a), ring(z, b), k, x)
                for a in range(4)
                for b in range(4)
                if (a, b) != (0, 0)
            ]
        )

        def first(packed, got, send, recv):
            copies = [
                remote(packed, got.at[t], send.at[d], recv.at[d], device(y, z, k, ring(x, d)))
                for d in steps
            ]
            for c in copies:
                c.start()
            return copies

        def crossing(packed, got, copies, send, recv):
            out = [remote(packed, got.at[t], send.at[0], recv.at[0], sib)]
            out[0].start()
            for d in steps:
                copies[d - 1].wait_recv()
                src = k * 4 + ring(x, 4 - d)
                c = remote(got.at[src], got.at[src], send.at[d], recv.at[d], sib)
                c.start()
                out.append(c)
            return out

        wide_one[...] = jnp.zeros_like(wide_one)
        wide_one[0:6, 0:1152] = wq_ref[:, 0:1152]
        wide_one[6:12, 0:1152] = wq_ref[:, 1152:2304]
        wide_one[0:6, 1152:1164] = wv_ref[...]
        packed_q[...] = wide_one[...].astype(BF)
        got_q[t] = packed_q[...]
        message_q = first(packed_q, got_q, mq_s, mq_r)
        token_copies = []
        for d in steps:
            c = remote(
                t_ref, x_ref.at[k, z], ts.at[d], tr.at[d], device(y, ring(z, d), k, x)
            )
            c.start()
            token_copies.append(c)
        token_cross = [remote(t_ref, x_ref.at[k, z], us.at[0], ur.at[0], sib)]
        token_cross[0].start()
        x_ref[k, z] = t_ref[...]
        wide_two[...] = jnp.zeros_like(wide_two)
        wide_two[0:6, 0:1920] = wf_ref[:, 0:1920]
        wide_two[6:12, 0:1152] = wf_ref[:, 1920:3072]
        wide_two[6:12, 1152:1920] = wo_ref[...]
        wide_two[0:12, 1920:2688] = wp_ref[0:12]
        wide_two[0:12, 2688:3456] = wp_ref[12:24]
        packed_r[...] = wide_two[...].astype(BF)
        got_r[t] = packed_r[...]
        cross_q = crossing(packed_q, got_q, message_q, fq_s, fq_r)
        message_r = first(packed_r, got_r, mr_s, mr_r)
        for c in cross_q:
            c.wait_recv()
        for i in range(8):
            piece = got_q[i].astype(F32)
            at = slice(6 * i, 6 * i + 6)
            qkv48[at, 0:1152] = piece[0:6, 0:1152]
            qkv48[at, 1152:2304] = piece[6:12, 0:1152]
            qkv48[at, 2304:2432] = piece[0:6, 1152:1280]
        for j in range(4):
            q_send[j, :, 0:192] = qkv48[:, 192 * j : 192 * j + 192].astype(BF)
            q_send[j, :, 192:384] = qkv48[:, 768 + 192 * j : 960 + 192 * j].astype(BF)
            q_send[j, :, 384:576] = qkv48[:, 1536 + 192 * j : 1728 + 192 * j].astype(BF)
            q_send[j, :, 576:640] = qkv48[:, 2304:2368].astype(BF)

        group = pl.ds(pl.multiple_of(16 * jnp.minimum(x, 2), 16), 16)

        def to_of(m):
            return ring(y, m // 4), ring(z, m % 4)

        def q_copy(m):
            ty, tz = to_of(m)
            return remote(
                q_send.at[tz, group], q_out.at[me, group], s1.at[m], r1.at[m],
                device(ty, tz, k, x),
            )

        def f_copy(m):
            ty, tz = to_of(m)
            return remote(
                f_send.at[tz * 2 + k], f_mid.at[me], s2.at[m], r2.at[m], device(ty, tz, k, x)
            )

        def o_copy(m):
            ty, tz = to_of(m)
            return remote(o_send.at[k], o_mid.at[me], s2.at[m], r2.at[m], device(ty, tz, k, x))

        def p_copy(a):
            return remote(
                p_send, p_mid.at[z % 2], ps.at[a], pr.at[z % 2], device(ring(y, a), y, k, x)
            )

        def each(copy, what):
            def step(m, carry):
                what(copy(m))
                return carry

            lax.fori_loop(1, 16, step, 0)

        start = lambda c: c.start()
        finish = lambda c: c.wait()

        @pl.when(x < 3)
        def _():
            each(q_copy, start)
            q_out[me, group] = q_send[z, group]

        cross_r = crossing(packed_r, got_r, message_r, fr_s, fr_r)
        for c in cross_r:
            c.wait_recv()
        for i in range(8):
            piece = got_r[i].astype(F32)
            at = slice(6 * i, 6 * i + 6)
            fc48[at, 0:1920] = piece[0:6, 0:1920]
            fc48[at, 1920:3072] = piece[6:12, 0:1152]
            out48[at] = piece[6:12, 1152:1920]
            proj_wide[24 * i : 24 * i + 12] = piece[0:12, 1920:2688]
            proj_wide[24 * i + 12 : 24 * i + 24] = piece[0:12, 2688:3456]
        for j in range(8):
            f_send[j] = fc48[:, 384 * j : 384 * j + 384].astype(BF)
        o_send[0] = out48[:, 0:384].astype(BF)
        o_send[1] = out48[:, 384:768].astype(BF)
        p_send[...] = proj_wide[...].astype(BF)

        half = pl.ds(8 * k, 8)
        other_half = pl.ds(8 * (1 - k), 8)

        def rows_of(plane):
            return pl.ds(pl.multiple_of(16 * plane, 16), 16)

        def x_copy(d):
            return remote(
                q_out.at[half, group], q_out.at[half, group], xs_s.at[d], xs_r.at[x],
                device(y, z, k, ring(x, d)),
            )

        @pl.when(x < 3)
        def _():
            each(q_copy, finish)
            for d in steps:
                x_copy(d).start()

        @pl.when(x == 1)
        def _():
            each(f_copy, start)
            f_mid[me] = f_send[z * 2 + k]

        @pl.when(x == 2)
        def _():
            each(o_copy, start)
            o_mid[me] = o_send[k]

        @pl.when((x == 3) & (k == z // 2))
        def _():
            for a in range(1, 4):
                p_copy(a).start()

            @pl.when(z != y)
            def _():
                p_copy(0).start()

            @pl.when(z == y)
            def _():
                p_mid[z % 2] = p_send[...]

        def pass_q(a):
            return remote(
                q_out.at[half, rows_of(a)], q_out.at[half, rows_of(a)], xf_s.at[a], xf_r.at[a], sib
            )

        for a in range(3):

            @pl.when(x != a)
            def _():
                remote(
                    q_out.at[half, rows_of(a)], q_out.at[half, rows_of(a)], xs_s.at[0],
                    xs_r.at[a], sib,
                ).wait_recv()
                pass_q(a).start()

        for d in steps:
            token_copies[d - 1].wait_recv()
            src = ring(z, 4 - d)
            c = remote(x_ref.at[k, src], x_ref.at[k, src], us.at[d], ur.at[d], sib)
            c.start()
            token_cross.append(c)
        normed, _ = normalize(x_ref[k].reshape(512, 768).astype(F32))
        n_ref[...] = normed.astype(BF)

        for a in range(3):

            @pl.when(x != a)
            def _():
                remote(
                    q_out.at[other_half, rows_of(a)], q_out.at[other_half, rows_of(a)],
                    xf_s.at[a], xf_r.at[a], sib,
                ).wait_recv()

        vec_ref[...] = q_out[:, :, 512:640].reshape(768, 128).astype(F32).T[64:80]
        bias[...] = jnp.zeros_like(bias)
        for b in range(4):

            @pl.when(z == b)
            def _():
                bias[:, 0:192] = vec_ref[2:3, 192 * b : 192 * b + 192]
                bias[:, 384:576] = vec_ref[3:4, 192 * b : 192 * b + 192]

        act = (normed * vec_ref[0:1] + vec_ref[1:2]).astype(BF)
        a_ref[...] = act
        mixed = dot(act, q_out[...].reshape(768, 640)) + bias[...]
        v_ref[...] = mixed[:, 192:576].astype(BF)

        def kv_copy(d):
            return remote(
                v_ref, vo_ref.at[y, k], vs.at[d], vr.at[d], device(ring(y, d), z, k, x)
            )

        for d in steps:

            @pl.when(y + d < 4)
            def _():
                kv_copy(d).start()

        swap = remote(v_ref, vo_ref.at[y, k], cs.at[0], cr.at[0], sib)
        swap.start()
        vo_ref[y, k] = v_ref[...]
        own_r = pltpu.make_async_copy(r_ref, ro_ref.at[k, z], loc.at[0])
        own_r.start()
        row_copies = []
        for d in steps:
            c = remote(
                r_ref, ro_ref.at[k, z], rs.at[d], rr.at[d], device(y, ring(z, d), k, x)
            )
            c.start()
            row_copies.append(c)
        row_first = remote(r_ref, ro_ref.at[k, z], ds.at[0], dr.at[0], sib)
        row_first.start()
        query = mixed[:, :192].astype(BF) * jnp.asarray(0.125, BF)
        q_ref[...] = query
        q_t = query.T
        for head in range(3):
            qt[head] = head_rows(q_t, head)
        m_ref[...] = jnp.full_like(m_ref, -1e30)
        l_ref[...] = jnp.zeros_like(l_ref)
        ot_ref[...] = jnp.zeros_like(ot_ref)

        def block(by, bk, masked):
            keys = vo_ref[by, bk, :, :192]
            values_t = vo_ref[by, bk, :, 192:].T
            if masked:
                key_at = place(lax.broadcasted_iota(jnp.int32, (512, 512), 0)) + 128 * bk
                query_at = place(lax.broadcasted_iota(jnp.int32, (512, 512), 1)) + 128 * k
                visible = query_at >= key_at
            for head in range(3):
                s = dot(keys, qt[head])
                if masked:
                    s = jnp.where(visible, s, -1e9)
                old = m_ref[head : head + 1]
                new = jnp.maximum(old, jnp.max(s, 0, keepdims=True))
                e = jnp.exp(s - new)
                scale = jnp.exp(old - new)
                m_ref[head : head + 1] = new
                l_ref[head : head + 1] = l_ref[head : head + 1] * scale + jnp.sum(
                    e, 0, keepdims=True
                )
                at = slice(64 * head, 64 * head + 64)
                ot_ref[at] = ot_ref[at] * scale + dot(values_t[at], e.astype(BF))

        weights = ((1, f_mid, fo_ref), (2, o_mid, oo_ref.at[k]), (3, p_mid, po_ref))

        def weight_copy(a, d):
            _, src, dst = weights[a - 1]
            return remote(src, dst, ws.at[d], wr.at[a], device(y, z, k, ring(x, d)))

        def weight_own(a):
            _, src, dst = weights[a - 1]
            return pltpu.make_async_copy(src, dst, loc.at[1])

        def diagonal(j, carry):
            @pl.when(j == 1)
            def _():
                remote(v_ref, vo_ref.at[y, 1 - k], cs.at[0], cr.at[0], sib).wait_recv()

            block(y, lax.rem(k + j, 2), True)

            @pl.when((j == 0) & (x == 1))
            def _():
                each(f_copy, finish)

            @pl.when((j == 0) & (x == 2))
            def _():
                each(o_copy, finish)

            for i in range(2):
                @pl.when((j == 0) & (x == 3) & jnp.logical_not((y == z) & (z == 2 * k + i)))
                def _():
                    remote(p_send, p_mid.at[i], ps.at[0], pr.at[i], sib).wait_recv()

            for a in steps:

                @pl.when((j == 0) & (x == a))
                def _():
                    for d in steps:
                        weight_copy(a, d).start()
                    weight_own(a).start()

            return carry

        lax.fori_loop(0, 2, diagonal, 0)

        def pass_on(d):
            return remote(
                vo_ref.at[y - d, k], vo_ref.at[y - d, k], cs.at[d], cr.at[d], sib
            )

        def earlier(i, carry):
            d, j = i // 2 + 1, i % 2

            @pl.when(j == 0)
            def _():
                remote(v_ref, vo_ref.at[y - d, k], vs.at[d], vr.at[d], sib).wait_recv()
                pass_on(d).start()

            @pl.when(j == 1)
            def _():
                remote(v_ref, vo_ref.at[y - d, 1 - k], cs.at[d], cr.at[d], sib).wait_recv()

            block(y - d, lax.rem(k + j, 2), False)
            return carry

        lax.fori_loop(0, 2 * y, earlier, 0)
        for head in range(3):
            at = slice(64 * head, 64 * head + 64)
            total = l_ref[head : head + 1]
            ot_ref[at] = ot_ref[at] / total
            lse_ref[head : head + 1] = m_ref[head : head + 1] + jnp.log(total)
        h_buf[...] = ot_ref[...].T.astype(BF)
        heads_copies = []
        for d in steps:
            c = remote(
                h_buf, ho_ref.at[z, k], hs.at[d], hr.at[d], device(y, ring(z, d), k, x)
            )
            c.start()
            heads_copies.append(c)
        c = remote(h_buf, ho_ref.at[z, k], gs.at[0], gr.at[0], sib)
        c.start()
        forward_copies = [c, row_first]
        own_h = pltpu.make_async_copy(h_buf, ho_ref.at[z, k], loc.at[2])
        own_h.start()
        for d in steps:
            row_copies[d - 1].wait_recv()
            src = ring(z, 4 - d)
            c = remote(ro_ref.at[k, src], ro_ref.at[k, src], ds.at[d], dr.at[d], sib)
            c.start()
            forward_copies.append(c)
        for a in steps:

            @pl.when(x == a)
            def _():
                weight_own(a).wait()

            @pl.when(x != a)
            def _():
                weight_copy(a, 1).wait_recv()

        c = remote(oo_ref.at[k], oo_ref.at[k], os.at[0], orr.at[0], sib)
        c.start()
        forward_copies.append(c)
        for d in steps:
            heads_copies[d - 1].wait_recv()
            src = ring(z, 4 - d)
            c = remote(ho_ref.at[src, k], ho_ref.at[src, k], gs.at[d], gr.at[d], sib)
            c.start()
            forward_copies.append(c)
        for c in forward_copies + token_cross:
            c.wait()
        for c in row_copies + heads_copies + token_copies + [swap]:
            c.wait_send()
        for c in message_q + cross_q + message_r + cross_r:
            c.wait_send()
        for d in steps:

            @pl.when(y + d < 4)
            def _():
                kv_copy(d).wait_send()

            @pl.when(y >= d)
            def _():
                pass_on(d).wait_send()

        for a in steps:

            @pl.when(x == a)
            def _():
                for d in steps:
                    weight_copy(a, d).wait_send()

        @pl.when((x == 3) & (k == z // 2))
        def _():
            for a in range(1, 4):
                p_copy(a).wait_send()

            @pl.when(z != y)
            def _():
                p_copy(0).wait_send()

        @pl.when(x < 3)
        def _():
            for d in steps:
                x_copy(d).wait_send()

        for a in range(3):

            @pl.when(x != a)
            def _():
                pass_q(a).wait_send()

        own_r.wait()
        own_h.wait()

    return comm(
        kernel,
        [
            jax.ShapeDtypeStruct((4, 2, 512, 192), BF),
            jax.ShapeDtypeStruct((192, 512), F32),
            jax.ShapeDtypeStruct((8, 512), F32),
            jax.ShapeDtypeStruct((4, 2, 512, 384), BF),
            jax.ShapeDtypeStruct((2, 4, 128, 768), BF),
            jax.ShapeDtypeStruct((16, 48, 384), BF),
            jax.ShapeDtypeStruct((2, 16, 48, 384), BF),
            jax.ShapeDtypeStruct((2, 192, 768), BF),
            jax.ShapeDtypeStruct((512, 192), BF),
            jax.ShapeDtypeStruct((512, 768), BF),
            jax.ShapeDtypeStruct((512, 768), BF),
            jax.ShapeDtypeStruct((16, 48, 640), BF),
            jax.ShapeDtypeStruct((2, 4, 128, 768), BF),
            jax.ShapeDtypeStruct((16, 768), F32),
        ],
        0,
        (4,) * 8 + (16,) * 4 + (4, 2) + (4,) * 8
        + (4, 4, 4, 4, 4, 4, 4, 4, 4, 4, 1, 1, 4, 4, 4, 4, 3),
        (w_qkv, w_fc, w_out, w_proj, vectors, tokens, cotangent),
        scratch=[
            pltpu.VMEM((16, wide_q), F32),
            pltpu.VMEM((16, wide_r), F32),
            pltpu.VMEM((16, wide_q), BF),
            pltpu.VMEM((16, wide_r), BF),
            pltpu.VMEM((8, 16, wide_q), BF),
            pltpu.VMEM((8, 16, wide_r), BF),
            pltpu.VMEM((48, 3072), F32),
            pltpu.VMEM((48, 2432), F32),
            pltpu.VMEM((48, 768), F32),
            pltpu.VMEM((192, 768), F32),
            pltpu.VMEM((4, 48, 640), BF),
            pltpu.VMEM((8, 48, 384), BF),
            pltpu.VMEM((2, 48, 384), BF),
            pltpu.VMEM((192, 768), BF),
            pltpu.VMEM((16, 48, 384), BF),
            pltpu.VMEM((16, 48, 384), BF),
            pltpu.VMEM((2, 192, 768), BF),
            pltpu.VMEM((1, 640), F32),
            pltpu.VMEM((3, 192, 512), BF),
            pltpu.VMEM((8, 512), F32),
            pltpu.VMEM((8, 512), F32),
            pltpu.VMEM((512, 192), BF),
            pltpu.VMEM((512, 384), BF),
        ],
        spaces=(
            [VMEM] * 6 + [ANY],
            [ANY, VMEM, VMEM, VMEM, ANY, ANY, ANY, ANY] + [VMEM] * 6,
        ),
        name="forward",
    )


def attend_back(query, branch, wo, kv_all, out_t, lse, fc, proj, base, result):
    def kernel(
        q_ref, b_ref, w_ref, kv_ref, ot_ref, lse_ref, f_ref, p_ref, base_ref, res_ref,
        dq_ref, dkv_ref, fo_ref, po_ref, out_ref,
        qt, gt, qm, gm, delta, dqt, out_buf, keep, got, far, f_far, p_far, r_far,
        cs, cr, ys, yr, fs, fr, ps, pr, rs, rr,
    ):
        y, z, k, x = coords()
        sib = device(y, z, 1 - k, x)
        steps = (1, 2, 3)
        greet(
            [sib]
            + [device(ring(y, d), z, k, x) for d in steps]
            + [device(y, ring(z, d), k, x) for d in steps]
            + [device(y, z, k, ring(x, d)) for d in steps]
        )
        results = []
        for d in steps:
            b = ring(z, d)
            c = remote(
                res_ref.at[b], r_far.at[d - 1], rs.at[d - 1], rr.at[d - 1], device(y, b, k, x)
            )
            c.start()
            results.append(c)
        weights = []
        for d in steps:
            b = ring(x, d)
            to = device(y, z, k, b)
            weights.append(
                remote(f_ref.at[:, b], f_far.at[d - 1], fs.at[d - 1], fr.at[d - 1], to)
            )
            weights.append(
                remote(p_ref.at[:, b], p_far.at[d - 1], ps.at[d - 1], pr.at[d - 1], to)
            )
        for c in weights:
            c.start()
        query_blk = q_ref[...]
        q_t = query_blk.T
        for head in range(3):
            qt[head] = head_rows(q_t, head)
            qm[head] = head_cols(query_blk, head)
        dqt[...] = jnp.zeros_like(dqt)
        nt = (((1,), (1,)), ((), ()))
        own_heads = pl.ds(pl.multiple_of(192 * z, 64), 192)
        grad_blk = lax.dot_general(
            b_ref[:, :384], w_ref[0, own_heads], nt, preferred_element_type=F32
        )
        grad_blk += lax.dot_general(
            b_ref[:, 384:], w_ref[1, own_heads], nt, preferred_element_type=F32
        )
        grad_blk = grad_blk.astype(BF)
        g_t = grad_blk.T
        for head in range(3):
            at = slice(64 * head, 64 * head + 64)
            gt[head] = head_rows(g_t, head)
            gm[head] = head_cols(grad_blk, head)
            delta[head : head + 1] = jnp.sum(g_t[at].astype(F32) * ot_ref[at], 0, keepdims=True)

        def block(by, bk, masked, to_ref, to):
            keys = kv_ref[by, bk, :, :192]
            values = kv_ref[by, bk, :, 192:]
            keys_t = keys.T
            if masked:
                key_at = place(lax.broadcasted_iota(jnp.int32, (512, 512), 0)) + 128 * bk
                query_at = place(lax.broadcasted_iota(jnp.int32, (512, 512), 1)) + 128 * k
                visible = query_at >= key_at
            dk = dv = None
            for head in range(3):
                s = dot(keys, qt[head])
                p = jnp.exp(s - lse_ref[head : head + 1])
                if masked:
                    p = jnp.where(visible, p, 0.0)
                dp = dot(values, gt[head])
                ds = (p * (dp - delta[head : head + 1])).astype(BF)
                pv = dot(p.astype(BF), gm[head])
                pk = dot(ds, qm[head])
                dv = pv if dv is None else dv + pv
                dk = pk if dk is None else dk + pk
                at = slice(64 * head, 64 * head + 64)
                dqt[at] += dot(keys_t[at], ds)
            to_ref[to, :, :192] = dk.astype(BF)
            to_ref[to, :, 192:] = dv.astype(BF)

        def cross(d):
            return remote(out_buf.at[d], got.at[d], cs.at[d], cr.at[d], sib)

        def up(d):
            return remote(keep.at[d], far.at[d], ys.at[d], yr.at[d], device(y - d, z, k, x))

        def earlier(i, carry):
            d = y - i
            block(y - d, 1 - k, False, out_buf, d)
            cross(d).start()
            block(y - d, k, False, keep, d)
            cross(d).wait_recv()
            keep[d] = (keep[d].astype(F32) + got[d].astype(F32)).astype(BF)
            up(d).start()
            return carry

        lax.fori_loop(0, y, earlier, 0)
        block(y, 1 - k, True, out_buf, 0)
        cross(0).start()
        block(y, k, True, keep, 0)
        dq_ref[...] = (dqt[...].T * 0.125).astype(BF)
        cross(0).wait_recv()
        for c in weights:
            c.wait()
        fo_ref[...] = (
            f_ref[:, x].astype(F32)
            + f_far[0].astype(F32)
            + f_far[1].astype(F32)
            + f_far[2].astype(F32)
        ).astype(BF)
        po_ref[...] = (
            p_ref[:, x].astype(F32)
            + p_far[0].astype(F32)
            + p_far[1].astype(F32)
            + p_far[2].astype(F32)
        ).astype(BF)
        for c in results:
            c.wait()
        out_ref[...] = (
            base_ref[...]
            + res_ref[z].astype(F32)
            + r_far[0].astype(F32)
            + r_far[1].astype(F32)
            + r_far[2].astype(F32)
        )
        dkv_ref[...] = keep[0].astype(F32) + got[0].astype(F32)
        for d in (1, 2, 3):

            @pl.when(y + d < 4)
            def _():
                remote(keep.at[d], far.at[d], ys.at[d], yr.at[d], sib).wait_recv()
                dkv_ref[...] += far[d].astype(F32)

        cross(0).wait_send()
        for d in (1, 2, 3):

            @pl.when(y >= d)
            def _():
                cross(d).wait_send()
                up(d).wait_send()

    return comm(
        kernel,
        [
            jax.ShapeDtypeStruct((512, 192), BF),
            jax.ShapeDtypeStruct((512, 384), F32),
            jax.ShapeDtypeStruct((4, 48, 384), BF),
            jax.ShapeDtypeStruct((2, 48, 768), BF),
            jax.ShapeDtypeStruct((128, 768), F32),
        ],
        5,
        (4, 4, 4, 4, 3, 3, 3, 3, 3, 3),
        (query, branch, wo, kv_all, out_t, lse, fc, proj, base, result),
        scratch=[
            pltpu.VMEM((3, 192, 512), BF),
            pltpu.VMEM((3, 192, 512), BF),
            pltpu.VMEM((3, 512, 192), BF),
            pltpu.VMEM((3, 512, 192), BF),
            pltpu.VMEM((8, 512), F32),
            pltpu.VMEM((192, 512), F32),
            pltpu.VMEM((4, 512, 384), BF),
            pltpu.VMEM((4, 512, 384), BF),
            pltpu.VMEM((4, 512, 384), BF),
            pltpu.VMEM((4, 512, 384), BF),
            pltpu.VMEM((3, 4, 48, 384), BF),
            pltpu.VMEM((3, 2, 48, 768), BF),
            pltpu.VMEM((3, 128, 768), BF),
        ],
        spaces=([VMEM] * 10, [VMEM] * 5),
        name="attend_back",
    )


def normalize(rows):
    centered = rows - jnp.mean(rows, -1, keepdims=True)
    inverse = lax.rsqrt(jnp.mean(centered * centered, -1, keepdims=True) + EPSILON)
    return centered * inverse, inverse


def normalize_back(normed, inverse, gain, grad):
    scaled = grad * gain
    return inverse * (
        scaled
        - jnp.mean(scaled, -1, keepdims=True)
        - normed * jnp.mean(scaled * normed, -1, keepdims=True)
    )


def feed_forward(heads_all, x_group, dy_group, wo, wf, wp, vec_rows):
    def kernel(
        h_ref, x_ref, dy_ref, wo_ref, wf_ref, wp_ref, v_ref,
        base_ref, res_mine, gx_ref, bo_ref, gwf_ref, gwp_ref, gfb_ref, gv_ref,
        a2, act, df, x_two, normed, inverse, norm_other, norm_mine, res_other,
        norm_got, res_got, norm_far, branch,
        cs, cr, es, er, zs, zr, bs, br,
    ):
        y, z, k, x = coords()
        sib = device(y, z, 1 - k, x)
        steps = (1, 2, 3)
        greet([sib] + [device(y, ring(z, d), k, x) for d in steps])
        out_bias, gain, shift, proj_bias = (v_ref[i : i + 1] for i in range(4, 8))
        fc_bias = jnp.zeros((1, 384), F32)
        for b in range(4):
            row = v_ref[8 + b : 9 + b, pl.ds(pl.multiple_of(384 * k, 128), 384)]
            fc_bias = fc_bias + jnp.where(z == b, row, 0.0)

        def half(kk, norm_ref, res_ref):
            two = x_ref[kk].reshape(512, 768).astype(F32) + out_bias
            for g in range(4):
                h = h_ref[g, kk]
                at = slice(192 * g, 192 * g + 192)
                part = jnp.concatenate([dot(h, wo_ref[0, at]), dot(h, wo_ref[1, at])], 1)
                two = two + part
            x_two[...] = two
            n, inv = normalize(two)
            normed[...] = n
            inverse[...] = jnp.broadcast_to(inv, (512, 128))
            a = (n * gain + shift).astype(BF)
            a2[kk] = a
            hidden = dot(a, wf_ref[...]) + fc_bias
            square = hidden * hidden
            t = jnp.tanh(0.7978845608028654 * (hidden + 0.044715 * square * hidden))
            act_blk = (0.5 * hidden * (1.0 + t)).astype(BF)
            act[kk] = act_blk
            slope = 0.5 * (1.0 + t) + 0.5 * hidden * (1.0 - t * t) * (
                0.7978845608028654 * (1.0 + 3 * 0.044715 * square)
            )
            dy = dy_ref[kk].reshape(512, 768)
            back = lax.dot_general(
                dy, wp_ref[...], (((1,), (1,)), ((), ())), preferred_element_type=F32
            )
            df_blk = (back * slope).astype(BF)
            df[kk] = df_blk
            norm_part = lax.dot_general(
                df_blk, wf_ref[...], (((1,), (1,)), ((), ())), preferred_element_type=F32
            )
            norm_ref[...] = norm_part.astype(BF).reshape(4, 128, 768)
            res_ref[...] = dot(act_blk, wp_ref[...]).astype(BF).reshape(4, 128, 768)

        half(1 - k, norm_other, res_other)
        swaps = []
        for d in (1, 2, 3, 0):
            b = ring(z, d)
            c = remote(norm_other.at[b], norm_got.at[b], cs.at[d], cr.at[d], sib)
            c.start()
            swaps.append(c)
        for d in (1, 2, 3, 0):
            b = ring(z, d)
            c = remote(res_other.at[b], res_got.at[b], es.at[d], er.at[d], sib)
            c.start()
            swaps.append(c)
        half(k, norm_mine, res_mine)
        sends = []
        for d in steps:
            b = ring(z, d)
            swaps[d - 1].wait_recv()
            norm_mine[b] = (norm_mine[b].astype(F32) + norm_got[b].astype(F32)).astype(BF)
            c = remote(
                norm_mine.at[b], norm_far.at[d - 1], zs.at[d - 1], zr.at[d - 1],
                device(y, b, k, x),
            )
            c.start()
            sends.append(c)
        tn = (((0,), (0,)), ((), ()))
        gwf = lax.dot_general(a2[0], df[0], tn, preferred_element_type=F32)
        gwf += lax.dot_general(a2[1], df[1], tn, preferred_element_type=F32)
        gwf_ref[...] = gwf.astype(BF)
        own_rows = pl.ds(pl.multiple_of(128 * z, 128), 128)
        swaps[3].wait_recv()
        for c in sends:
            c.wait_recv()
        da = (
            norm_mine[z].astype(F32)
            + norm_got[z].astype(F32)
            + norm_far[0].astype(F32)
            + norm_far[1].astype(F32)
            + norm_far[2].astype(F32)
        )
        n = normed[own_rows]
        dy = dy_ref[k, z].astype(F32)
        gx = dy + normalize_back(n, inverse[own_rows, 0:1], gain, da)
        gx_ref[...] = gx
        low = gx.astype(BF)
        branch[...] = low
        bo_ref[z] = low
        branches = []
        for d in steps:
            c = remote(
                branch, bo_ref.at[z], bs.at[d - 1], br.at[d - 1], device(y, ring(z, d), k, x)
            )
            c.start()
            branches.append(c)
        gwp = lax.dot_general(
            act[0], dy_ref[0].reshape(512, 768), tn, preferred_element_type=F32
        )
        gwp += lax.dot_general(
            act[1], dy_ref[1].reshape(512, 768), tn, preferred_element_type=F32
        )
        gwp_ref[...] = gwp.astype(BF)
        gfb_ref[...] = jnp.sum(df[0].astype(F32), 0, keepdims=True) + jnp.sum(
            df[1].astype(F32), 0, keepdims=True
        )
        gv_ref[0:1] = jnp.sum(low.astype(F32), 0, keepdims=True)
        gv_ref[1:2] = jnp.sum(da * n, 0, keepdims=True)
        gv_ref[2:3] = jnp.sum(da, 0, keepdims=True)
        gv_ref[3:4] = jnp.sum(dy, 0, keepdims=True)
        for c in swaps[4:]:
            c.wait_recv()
        res_mine[...] = (res_mine[...].astype(F32) + res_got[...].astype(F32)).astype(BF)
        base_ref[...] = x_two[own_rows] + proj_bias
        for c in branches:
            c.wait()
        for c in swaps + sends:
            c.wait_send()

    return comm(
        kernel,
        [
            jax.ShapeDtypeStruct((128, 768), F32),
            jax.ShapeDtypeStruct((4, 128, 768), BF),
            jax.ShapeDtypeStruct((128, 768), F32),
            jax.ShapeDtypeStruct((4, 128, 768), BF),
            jax.ShapeDtypeStruct((768, 384), BF),
            jax.ShapeDtypeStruct((384, 768), BF),
            jax.ShapeDtypeStruct((1, 384), F32),
            jax.ShapeDtypeStruct((4, 768), F32),
        ],
        3,
        (4, 4, 4, 4, 3, 3, 3, 3),
        (heads_all, x_group, dy_group, wo, wf, wp, vec_rows),
        scratch=[
            pltpu.VMEM((2, 512, 768), BF),
            pltpu.VMEM((2, 512, 384), BF),
            pltpu.VMEM((2, 512, 384), BF),
            pltpu.VMEM((512, 768), F32),
            pltpu.VMEM((512, 768), F32),
            pltpu.VMEM((512, 128), F32),
        ]
        + [pltpu.VMEM((4, 128, 768), BF)] * 5
        + [pltpu.VMEM((3, 128, 768), BF)]
        + [pltpu.VMEM((128, 768), BF)],
        spaces=([VMEM] * 7, [VMEM] * 8),
        name="feed_forward",
    )


def adam_update(weight, moment_one, moment_two, gradient, rate, decay):
    new_one = BETA_ONE * moment_one + (1.0 - BETA_ONE) * gradient
    new_two = BETA_TWO * moment_two + (1.0 - BETA_TWO) * gradient * gradient
    fix_one = 1.0 - BETA_ONE**STEP
    fix_two = 1.0 - BETA_TWO**STEP
    direction = new_one / fix_one / (jnp.sqrt(new_two / fix_two) + ADAM_EPSILON)
    return (weight - rate * (direction + decay * weight), new_one, new_two)


def shards(
    tokens,
    cotangent,
    w_qkv,
    qkv_m,
    qkv_v,
    w_out,
    out_m,
    out_v,
    w_fc,
    fc_m,
    fc_v,
    w_proj,
    proj_m,
    proj_v,
    vectors,
    vec_m,
    vec_v,
):
    state = (
        w_qkv, qkv_m, qkv_v, w_out, out_m, out_v, w_fc, fc_m, fc_v, w_proj, proj_m, proj_v,
        vectors, vec_m, vec_v,
    )
    (
        heads_all, out_t, lse, kv_all, dy_group, wf, wo, wp, query, act_one, normed_core,
        wq, x_group, vec_rows,
    ) = forward(w_qkv, w_fc, w_out, w_proj, vectors, tokens[0], cotangent[0])
    wq = wq.reshape(768, 640)
    wo = wo.reshape(2, 768, 384)
    base, result, grad_x_two, branch_core, grad_w_fc, grad_w_proj, grad_fc_bias, vec_sums = feed_forward(
        heads_all,
        x_group,
        dy_group,
        wo,
        wf.reshape(768, 384),
        wp.reshape(384, 768),
        vec_rows,
    )
    branch_core = branch_core.reshape(512, 768)
    grad_query, grad_kv, fc_sum, proj_sum, result_sum = attend_back(
        query,
        branch_core,
        wo,
        kv_all,
        out_t,
        lse,
        grad_w_fc.reshape(4, 4, 48, 384),
        grad_w_proj.reshape(2, 4, 48, 768),
        base,
        result,
    )
    grad_one, last_rows, proj_rows = last_sums(
        (
            act_one,
            normed_core,
            heads_all,
            grad_query,
            grad_kv,
            branch_core,
            wq,
            vec_sums,
            grad_fc_bias,
        ),
        fc_sum,
        proj_sum,
    )
    output, grad_inputs, *new_state = finish(
        grad_one, grad_x_two, tokens[0], vec_rows, last_rows, proj_rows, result_sum, state
    )
    return (output[None], grad_inputs[None], *new_state)


def solution(mesh):
    split = P("fsdp", "ctx", None)
    rows = P(("ctx", "fsdp"), None)
    return jax.shard_map(
        shards,
        mesh=mesh,
        in_specs=(split, split) + (rows,) * 15,
        out_specs=(split, split) + (rows,) * 15,
        check_vma=False,
    )
```

```python
import jax
import jax.numpy as jnp
from jax import lax
from jax.experimental import pallas as pl
from jax.experimental.pallas import tpu as pltpu
from jax.sharding import PartitionSpec as P

STEP = 10
EPSILON = 1e-05
BETA_ONE = 0.9
BETA_TWO = 0.999
ADAM_EPSILON = 1e-08
MESH = pl.DeviceIdType.MESH
BF = jnp.bfloat16
F32 = jnp.float32
ANY = pl.BlockSpec(memory_space=pl.ANY)
VMEM = pl.BlockSpec(memory_space=pltpu.VMEM)
LIMIT = 56 * 1024 * 1024


def coords():
    c = lax.axis_index("ctx")
    return c // 8, (c // 2) % 4, c % 2, lax.axis_index("fsdp")


def device(y, z, k, x):
    return ((y * 4 + z) * 2 + k, x)


def ring(v, step):
    return lax.rem(v + step, 4)


def greet(devices):
    barrier = pltpu.get_barrier_semaphore()
    for one in devices:
        pl.semaphore_signal(barrier, inc=1, device_id=one, device_id_type=MESH)
    return lambda: pl.semaphore_wait(barrier, len(devices))


def remote(src, dst, send, recv, to):
    return pltpu.make_async_remote_copy(
        src, dst, send, recv, device_id=to, device_id_type=MESH
    )


def comm(kernel, outs, cid, sems, args, scratch=(), spaces=None, name=None):
    return pl.pallas_call(
        kernel,
        out_shape=outs,
        in_specs=[ANY] * len(args) if spaces is None else spaces[0],
        out_specs=[ANY] * len(outs) if spaces is None else spaces[1],
        scratch_shapes=list(scratch) + [pltpu.SemaphoreType.DMA((n,)) for n in sems],
        compiler_params=pltpu.CompilerParams(
            collective_id=cid, has_side_effects=True, vmem_limit_bytes=LIMIT
        ),
        name=name,
    )(*args)


def last_sums(pieces, fc, proj):
    wide = 1664

    def kernel(*refs):
        (
            act_ref, n_ref, h_ref, gq_ref, gkv_ref, br_ref, wq_ref, vs_ref, fb_ref,
            fc_ref, proj_ref,
        ) = refs[:11]
        one_out, rows_out, proj_out, fc_out = refs[11:15]
        (
            one_far, mix_got, mix_sum, mix_far, vec_far, mix_mine, vec_mine,
            mix_all, vec_all, proj_sum, out_send, fc_send,
            one_ref, mix_other, mix_ref, vec_ref,
            act_t, heads, heads_t, d_ref, right_one, right_two, vec_rows,
        ) = refs[15:38]
        (
        zs, zr, cs, cr, s1, r1, s2, r2, s3, r3, s4, r4, s5, r5, s7, r7, s8, r8, loc,
        ) = refs[38:]
        y, z, k, x = coords()
        me = y * 4 + z
        sib = device(y, z, 1 - k, x)
        steps = (1, 2, 3)
        everyone = greet(
            [sib]
            + [device(y, z, j, ring(x, d)) for d in steps for j in (k, 1 - k)]
            + [
                device(ring(y, a), ring(z, b), k, x)
                for a in range(4)
                for b in range(4)
                if (a, b) != (0, 0)
            ]
        )
        d_ref[:, 0:192] = gq_ref[...]
        d_ref[:, 192:576] = gkv_ref[...].astype(BF)
        d_ref[:, 576:640] = jnp.zeros((512, 64), BF)
        right_one[...] = jnp.zeros_like(right_one)
        right_one[:, 0:288] = d_ref[:, 0:288]
        right_one[:, 384:672] = d_ref[:, 288:576]
        right_two[...] = jnp.zeros_like(right_two)
        vec_rows[...] = jnp.zeros_like(vec_rows)
        sums = jnp.sum(d_ref[...].astype(F32), 0, keepdims=True)
        at_half = pl.ds(pl.multiple_of(384 * k, 128), 384)
        for b in range(4):
            heads[:, 192 * b : 192 * b + 192] = h_ref[b, k]

            @pl.when(z == b)
            def _():
                right_two[:, 288:384] = br_ref[:, 192 * b : 192 * b + 96]
                right_two[:, 672:768] = br_ref[:, 192 * b + 96 : 192 * b + 192]
                vec_rows[2:3, 192 * b : 192 * b + 192] = sums[:, 0:192]
                vec_rows[3:4, 192 * b : 192 * b + 192] = sums[:, 384:576]
                vec_rows[8 + b : 9 + b, at_half] = fb_ref[...]

        vec_rows[4:8] = vs_ref[...]
        act_t[...] = act_ref[...].T
        heads_t[...] = heads[...].T

        def product(h):
            at = pl.ds(pl.multiple_of(384 * h, 128), 384)
            total = dot(act_t[...], right_one[:, at]) + dot(heads_t[...], right_two[:, at])
            return total.reshape(4, 4, 48, 384)

        mix_other[...] = product(1 - k).astype(BF)
        everyone()
        swap = []
        for d in (1, 2, 3, 0):
            b = ring(x, d)
            c = remote(mix_other.at[:, b], mix_got.at[b], cs.at[d], cr.at[d], sib)
            c.start()
            swap.append(c)
        def proj_last(i):
            return remote(
                proj_sum.at[i], proj_out, s8.at[i], r8.at[0],
                device(y, z, x // 2, lax.rem(2 * x + i, 4)),
            )

        def proj_here(i):
            return (k == x // 2) & (x == lax.rem(2 * x + i, 4))

        holder = k == z // 2

        @pl.when(holder)
        def _():
            for i in range(2):
                proj_sum[i] = proj_ref[24 * i : 24 * i + 24]

                @pl.when(jnp.logical_not(proj_here(i)))
                def _():
                    proj_last(i).start()

                @pl.when(proj_here(i))
                def _():
                    proj_out[...] = proj_sum[i]

        def last_here(i):
            return k * 4 + x == i

        def fc_last(i):
            return remote(
                fc_send.at[i], fc_out.at[k], s4.at[i], r4.at[k], device(y, z, i // 4, i % 4)
            )

        @pl.when(z == x)
        def _():
            for i in range(8):
                fc_send[i, 0:6] = fc_ref[6 * i : 6 * i + 6]
                fc_send[i, 6:8] = jnp.zeros((2, 1536), F32)

                @pl.when(jnp.logical_not(last_here(i)))
                def _():
                    fc_last(i).start()

                @pl.when(last_here(i))
                def _():
                    fc_out[k] = fc_send[i]

        mix_ref[...] = product(k).astype(BF)
        one = lax.dot_general(
            d_ref[...], wq_ref[...], (((1,), (1,)), ((), ())), preferred_element_type=F32
        )
        one_ref[...] = one.astype(BF).reshape(4, 128, 768)
        vec_rows[0:1] = jnp.sum(one * n_ref[...].astype(F32), 0, keepdims=True)
        vec_rows[1:2] = jnp.sum(one, 0, keepdims=True)
        vec_ref[...] = vec_rows[...].T.astype(BF).reshape(4, 4, 48, 128)
        along = []
        for d in steps:
            b = ring(x, d)
            to = device(y, z, k, b)
            swap[d - 1].wait_recv()
            mix_sum[d] = (mix_ref[:, b].astype(F32) + mix_got[b].astype(F32)).astype(BF)
            c = remote(mix_sum.at[d], mix_far.at[d - 1], s1.at[d - 1], r1.at[d - 1], to)
            c.start()
            along.append(c)
            c = remote(vec_ref.at[:, b], vec_far.at[d - 1], s2.at[d - 1], r2.at[d - 1], to)
            c.start()
            along.append(c)
        ones = []
        for d in steps:
            c = remote(
                one_ref.at[ring(z, d)], one_far.at[d - 1], zs.at[d - 1], zr.at[d - 1],
                device(y, ring(z, d), k, x),
            )
            c.start()
            ones.append(c)

        def plane(src, dst, send, recv, a):
            return remote(src.at[a], dst.at[me], send.at[a], recv.at[me], device(a, x, k, x))

        def all_start(src, dst, send, recv):
            for a in range(4):
                here = (a == y) & (z == x)

                @pl.when(jnp.logical_not(here))
                def _():
                    plane(src, dst, send, recv, a).start()

                @pl.when(here)
                def _():
                    c = pltpu.make_async_copy(src.at[a], dst.at[me], loc.at[0])
                    c.start()
                    c.wait()

        def all_finish(src, dst, send, recv):
            for a in range(4):

                @pl.when(jnp.logical_not((a == y) & (z == x)))
                def _():
                    plane(src, dst, send, recv, a).wait_send()

        def all_receive(src, dst, send, recv):
            def step(i, carry):
                @pl.when(i != me)
                def _():
                    remote(src.at[0], dst.at[i], send.at[0], recv.at[i], sib).wait_recv()

                return carry

            lax.fori_loop(0, 16, step, 0)

        swap[3].wait_recv()
        for c in along:
            c.wait_recv()
        mix_mine[...] = (
            mix_ref[:, x].astype(F32)
            + mix_got[x].astype(F32)
            + mix_far[0].astype(F32)
            + mix_far[1].astype(F32)
            + mix_far[2].astype(F32)
        ).astype(BF)
        vec_mine[...] = (
            vec_ref[:, x].astype(F32)
            + vec_far[0].astype(F32)
            + vec_far[1].astype(F32)
            + vec_far[2].astype(F32)
        ).astype(BF)
        all_start(mix_mine, mix_all, s3, r3)
        all_start(vec_mine, vec_all, s5, r5)
        for c in ones:
            c.wait_recv()
        one_out[...] = (
            one_ref[z].astype(F32)
            + one_far[0].astype(F32)
            + one_far[1].astype(F32)
            + one_far[2].astype(F32)
        )

        def last_copy(i):
            return remote(
                out_send.at[i], rows_out.at[k], s7.at[i], r7.at[k], device(y, z, i // 4, i % 4)
            )

        @pl.when(z == x)
        def _():
            all_receive(mix_mine, mix_all, s3, r3)
            all_receive(vec_mine, vec_all, s5, r5)

            def four(ref, b):
                return (
                    ref[b].astype(F32)
                    + ref[4 + b].astype(F32)
                    + ref[8 + b].astype(F32)
                    + ref[12 + b].astype(F32)
                )

            for b in range(4):
                m = four(mix_all, b)
                for i in range(8):
                    rows = slice(6 * i, 6 * i + 6)
                    out_send[i, 0:6, 384 * b : 384 * b + 384] = m[rows]
            v = four(vec_all, 0) + four(vec_all, 1) + four(vec_all, 2) + four(vec_all, 3)
            for i in range(8):
                out_send[i, 0:6, 1536:1664] = v[6 * i : 6 * i + 6]
                out_send[i, 6:8, :] = jnp.zeros((2, wide), F32)
            for i in range(8):

                @pl.when(jnp.logical_not(last_here(i)))
                def _():
                    last_copy(i).start()

                @pl.when(last_here(i))
                def _():
                    c = pltpu.make_async_copy(out_send.at[i], rows_out.at[k], loc.at[3])
                    c.start()
                    c.wait()

        for j in range(2):

            @pl.when(jnp.logical_not((z == x) & (k == j)))
            def _():
                remote(out_send.at[0], rows_out.at[j], s7.at[0], r7.at[j], sib).wait_recv()
                remote(fc_send.at[0], fc_out.at[j], s4.at[0], r4.at[j], sib).wait_recv()

        @pl.when(jnp.logical_not((k == z // 2) & (x == (4 * k + x) // 2)))
        def _():
            remote(proj_sum.at[0], proj_out, s8.at[0], r8.at[0], sib).wait_recv()

        @pl.when(z == x)
        def _():
            for i in range(8):

                @pl.when(jnp.logical_not(last_here(i)))
                def _():
                    last_copy(i).wait_send()
                    fc_last(i).wait_send()

        for i in range(2):

            @pl.when(holder & jnp.logical_not(proj_here(i)))
            def _():
                proj_last(i).wait_send()

        all_finish(mix_mine, mix_all, s3, r3)
        all_finish(vec_mine, vec_all, s5, r5)
        for c in swap + along + ones:
            c.wait_send()

    return comm(
        kernel,
        [
            jax.ShapeDtypeStruct((128, 768), F32),
            jax.ShapeDtypeStruct((2, 8, wide), F32),
            jax.ShapeDtypeStruct((24, 768), F32),
            jax.ShapeDtypeStruct((2, 8, 1536), F32),
        ],
        6,
        (3, 3, 4, 4, 3, 3, 3, 3, 4, 16, 8, 2, 4, 16, 8, 2, 2, 1, 4),
        (*pieces, fc, proj),
        scratch=[
            pltpu.VMEM((3, 128, 768), BF),
            pltpu.VMEM((4, 4, 48, 384), BF),
            pltpu.VMEM((4, 4, 48, 384), BF),
            pltpu.VMEM((3, 4, 48, 384), BF),
            pltpu.VMEM((3, 4, 48, 128), BF),
            pltpu.VMEM((4, 48, 384), BF),
            pltpu.VMEM((4, 48, 128), BF),
            pltpu.VMEM((16, 48, 384), BF),
            pltpu.VMEM((16, 48, 128), BF),
            pltpu.VMEM((2, 24, 768), F32),
            pltpu.VMEM((8, 8, wide), F32),
            pltpu.VMEM((8, 8, 1536), F32),
            pltpu.VMEM((4, 128, 768), BF),
            pltpu.VMEM((4, 4, 48, 384), BF),
            pltpu.VMEM((4, 4, 48, 384), BF),
            pltpu.VMEM((4, 4, 48, 128), BF),
            pltpu.VMEM((768, 512), BF),
            pltpu.VMEM((512, 768), BF),
            pltpu.VMEM((768, 512), BF),
            pltpu.VMEM((512, 640), BF),
            pltpu.VMEM((512, 768), BF),
            pltpu.VMEM((512, 768), BF),
            pltpu.VMEM((128, 768), F32),
        ],
        spaces=([VMEM] * 11, [VMEM] * 4),
        name="last_sums",
    )


def finish(grad_one, grad_x_two, tokens, vec_rows, rows, proj_rows, fc_rows, result, state):
    def kernel(*refs):
        one_ref, gx_ref, t_ref, v_ref, rows_ref, p_ref, f_ref, res_ref = refs[:8]
        state_ref = refs[8:23]
        out_ref, gin_ref = refs[23:25]
        new_ref = refs[25:40]
        g_qkv, g_out, g_fc = refs[40:]
        out_ref[...] = res_ref[...]
        normed, inverse = normalize(t_ref[...].astype(F32))
        gin_ref[...] = gx_ref[...] + normalize_back(normed, inverse, v_ref[0:1], one_ref[...])
        for b in range(4):
            one_half = rows_ref[0, 0:6, 384 * b : 384 * b + 384]
            two_half = rows_ref[1, 0:6, 384 * b : 384 * b + 384]
            q = 192 * b
            g_qkv[:, q : q + 192] = one_half[:, 0:192]
            g_qkv[:, 768 + q : 864 + q] = one_half[:, 192:288]
            g_qkv[:, 864 + q : 960 + q] = two_half[:, 0:96]
            g_qkv[:, 1536 + q : 1728 + q] = two_half[:, 96:288]
            g_out[:, q : q + 96] = one_half[:, 288:384]
            g_out[:, q + 96 : q + 192] = two_half[:, 288:384]
            for j in range(2):
                at = 384 * (2 * b + j)
                g_fc[:, at : at + 384] = f_ref[j, 0:6, 384 * b : 384 * b + 384]
        g_vec = rows_ref[0, 0:6, 1536:1548] + rows_ref[1, 0:6, 1536:1548]
        for i, (gradient, rate, decay) in enumerate(
            (
                (g_qkv[...], 0.1, 0.1),
                (g_out[...], 0.3, 0.1),
                (g_fc[...], 0.05, 0.1),
                (p_ref[...], 0.03, 0.1),
                (g_vec, 0.5, 0.0),
            )
        ):
            w, m, v = state_ref[3 * i : 3 * i + 3]
            results = adam_update(w[...], m[...], v[...], gradient, rate, decay)
            for j in range(3):
                new_ref[3 * i + j][...] = results[j]

    return pl.pallas_call(
        kernel,
        out_shape=[jax.ShapeDtypeStruct((128, 768), F32)] * 2
        + [jax.ShapeDtypeStruct(one.shape, F32) for one in state],
        in_specs=[VMEM] * 23,
        out_specs=[VMEM] * 17,
        scratch_shapes=[
            pltpu.VMEM((6, 2304), F32),
            pltpu.VMEM((6, 768), F32),
            pltpu.VMEM((6, 3072), F32),
        ],
        compiler_params=pltpu.CompilerParams(vmem_limit_bytes=LIMIT),
        name="finish",
    )(grad_one, grad_x_two, tokens, vec_rows, rows, proj_rows, fc_rows, result, *state)


def head_rows(matrix, head):
    row = lax.broadcasted_iota(jnp.int32, matrix.shape, 0)
    keep = (row >= 64 * head) & (row < 64 * head + 64)
    return jnp.where(keep, matrix, jnp.zeros_like(matrix))


def head_cols(matrix, head):
    col = lax.broadcasted_iota(jnp.int32, matrix.shape, 1)
    keep = (col >= 64 * head) & (col < 64 * head + 64)
    return jnp.where(keep, matrix, jnp.zeros_like(matrix))


def place(index):
    return (index // 128) * 256 + index % 128


def dot(a, b):
    return jnp.dot(a, b, preferred_element_type=F32)


def forward(w_qkv, w_fc, w_out, w_proj, vectors, tokens, cotangent):
    wide_q, wide_r = 1280, 3456

    def kernel(
        wq_ref, wf_ref, wo_ref, wp_ref, wv_ref, t_ref, r_ref,
        ho_ref, ot_ref, lse_ref, vo_ref, ro_ref, fo_ref, oo_ref, po_ref, q_ref, a_ref, n_ref,
        q_out, x_ref, vec_ref,
        wide_one, wide_two, packed_q, packed_r, got_q, got_r,
        fc48, qkv48, out48, proj_wide, q_send, f_send, o_send, p_send, f_mid, o_mid, p_mid,
        bias, qt, m_ref, l_ref, h_buf, v_ref,
        mq_s, mq_r, fq_s, fq_r, mr_s, mr_r, fr_s, fr_r, s1, r1, s2, r2, ps, pr,
        xs_s, xs_r, xf_s, xf_r, ts, tr, us, ur,
        vs, vr, rs, rr, cs, cr, ds, dr, ws, wr, wf, os, orr, hs, hr, gs, gr, loc,
    ):
        y, z, k, x = coords()
        me = y * 4 + z
        t = k * 4 + x
        sib = device(y, z, 1 - k, x)
        steps = (1, 2, 3)
        everyone = greet(
            [sib]
            + [device(y, z, k, ring(x, d)) for d in steps]
            + [
                device(ring(y, a), ring(z, b), k, x)
                for a in range(4)
                for b in range(4)
                if (a, b) != (0, 0)
            ]
        )

        def first(packed, got, send, recv):
            copies = [
                remote(packed, got.at[t], send.at[d], recv.at[d], device(y, z, k, ring(x, d)))
                for d in steps
            ]
            for c in copies:
                c.start()
            return copies

        def crossing(packed, got, copies, send, recv):
            out = [remote(packed, got.at[t], send.at[0], recv.at[0], sib)]
            out[0].start()
            for d in steps:
                copies[d - 1].wait_recv()
                src = k * 4 + ring(x, 4 - d)
                c = remote(got.at[src], got.at[src], send.at[d], recv.at[d], sib)
                c.start()
                out.append(c)
            return out

        wide_one[...] = jnp.zeros_like(wide_one)
        wide_one[0:6, 0:1152] = wq_ref[:, 0:1152]
        wide_one[6:12, 0:1152] = wq_ref[:, 1152:2304]
        wide_one[0:6, 1152:1164] = wv_ref[...]
        packed_q[...] = wide_one[...].astype(BF)
        got_q[t] = packed_q[...]
        everyone()
        message_q = first(packed_q, got_q, mq_s, mq_r)
        token_copies = []
        for d in steps:
            c = remote(
                t_ref, x_ref.at[k, z], ts.at[d], tr.at[d], device(y, ring(z, d), k, x)
            )
            c.start()
            token_copies.append(c)
        token_cross = [remote(t_ref, x_ref.at[k, z], us.at[0], ur.at[0], sib)]
        token_cross[0].start()
        x_ref[k, z] = t_ref[...]
        wide_two[...] = jnp.zeros_like(wide_two)
        wide_two[0:6, 0:1920] = wf_ref[:, 0:1920]
        wide_two[6:12, 0:1152] = wf_ref[:, 1920:3072]
        wide_two[6:12, 1152:1920] = wo_ref[...]
        wide_two[0:12, 1920:2688] = wp_ref[0:12]
        wide_two[0:12, 2688:3456] = wp_ref[12:24]
        packed_r[...] = wide_two[...].astype(BF)
        got_r[t] = packed_r[...]
        cross_q = crossing(packed_q, got_q, message_q, fq_s, fq_r)
        message_r = first(packed_r, got_r, mr_s, mr_r)
        for c in cross_q:
            c.wait_recv()
        for i in range(8):
            piece = got_q[i].astype(F32)
            at = slice(6 * i, 6 * i + 6)
            qkv48[at, 0:1152] = piece[0:6, 0:1152]
            qkv48[at, 1152:2304] = piece[6:12, 0:1152]
            qkv48[at, 2304:2432] = piece[0:6, 1152:1280]
        for j in range(4):
            q_send[j, :, 0:192] = qkv48[:, 192 * j : 192 * j + 192].astype(BF)
            q_send[j, :, 192:384] = qkv48[:, 768 + 192 * j : 960 + 192 * j].astype(BF)
            q_send[j, :, 384:576] = qkv48[:, 1536 + 192 * j : 1728 + 192 * j].astype(BF)
            q_send[j, :, 576:640] = qkv48[:, 2304:2368].astype(BF)

        group = pl.ds(pl.multiple_of(16 * jnp.minimum(x, 2), 16), 16)

        def to_of(m):
            return ring(y, m // 4), ring(z, m % 4)

        def q_copy(m):
            ty, tz = to_of(m)
            return remote(
                q_send.at[tz, group], q_out.at[me, group], s1.at[m], r1.at[m],
                device(ty, tz, k, x),
            )

        def f_copy(m):
            ty, tz = to_of(m)
            return remote(
                f_send.at[tz * 2 + k], f_mid.at[me], s2.at[m], r2.at[m], device(ty, tz, k, x)
            )

        def o_copy(m):
            ty, tz = to_of(m)
            return remote(o_send.at[k], o_mid.at[me], s2.at[m], r2.at[m], device(ty, tz, k, x))

        def p_copy(a):
            return remote(
                p_send, p_mid.at[z % 2], ps.at[a], pr.at[z % 2], device(ring(y, a), y, k, x)
            )

        def each(copy, what):
            def step(m, carry):
                what(copy(m))
                return carry

            lax.fori_loop(1, 16, step, 0)

        start = lambda c: c.start()
        finish = lambda c: c.wait()

        @pl.when(x < 3)
        def _():
            each(q_copy, start)
            q_out[me, group] = q_send[z, group]

        cross_r = crossing(packed_r, got_r, message_r, fr_s, fr_r)
        for c in cross_r:
            c.wait_recv()
        for i in range(8):
            piece = got_r[i].astype(F32)
            at = slice(6 * i, 6 * i + 6)
            fc48[at, 0:1920] = piece[0:6, 0:1920]
            fc48[at, 1920:3072] = piece[6:12, 0:1152]
            out48[at] = piece[6:12, 1152:1920]
            proj_wide[24 * i : 24 * i + 12] = piece[0:12, 1920:2688]
            proj_wide[24 * i + 12 : 24 * i + 24] = piece[0:12, 2688:3456]
        for j in range(8):
            f_send[j] = fc48[:, 384 * j : 384 * j + 384].astype(BF)
        o_send[0] = out48[:, 0:384].astype(BF)
        o_send[1] = out48[:, 384:768].astype(BF)
        p_send[...] = proj_wide[...].astype(BF)

        half = pl.ds(8 * k, 8)
        other_half = pl.ds(8 * (1 - k), 8)

        def rows_of(plane):
            return pl.ds(pl.multiple_of(16 * plane, 16), 16)

        def x_copy(d):
            return remote(
                q_out.at[half, group], q_out.at[half, group], xs_s.at[d], xs_r.at[x],
                device(y, z, k, ring(x, d)),
            )

        @pl.when(x < 3)
        def _():
            each(q_copy, finish)
            for d in steps:
                x_copy(d).start()

        @pl.when(x == 1)
        def _():
            each(f_copy, start)
            f_mid[me] = f_send[z * 2 + k]

        @pl.when(x == 2)
        def _():
            each(o_copy, start)
            o_mid[me] = o_send[k]

        @pl.when((x == 3) & (k == z // 2))
        def _():
            for a in range(1, 4):
                p_copy(a).start()

            @pl.when(z != y)
            def _():
                p_copy(0).start()

            @pl.when(z == y)
            def _():
                p_mid[z % 2] = p_send[...]

        def pass_q(a):
            return remote(
                q_out.at[half, rows_of(a)], q_out.at[half, rows_of(a)], xf_s.at[a], xf_r.at[a], sib
            )

        for a in range(3):

            @pl.when(x != a)
            def _():
                remote(
                    q_out.at[half, rows_of(a)], q_out.at[half, rows_of(a)], xs_s.at[0],
                    xs_r.at[a], sib,
                ).wait_recv()
                pass_q(a).start()

        for d in steps:
            token_copies[d - 1].wait_recv()
            src = ring(z, 4 - d)
            c = remote(x_ref.at[k, src], x_ref.at[k, src], us.at[d], ur.at[d], sib)
            c.start()
            token_cross.append(c)
        normed, _ = normalize(x_ref[k].reshape(512, 768).astype(F32))
        n_ref[...] = normed.astype(BF)

        weights = ((1, f_mid, fo_ref, 8), (2, o_mid, oo_ref, 8), (3, p_mid, po_ref, 1))

        def ends(a, half):
            _, src, dst, n = weights[a - 1]
            at = pl.ds(n * half, n)
            return src.at[at], (dst.at[k, at] if a == 2 else dst.at[at])

        def direct(a, half, d):
            src, dst = ends(a, half)
            return remote(
                src, dst, ws.at[4 * half + d], wr.at[2 * a + half], device(y, z, k, ring(x, d))
            )

        def onward(a, half, d):
            _, dst = ends(a, half)
            return remote(
                dst, dst, wf.at[a], wr.at[2 * a + half], device(y, z, k, ring(x, d))
            )

        def weight_own(a):
            _, src, dst, _ = weights[a - 1]
            return pltpu.make_async_copy(src, dst.at[k] if a == 2 else dst, loc.at[1])

        @pl.when(x == 1)
        def _():
            each(f_copy, finish)

        @pl.when(x == 2)
        def _():
            each(o_copy, finish)

        for i in range(2):
            @pl.when((x == 3) & jnp.logical_not((y == z) & (z == 2 * k + i)))
            def _():
                remote(p_send, p_mid.at[i], ps.at[0], pr.at[i], sib).wait_recv()

        for a in steps:

            @pl.when(x == a)
            def _():
                for half_at, d in ((0, 1), (1, 3), (1, 1), (0, 3)):
                    direct(a, half_at, d).start()
                weight_own(a).start()

        def move_on():
            for a in steps:

                @pl.when(x == (a + 1) % 4)
                def _():
                    direct(a, 0, 1).wait_recv()
                    onward(a, 0, 1).start()

                @pl.when(x == (a + 3) % 4)
                def _():
                    direct(a, 1, 1).wait_recv()
                    onward(a, 1, 3).start()

        for a in range(3):

            @pl.when(x != a)
            def _():
                remote(
                    q_out.at[other_half, rows_of(a)], q_out.at[other_half, rows_of(a)],
                    xf_s.at[a], xf_r.at[a], sib,
                ).wait_recv()

        vec_ref[...] = q_out[:, :, 512:640].reshape(768, 128).astype(F32).T[64:80]
        bias[...] = jnp.zeros_like(bias)
        for b in range(4):

            @pl.when(z == b)
            def _():
                bias[:, 0:192] = vec_ref[2:3, 192 * b : 192 * b + 192]
                bias[:, 384:576] = vec_ref[3:4, 192 * b : 192 * b + 192]

        act = (normed * vec_ref[0:1] + vec_ref[1:2]).astype(BF)
        a_ref[...] = act
        mixed = dot(act, q_out[...].reshape(768, 640)) + bias[...]
        v_ref[...] = mixed[:, 192:576].astype(BF)

        def kv_copy(d):
            return remote(
                v_ref, vo_ref.at[y, k], vs.at[d], vr.at[d], device(ring(y, d), z, k, x)
            )

        for d in steps:

            @pl.when(y + d < 4)
            def _():
                kv_copy(d).start()

        swap = remote(v_ref, vo_ref.at[y, k], cs.at[0], cr.at[0], sib)
        swap.start()
        vo_ref[y, k] = v_ref[...]
        own_r = pltpu.make_async_copy(r_ref, ro_ref.at[k, z], loc.at[0])
        own_r.start()
        row_copies = []
        for d in steps:
            c = remote(
                r_ref, ro_ref.at[k, z], rs.at[d], rr.at[d], device(y, ring(z, d), k, x)
            )
            c.start()
            row_copies.append(c)
        row_first = remote(r_ref, ro_ref.at[k, z], ds.at[0], dr.at[0], sib)
        row_first.start()
        query = mixed[:, :192].astype(BF) * jnp.asarray(0.125, BF)
        q_ref[...] = query
        q_t = query.T
        for head in range(3):
            qt[head] = head_rows(q_t, head)
        m_ref[...] = jnp.full_like(m_ref, -1e30)
        l_ref[...] = jnp.zeros_like(l_ref)
        ot_ref[...] = jnp.zeros_like(ot_ref)

        def block(by, bk, masked):
            keys = vo_ref[by, bk, :, :192]
            values_t = vo_ref[by, bk, :, 192:].T
            if masked:
                key_at = place(lax.broadcasted_iota(jnp.int32, (512, 512), 0)) + 128 * bk
                query_at = place(lax.broadcasted_iota(jnp.int32, (512, 512), 1)) + 128 * k
                visible = query_at >= key_at
            for head in range(3):
                s = dot(keys, qt[head])
                if masked:
                    s = jnp.where(visible, s, -1e9)
                old = m_ref[head : head + 1]
                new = jnp.maximum(old, jnp.max(s, 0, keepdims=True))
                e = jnp.exp(s - new)
                scale = jnp.exp(old - new)
                m_ref[head : head + 1] = new
                l_ref[head : head + 1] = l_ref[head : head + 1] * scale + jnp.sum(
                    e, 0, keepdims=True
                )
                at = slice(64 * head, 64 * head + 64)
                ot_ref[at] = ot_ref[at] * scale + dot(values_t[at], e.astype(BF))

        def diagonal(j, carry):
            @pl.when(j == 1)
            def _():
                remote(v_ref, vo_ref.at[y, 1 - k], cs.at[0], cr.at[0], sib).wait_recv()

            block(y, lax.rem(k + j, 2), True)

            return carry

        lax.fori_loop(0, 2, diagonal, 0)

        def pass_on(d):
            return remote(
                vo_ref.at[y - d, k], vo_ref.at[y - d, k], cs.at[d], cr.at[d], sib
            )

        def earlier(i, carry):
            d, j = i // 2 + 1, i % 2

            @pl.when(j == 0)
            def _():
                remote(v_ref, vo_ref.at[y - d, k], vs.at[d], vr.at[d], sib).wait_recv()
                pass_on(d).start()

            @pl.when(j == 1)
            def _():
                remote(v_ref, vo_ref.at[y - d, 1 - k], cs.at[d], cr.at[d], sib).wait_recv()

            block(y - d, lax.rem(k + j, 2), False)

            @pl.when(i == jnp.minimum(2, 2 * y - 1))
            def _():
                move_on()

            return carry

        @pl.when(y == 0)
        def _():
            move_on()

        lax.fori_loop(0, 2 * y, earlier, 0)
        for head in range(3):
            at = slice(64 * head, 64 * head + 64)
            total = l_ref[head : head + 1]
            ot_ref[at] = ot_ref[at] / total
            lse_ref[head : head + 1] = m_ref[head : head + 1] + jnp.log(total)
        h_buf[...] = ot_ref[...].T.astype(BF)
        heads_copies = []
        for d in steps:
            c = remote(
                h_buf, ho_ref.at[z, k], hs.at[d], hr.at[d], device(y, ring(z, d), k, x)
            )
            c.start()
            heads_copies.append(c)
        c = remote(h_buf, ho_ref.at[z, k], gs.at[0], gr.at[0], sib)
        c.start()
        forward_copies = [c, row_first]
        own_h = pltpu.make_async_copy(h_buf, ho_ref.at[z, k], loc.at[2])
        own_h.start()
        for d in steps:
            row_copies[d - 1].wait_recv()
            src = ring(z, 4 - d)
            c = remote(ro_ref.at[k, src], ro_ref.at[k, src], ds.at[d], dr.at[d], sib)
            c.start()
            forward_copies.append(c)
        for a in steps:

            @pl.when(x == a)
            def _():
                weight_own(a).wait()

            @pl.when(x == (a + 1) % 4)
            def _():
                direct(a, 1, 1).wait_recv()

            @pl.when(x == (a + 3) % 4)
            def _():
                direct(a, 0, 1).wait_recv()

            @pl.when(x == (a + 2) % 4)
            def _():
                direct(a, 0, 1).wait_recv()
                direct(a, 1, 1).wait_recv()

        c = remote(oo_ref.at[k], oo_ref.at[k], os.at[0], orr.at[0], sib)
        c.start()
        forward_copies.append(c)
        for d in steps:
            heads_copies[d - 1].wait_recv()
            src = ring(z, 4 - d)
            c = remote(ho_ref.at[src, k], ho_ref.at[src, k], gs.at[d], gr.at[d], sib)
            c.start()
            forward_copies.append(c)
        for c in forward_copies + token_cross:
            c.wait()
        for c in row_copies + heads_copies + token_copies + [swap]:
            c.wait_send()
        for c in message_q + cross_q + message_r + cross_r:
            c.wait_send()
        for d in steps:

            @pl.when(y + d < 4)
            def _():
                kv_copy(d).wait_send()

            @pl.when(y >= d)
            def _():
                pass_on(d).wait_send()

        for a in steps:

            @pl.when(x == a)
            def _():
                for half_at, d in ((0, 1), (1, 3), (1, 1), (0, 3)):
                    direct(a, half_at, d).wait_send()

            @pl.when(x == (a + 1) % 4)
            def _():
                onward(a, 0, 1).wait_send()

            @pl.when(x == (a + 3) % 4)
            def _():
                onward(a, 1, 3).wait_send()

        @pl.when((x == 3) & (k == z // 2))
        def _():
            for a in range(1, 4):
                p_copy(a).wait_send()

            @pl.when(z != y)
            def _():
                p_copy(0).wait_send()

        @pl.when(x < 3)
        def _():
            for d in steps:
                x_copy(d).wait_send()

        for a in range(3):

            @pl.when(x != a)
            def _():
                pass_q(a).wait_send()

        own_r.wait()
        own_h.wait()

    return comm(
        kernel,
        [
            jax.ShapeDtypeStruct((4, 2, 512, 192), BF),
            jax.ShapeDtypeStruct((192, 512), F32),
            jax.ShapeDtypeStruct((8, 512), F32),
            jax.ShapeDtypeStruct((4, 2, 512, 384), BF),
            jax.ShapeDtypeStruct((2, 4, 128, 768), BF),
            jax.ShapeDtypeStruct((16, 48, 384), BF),
            jax.ShapeDtypeStruct((2, 16, 48, 384), BF),
            jax.ShapeDtypeStruct((2, 192, 768), BF),
            jax.ShapeDtypeStruct((512, 192), BF),
            jax.ShapeDtypeStruct((512, 768), BF),
            jax.ShapeDtypeStruct((512, 768), BF),
            jax.ShapeDtypeStruct((16, 48, 640), BF),
            jax.ShapeDtypeStruct((2, 4, 128, 768), BF),
            jax.ShapeDtypeStruct((16, 768), F32),
        ],
        0,
        (4,) * 8 + (16,) * 4 + (4, 2) + (4,) * 8
        + (4, 4, 4, 4, 4, 4, 4, 4, 8, 8, 4, 1, 1, 4, 4, 4, 4, 3),
        (w_qkv, w_fc, w_out, w_proj, vectors, tokens, cotangent),
        scratch=[
            pltpu.VMEM((16, wide_q), F32),
            pltpu.VMEM((16, wide_r), F32),
            pltpu.VMEM((16, wide_q), BF),
            pltpu.VMEM((16, wide_r), BF),
            pltpu.VMEM((8, 16, wide_q), BF),
            pltpu.VMEM((8, 16, wide_r), BF),
            pltpu.VMEM((48, 3072), F32),
            pltpu.VMEM((48, 2432), F32),
            pltpu.VMEM((48, 768), F32),
            pltpu.VMEM((192, 768), F32),
            pltpu.VMEM((4, 48, 640), BF),
            pltpu.VMEM((8, 48, 384), BF),
            pltpu.VMEM((2, 48, 384), BF),
            pltpu.VMEM((192, 768), BF),
            pltpu.VMEM((16, 48, 384), BF),
            pltpu.VMEM((16, 48, 384), BF),
            pltpu.VMEM((2, 192, 768), BF),
            pltpu.VMEM((1, 640), F32),
            pltpu.VMEM((3, 192, 512), BF),
            pltpu.VMEM((8, 512), F32),
            pltpu.VMEM((8, 512), F32),
            pltpu.VMEM((512, 192), BF),
            pltpu.VMEM((512, 384), BF),
        ],
        spaces=(
            [VMEM] * 6 + [ANY],
            [ANY, VMEM, VMEM, VMEM, ANY, ANY, ANY, ANY] + [VMEM] * 6,
        ),
        name="forward",
    )


def attend_back(query, branch, wo, kv_all, out_t, lse, fc, proj, base, result):
    def kernel(
        q_ref, b_ref, w_ref, kv_ref, ot_ref, lse_ref, f_ref, p_ref, base_ref, res_ref,
        dq_ref, dkv_ref, fo_ref, po_ref, out_ref,
        qt, gt, qm, gm, delta, dqt, out_buf, keep, got, far, f_far, p_far, r_far,
        f_sum, p_sum, f_all, p_all,
        cs, cr, ys, yr, fs, fr, ps, pr, rs, rr, s4, r4, s6, r6,
    ):
        y, z, k, x = coords()
        sib = device(y, z, 1 - k, x)
        steps = (1, 2, 3)
        me = y * 4 + z
        everyone = greet(
            [sib]
            + [device(y, z, k, ring(x, d)) for d in steps]
            + [
                device(ring(y, a), ring(z, b), k, x)
                for a in range(4)
                for b in range(4)
                if (a, b) != (0, 0)
            ]
        )
        query_blk = q_ref[...]
        q_t = query_blk.T
        for head in range(3):
            qt[head] = head_rows(q_t, head)
            qm[head] = head_cols(query_blk, head)
        dqt[...] = jnp.zeros_like(dqt)
        nt = (((1,), (1,)), ((), ()))
        own_heads = pl.ds(pl.multiple_of(192 * z, 64), 192)
        grad_blk = lax.dot_general(
            b_ref[:, :384], w_ref[0, own_heads], nt, preferred_element_type=F32
        )
        grad_blk += lax.dot_general(
            b_ref[:, 384:], w_ref[1, own_heads], nt, preferred_element_type=F32
        )
        grad_blk = grad_blk.astype(BF)
        g_t = grad_blk.T
        for head in range(3):
            at = slice(64 * head, 64 * head + 64)
            gt[head] = head_rows(g_t, head)
            gm[head] = head_cols(grad_blk, head)
            delta[head : head + 1] = jnp.sum(g_t[at].astype(F32) * ot_ref[at], 0, keepdims=True)

        everyone()
        results = []
        for d in steps:
            b = ring(z, d)
            c = remote(
                res_ref.at[b], r_far.at[d - 1], rs.at[d - 1], rr.at[d - 1], device(y, b, k, x)
            )
            c.start()
            results.append(c)
        weights = []
        for d in steps:
            b = ring(x, d)
            to = device(y, z, k, b)
            weights.append(
                remote(f_ref.at[:, b], f_far.at[d - 1], fs.at[d - 1], fr.at[d - 1], to)
            )
            weights.append(
                remote(p_ref.at[:, b], p_far.at[d - 1], ps.at[d - 1], pr.at[d - 1], to)
            )
        for c in weights:
            c.start()
        def block(by, bk, masked, to_ref, to):
            keys = kv_ref[by, bk, :, :192]
            values = kv_ref[by, bk, :, 192:]
            keys_t = keys.T
            if masked:
                key_at = place(lax.broadcasted_iota(jnp.int32, (512, 512), 0)) + 128 * bk
                query_at = place(lax.broadcasted_iota(jnp.int32, (512, 512), 1)) + 128 * k
                visible = query_at >= key_at
            dk = dv = None
            for head in range(3):
                s = dot(keys, qt[head])
                p = jnp.exp(s - lse_ref[head : head + 1])
                if masked:
                    p = jnp.where(visible, p, 0.0)
                dp = dot(values, gt[head])
                ds = (p * (dp - delta[head : head + 1])).astype(BF)
                pv = dot(p.astype(BF), gm[head])
                pk = dot(ds, qm[head])
                dv = pv if dv is None else dv + pv
                dk = pk if dk is None else dk + pk
                at = slice(64 * head, 64 * head + 64)
                dqt[at] += dot(keys_t[at], ds)
            to_ref[to, :, :192] = dk.astype(BF)
            to_ref[to, :, 192:] = dv.astype(BF)

        def cross(d):
            return remote(out_buf.at[d], got.at[d], cs.at[d], cr.at[d], sib)

        def up(d):
            return remote(keep.at[d], far.at[d], ys.at[d], yr.at[d], device(y - d, z, k, x))

        def earlier(i, carry):
            d = y - i
            block(y - d, 1 - k, False, out_buf, d)
            cross(d).start()
            block(y - d, k, False, keep, d)
            cross(d).wait_recv()
            keep[d] = (keep[d].astype(F32) + got[d].astype(F32)).astype(BF)
            up(d).start()
            return carry

        lax.fori_loop(0, y, earlier, 0)
        block(y, 1 - k, True, out_buf, 0)
        cross(0).start()

        for c in weights:
            c.wait()
        f_sum[...] = (
            f_ref[:, x].astype(F32)
            + f_far[0].astype(F32)
            + f_far[1].astype(F32)
            + f_far[2].astype(F32)
        ).astype(BF)
        p_sum[...] = (
            p_ref[:, x].astype(F32)
            + p_far[0].astype(F32)
            + p_far[1].astype(F32)
            + p_far[2].astype(F32)
        ).astype(BF)

        def f_copy(a):
            return remote(
                f_sum.at[a], f_all.at[me], s4.at[a], r4.at[me], device(a, x, k, x)
            )

        def p_copy(j):
            return remote(
                p_sum.at[j], p_all.at[y], s6.at[j], r6.at[y], device(z, 2 * k + j, k, x)
            )

        f_here = [(a == y) & (z == x) for a in range(4)]
        p_here = [(y == z) & (z == 2 * k + j) for j in range(2)]
        for a in range(4):

            @pl.when(jnp.logical_not(f_here[a]))
            def _():
                f_copy(a).start()

            @pl.when(f_here[a])
            def _():
                f_all[me] = f_sum[a]

        for j in range(2):

            @pl.when(jnp.logical_not(p_here[j]))
            def _():
                p_copy(j).start()

            @pl.when(p_here[j])
            def _():
                p_all[y] = p_sum[j]

        block(y, k, True, keep, 0)
        dq_ref[...] = (dqt[...].T * 0.125).astype(BF)
        cross(0).wait_recv()
        for c in results:
            c.wait()
        out_ref[...] = (
            base_ref[...]
            + res_ref[z].astype(F32)
            + r_far[0].astype(F32)
            + r_far[1].astype(F32)
            + r_far[2].astype(F32)
        )
        dkv_ref[...] = keep[0].astype(F32) + got[0].astype(F32)
        for d in (1, 2, 3):

            @pl.when(y + d < 4)
            def _():
                remote(keep.at[d], far.at[d], ys.at[d], yr.at[d], sib).wait_recv()
                dkv_ref[...] += far[d].astype(F32)

        @pl.when(z == x)
        def _():
            def arrive(i, carry):
                @pl.when(i != me)
                def _():
                    remote(f_sum.at[0], f_all.at[i], s4.at[0], r4.at[i], sib).wait_recv()

                return carry

            lax.fori_loop(0, 16, arrive, 0)
            for b in range(4):
                fo_ref[:, 384 * b : 384 * b + 384] = (
                    f_all[b].astype(F32)
                    + f_all[4 + b].astype(F32)
                    + f_all[8 + b].astype(F32)
                    + f_all[12 + b].astype(F32)
                )

        for a in range(4):

            @pl.when((k == z // 2) & jnp.logical_not((a == y) & (z == y)))
            def _():
                remote(p_sum.at[0], p_all.at[a], s6.at[0], r6.at[a], sib).wait_recv()

        @pl.when(k == z // 2)
        def _():
            po_ref[...] = (
                p_all[0].astype(F32)
                + p_all[1].astype(F32)
                + p_all[2].astype(F32)
                + p_all[3].astype(F32)
            )

        for a in range(4):

            @pl.when(jnp.logical_not(f_here[a]))
            def _():
                f_copy(a).wait_send()

        for j in range(2):

            @pl.when(jnp.logical_not(p_here[j]))
            def _():
                p_copy(j).wait_send()

        cross(0).wait_send()
        for d in (1, 2, 3):

            @pl.when(y >= d)
            def _():
                cross(d).wait_send()
                up(d).wait_send()

    return comm(
        kernel,
        [
            jax.ShapeDtypeStruct((512, 192), BF),
            jax.ShapeDtypeStruct((512, 384), F32),
            jax.ShapeDtypeStruct((48, 1536), F32),
            jax.ShapeDtypeStruct((48, 768), F32),
            jax.ShapeDtypeStruct((128, 768), F32),
        ],
        5,
        (4, 4, 4, 4, 3, 3, 3, 3, 3, 3, 4, 16, 2, 4),
        (query, branch, wo, kv_all, out_t, lse, fc, proj, base, result),
        scratch=[
            pltpu.VMEM((3, 192, 512), BF),
            pltpu.VMEM((3, 192, 512), BF),
            pltpu.VMEM((3, 512, 192), BF),
            pltpu.VMEM((3, 512, 192), BF),
            pltpu.VMEM((8, 512), F32),
            pltpu.VMEM((192, 512), F32),
            pltpu.VMEM((4, 512, 384), BF),
            pltpu.VMEM((4, 512, 384), BF),
            pltpu.VMEM((4, 512, 384), BF),
            pltpu.VMEM((4, 512, 384), BF),
            pltpu.VMEM((3, 4, 48, 384), BF),
            pltpu.VMEM((3, 2, 48, 768), BF),
            pltpu.VMEM((3, 128, 768), BF),
            pltpu.VMEM((4, 48, 384), BF),
            pltpu.VMEM((2, 48, 768), BF),
            pltpu.VMEM((16, 48, 384), BF),
            pltpu.VMEM((4, 48, 768), BF),
        ],
        spaces=([VMEM] * 10, [VMEM] * 5),
        name="attend_back",
    )


def normalize(rows):
    centered = rows - jnp.mean(rows, -1, keepdims=True)
    inverse = lax.rsqrt(jnp.mean(centered * centered, -1, keepdims=True) + EPSILON)
    return centered * inverse, inverse


def normalize_back(normed, inverse, gain, grad):
    scaled = grad * gain
    return inverse * (
        scaled
        - jnp.mean(scaled, -1, keepdims=True)
        - normed * jnp.mean(scaled * normed, -1, keepdims=True)
    )


def feed_forward(heads_all, x_group, dy_group, wo, wf, wp, vec_rows):
    def kernel(
        h_ref, x_ref, dy_ref, wo_ref, wf_ref, wp_ref, v_ref,
        base_ref, res_mine, gx_ref, bo_ref, gwf_ref, gwp_ref, gfb_ref, gv_ref,
        a2, act, df, x_two, normed, inverse, norm_other, norm_mine, res_other,
        norm_got, res_got, norm_far, branch,
        cs, cr, es, er, zs, zr, bs, br,
    ):
        y, z, k, x = coords()
        sib = device(y, z, 1 - k, x)
        steps = (1, 2, 3)
        everyone = greet([sib] + [device(y, ring(z, d), k, x) for d in steps])
        out_bias, gain, shift, proj_bias = (v_ref[i : i + 1] for i in range(4, 8))
        fc_bias = jnp.zeros((1, 384), F32)
        for b in range(4):
            row = v_ref[8 + b : 9 + b, pl.ds(pl.multiple_of(384 * k, 128), 384)]
            fc_bias = fc_bias + jnp.where(z == b, row, 0.0)

        def half(kk, norm_ref):
            two = x_ref[kk].reshape(512, 768).astype(F32) + out_bias
            for g in range(4):
                h = h_ref[g, kk]
                at = slice(192 * g, 192 * g + 192)
                part = jnp.concatenate([dot(h, wo_ref[0, at]), dot(h, wo_ref[1, at])], 1)
                two = two + part
            x_two[...] = two
            n, inv = normalize(two)
            normed[...] = n
            inverse[...] = jnp.broadcast_to(inv, (512, 128))
            a = (n * gain + shift).astype(BF)
            a2[kk] = a
            hidden = dot(a, wf_ref[...]) + fc_bias
            square = hidden * hidden
            t = jnp.tanh(0.7978845608028654 * (hidden + 0.044715 * square * hidden))
            act_blk = (0.5 * hidden * (1.0 + t)).astype(BF)
            act[kk] = act_blk
            slope = 0.5 * (1.0 + t) + 0.5 * hidden * (1.0 - t * t) * (
                0.7978845608028654 * (1.0 + 3 * 0.044715 * square)
            )
            dy = dy_ref[kk].reshape(512, 768)
            back = lax.dot_general(
                dy, wp_ref[...], (((1,), (1,)), ((), ())), preferred_element_type=F32
            )
            df_blk = (back * slope).astype(BF)
            df[kk] = df_blk
            norm_part = lax.dot_general(
                df_blk, wf_ref[...], (((1,), (1,)), ((), ())), preferred_element_type=F32
            )
            norm_ref[...] = norm_part.astype(BF).reshape(4, 128, 768)

        def result(kk, res_ref):
            res_ref[...] = dot(act[kk], wp_ref[...]).astype(BF).reshape(4, 128, 768)

        half(1 - k, norm_other)
        everyone()
        swaps = []
        for d in (1, 2, 3, 0):
            b = ring(z, d)
            c = remote(norm_other.at[b], norm_got.at[b], cs.at[d], cr.at[d], sib)
            c.start()
            swaps.append(c)
        half(k, norm_mine)
        sends = []
        for d in steps:
            b = ring(z, d)
            swaps[d - 1].wait_recv()
            norm_mine[b] = (norm_mine[b].astype(F32) + norm_got[b].astype(F32)).astype(BF)
            c = remote(
                norm_mine.at[b], norm_far.at[d - 1], zs.at[d - 1], zr.at[d - 1],
                device(y, b, k, x),
            )
            c.start()
            sends.append(c)
        result(1 - k, res_other)
        for d in (1, 2, 3, 0):
            b = ring(z, d)
            c = remote(res_other.at[b], res_got.at[b], es.at[d], er.at[d], sib)
            c.start()
            swaps.append(c)
        tn = (((0,), (0,)), ((), ()))
        gwf = lax.dot_general(a2[0], df[0], tn, preferred_element_type=F32)
        gwf += lax.dot_general(a2[1], df[1], tn, preferred_element_type=F32)
        gwf_ref[...] = gwf.astype(BF)
        own_rows = pl.ds(pl.multiple_of(128 * z, 128), 128)
        swaps[3].wait_recv()
        for c in sends:
            c.wait_recv()
        da = (
            norm_mine[z].astype(F32)
            + norm_got[z].astype(F32)
            + norm_far[0].astype(F32)
            + norm_far[1].astype(F32)
            + norm_far[2].astype(F32)
        )
        n = normed[own_rows]
        dy = dy_ref[k, z].astype(F32)
        gx = dy + normalize_back(n, inverse[own_rows, 0:1], gain, da)
        gx_ref[...] = gx
        low = gx.astype(BF)
        branch[...] = low
        bo_ref[z] = low
        branches = []
        for d in steps:
            c = remote(
                branch, bo_ref.at[z], bs.at[d - 1], br.at[d - 1], device(y, ring(z, d), k, x)
            )
            c.start()
            branches.append(c)
        result(k, res_mine)
        gwp = lax.dot_general(
            act[0], dy_ref[0].reshape(512, 768), tn, preferred_element_type=F32
        )
        gwp += lax.dot_general(
            act[1], dy_ref[1].reshape(512, 768), tn, preferred_element_type=F32
        )
        gwp_ref[...] = gwp.astype(BF)
        gfb_ref[...] = jnp.sum(df[0].astype(F32), 0, keepdims=True) + jnp.sum(
            df[1].astype(F32), 0, keepdims=True
        )
        gv_ref[0:1] = jnp.sum(low.astype(F32), 0, keepdims=True)
        gv_ref[1:2] = jnp.sum(da * n, 0, keepdims=True)
        gv_ref[2:3] = jnp.sum(da, 0, keepdims=True)
        gv_ref[3:4] = jnp.sum(dy, 0, keepdims=True)
        for c in swaps[4:]:
            c.wait_recv()
        res_mine[...] = (res_mine[...].astype(F32) + res_got[...].astype(F32)).astype(BF)
        base_ref[...] = x_two[own_rows] + proj_bias
        for c in branches:
            c.wait()
        for c in swaps + sends:
            c.wait_send()

    return comm(
        kernel,
        [
            jax.ShapeDtypeStruct((128, 768), F32),
            jax.ShapeDtypeStruct((4, 128, 768), BF),
            jax.ShapeDtypeStruct((128, 768), F32),
            jax.ShapeDtypeStruct((4, 128, 768), BF),
            jax.ShapeDtypeStruct((768, 384), BF),
            jax.ShapeDtypeStruct((384, 768), BF),
            jax.ShapeDtypeStruct((1, 384), F32),
            jax.ShapeDtypeStruct((4, 768), F32),
        ],
        3,
        (4, 4, 4, 4, 3, 3, 3, 3),
        (heads_all, x_group, dy_group, wo, wf, wp, vec_rows),
        scratch=[
            pltpu.VMEM((2, 512, 768), BF),
            pltpu.VMEM((2, 512, 384), BF),
            pltpu.VMEM((2, 512, 384), BF),
            pltpu.VMEM((512, 768), F32),
            pltpu.VMEM((512, 768), F32),
            pltpu.VMEM((512, 128), F32),
        ]
        + [pltpu.VMEM((4, 128, 768), BF)] * 5
        + [pltpu.VMEM((3, 128, 768), BF)]
        + [pltpu.VMEM((128, 768), BF)],
        spaces=([VMEM] * 7, [VMEM] * 8),
        name="feed_forward",
    )


def adam_update(weight, moment_one, moment_two, gradient, rate, decay):
    new_one = BETA_ONE * moment_one + (1.0 - BETA_ONE) * gradient
    new_two = BETA_TWO * moment_two + (1.0 - BETA_TWO) * gradient * gradient
    fix_one = 1.0 - BETA_ONE**STEP
    fix_two = 1.0 - BETA_TWO**STEP
    direction = new_one / fix_one / (jnp.sqrt(new_two / fix_two) + ADAM_EPSILON)
    return (weight - rate * (direction + decay * weight), new_one, new_two)


def shards(
    tokens,
    cotangent,
    w_qkv,
    qkv_m,
    qkv_v,
    w_out,
    out_m,
    out_v,
    w_fc,
    fc_m,
    fc_v,
    w_proj,
    proj_m,
    proj_v,
    vectors,
    vec_m,
    vec_v,
):
    state = (
        w_qkv, qkv_m, qkv_v, w_out, out_m, out_v, w_fc, fc_m, fc_v, w_proj, proj_m, proj_v,
        vectors, vec_m, vec_v,
    )
    (
        heads_all, out_t, lse, kv_all, dy_group, wf, wo, wp, query, act_one, normed_core,
        wq, x_group, vec_rows,
    ) = forward(w_qkv, w_fc, w_out, w_proj, vectors, tokens[0], cotangent[0])
    wq = wq.reshape(768, 640)
    wo = wo.reshape(2, 768, 384)
    base, result, grad_x_two, branch_core, grad_w_fc, grad_w_proj, grad_fc_bias, vec_sums = feed_forward(
        heads_all,
        x_group,
        dy_group,
        wo,
        wf.reshape(768, 384),
        wp.reshape(384, 768),
        vec_rows,
    )
    branch_core = branch_core.reshape(512, 768)
    grad_query, grad_kv, fc_sum, proj_sum, result_sum = attend_back(
        query,
        branch_core,
        wo,
        kv_all,
        out_t,
        lse,
        grad_w_fc.reshape(4, 4, 48, 384),
        grad_w_proj.reshape(2, 4, 48, 768),
        base,
        result,
    )
    grad_one, last_rows, proj_rows, fc_rows = last_sums(
        (
            act_one,
            normed_core,
            heads_all,
            grad_query,
            grad_kv,
            branch_core,
            wq,
            vec_sums,
            grad_fc_bias,
        ),
        fc_sum,
        proj_sum,
    )
    output, grad_inputs, *new_state = finish(
        grad_one, grad_x_two, tokens[0], vec_rows, last_rows, proj_rows, fc_rows, result_sum, state
    )
    return (output[None], grad_inputs[None], *new_state)


def solution(mesh):
    split = P("fsdp", "ctx", None)
    rows = P(("ctx", "fsdp"), None)
    return jax.shard_map(
        shards,
        mesh=mesh,
        in_specs=(split, split) + (rows,) * 15,
        out_specs=(split, split) + (rows,) * 15,
        check_vma=False,
    )
```

```python
import jax
import jax.numpy as jnp
from jax import lax
from jax.experimental import pallas as pl
from jax.experimental.pallas import tpu as pltpu
from jax.sharding import PartitionSpec as P

STEP = 10
EPSILON = 1e-05
BETA_ONE = 0.9
BETA_TWO = 0.999
ADAM_EPSILON = 1e-08
MESH = pl.DeviceIdType.MESH
BF = jnp.bfloat16
F32 = jnp.float32
ANY = pl.BlockSpec(memory_space=pl.ANY)
VMEM = pl.BlockSpec(memory_space=pltpu.VMEM)
LIMIT = 56 * 1024 * 1024


def coords():
    c = lax.axis_index("ctx")
    return c // 8, (c // 2) % 4, c % 2, lax.axis_index("fsdp")


def device(y, z, k, x):
    return ((y * 4 + z) * 2 + k, x)


def ring(v, step):
    return lax.rem(v + step, 4)


def greet(devices):
    barrier = pltpu.get_barrier_semaphore()
    for one in devices:
        pl.semaphore_signal(barrier, inc=1, device_id=one, device_id_type=MESH)
    return lambda: pl.semaphore_wait(barrier, len(devices))


def remote(src, dst, send, recv, to):
    return pltpu.make_async_remote_copy(
        src, dst, send, recv, device_id=to, device_id_type=MESH
    )


def comm(kernel, outs, cid, sems, args, scratch=(), spaces=None, name=None):
    return pl.pallas_call(
        kernel,
        out_shape=outs,
        in_specs=[ANY] * len(args) if spaces is None else spaces[0],
        out_specs=[ANY] * len(outs) if spaces is None else spaces[1],
        scratch_shapes=list(scratch) + [pltpu.SemaphoreType.DMA((n,)) for n in sems],
        compiler_params=pltpu.CompilerParams(
            collective_id=cid, has_side_effects=True, vmem_limit_bytes=LIMIT
        ),
        name=name,
    )(*args)


def last_sums(pieces, fc, proj):
    wide = 1664

    def kernel(*refs):
        (
            act_ref, n_ref, h_ref, gq_ref, gkv_ref, br_ref, wq_ref, vs_ref, fb_ref,
            fc_ref, proj_ref,
        ) = refs[:11]
        one_out, rows_out, proj_out, fc_out = refs[11:15]
        (
            one_far, mix_got, mix_sum, mix_all, vec_all, proj_sum, out_send, fc_send,
            one_ref, mix_other, mix_ref, vec_ref,
            act_t, heads, heads_t, d_ref, right_one, right_two, vec_rows,
        ) = refs[15:34]
        (
        zs, zr, cs, cr, s3, r3, s4, r4, s5, r5, s7, r7, s8, r8, loc,
        ) = refs[34:]
        y, z, k, x = coords()
        me = y * 4 + z
        sib = device(y, z, 1 - k, x)
        steps = (1, 2, 3)
        everyone = greet(
            [sib]
            + [device(y, z, j, ring(x, d)) for d in steps for j in (k, 1 - k)]
            + [
                device(ring(y, a), ring(z, b), k, x)
                for a in range(4)
                for b in range(4)
                if (a, b) != (0, 0)
            ]
        )
        d_ref[:, 0:192] = gq_ref[...]
        d_ref[:, 192:576] = gkv_ref[...].astype(BF)
        d_ref[:, 576:640] = jnp.zeros((512, 64), BF)
        right_one[...] = jnp.zeros_like(right_one)
        right_one[:, 0:288] = d_ref[:, 0:288]
        right_one[:, 384:672] = d_ref[:, 288:576]
        right_two[...] = jnp.zeros_like(right_two)
        vec_rows[...] = jnp.zeros_like(vec_rows)
        sums = jnp.sum(d_ref[...].astype(F32), 0, keepdims=True)
        at_half = pl.ds(pl.multiple_of(384 * k, 128), 384)
        for b in range(4):
            heads[:, 192 * b : 192 * b + 192] = h_ref[b, k]

            @pl.when(z == b)
            def _():
                right_two[:, 288:384] = br_ref[:, 192 * b : 192 * b + 96]
                right_two[:, 672:768] = br_ref[:, 192 * b + 96 : 192 * b + 192]
                vec_rows[2:3, 192 * b : 192 * b + 192] = sums[:, 0:192]
                vec_rows[3:4, 192 * b : 192 * b + 192] = sums[:, 384:576]
                vec_rows[8 + b : 9 + b, at_half] = fb_ref[...]

        vec_rows[4:8] = vs_ref[...]
        act_t[...] = act_ref[...].T
        heads_t[...] = heads[...].T

        def product(h):
            at = pl.ds(pl.multiple_of(384 * h, 128), 384)
            total = dot(act_t[...], right_one[:, at]) + dot(heads_t[...], right_two[:, at])
            return total.reshape(4, 4, 48, 384)

        mix_other[...] = product(1 - k).astype(BF)
        everyone()
        swap = []
        for d in (1, 2, 3, 0):
            b = ring(y, d)
            c = remote(mix_other.at[b], mix_got.at[b], cs.at[d], cr.at[d], sib)
            c.start()
            swap.append(c)
        def proj_last(i):
            return remote(
                proj_sum.at[i], proj_out, s8.at[i], r8.at[0],
                device(y, z, x // 2, lax.rem(2 * x + i, 4)),
            )

        def proj_here(i):
            return (k == x // 2) & (x == lax.rem(2 * x + i, 4))

        holder = k == z // 2

        @pl.when(holder)
        def _():
            for i in range(2):
                proj_sum[i] = proj_ref[24 * i : 24 * i + 24]

                @pl.when(jnp.logical_not(proj_here(i)))
                def _():
                    proj_last(i).start()

                @pl.when(proj_here(i))
                def _():
                    proj_out[...] = proj_sum[i]

        def last_here(i):
            return k * 4 + x == i

        def fc_last(i):
            return remote(
                fc_send.at[i], fc_out.at[k], s4.at[i], r4.at[k], device(y, z, i // 4, i % 4)
            )

        @pl.when(z == x)
        def _():
            for i in range(8):
                fc_send[i, 0:6] = fc_ref[6 * i : 6 * i + 6]
                fc_send[i, 6:8] = jnp.zeros((2, 1536), F32)

                @pl.when(jnp.logical_not(last_here(i)))
                def _():
                    fc_last(i).start()

                @pl.when(last_here(i))
                def _():
                    fc_out[k] = fc_send[i]

        mix_ref[...] = product(k).astype(BF)
        one = lax.dot_general(
            d_ref[...], wq_ref[...], (((1,), (1,)), ((), ())), preferred_element_type=F32
        )
        one_ref[...] = one.astype(BF).reshape(4, 128, 768)
        vec_rows[0:1] = jnp.sum(one * n_ref[...].astype(F32), 0, keepdims=True)
        vec_rows[1:2] = jnp.sum(one, 0, keepdims=True)
        vec_ref[...] = vec_rows[...].T.astype(BF).reshape(4, 4, 48, 128)
        ones = []
        for d in steps:
            c = remote(
                one_ref.at[ring(z, d)], one_far.at[d - 1], zs.at[d - 1], zr.at[d - 1],
                device(y, ring(z, d), k, x),
            )
            c.start()
            ones.append(c)

        def plane(src, dst, send, recv, m):
            ty, tz = ring(y, m // 4), ring(z, m % 4)
            return remote(
                src.at[ty, tz], dst.at[me], send.at[m], recv.at[m], device(ty, tz, k, x)
            )

        def vec_copy(m):
            return plane(vec_ref, vec_all, s5, r5, m)

        def mix_copy(m):
            return plane(mix_sum, mix_all, s3, r3, m)

        def each(copy, what, first, last):
            def step(m, carry):
                what(copy(m))
                return carry

            lax.fori_loop(first, last, step, 0)

        start = lambda c: c.start()
        finish_all = lambda c: c.wait()
        each(vec_copy, start, 1, 16)
        vec_all[me] = vec_ref[y, z]
        for d in (1, 2, 3, 0):
            b = ring(y, d)
            swap[d - 1].wait_recv()
            mix_sum[b] = (mix_ref[b].astype(F32) + mix_got[b].astype(F32)).astype(BF)
            each(mix_copy, start, max(4 * d, 1), 4 * d + 4)
        mix_all[me] = mix_sum[y, z]
        for c in ones:
            c.wait_recv()
        one_out[...] = (
            one_ref[z].astype(F32)
            + one_far[0].astype(F32)
            + one_far[1].astype(F32)
            + one_far[2].astype(F32)
        )

        def last_copy(i):
            return remote(
                out_send.at[i], rows_out.at[k * 4 + x], s7.at[i], r7.at[k * 4 + x],
                device(y, z, i // 4, i % 4),
            )

        each(vec_copy, finish_all, 1, 16)
        each(mix_copy, finish_all, 1, 16)

        def four(ref, b):
            return (
                ref[b].astype(F32)
                + ref[4 + b].astype(F32)
                + ref[8 + b].astype(F32)
                + ref[12 + b].astype(F32)
            )

        for b in range(4):
            m = four(mix_all, b)
            for i in range(8):
                out_send[i, 0:6, 384 * b : 384 * b + 384] = m[6 * i : 6 * i + 6]
        v = four(vec_all, 0) + four(vec_all, 1) + four(vec_all, 2) + four(vec_all, 3)
        for i in range(8):
            out_send[i, 0:6, 1536:1664] = v[6 * i : 6 * i + 6]
            out_send[i, 6:8, :] = jnp.zeros((2, wide), F32)
        for i in range(8):

            @pl.when(jnp.logical_not(last_here(i)))
            def _():
                last_copy(i).start()

            @pl.when(last_here(i))
            def _():
                rows_out[i] = out_send[i]

        for j in range(2):

            @pl.when(jnp.logical_not((z == x) & (k == j)))
            def _():
                remote(fc_send.at[0], fc_out.at[j], s4.at[0], r4.at[j], sib).wait_recv()

        for i in range(8):

            @pl.when(jnp.logical_not(last_here(i)))
            def _():
                remote(out_send.at[0], rows_out.at[i], s7.at[0], r7.at[i], sib).wait_recv()
                last_copy(i).wait_send()

        @pl.when(jnp.logical_not((k == z // 2) & (x == (4 * k + x) // 2)))
        def _():
            remote(proj_sum.at[0], proj_out, s8.at[0], r8.at[0], sib).wait_recv()

        @pl.when(z == x)
        def _():
            for i in range(8):

                @pl.when(jnp.logical_not(last_here(i)))
                def _():
                    fc_last(i).wait_send()

        for i in range(2):

            @pl.when(holder & jnp.logical_not(proj_here(i)))
            def _():
                proj_last(i).wait_send()

        for c in swap + ones:
            c.wait_send()

    return comm(
        kernel,
        [
            jax.ShapeDtypeStruct((128, 768), F32),
            jax.ShapeDtypeStruct((8, 8, wide), F32),
            jax.ShapeDtypeStruct((24, 768), F32),
            jax.ShapeDtypeStruct((2, 8, 1536), F32),
        ],
        6,
        (3, 3, 4, 4, 16, 16, 8, 2, 16, 16, 8, 8, 2, 1, 4),
        (*pieces, fc, proj),
        scratch=[
            pltpu.VMEM((3, 128, 768), BF),
            pltpu.VMEM((4, 4, 48, 384), BF),
            pltpu.VMEM((4, 4, 48, 384), BF),
            pltpu.VMEM((16, 48, 384), BF),
            pltpu.VMEM((16, 48, 128), BF),
            pltpu.VMEM((2, 24, 768), F32),
            pltpu.VMEM((8, 8, wide), F32),
            pltpu.VMEM((8, 8, 1536), F32),
            pltpu.VMEM((4, 128, 768), BF),
            pltpu.VMEM((4, 4, 48, 384), BF),
            pltpu.VMEM((4, 4, 48, 384), BF),
            pltpu.VMEM((4, 4, 48, 128), BF),
            pltpu.VMEM((768, 512), BF),
            pltpu.VMEM((512, 768), BF),
            pltpu.VMEM((768, 512), BF),
            pltpu.VMEM((512, 640), BF),
            pltpu.VMEM((512, 768), BF),
            pltpu.VMEM((512, 768), BF),
            pltpu.VMEM((128, 768), F32),
        ],
        spaces=([VMEM] * 11, [VMEM] * 4),
        name="last_sums",
    )


def finish(grad_one, grad_x_two, tokens, vec_rows, rows, proj_rows, fc_rows, result, state):
    def kernel(*refs):
        one_ref, gx_ref, t_ref, v_ref, rows_ref, p_ref, f_ref, res_ref = refs[:8]
        state_ref = refs[8:23]
        out_ref, gin_ref = refs[23:25]
        new_ref = refs[25:40]
        g_qkv, g_out, g_fc = refs[40:]
        out_ref[...] = res_ref[...]
        normed, inverse = normalize(t_ref[...].astype(F32))
        gin_ref[...] = gx_ref[...] + normalize_back(normed, inverse, v_ref[0:1], one_ref[...])
        for b in range(4):
            at_z = slice(384 * b, 384 * b + 384)
            one_half = jnp.sum(rows_ref[0:4, 0:6, at_z], 0)
            two_half = jnp.sum(rows_ref[4:8, 0:6, at_z], 0)
            q = 192 * b
            g_qkv[:, q : q + 192] = one_half[:, 0:192]
            g_qkv[:, 768 + q : 864 + q] = one_half[:, 192:288]
            g_qkv[:, 864 + q : 960 + q] = two_half[:, 0:96]
            g_qkv[:, 1536 + q : 1728 + q] = two_half[:, 96:288]
            g_out[:, q : q + 96] = one_half[:, 288:384]
            g_out[:, q + 96 : q + 192] = two_half[:, 288:384]
            for j in range(2):
                at = 384 * (2 * b + j)
                g_fc[:, at : at + 384] = f_ref[j, 0:6, 384 * b : 384 * b + 384]
        g_vec = jnp.sum(rows_ref[:, 0:6, 1536:1548], 0)
        for i, (gradient, rate, decay) in enumerate(
            (
                (g_qkv[...], 0.1, 0.1),
                (g_out[...], 0.3, 0.1),
                (g_fc[...], 0.05, 0.1),
                (p_ref[...], 0.03, 0.1),
                (g_vec, 0.5, 0.0),
            )
        ):
            w, m, v = state_ref[3 * i : 3 * i + 3]
            results = adam_update(w[...], m[...], v[...], gradient, rate, decay)
            for j in range(3):
                new_ref[3 * i + j][...] = results[j]

    return pl.pallas_call(
        kernel,
        out_shape=[jax.ShapeDtypeStruct((128, 768), F32)] * 2
        + [jax.ShapeDtypeStruct(one.shape, F32) for one in state],
        in_specs=[VMEM] * 23,
        out_specs=[VMEM] * 17,
        scratch_shapes=[
            pltpu.VMEM((6, 2304), F32),
            pltpu.VMEM((6, 768), F32),
            pltpu.VMEM((6, 3072), F32),
        ],
        compiler_params=pltpu.CompilerParams(vmem_limit_bytes=LIMIT),
        name="finish",
    )(grad_one, grad_x_two, tokens, vec_rows, rows, proj_rows, fc_rows, result, *state)


def head_rows(matrix, head):
    row = lax.broadcasted_iota(jnp.int32, matrix.shape, 0)
    keep = (row >= 64 * head) & (row < 64 * head + 64)
    return jnp.where(keep, matrix, jnp.zeros_like(matrix))


def head_cols(matrix, head):
    col = lax.broadcasted_iota(jnp.int32, matrix.shape, 1)
    keep = (col >= 64 * head) & (col < 64 * head + 64)
    return jnp.where(keep, matrix, jnp.zeros_like(matrix))


def place(index):
    return (index // 128) * 256 + index % 128


def dot(a, b):
    return jnp.dot(a, b, preferred_element_type=F32)


def forward(w_qkv, w_fc, w_out, w_proj, vectors, tokens, cotangent):
    wide_q, wide_r = 1280, 3456

    def kernel(
        wq_ref, wf_ref, wo_ref, wp_ref, wv_ref, t_ref, r_ref,
        ho_ref, ot_ref, lse_ref, vo_ref, ro_ref, fo_ref, oo_ref, po_ref, q_ref, a_ref, n_ref,
        q_out, x_ref, vec_ref,
        wide_one, wide_two, packed_q, packed_r, got_q, got_r,
        fc48, qkv48, out48, proj_wide, q_send, f_send, o_send, p_send, f_mid, o_mid, p_mid,
        bias, qt, m_ref, l_ref, h_buf, v_ref,
        mq_s, mq_r, fq_s, fq_r, mr_s, mr_r, fr_s, fr_r, s1, r1, s2, r2, ps, pr,
        xs_s, xs_r, xf_s, xf_r, ts, tr, us, ur,
        vs, vr, rs, rr, cs, cr, ds, dr, ws, wr, wf, os, orr, hs, hr, gs, gr, loc,
    ):
        y, z, k, x = coords()
        me = y * 4 + z
        t = k * 4 + x
        sib = device(y, z, 1 - k, x)
        steps = (1, 2, 3)
        everyone = greet(
            [sib]
            + [device(y, z, k, ring(x, d)) for d in steps]
            + [
                device(ring(y, a), ring(z, b), k, x)
                for a in range(4)
                for b in range(4)
                if (a, b) != (0, 0)
            ]
        )

        def first(packed, got, send, recv):
            copies = [
                remote(packed, got.at[t], send.at[d], recv.at[d], device(y, z, k, ring(x, d)))
                for d in steps
            ]
            for c in copies:
                c.start()
            return copies

        def crossing(packed, got, copies, send, recv):
            out = [remote(packed, got.at[t], send.at[0], recv.at[0], sib)]
            out[0].start()
            for d in steps:
                copies[d - 1].wait_recv()
                src = k * 4 + ring(x, 4 - d)
                c = remote(got.at[src], got.at[src], send.at[d], recv.at[d], sib)
                c.start()
                out.append(c)
            return out

        wide_one[...] = jnp.zeros_like(wide_one)
        wide_one[0:6, 0:1152] = wq_ref[:, 0:1152]
        wide_one[6:12, 0:1152] = wq_ref[:, 1152:2304]
        wide_one[0:6, 1152:1164] = wv_ref[...]
        packed_q[...] = wide_one[...].astype(BF)
        got_q[t] = packed_q[...]
        everyone()
        message_q = first(packed_q, got_q, mq_s, mq_r)
        token_copies = []
        for d in steps:
            c = remote(
                t_ref, x_ref.at[k, z], ts.at[d], tr.at[d], device(y, ring(z, d), k, x)
            )
            c.start()
            token_copies.append(c)
        token_cross = [remote(t_ref, x_ref.at[k, z], us.at[0], ur.at[0], sib)]
        token_cross[0].start()
        x_ref[k, z] = t_ref[...]
        wide_two[...] = jnp.zeros_like(wide_two)
        wide_two[0:6, 0:1920] = wf_ref[:, 0:1920]
        wide_two[6:12, 0:1152] = wf_ref[:, 1920:3072]
        wide_two[6:12, 1152:1920] = wo_ref[...]
        wide_two[0:12, 1920:2688] = wp_ref[0:12]
        wide_two[0:12, 2688:3456] = wp_ref[12:24]
        packed_r[...] = wide_two[...].astype(BF)
        got_r[t] = packed_r[...]
        cross_q = crossing(packed_q, got_q, message_q, fq_s, fq_r)
        message_r = first(packed_r, got_r, mr_s, mr_r)
        for c in cross_q:
            c.wait_recv()
        for i in range(8):
            piece = got_q[i].astype(F32)
            at = slice(6 * i, 6 * i + 6)
            qkv48[at, 0:1152] = piece[0:6, 0:1152]
            qkv48[at, 1152:2304] = piece[6:12, 0:1152]
            qkv48[at, 2304:2432] = piece[0:6, 1152:1280]
        for j in range(4):
            q_send[j, :, 0:192] = qkv48[:, 192 * j : 192 * j + 192].astype(BF)
            q_send[j, :, 192:384] = qkv48[:, 768 + 192 * j : 960 + 192 * j].astype(BF)
            q_send[j, :, 384:576] = qkv48[:, 1536 + 192 * j : 1728 + 192 * j].astype(BF)
            q_send[j, :, 576:640] = qkv48[:, 2304:2368].astype(BF)

        group = pl.ds(pl.multiple_of(16 * jnp.minimum(x, 2), 16), 16)

        def to_of(m):
            return ring(y, m // 4), ring(z, m % 4)

        def q_copy(m):
            ty, tz = to_of(m)
            return remote(
                q_send.at[tz, group], q_out.at[me, group], s1.at[m], r1.at[m],
                device(ty, tz, k, x),
            )

        def f_copy(m):
            ty, tz = to_of(m)
            return remote(
                f_send.at[tz * 2 + k], f_mid.at[me], s2.at[m], r2.at[m], device(ty, tz, k, x)
            )

        def o_copy(m):
            ty, tz = to_of(m)
            return remote(o_send.at[k], o_mid.at[me], s2.at[m], r2.at[m], device(ty, tz, k, x))

        def p_copy(a):
            return remote(
                p_send, p_mid.at[z % 2], ps.at[a], pr.at[z % 2], device(ring(y, a), y, k, x)
            )

        def each(copy, what):
            def step(m, carry):
                what(copy(m))
                return carry

            lax.fori_loop(1, 16, step, 0)

        start = lambda c: c.start()
        finish = lambda c: c.wait()

        @pl.when(x < 3)
        def _():
            each(q_copy, start)
            q_out[me, group] = q_send[z, group]

        half = pl.ds(8 * k, 8)
        other_half = pl.ds(8 * (1 - k), 8)

        def rows_of(plane):
            return pl.ds(pl.multiple_of(16 * plane, 16), 16)

        def x_copy(d):
            return remote(
                q_out.at[half, group], q_out.at[half, group], xs_s.at[d], xs_r.at[x],
                device(y, z, k, ring(x, d)),
            )

        @pl.when(x < 3)
        def _():
            each(q_copy, finish)
            for d in steps:
                x_copy(d).start()

        cross_r = crossing(packed_r, got_r, message_r, fr_s, fr_r)
        for c in cross_r:
            c.wait_recv()
        for i in range(8):
            piece = got_r[i].astype(F32)
            at = slice(6 * i, 6 * i + 6)
            fc48[at, 0:1920] = piece[0:6, 0:1920]
            fc48[at, 1920:3072] = piece[6:12, 0:1152]
            out48[at] = piece[6:12, 1152:1920]
            proj_wide[24 * i : 24 * i + 12] = piece[0:12, 1920:2688]
            proj_wide[24 * i + 12 : 24 * i + 24] = piece[0:12, 2688:3456]
        for j in range(8):
            f_send[j] = fc48[:, 384 * j : 384 * j + 384].astype(BF)
        o_send[0] = out48[:, 0:384].astype(BF)
        o_send[1] = out48[:, 384:768].astype(BF)
        p_send[...] = proj_wide[...].astype(BF)

        @pl.when(x == 1)
        def _():
            each(f_copy, start)
            f_mid[me] = f_send[z * 2 + k]

        @pl.when(x == 2)
        def _():
            each(o_copy, start)
            o_mid[me] = o_send[k]

        @pl.when((x == 3) & (k == z // 2))
        def _():
            for a in range(1, 4):
                p_copy(a).start()

            @pl.when(z != y)
            def _():
                p_copy(0).start()

            @pl.when(z == y)
            def _():
                p_mid[z % 2] = p_send[...]

        def pass_q(a):
            return remote(
                q_out.at[half, rows_of(a)], q_out.at[half, rows_of(a)], xf_s.at[a], xf_r.at[a], sib
            )

        for a in range(3):

            @pl.when(x != a)
            def _():
                remote(
                    q_out.at[half, rows_of(a)], q_out.at[half, rows_of(a)], xs_s.at[0],
                    xs_r.at[a], sib,
                ).wait_recv()
                pass_q(a).start()

        for d in steps:
            token_copies[d - 1].wait_recv()
            src = ring(z, 4 - d)
            c = remote(x_ref.at[k, src], x_ref.at[k, src], us.at[d], ur.at[d], sib)
            c.start()
            token_cross.append(c)
        normed, _ = normalize(x_ref[k].reshape(512, 768).astype(F32))
        n_ref[...] = normed.astype(BF)

        weights = ((1, f_mid, fo_ref, 8), (2, o_mid, oo_ref, 8), (3, p_mid, po_ref, 1))

        def ends(a, half):
            _, src, dst, n = weights[a - 1]
            at = pl.ds(n * half, n)
            return src.at[at], (dst.at[k, at] if a == 2 else dst.at[at])

        def direct(a, half, d):
            src, dst = ends(a, half)
            return remote(
                src, dst, ws.at[4 * half + d], wr.at[2 * a + half], device(y, z, k, ring(x, d))
            )

        def onward(a, half, d):
            _, dst = ends(a, half)
            return remote(
                dst, dst, wf.at[a], wr.at[2 * a + half], device(y, z, k, ring(x, d))
            )

        def weight_own(a):
            _, src, dst, _ = weights[a - 1]
            return pltpu.make_async_copy(src, dst.at[k] if a == 2 else dst, loc.at[1])

        @pl.when(x == 1)
        def _():
            each(f_copy, finish)

        @pl.when(x == 2)
        def _():
            each(o_copy, finish)

        for i in range(2):
            @pl.when((x == 3) & jnp.logical_not((y == z) & (z == 2 * k + i)))
            def _():
                remote(p_send, p_mid.at[i], ps.at[0], pr.at[i], sib).wait_recv()

        for a in steps:

            @pl.when(x == a)
            def _():
                for half_at, d in ((0, 1), (1, 3), (1, 1), (0, 3)):
                    direct(a, half_at, d).start()
                weight_own(a).start()

        def move_on():
            for a in steps:

                @pl.when(x == (a + 1) % 4)
                def _():
                    direct(a, 0, 1).wait_recv()
                    onward(a, 0, 1).start()

                @pl.when(x == (a + 3) % 4)
                def _():
                    direct(a, 1, 1).wait_recv()
                    onward(a, 1, 3).start()

        for a in range(3):

            @pl.when(x != a)
            def _():
                remote(
                    q_out.at[other_half, rows_of(a)], q_out.at[other_half, rows_of(a)],
                    xf_s.at[a], xf_r.at[a], sib,
                ).wait_recv()

        vec_ref[...] = q_out[:, :, 512:640].reshape(768, 128).astype(F32).T[64:80]
        bias[...] = jnp.zeros_like(bias)
        for b in range(4):

            @pl.when(z == b)
            def _():
                bias[:, 0:192] = vec_ref[2:3, 192 * b : 192 * b + 192]
                bias[:, 384:576] = vec_ref[3:4, 192 * b : 192 * b + 192]

        act = (normed * vec_ref[0:1] + vec_ref[1:2]).astype(BF)
        a_ref[...] = act
        mixed = dot(act, q_out[...].reshape(768, 640)) + bias[...]
        v_ref[...] = mixed[:, 192:576].astype(BF)

        def kv_copy(d):
            return remote(
                v_ref, vo_ref.at[y, k], vs.at[d], vr.at[d], device(ring(y, d), z, k, x)
            )

        for d in steps:

            @pl.when(y + d < 4)
            def _():
                kv_copy(d).start()

        swap = remote(v_ref, vo_ref.at[y, k], cs.at[0], cr.at[0], sib)
        swap.start()
        vo_ref[y, k] = v_ref[...]
        own_r = pltpu.make_async_copy(r_ref, ro_ref.at[k, z], loc.at[0])
        own_r.start()
        row_copies = []
        for d in steps:
            c = remote(
                r_ref, ro_ref.at[k, z], rs.at[d], rr.at[d], device(y, ring(z, d), k, x)
            )
            c.start()
            row_copies.append(c)
        row_first = remote(r_ref, ro_ref.at[k, z], ds.at[0], dr.at[0], sib)
        row_first.start()
        query = mixed[:, :192].astype(BF) * jnp.asarray(0.125, BF)
        q_ref[...] = query
        q_t = query.T
        for head in range(3):
            qt[head] = head_rows(q_t, head)
        m_ref[...] = jnp.full_like(m_ref, -1e30)
        l_ref[...] = jnp.zeros_like(l_ref)
        ot_ref[...] = jnp.zeros_like(ot_ref)

        def block(by, bk, masked):
            keys = vo_ref[by, bk, :, :192]
            values_t = vo_ref[by, bk, :, 192:].T
            if masked:
                key_at = place(lax.broadcasted_iota(jnp.int32, (512, 512), 0)) + 128 * bk
                query_at = place(lax.broadcasted_iota(jnp.int32, (512, 512), 1)) + 128 * k
                visible = query_at >= key_at
            for head in range(3):
                s = dot(keys, qt[head])
                if masked:
                    s = jnp.where(visible, s, -1e9)
                old = m_ref[head : head + 1]
                new = jnp.maximum(old, jnp.max(s, 0, keepdims=True))
                e = jnp.exp(s - new)
                scale = jnp.exp(old - new)
                m_ref[head : head + 1] = new
                l_ref[head : head + 1] = l_ref[head : head + 1] * scale + jnp.sum(
                    e, 0, keepdims=True
                )
                at = slice(64 * head, 64 * head + 64)
                ot_ref[at] = ot_ref[at] * scale + dot(values_t[at], e.astype(BF))

        def diagonal(j, carry):
            @pl.when(j == 1)
            def _():
                remote(v_ref, vo_ref.at[y, 1 - k], cs.at[0], cr.at[0], sib).wait_recv()

            block(y, lax.rem(k + j, 2), True)

            return carry

        lax.fori_loop(0, 2, diagonal, 0)

        def pass_on(d):
            return remote(
                vo_ref.at[y - d, k], vo_ref.at[y - d, k], cs.at[d], cr.at[d], sib
            )

        def earlier(i, carry):
            d, j = i // 2 + 1, i % 2

            @pl.when(j == 0)
            def _():
                remote(v_ref, vo_ref.at[y - d, k], vs.at[d], vr.at[d], sib).wait_recv()
                pass_on(d).start()

            @pl.when(j == 1)
            def _():
                remote(v_ref, vo_ref.at[y - d, 1 - k], cs.at[d], cr.at[d], sib).wait_recv()

            block(y - d, lax.rem(k + j, 2), False)

            @pl.when(i == jnp.minimum(2, 2 * y - 1))
            def _():
                move_on()

            return carry

        @pl.when(y == 0)
        def _():
            move_on()

        lax.fori_loop(0, 2 * y, earlier, 0)
        for head in range(3):
            at = slice(64 * head, 64 * head + 64)
            total = l_ref[head : head + 1]
            ot_ref[at] = ot_ref[at] / total
            lse_ref[head : head + 1] = m_ref[head : head + 1] + jnp.log(total)
        h_buf[...] = ot_ref[...].T.astype(BF)
        heads_copies = []
        for d in steps:
            c = remote(
                h_buf, ho_ref.at[z, k], hs.at[d], hr.at[d], device(y, ring(z, d), k, x)
            )
            c.start()
            heads_copies.append(c)
        c = remote(h_buf, ho_ref.at[z, k], gs.at[0], gr.at[0], sib)
        c.start()
        forward_copies = [c, row_first]
        own_h = pltpu.make_async_copy(h_buf, ho_ref.at[z, k], loc.at[2])
        own_h.start()
        for d in steps:
            row_copies[d - 1].wait_recv()
            src = ring(z, 4 - d)
            c = remote(ro_ref.at[k, src], ro_ref.at[k, src], ds.at[d], dr.at[d], sib)
            c.start()
            forward_copies.append(c)
        for a in steps:

            @pl.when(x == a)
            def _():
                weight_own(a).wait()

            @pl.when(x == (a + 1) % 4)
            def _():
                direct(a, 1, 1).wait_recv()

            @pl.when(x == (a + 3) % 4)
            def _():
                direct(a, 0, 1).wait_recv()

            @pl.when(x == (a + 2) % 4)
            def _():
                direct(a, 0, 1).wait_recv()
                direct(a, 1, 1).wait_recv()

        c = remote(oo_ref.at[k], oo_ref.at[k], os.at[0], orr.at[0], sib)
        c.start()
        forward_copies.append(c)
        for d in steps:
            heads_copies[d - 1].wait_recv()
            src = ring(z, 4 - d)
            c = remote(ho_ref.at[src, k], ho_ref.at[src, k], gs.at[d], gr.at[d], sib)
            c.start()
            forward_copies.append(c)
        for c in forward_copies + token_cross:
            c.wait()
        for c in row_copies + heads_copies + token_copies + [swap]:
            c.wait_send()
        for c in message_q + cross_q + message_r + cross_r:
            c.wait_send()
        for d in steps:

            @pl.when(y + d < 4)
            def _():
                kv_copy(d).wait_send()

            @pl.when(y >= d)
            def _():
                pass_on(d).wait_send()

        for a in steps:

            @pl.when(x == a)
            def _():
                for half_at, d in ((0, 1), (1, 3), (1, 1), (0, 3)):
                    direct(a, half_at, d).wait_send()

            @pl.when(x == (a + 1) % 4)
            def _():
                onward(a, 0, 1).wait_send()

            @pl.when(x == (a + 3) % 4)
            def _():
                onward(a, 1, 3).wait_send()

        @pl.when((x == 3) & (k == z // 2))
        def _():
            for a in range(1, 4):
                p_copy(a).wait_send()

            @pl.when(z != y)
            def _():
                p_copy(0).wait_send()

        @pl.when(x < 3)
        def _():
            for d in steps:
                x_copy(d).wait_send()

        for a in range(3):

            @pl.when(x != a)
            def _():
                pass_q(a).wait_send()

        own_r.wait()
        own_h.wait()

    return comm(
        kernel,
        [
            jax.ShapeDtypeStruct((4, 2, 512, 192), BF),
            jax.ShapeDtypeStruct((192, 512), F32),
            jax.ShapeDtypeStruct((8, 512), F32),
            jax.ShapeDtypeStruct((4, 2, 512, 384), BF),
            jax.ShapeDtypeStruct((2, 4, 128, 768), BF),
            jax.ShapeDtypeStruct((16, 48, 384), BF),
            jax.ShapeDtypeStruct((2, 16, 48, 384), BF),
            jax.ShapeDtypeStruct((2, 192, 768), BF),
            jax.ShapeDtypeStruct((512, 192), BF),
            jax.ShapeDtypeStruct((512, 768), BF),
            jax.ShapeDtypeStruct((512, 768), BF),
            jax.ShapeDtypeStruct((16, 48, 640), BF),
            jax.ShapeDtypeStruct((2, 4, 128, 768), BF),
            jax.ShapeDtypeStruct((16, 768), F32),
        ],
        0,
        (4,) * 8 + (16,) * 4 + (4, 2) + (4,) * 8
        + (4, 4, 4, 4, 4, 4, 4, 4, 8, 8, 4, 1, 1, 4, 4, 4, 4, 3),
        (w_qkv, w_fc, w_out, w_proj, vectors, tokens, cotangent),
        scratch=[
            pltpu.VMEM((16, wide_q), F32),
            pltpu.VMEM((16, wide_r), F32),
            pltpu.VMEM((16, wide_q), BF),
            pltpu.VMEM((16, wide_r), BF),
            pltpu.VMEM((8, 16, wide_q), BF),
            pltpu.VMEM((8, 16, wide_r), BF),
            pltpu.VMEM((48, 3072), F32),
            pltpu.VMEM((48, 2432), F32),
            pltpu.VMEM((48, 768), F32),
            pltpu.VMEM((192, 768), F32),
            pltpu.VMEM((4, 48, 640), BF),
            pltpu.VMEM((8, 48, 384), BF),
            pltpu.VMEM((2, 48, 384), BF),
            pltpu.VMEM((192, 768), BF),
            pltpu.VMEM((16, 48, 384), BF),
            pltpu.VMEM((16, 48, 384), BF),
            pltpu.VMEM((2, 192, 768), BF),
            pltpu.VMEM((1, 640), F32),
            pltpu.VMEM((3, 192, 512), BF),
            pltpu.VMEM((8, 512), F32),
            pltpu.VMEM((8, 512), F32),
            pltpu.VMEM((512, 192), BF),
            pltpu.VMEM((512, 384), BF),
        ],
        spaces=(
            [VMEM] * 6 + [ANY],
            [ANY, VMEM, VMEM, VMEM, ANY, ANY, ANY, ANY] + [VMEM] * 6,
        ),
        name="forward",
    )


def attend_back(query, branch, wo, kv_all, out_t, lse, fc, proj, base, result):
    def kernel(
        q_ref, b_ref, w_ref, kv_ref, ot_ref, lse_ref, f_ref, p_ref, base_ref, res_ref,
        dq_ref, dkv_ref, fo_ref, po_ref, out_ref,
        qt, gt, qm, gm, delta, dqt, out_buf, keep, got, far, f_far, p_far, r_far,
        f_sum, p_sum, f_all, p_all,
        cs, cr, ys, yr, fs, fr, ps, pr, rs, rr, s4, r4, s6, r6,
    ):
        y, z, k, x = coords()
        sib = device(y, z, 1 - k, x)
        steps = (1, 2, 3)
        me = y * 4 + z
        everyone = greet(
            [sib]
            + [device(y, z, k, ring(x, d)) for d in steps]
            + [
                device(ring(y, a), ring(z, b), k, x)
                for a in range(4)
                for b in range(4)
                if (a, b) != (0, 0)
            ]
        )
        query_blk = q_ref[...]
        q_t = query_blk.T
        for head in range(3):
            qt[head] = head_rows(q_t, head)
            qm[head] = head_cols(query_blk, head)
        dqt[...] = jnp.zeros_like(dqt)
        nt = (((1,), (1,)), ((), ()))
        own_heads = pl.ds(pl.multiple_of(192 * z, 64), 192)
        grad_blk = lax.dot_general(
            b_ref[:, :384], w_ref[0, own_heads], nt, preferred_element_type=F32
        )
        grad_blk += lax.dot_general(
            b_ref[:, 384:], w_ref[1, own_heads], nt, preferred_element_type=F32
        )
        grad_blk = grad_blk.astype(BF)
        g_t = grad_blk.T
        for head in range(3):
            at = slice(64 * head, 64 * head + 64)
            gt[head] = head_rows(g_t, head)
            gm[head] = head_cols(grad_blk, head)
            delta[head : head + 1] = jnp.sum(g_t[at].astype(F32) * ot_ref[at], 0, keepdims=True)

        everyone()
        results = []
        for d in steps:
            b = ring(z, d)
            c = remote(
                res_ref.at[b], r_far.at[d - 1], rs.at[d - 1], rr.at[d - 1], device(y, b, k, x)
            )
            c.start()
            results.append(c)
        weights = []
        for d in steps:
            b = ring(x, d)
            to = device(y, z, k, b)
            weights.append(
                remote(f_ref.at[:, b], f_far.at[d - 1], fs.at[d - 1], fr.at[d - 1], to)
            )
            weights.append(
                remote(p_ref.at[:, b], p_far.at[d - 1], ps.at[d - 1], pr.at[d - 1], to)
            )
        for c in weights:
            c.start()
        def block(by, bk, masked, to_ref, to):
            keys = kv_ref[by, bk, :, :192]
            values = kv_ref[by, bk, :, 192:]
            keys_t = keys.T
            if masked:
                key_at = place(lax.broadcasted_iota(jnp.int32, (512, 512), 0)) + 128 * bk
                query_at = place(lax.broadcasted_iota(jnp.int32, (512, 512), 1)) + 128 * k
                visible = query_at >= key_at
            dk = dv = None
            for head in range(3):
                s = dot(keys, qt[head])
                p = jnp.exp(s - lse_ref[head : head + 1])
                if masked:
                    p = jnp.where(visible, p, 0.0)
                dp = dot(values, gt[head])
                ds = (p * (dp - delta[head : head + 1])).astype(BF)
                pv = dot(p.astype(BF), gm[head])
                pk = dot(ds, qm[head])
                dv = pv if dv is None else dv + pv
                dk = pk if dk is None else dk + pk
                at = slice(64 * head, 64 * head + 64)
                dqt[at] += dot(keys_t[at], ds)
            to_ref[to, :, :192] = dk.astype(BF)
            to_ref[to, :, 192:] = dv.astype(BF)

        def cross(d):
            return remote(out_buf.at[d], got.at[d], cs.at[d], cr.at[d], sib)

        def up(d):
            return remote(keep.at[d], far.at[d], ys.at[d], yr.at[d], device(y - d, z, k, x))

        def earlier(i, carry):
            d = y - i
            block(y - d, 1 - k, False, out_buf, d)
            cross(d).start()
            block(y - d, k, False, keep, d)
            cross(d).wait_recv()
            keep[d] = (keep[d].astype(F32) + got[d].astype(F32)).astype(BF)
            up(d).start()
            return carry

        lax.fori_loop(0, y, earlier, 0)
        block(y, 1 - k, True, out_buf, 0)
        cross(0).start()

        for c in weights:
            c.wait()
        f_sum[...] = (
            f_ref[:, x].astype(F32)
            + f_far[0].astype(F32)
            + f_far[1].astype(F32)
            + f_far[2].astype(F32)
        ).astype(BF)
        p_sum[...] = (
            p_ref[:, x].astype(F32)
            + p_far[0].astype(F32)
            + p_far[1].astype(F32)
            + p_far[2].astype(F32)
        ).astype(BF)

        def f_copy(a):
            return remote(
                f_sum.at[a], f_all.at[me], s4.at[a], r4.at[me], device(a, x, k, x)
            )

        def p_copy(j):
            return remote(
                p_sum.at[j], p_all.at[y], s6.at[j], r6.at[y], device(z, 2 * k + j, k, x)
            )

        f_here = [(a == y) & (z == x) for a in range(4)]
        p_here = [(y == z) & (z == 2 * k + j) for j in range(2)]
        for a in range(4):

            @pl.when(jnp.logical_not(f_here[a]))
            def _():
                f_copy(a).start()

            @pl.when(f_here[a])
            def _():
                f_all[me] = f_sum[a]

        for j in range(2):

            @pl.when(jnp.logical_not(p_here[j]))
            def _():
                p_copy(j).start()

            @pl.when(p_here[j])
            def _():
                p_all[y] = p_sum[j]

        block(y, k, True, keep, 0)
        dq_ref[...] = (dqt[...].T * 0.125).astype(BF)
        cross(0).wait_recv()
        for c in results:
            c.wait()
        out_ref[...] = (
            base_ref[...]
            + res_ref[z].astype(F32)
            + r_far[0].astype(F32)
            + r_far[1].astype(F32)
            + r_far[2].astype(F32)
        )
        dkv_ref[...] = keep[0].astype(F32) + got[0].astype(F32)
        for d in (1, 2, 3):

            @pl.when(y + d < 4)
            def _():
                remote(keep.at[d], far.at[d], ys.at[d], yr.at[d], sib).wait_recv()
                dkv_ref[...] += far[d].astype(F32)

        @pl.when(z == x)
        def _():
            def arrive(i, carry):
                @pl.when(i != me)
                def _():
                    remote(f_sum.at[0], f_all.at[i], s4.at[0], r4.at[i], sib).wait_recv()

                return carry

            lax.fori_loop(0, 16, arrive, 0)
            for b in range(4):
                fo_ref[:, 384 * b : 384 * b + 384] = (
                    f_all[b].astype(F32)
                    + f_all[4 + b].astype(F32)
                    + f_all[8 + b].astype(F32)
                    + f_all[12 + b].astype(F32)
                )

        for a in range(4):

            @pl.when((k == z // 2) & jnp.logical_not((a == y) & (z == y)))
            def _():
                remote(p_sum.at[0], p_all.at[a], s6.at[0], r6.at[a], sib).wait_recv()

        @pl.when(k == z // 2)
        def _():
            po_ref[...] = (
                p_all[0].astype(F32)
                + p_all[1].astype(F32)
                + p_all[2].astype(F32)
                + p_all[3].astype(F32)
            )

        for a in range(4):

            @pl.when(jnp.logical_not(f_here[a]))
            def _():
                f_copy(a).wait_send()

        for j in range(2):

            @pl.when(jnp.logical_not(p_here[j]))
            def _():
                p_copy(j).wait_send()

        cross(0).wait_send()
        for d in (1, 2, 3):

            @pl.when(y >= d)
            def _():
                cross(d).wait_send()
                up(d).wait_send()

    return comm(
        kernel,
        [
            jax.ShapeDtypeStruct((512, 192), BF),
            jax.ShapeDtypeStruct((512, 384), F32),
            jax.ShapeDtypeStruct((48, 1536), F32),
            jax.ShapeDtypeStruct((48, 768), F32),
            jax.ShapeDtypeStruct((128, 768), F32),
        ],
        5,
        (4, 4, 4, 4, 3, 3, 3, 3, 3, 3, 4, 16, 2, 4),
        (query, branch, wo, kv_all, out_t, lse, fc, proj, base, result),
        scratch=[
            pltpu.VMEM((3, 192, 512), BF),
            pltpu.VMEM((3, 192, 512), BF),
            pltpu.VMEM((3, 512, 192), BF),
            pltpu.VMEM((3, 512, 192), BF),
            pltpu.VMEM((8, 512), F32),
            pltpu.VMEM((192, 512), F32),
            pltpu.VMEM((4, 512, 384), BF),
            pltpu.VMEM((4, 512, 384), BF),
            pltpu.VMEM((4, 512, 384), BF),
            pltpu.VMEM((4, 512, 384), BF),
            pltpu.VMEM((3, 4, 48, 384), BF),
            pltpu.VMEM((3, 2, 48, 768), BF),
            pltpu.VMEM((3, 128, 768), BF),
            pltpu.VMEM((4, 48, 384), BF),
            pltpu.VMEM((2, 48, 768), BF),
            pltpu.VMEM((16, 48, 384), BF),
            pltpu.VMEM((4, 48, 768), BF),
        ],
        spaces=([VMEM] * 10, [VMEM] * 5),
        name="attend_back",
    )


def normalize(rows):
    centered = rows - jnp.mean(rows, -1, keepdims=True)
    inverse = lax.rsqrt(jnp.mean(centered * centered, -1, keepdims=True) + EPSILON)
    return centered * inverse, inverse


def normalize_back(normed, inverse, gain, grad):
    scaled = grad * gain
    return inverse * (
        scaled
        - jnp.mean(scaled, -1, keepdims=True)
        - normed * jnp.mean(scaled * normed, -1, keepdims=True)
    )


def feed_forward(heads_all, x_group, dy_group, wo, wf, wp, vec_rows):
    def kernel(
        h_ref, x_ref, dy_ref, wo_ref, wf_ref, wp_ref, v_ref,
        base_ref, res_mine, gx_ref, bo_ref, gwf_ref, gwp_ref, gfb_ref, gv_ref,
        a2, act, df, x_two, normed, inverse, norm_other, norm_mine, res_other,
        norm_got, res_got, norm_far, branch,
        cs, cr, es, er, zs, zr, bs, br,
    ):
        y, z, k, x = coords()
        sib = device(y, z, 1 - k, x)
        steps = (1, 2, 3)
        everyone = greet([sib] + [device(y, ring(z, d), k, x) for d in steps])
        out_bias, gain, shift, proj_bias = (v_ref[i : i + 1] for i in range(4, 8))
        fc_bias = jnp.zeros((1, 384), F32)
        for b in range(4):
            row = v_ref[8 + b : 9 + b, pl.ds(pl.multiple_of(384 * k, 128), 384)]
            fc_bias = fc_bias + jnp.where(z == b, row, 0.0)

        def half(kk, norm_ref):
            two = x_ref[kk].reshape(512, 768).astype(F32) + out_bias
            for g in range(4):
                h = h_ref[g, kk]
                at = slice(192 * g, 192 * g + 192)
                part = jnp.concatenate([dot(h, wo_ref[0, at]), dot(h, wo_ref[1, at])], 1)
                two = two + part
            x_two[...] = two
            n, inv = normalize(two)
            normed[...] = n
            inverse[...] = jnp.broadcast_to(inv, (512, 128))
            a = (n * gain + shift).astype(BF)
            a2[kk] = a
            hidden = dot(a, wf_ref[...]) + fc_bias
            square = hidden * hidden
            t = jnp.tanh(0.7978845608028654 * (hidden + 0.044715 * square * hidden))
            act_blk = (0.5 * hidden * (1.0 + t)).astype(BF)
            act[kk] = act_blk
            slope = 0.5 * (1.0 + t) + 0.5 * hidden * (1.0 - t * t) * (
                0.7978845608028654 * (1.0 + 3 * 0.044715 * square)
            )
            dy = dy_ref[kk].reshape(512, 768)
            back = lax.dot_general(
                dy, wp_ref[...], (((1,), (1,)), ((), ())), preferred_element_type=F32
            )
            df_blk = (back * slope).astype(BF)
            df[kk] = df_blk
            norm_part = lax.dot_general(
                df_blk, wf_ref[...], (((1,), (1,)), ((), ())), preferred_element_type=F32
            )
            norm_ref[...] = norm_part.astype(BF).reshape(4, 128, 768)

        def result(kk, res_ref):
            res_ref[...] = dot(act[kk], wp_ref[...]).astype(BF).reshape(4, 128, 768)

        half(1 - k, norm_other)
        everyone()
        swaps = []
        for d in (1, 2, 3, 0):
            b = ring(z, d)
            c = remote(norm_other.at[b], norm_got.at[b], cs.at[d], cr.at[d], sib)
            c.start()
            swaps.append(c)
        half(k, norm_mine)
        sends = []
        for d in steps:
            b = ring(z, d)
            swaps[d - 1].wait_recv()
            norm_mine[b] = (norm_mine[b].astype(F32) + norm_got[b].astype(F32)).astype(BF)
            c = remote(
                norm_mine.at[b], norm_far.at[d - 1], zs.at[d - 1], zr.at[d - 1],
                device(y, b, k, x),
            )
            c.start()
            sends.append(c)
        result(1 - k, res_other)
        for d in (1, 2, 3, 0):
            b = ring(z, d)
            c = remote(res_other.at[b], res_got.at[b], es.at[d], er.at[d], sib)
            c.start()
            swaps.append(c)
        tn = (((0,), (0,)), ((), ()))
        gwf = lax.dot_general(a2[0], df[0], tn, preferred_element_type=F32)
        gwf += lax.dot_general(a2[1], df[1], tn, preferred_element_type=F32)
        gwf_ref[...] = gwf.astype(BF)
        own_rows = pl.ds(pl.multiple_of(128 * z, 128), 128)
        swaps[3].wait_recv()
        for c in sends:
            c.wait_recv()
        da = (
            norm_mine[z].astype(F32)
            + norm_got[z].astype(F32)
            + norm_far[0].astype(F32)
            + norm_far[1].astype(F32)
            + norm_far[2].astype(F32)
        )
        n = normed[own_rows]
        dy = dy_ref[k, z].astype(F32)
        gx = dy + normalize_back(n, inverse[own_rows, 0:1], gain, da)
        gx_ref[...] = gx
        low = gx.astype(BF)
        branch[...] = low
        bo_ref[z] = low
        branches = []
        for d in steps:
            c = remote(
                branch, bo_ref.at[z], bs.at[d - 1], br.at[d - 1], device(y, ring(z, d), k, x)
            )
            c.start()
            branches.append(c)
        result(k, res_mine)
        gwp = lax.dot_general(
            act[0], dy_ref[0].reshape(512, 768), tn, preferred_element_type=F32
        )
        gwp += lax.dot_general(
            act[1], dy_ref[1].reshape(512, 768), tn, preferred_element_type=F32
        )
        gwp_ref[...] = gwp.astype(BF)
        gfb_ref[...] = jnp.sum(df[0].astype(F32), 0, keepdims=True) + jnp.sum(
            df[1].astype(F32), 0, keepdims=True
        )
        gv_ref[0:1] = jnp.sum(low.astype(F32), 0, keepdims=True)
        gv_ref[1:2] = jnp.sum(da * n, 0, keepdims=True)
        gv_ref[2:3] = jnp.sum(da, 0, keepdims=True)
        gv_ref[3:4] = jnp.sum(dy, 0, keepdims=True)
        for c in swaps[4:]:
            c.wait_recv()
        res_mine[...] = (res_mine[...].astype(F32) + res_got[...].astype(F32)).astype(BF)
        base_ref[...] = x_two[own_rows] + proj_bias
        for c in branches:
            c.wait()
        for c in swaps + sends:
            c.wait_send()

    return comm(
        kernel,
        [
            jax.ShapeDtypeStruct((128, 768), F32),
            jax.ShapeDtypeStruct((4, 128, 768), BF),
            jax.ShapeDtypeStruct((128, 768), F32),
            jax.ShapeDtypeStruct((4, 128, 768), BF),
            jax.ShapeDtypeStruct((768, 384), BF),
            jax.ShapeDtypeStruct((384, 768), BF),
            jax.ShapeDtypeStruct((1, 384), F32),
            jax.ShapeDtypeStruct((4, 768), F32),
        ],
        3,
        (4, 4, 4, 4, 3, 3, 3, 3),
        (heads_all, x_group, dy_group, wo, wf, wp, vec_rows),
        scratch=[
            pltpu.VMEM((2, 512, 768), BF),
            pltpu.VMEM((2, 512, 384), BF),
            pltpu.VMEM((2, 512, 384), BF),
            pltpu.VMEM((512, 768), F32),
            pltpu.VMEM((512, 768), F32),
            pltpu.VMEM((512, 128), F32),
        ]
        + [pltpu.VMEM((4, 128, 768), BF)] * 5
        + [pltpu.VMEM((3, 128, 768), BF)]
        + [pltpu.VMEM((128, 768), BF)],
        spaces=([VMEM] * 7, [VMEM] * 8),
        name="feed_forward",
    )


def adam_update(weight, moment_one, moment_two, gradient, rate, decay):
    new_one = BETA_ONE * moment_one + (1.0 - BETA_ONE) * gradient
    new_two = BETA_TWO * moment_two + (1.0 - BETA_TWO) * gradient * gradient
    fix_one = 1.0 - BETA_ONE**STEP
    fix_two = 1.0 - BETA_TWO**STEP
    direction = new_one / fix_one / (jnp.sqrt(new_two / fix_two) + ADAM_EPSILON)
    return (weight - rate * (direction + decay * weight), new_one, new_two)


def shards(
    tokens,
    cotangent,
    w_qkv,
    qkv_m,
    qkv_v,
    w_out,
    out_m,
    out_v,
    w_fc,
    fc_m,
    fc_v,
    w_proj,
    proj_m,
    proj_v,
    vectors,
    vec_m,
    vec_v,
):
    state = (
        w_qkv, qkv_m, qkv_v, w_out, out_m, out_v, w_fc, fc_m, fc_v, w_proj, proj_m, proj_v,
        vectors, vec_m, vec_v,
    )
    (
        heads_all, out_t, lse, kv_all, dy_group, wf, wo, wp, query, act_one, normed_core,
        wq, x_group, vec_rows,
    ) = forward(w_qkv, w_fc, w_out, w_proj, vectors, tokens[0], cotangent[0])
    wq = wq.reshape(768, 640)
    wo = wo.reshape(2, 768, 384)
    base, result, grad_x_two, branch_core, grad_w_fc, grad_w_proj, grad_fc_bias, vec_sums = feed_forward(
        heads_all,
        x_group,
        dy_group,
        wo,
        wf.reshape(768, 384),
        wp.reshape(384, 768),
        vec_rows,
    )
    branch_core = branch_core.reshape(512, 768)
    grad_query, grad_kv, fc_sum, proj_sum, result_sum = attend_back(
        query,
        branch_core,
        wo,
        kv_all,
        out_t,
        lse,
        grad_w_fc.reshape(4, 4, 48, 384),
        grad_w_proj.reshape(2, 4, 48, 768),
        base,
        result,
    )
    grad_one, last_rows, proj_rows, fc_rows = last_sums(
        (
            act_one,
            normed_core,
            heads_all,
            grad_query,
            grad_kv,
            branch_core,
            wq,
            vec_sums,
            grad_fc_bias,
        ),
        fc_sum,
        proj_sum,
    )
    output, grad_inputs, *new_state = finish(
        grad_one, grad_x_two, tokens[0], vec_rows, last_rows, proj_rows, fc_rows, result_sum, state
    )
    return (output[None], grad_inputs[None], *new_state)


def solution(mesh):
    split = P("fsdp", "ctx", None)
    rows = P(("ctx", "fsdp"), None)
    return jax.shard_map(
        shards,
        mesh=mesh,
        in_specs=(split, split) + (rows,) * 15,
        out_specs=(split, split) + (rows,) * 15,
        check_vma=False,
    )
```

```python
import jax
import jax.numpy as jnp
from jax import lax
from jax.experimental import pallas as pl
from jax.experimental.pallas import tpu as pltpu
from jax.sharding import PartitionSpec as P

STEP = 10
EPSILON = 1e-05
BETA_ONE = 0.9
BETA_TWO = 0.999
ADAM_EPSILON = 1e-08
MESH = pl.DeviceIdType.MESH
BF = jnp.bfloat16
F32 = jnp.float32
ANY = pl.BlockSpec(memory_space=pl.ANY)
VMEM = pl.BlockSpec(memory_space=pltpu.VMEM)
LIMIT = 56 * 1024 * 1024


def coords():
    c = lax.axis_index("ctx")
    return c // 8, (c // 2) % 4, c % 2, lax.axis_index("fsdp")


def device(y, z, k, x):
    return ((y * 4 + z) * 2 + k, x)


def ring(v, step):
    return lax.rem(v + step, 4)


def greet(devices):
    barrier = pltpu.get_barrier_semaphore()
    for one in devices:
        pl.semaphore_signal(barrier, inc=1, device_id=one, device_id_type=MESH)
    return lambda: pl.semaphore_wait(barrier, len(devices))


def remote(src, dst, send, recv, to):
    return pltpu.make_async_remote_copy(
        src, dst, send, recv, device_id=to, device_id_type=MESH
    )


def comm(kernel, outs, cid, sems, args, scratch=(), spaces=None, name=None):
    return pl.pallas_call(
        kernel,
        out_shape=outs,
        in_specs=[ANY] * len(args) if spaces is None else spaces[0],
        out_specs=[ANY] * len(outs) if spaces is None else spaces[1],
        scratch_shapes=list(scratch) + [pltpu.SemaphoreType.DMA((n,)) for n in sems],
        compiler_params=pltpu.CompilerParams(
            collective_id=cid, has_side_effects=True, vmem_limit_bytes=LIMIT
        ),
        name=name,
    )(*args)


def last_sums(pieces, fc, proj):
    wide = 1664

    def kernel(*refs):
        (
            act_ref, n_ref, h_ref, gq_ref, gkv_ref, br_ref, wq_ref, vs_ref, fb_ref,
            fc_ref, proj_ref,
        ) = refs[:11]
        one_out, rows_out, proj_out, fc_out = refs[11:15]
        (
            one_far, mix_got, mix_sum, mix_all, vec_all, proj_sum, out_send, fc_send,
            one_ref, mix_other, mix_ref, vec_ref,
            act_t, heads, heads_t, d_ref, right_one, right_two, vec_rows,
        ) = refs[15:34]
        (
        zs, zr, cs, cr, s3, r3, s4, r4, s5, r5, s7, r7, s8, r8, loc,
        ) = refs[34:]
        y, z, k, x = coords()
        me = y * 4 + z
        sib = device(y, z, 1 - k, x)
        steps = (1, 2, 3)
        everyone = greet(
            [sib]
            + [device(y, z, j, ring(x, d)) for d in steps for j in (k, 1 - k)]
            + [
                device(ring(y, a), ring(z, b), k, x)
                for a in range(4)
                for b in range(4)
                if (a, b) != (0, 0)
            ]
        )
        d_ref[:, 0:192] = gq_ref[...]
        d_ref[:, 192:576] = gkv_ref[...].astype(BF)
        d_ref[:, 576:640] = jnp.zeros((512, 64), BF)
        right_one[...] = jnp.zeros_like(right_one)
        right_one[:, 0:288] = d_ref[:, 0:288]
        right_one[:, 384:672] = d_ref[:, 288:576]
        right_two[...] = jnp.zeros_like(right_two)
        vec_rows[...] = jnp.zeros_like(vec_rows)
        sums = jnp.sum(d_ref[...].astype(F32), 0, keepdims=True)
        at_half = pl.ds(pl.multiple_of(384 * k, 128), 384)
        for b in range(4):
            heads[:, 192 * b : 192 * b + 192] = h_ref[b, k]

            @pl.when(z == b)
            def _():
                right_two[:, 288:384] = br_ref[:, 192 * b : 192 * b + 96]
                right_two[:, 672:768] = br_ref[:, 192 * b + 96 : 192 * b + 192]
                vec_rows[2:3, 192 * b : 192 * b + 192] = sums[:, 0:192]
                vec_rows[3:4, 192 * b : 192 * b + 192] = sums[:, 384:576]
                vec_rows[8 + b : 9 + b, at_half] = fb_ref[...]

        vec_rows[4:8] = vs_ref[...]
        act_t[...] = act_ref[...].T
        heads_t[...] = heads[...].T

        def product(h):
            at = pl.ds(pl.multiple_of(384 * h, 128), 384)
            total = dot(act_t[...], right_one[:, at]) + dot(heads_t[...], right_two[:, at])
            return total.reshape(4, 4, 48, 384)

        mix_other[...] = product(1 - k).astype(BF)
        everyone()
        swap = []
        for d in (1, 2, 3, 0):
            b = ring(y, d)
            c = remote(mix_other.at[b], mix_got.at[b], cs.at[d], cr.at[d], sib)
            c.start()
            swap.append(c)
        def proj_last(i):
            return remote(
                proj_sum.at[i], proj_out, s8.at[i], r8.at[0],
                device(y, z, x // 2, lax.rem(2 * x + i, 4)),
            )

        def proj_here(i):
            return (k == x // 2) & (x == lax.rem(2 * x + i, 4))

        holder = k == z // 2

        @pl.when(holder)
        def _():
            for i in range(2):
                proj_sum[i] = proj_ref[24 * i : 24 * i + 24]

                @pl.when(jnp.logical_not(proj_here(i)))
                def _():
                    proj_last(i).start()

                @pl.when(proj_here(i))
                def _():
                    proj_out[...] = proj_sum[i]

        def last_here(i):
            return k * 4 + x == i

        def fc_last(i):
            return remote(
                fc_send.at[i], fc_out.at[k], s4.at[i], r4.at[k], device(y, z, i // 4, i % 4)
            )

        @pl.when(z == x)
        def _():
            for i in range(8):
                fc_send[i, 0:6] = fc_ref[6 * i : 6 * i + 6]
                fc_send[i, 6:8] = jnp.zeros((2, 1536), F32)

                @pl.when(jnp.logical_not(last_here(i)))
                def _():
                    fc_last(i).start()

                @pl.when(last_here(i))
                def _():
                    fc_out[k] = fc_send[i]

        mix_ref[...] = product(k).astype(BF)
        one = lax.dot_general(
            d_ref[...], wq_ref[...], (((1,), (1,)), ((), ())), preferred_element_type=F32
        )
        one_ref[...] = one.astype(BF).reshape(4, 128, 768)
        vec_rows[0:1] = jnp.sum(one * n_ref[...].astype(F32), 0, keepdims=True)
        vec_rows[1:2] = jnp.sum(one, 0, keepdims=True)
        vec_ref[...] = vec_rows[...].T.astype(BF).reshape(4, 4, 48, 128)
        ones = []
        for d in steps:
            c = remote(
                one_ref.at[ring(z, d)], one_far.at[d - 1], zs.at[d - 1], zr.at[d - 1],
                device(y, ring(z, d), k, x),
            )
            c.start()
            ones.append(c)

        def plane(src, dst, send, recv, m):
            ty, tz = ring(y, m // 4), ring(z, m % 4)
            return remote(
                src.at[ty, tz], dst.at[me], send.at[m], recv.at[m], device(ty, tz, k, x)
            )

        def vec_copy(m):
            return plane(vec_ref, vec_all, s5, r5, m)

        def mix_copy(m):
            return plane(mix_sum, mix_all, s3, r3, m)

        def each(copy, what, first, last):
            def step(m, carry):
                what(copy(m))
                return carry

            lax.fori_loop(first, last, step, 0)

        start = lambda c: c.start()
        finish_all = lambda c: c.wait()
        each(vec_copy, start, 1, 16)
        vec_all[me] = vec_ref[y, z]
        for d in (1, 2, 3, 0):
            b = ring(y, d)
            swap[d - 1].wait_recv()
            mix_sum[b] = (mix_ref[b].astype(F32) + mix_got[b].astype(F32)).astype(BF)
            each(mix_copy, start, max(4 * d, 1), 4 * d + 4)
        mix_all[me] = mix_sum[y, z]
        for c in ones:
            c.wait_recv()
        one_out[...] = (
            one_ref[z].astype(F32)
            + one_far[0].astype(F32)
            + one_far[1].astype(F32)
            + one_far[2].astype(F32)
        )

        def last_copy(i):
            return remote(
                out_send.at[i], rows_out.at[k * 4 + x], s7.at[i], r7.at[k * 4 + x],
                device(y, z, i // 4, i % 4),
            )

        each(vec_copy, finish_all, 1, 16)
        each(mix_copy, finish_all, 1, 16)

        def four(ref, b):
            return (
                ref[b].astype(F32)
                + ref[4 + b].astype(F32)
                + ref[8 + b].astype(F32)
                + ref[12 + b].astype(F32)
            )

        for b in range(4):
            m = four(mix_all, b)
            for i in range(8):
                out_send[i, 0:6, 384 * b : 384 * b + 384] = m[6 * i : 6 * i + 6]
        v = four(vec_all, 0) + four(vec_all, 1) + four(vec_all, 2) + four(vec_all, 3)
        for i in range(8):
            out_send[i, 0:6, 1536:1664] = v[6 * i : 6 * i + 6]
            out_send[i, 6:8, :] = jnp.zeros((2, wide), F32)
        for i in range(8):

            @pl.when(jnp.logical_not(last_here(i)))
            def _():
                last_copy(i).start()

            @pl.when(last_here(i))
            def _():
                rows_out[i] = out_send[i]

        for j in range(2):

            @pl.when(jnp.logical_not((z == x) & (k == j)))
            def _():
                remote(fc_send.at[0], fc_out.at[j], s4.at[0], r4.at[j], sib).wait_recv()

        for i in range(8):

            @pl.when(jnp.logical_not(last_here(i)))
            def _():
                remote(out_send.at[0], rows_out.at[i], s7.at[0], r7.at[i], sib).wait_recv()
                last_copy(i).wait_send()

        @pl.when(jnp.logical_not((k == z // 2) & (x == (4 * k + x) // 2)))
        def _():
            remote(proj_sum.at[0], proj_out, s8.at[0], r8.at[0], sib).wait_recv()

        @pl.when(z == x)
        def _():
            for i in range(8):

                @pl.when(jnp.logical_not(last_here(i)))
                def _():
                    fc_last(i).wait_send()

        for i in range(2):

            @pl.when(holder & jnp.logical_not(proj_here(i)))
            def _():
                proj_last(i).wait_send()

        for c in swap + ones:
            c.wait_send()

    return comm(
        kernel,
        [
            jax.ShapeDtypeStruct((128, 768), F32),
            jax.ShapeDtypeStruct((8, 8, wide), F32),
            jax.ShapeDtypeStruct((24, 768), F32),
            jax.ShapeDtypeStruct((2, 8, 1536), F32),
        ],
        6,
        (3, 3, 4, 4, 16, 16, 8, 2, 16, 16, 8, 8, 2, 1, 4),
        (*pieces, fc, proj),
        scratch=[
            pltpu.VMEM((3, 128, 768), BF),
            pltpu.VMEM((4, 4, 48, 384), BF),
            pltpu.VMEM((4, 4, 48, 384), BF),
            pltpu.VMEM((16, 48, 384), BF),
            pltpu.VMEM((16, 48, 128), BF),
            pltpu.VMEM((2, 24, 768), F32),
            pltpu.VMEM((8, 8, wide), F32),
            pltpu.VMEM((8, 8, 1536), F32),
            pltpu.VMEM((4, 128, 768), BF),
            pltpu.VMEM((4, 4, 48, 384), BF),
            pltpu.VMEM((4, 4, 48, 384), BF),
            pltpu.VMEM((4, 4, 48, 128), BF),
            pltpu.VMEM((768, 512), BF),
            pltpu.VMEM((512, 768), BF),
            pltpu.VMEM((768, 512), BF),
            pltpu.VMEM((512, 640), BF),
            pltpu.VMEM((512, 768), BF),
            pltpu.VMEM((512, 768), BF),
            pltpu.VMEM((128, 768), F32),
        ],
        spaces=([VMEM] * 11, [VMEM] * 4),
        name="last_sums",
    )


def finish(grad_one, grad_x_two, tokens, vec_rows, rows, proj_rows, fc_rows, result, state):
    def kernel(*refs):
        one_ref, gx_ref, t_ref, v_ref, rows_ref, p_ref, f_ref, res_ref = refs[:8]
        state_ref = refs[8:23]
        out_ref, gin_ref = refs[23:25]
        new_ref = refs[25:40]
        g_qkv, g_out, g_fc = refs[40:]
        out_ref[...] = res_ref[...]
        normed, inverse = normalize(t_ref[...].astype(F32))
        gin_ref[...] = gx_ref[...] + normalize_back(normed, inverse, v_ref[0:1], one_ref[...])
        for b in range(4):
            at_z = slice(384 * b, 384 * b + 384)
            one_half = jnp.sum(rows_ref[0:4, 0:6, at_z], 0)
            two_half = jnp.sum(rows_ref[4:8, 0:6, at_z], 0)
            q = 192 * b
            g_qkv[:, q : q + 192] = one_half[:, 0:192]
            g_qkv[:, 768 + q : 864 + q] = one_half[:, 192:288]
            g_qkv[:, 864 + q : 960 + q] = two_half[:, 0:96]
            g_qkv[:, 1536 + q : 1728 + q] = two_half[:, 96:288]
            g_out[:, q : q + 96] = one_half[:, 288:384]
            g_out[:, q + 96 : q + 192] = two_half[:, 288:384]
            for j in range(2):
                at = 384 * (2 * b + j)
                g_fc[:, at : at + 384] = f_ref[j, 0:6, 384 * b : 384 * b + 384]
        g_vec = jnp.sum(rows_ref[:, 0:6, 1536:1548], 0)
        for i, (gradient, rate, decay) in enumerate(
            (
                (g_qkv[...], 0.1, 0.1),
                (g_out[...], 0.3, 0.1),
                (g_fc[...], 0.05, 0.1),
                (p_ref[...], 0.03, 0.1),
                (g_vec, 0.5, 0.0),
            )
        ):
            w, m, v = state_ref[3 * i : 3 * i + 3]
            results = adam_update(w[...], m[...], v[...], gradient, rate, decay)
            for j in range(3):
                new_ref[3 * i + j][...] = results[j]

    return pl.pallas_call(
        kernel,
        out_shape=[jax.ShapeDtypeStruct((128, 768), F32)] * 2
        + [jax.ShapeDtypeStruct(one.shape, F32) for one in state],
        in_specs=[VMEM] * 23,
        out_specs=[VMEM] * 17,
        scratch_shapes=[
            pltpu.VMEM((6, 2304), F32),
            pltpu.VMEM((6, 768), F32),
            pltpu.VMEM((6, 3072), F32),
        ],
        compiler_params=pltpu.CompilerParams(vmem_limit_bytes=LIMIT),
        name="finish",
    )(grad_one, grad_x_two, tokens, vec_rows, rows, proj_rows, fc_rows, result, *state)


def head_rows(matrix, head):
    row = lax.broadcasted_iota(jnp.int32, matrix.shape, 0)
    keep = (row >= 64 * head) & (row < 64 * head + 64)
    return jnp.where(keep, matrix, jnp.zeros_like(matrix))


def head_cols(matrix, head):
    col = lax.broadcasted_iota(jnp.int32, matrix.shape, 1)
    keep = (col >= 64 * head) & (col < 64 * head + 64)
    return jnp.where(keep, matrix, jnp.zeros_like(matrix))


def place(index):
    return (index // 128) * 256 + index % 128


def dot(a, b):
    return jnp.dot(a, b, preferred_element_type=F32)


def forward(w_qkv, w_fc, w_out, w_proj, vectors, tokens, cotangent):
    wide_q, wide_r = 1280, 3456

    def kernel(
        wq_ref, wf_ref, wo_ref, wp_ref, wv_ref, t_ref, r_ref,
        ho_ref, ot_ref, lse_ref, vo_ref, ro_ref, fo_ref, oo_ref, po_ref, q_ref, a_ref, n_ref,
        q_out, x_ref, vec_ref,
        wide_one, wide_two, packed_q, packed_r, got_q, got_r,
        fc48, qkv48, out48, proj_wide, q_send, f_send, o_send, p_send, f_mid, o_mid, p_mid,
        bias, qt, m_ref, l_ref, h_buf, v_ref,
        mq_s, mq_r, fq_s, fq_r, mr_s, mr_r, fr_s, fr_r, s1, r1, s2, r2, ps, pr,
        xs_s, xs_r, xf_s, xf_r, ts, tr, us, ur,
        vs, vr, rs, rr, cs, cr, ds, dr, ws, wr, wf, os, orr, hs, hr, gs, gr, loc,
    ):
        y, z, k, x = coords()
        me = y * 4 + z
        t = k * 4 + x
        sib = device(y, z, 1 - k, x)
        steps = (1, 2, 3)
        everyone = greet(
            [sib]
            + [device(y, z, k, ring(x, d)) for d in steps]
            + [
                device(ring(y, a), ring(z, b), k, x)
                for a in range(4)
                for b in range(4)
                if (a, b) != (0, 0)
            ]
        )

        def first(packed, got, send, recv):
            copies = [
                remote(packed, got.at[t], send.at[d], recv.at[d], device(y, z, k, ring(x, d)))
                for d in steps
            ]
            for c in copies:
                c.start()
            return copies

        def crossing(packed, got, copies, send, recv):
            out = [remote(packed, got.at[t], send.at[0], recv.at[0], sib)]
            out[0].start()
            for d in steps:
                copies[d - 1].wait_recv()
                src = k * 4 + ring(x, 4 - d)
                c = remote(got.at[src], got.at[src], send.at[d], recv.at[d], sib)
                c.start()
                out.append(c)
            return out

        wide_one[...] = jnp.zeros_like(wide_one)
        wide_one[0:6, 0:1152] = wq_ref[:, 0:1152]
        wide_one[6:12, 0:1152] = wq_ref[:, 1152:2304]
        wide_one[0:6, 1152:1164] = wv_ref[...]
        packed_q[...] = wide_one[...].astype(BF)
        got_q[t] = packed_q[...]
        everyone()
        message_q = first(packed_q, got_q, mq_s, mq_r)
        token_copies = []
        for d in steps:
            c = remote(
                t_ref, x_ref.at[k, z], ts.at[d], tr.at[d], device(y, ring(z, d), k, x)
            )
            c.start()
            token_copies.append(c)
        token_cross = [remote(t_ref, x_ref.at[k, z], us.at[0], ur.at[0], sib)]
        token_cross[0].start()
        x_ref[k, z] = t_ref[...]
        wide_two[...] = jnp.zeros_like(wide_two)
        wide_two[0:6, 0:1920] = wf_ref[:, 0:1920]
        wide_two[6:12, 0:1152] = wf_ref[:, 1920:3072]
        wide_two[6:12, 1152:1920] = wo_ref[...]
        wide_two[0:12, 1920:2688] = wp_ref[0:12]
        wide_two[0:12, 2688:3456] = wp_ref[12:24]
        packed_r[...] = wide_two[...].astype(BF)
        got_r[t] = packed_r[...]
        cross_q = crossing(packed_q, got_q, message_q, fq_s, fq_r)
        message_r = first(packed_r, got_r, mr_s, mr_r)
        for c in cross_q:
            c.wait_recv()
        for i in range(8):
            piece = got_q[i].astype(F32)
            at = slice(6 * i, 6 * i + 6)
            qkv48[at, 0:1152] = piece[0:6, 0:1152]
            qkv48[at, 1152:2304] = piece[6:12, 0:1152]
            qkv48[at, 2304:2432] = piece[0:6, 1152:1280]
        for j in range(4):
            q_send[j, :, 0:192] = qkv48[:, 192 * j : 192 * j + 192].astype(BF)
            q_send[j, :, 192:384] = qkv48[:, 768 + 192 * j : 960 + 192 * j].astype(BF)
            q_send[j, :, 384:576] = qkv48[:, 1536 + 192 * j : 1728 + 192 * j].astype(BF)
            q_send[j, :, 576:640] = qkv48[:, 2304:2368].astype(BF)

        group = pl.ds(pl.multiple_of(16 * jnp.minimum(x, 2), 16), 16)

        def to_of(m):
            return ring(y, m // 4), ring(z, m % 4)

        def q_copy(m):
            ty, tz = to_of(m)
            return remote(
                q_send.at[tz, group], q_out.at[me, group], s1.at[m], r1.at[m],
                device(ty, tz, k, x),
            )

        def f_copy(m):
            ty, tz = to_of(m)
            return remote(
                f_send.at[tz * 2 + k], f_mid.at[me], s2.at[m], r2.at[m], device(ty, tz, k, x)
            )

        def o_copy(m):
            ty, tz = to_of(m)
            return remote(o_send.at[k], o_mid.at[me], s2.at[m], r2.at[m], device(ty, tz, k, x))

        def p_copy(a):
            return remote(
                p_send, p_mid.at[z % 2], ps.at[a], pr.at[z % 2], device(ring(y, a), y, k, x)
            )

        def each(copy, what):
            def step(m, carry):
                what(copy(m))
                return carry

            lax.fori_loop(1, 16, step, 0)

        start = lambda c: c.start()
        finish = lambda c: c.wait()

        @pl.when(x < 3)
        def _():
            each(q_copy, start)
            q_out[me, group] = q_send[z, group]

        half = pl.ds(8 * k, 8)
        other_half = pl.ds(8 * (1 - k), 8)

        def rows_of(plane):
            return pl.ds(pl.multiple_of(16 * plane, 16), 16)

        def x_copy(d):
            return remote(
                q_out.at[half, group], q_out.at[half, group], xs_s.at[d], xs_r.at[x],
                device(y, z, k, ring(x, d)),
            )

        @pl.when(x < 3)
        def _():
            each(q_copy, finish)
            for d in steps:
                x_copy(d).start()

        cross_r = crossing(packed_r, got_r, message_r, fr_s, fr_r)
        for c in cross_r:
            c.wait_recv()
        for i in range(8):
            piece = got_r[i].astype(F32)
            at = slice(6 * i, 6 * i + 6)
            fc48[at, 0:1920] = piece[0:6, 0:1920]
            fc48[at, 1920:3072] = piece[6:12, 0:1152]
            out48[at] = piece[6:12, 1152:1920]
            proj_wide[24 * i : 24 * i + 12] = piece[0:12, 1920:2688]
            proj_wide[24 * i + 12 : 24 * i + 24] = piece[0:12, 2688:3456]
        for j in range(8):
            f_send[j] = fc48[:, 384 * j : 384 * j + 384].astype(BF)
        o_send[0] = out48[:, 0:384].astype(BF)
        o_send[1] = out48[:, 384:768].astype(BF)
        p_send[...] = proj_wide[...].astype(BF)

        @pl.when(x == 1)
        def _():
            each(f_copy, start)
            f_mid[me] = f_send[z * 2 + k]

        @pl.when(x == 2)
        def _():
            each(o_copy, start)
            o_mid[me] = o_send[k]

        @pl.when((x == 3) & (k == z // 2))
        def _():
            for a in range(1, 4):
                p_copy(a).start()

            @pl.when(z != y)
            def _():
                p_copy(0).start()

            @pl.when(z == y)
            def _():
                p_mid[z % 2] = p_send[...]

        def pass_q(a):
            return remote(
                q_out.at[half, rows_of(a)], q_out.at[half, rows_of(a)], xf_s.at[a], xf_r.at[a], sib
            )

        for a in range(3):

            @pl.when(x != a)
            def _():
                remote(
                    q_out.at[half, rows_of(a)], q_out.at[half, rows_of(a)], xs_s.at[0],
                    xs_r.at[a], sib,
                ).wait_recv()
                pass_q(a).start()

        for d in steps:
            token_copies[d - 1].wait_recv()
            src = ring(z, 4 - d)
            c = remote(x_ref.at[k, src], x_ref.at[k, src], us.at[d], ur.at[d], sib)
            c.start()
            token_cross.append(c)
        normed, _ = normalize(x_ref[k].reshape(512, 768).astype(F32))
        n_ref[...] = normed.astype(BF)

        weights = ((1, f_mid, fo_ref, 8), (2, o_mid, oo_ref, 8), (3, p_mid, po_ref, 1))

        def ends(a, half):
            _, src, dst, n = weights[a - 1]
            at = pl.ds(n * half, n)
            return src.at[at], (dst.at[k, at] if a == 2 else dst.at[at])

        def direct(a, half, d):
            src, dst = ends(a, half)
            return remote(
                src, dst, ws.at[4 * half + d], wr.at[2 * a + half], device(y, z, k, ring(x, d))
            )

        def onward(a, half, d):
            _, dst = ends(a, half)
            return remote(
                dst, dst, wf.at[a], wr.at[2 * a + half], device(y, z, k, ring(x, d))
            )

        def weight_own(a):
            _, src, dst, _ = weights[a - 1]
            return pltpu.make_async_copy(src, dst.at[k] if a == 2 else dst, loc.at[1])

        @pl.when(x == 1)
        def _():
            each(f_copy, finish)

        @pl.when(x == 2)
        def _():
            each(o_copy, finish)

        for i in range(2):
            @pl.when((x == 3) & jnp.logical_not((y == z) & (z == 2 * k + i)))
            def _():
                remote(p_send, p_mid.at[i], ps.at[0], pr.at[i], sib).wait_recv()

        for a in steps:

            @pl.when(x == a)
            def _():
                for half_at, d in ((0, 1), (1, 3), (1, 1), (0, 3)):
                    direct(a, half_at, d).start()
                weight_own(a).start()

        def move_on():
            for a in steps:

                @pl.when(x == (a + 1) % 4)
                def _():
                    direct(a, 0, 1).wait_recv()
                    onward(a, 0, 1).start()

                @pl.when(x == (a + 3) % 4)
                def _():
                    direct(a, 1, 1).wait_recv()
                    onward(a, 1, 3).start()

        for a in range(3):

            @pl.when(x != a)
            def _():
                remote(
                    q_out.at[other_half, rows_of(a)], q_out.at[other_half, rows_of(a)],
                    xf_s.at[a], xf_r.at[a], sib,
                ).wait_recv()

        vec_ref[...] = q_out[:, :, 512:640].reshape(768, 128).astype(F32).T[64:80]
        bias[...] = jnp.zeros_like(bias)
        for b in range(4):

            @pl.when(z == b)
            def _():
                bias[:, 0:192] = vec_ref[2:3, 192 * b : 192 * b + 192]
                bias[:, 384:576] = vec_ref[3:4, 192 * b : 192 * b + 192]

        act = (normed * vec_ref[0:1] + vec_ref[1:2]).astype(BF)
        a_ref[...] = act
        mixed = dot(act, q_out[...].reshape(768, 640)) + bias[...]
        v_ref[...] = mixed[:, 192:576].astype(BF)

        def kv_copy(d):
            return remote(
                v_ref, vo_ref.at[y, k], vs.at[d], vr.at[d], device(ring(y, d), z, k, x)
            )

        for d in steps:

            @pl.when(y + d < 4)
            def _():
                kv_copy(d).start()

        swap = remote(v_ref, vo_ref.at[y, k], cs.at[0], cr.at[0], sib)
        swap.start()
        vo_ref[y, k] = v_ref[...]
        own_r = pltpu.make_async_copy(r_ref, ro_ref.at[k, z], loc.at[0])
        own_r.start()
        row_copies = []
        for d in steps:
            c = remote(
                r_ref, ro_ref.at[k, z], rs.at[d], rr.at[d], device(y, ring(z, d), k, x)
            )
            c.start()
            row_copies.append(c)
        row_first = remote(r_ref, ro_ref.at[k, z], ds.at[0], dr.at[0], sib)
        row_first.start()
        query = mixed[:, :192].astype(BF) * jnp.asarray(0.125, BF)
        q_ref[...] = query
        q_t = query.T
        for head in range(3):
            qt[head] = head_rows(q_t, head)
        m_ref[...] = jnp.full_like(m_ref, -1e30)
        l_ref[...] = jnp.zeros_like(l_ref)
        ot_ref[...] = jnp.zeros_like(ot_ref)

        def block(by, bk, masked):
            keys = vo_ref[by, bk, :, :192]
            values_t = vo_ref[by, bk, :, 192:].T
            if masked:
                key_at = place(lax.broadcasted_iota(jnp.int32, (512, 512), 0)) + 128 * bk
                query_at = place(lax.broadcasted_iota(jnp.int32, (512, 512), 1)) + 128 * k
                visible = query_at >= key_at
            for head in range(3):
                s = dot(keys, qt[head])
                if masked:
                    s = jnp.where(visible, s, -1e9)
                old = m_ref[head : head + 1]
                new = jnp.maximum(old, jnp.max(s, 0, keepdims=True))
                e = jnp.exp(s - new)
                scale = jnp.exp(old - new)
                m_ref[head : head + 1] = new
                l_ref[head : head + 1] = l_ref[head : head + 1] * scale + jnp.sum(
                    e, 0, keepdims=True
                )
                at = slice(64 * head, 64 * head + 64)
                ot_ref[at] = ot_ref[at] * scale + dot(values_t[at], e.astype(BF))

        def diagonal(j, carry):
            @pl.when(j == 1)
            def _():
                remote(v_ref, vo_ref.at[y, 1 - k], cs.at[0], cr.at[0], sib).wait_recv()

            block(y, lax.rem(k + j, 2), True)

            return carry

        lax.fori_loop(0, 2, diagonal, 0)

        def pass_on(d):
            return remote(
                vo_ref.at[y - d, k], vo_ref.at[y - d, k], cs.at[d], cr.at[d], sib
            )

        def earlier(i, carry):
            d, j = i // 2 + 1, i % 2

            @pl.when(j == 0)
            def _():
                remote(v_ref, vo_ref.at[y - d, k], vs.at[d], vr.at[d], sib).wait_recv()
                pass_on(d).start()

            @pl.when(j == 1)
            def _():
                remote(v_ref, vo_ref.at[y - d, 1 - k], cs.at[d], cr.at[d], sib).wait_recv()

            block(y - d, lax.rem(k + j, 2), False)

            @pl.when(i == jnp.minimum(2, 2 * y - 1))
            def _():
                move_on()

            return carry

        @pl.when(y == 0)
        def _():
            move_on()

        lax.fori_loop(0, 2 * y, earlier, 0)
        for head in range(3):
            at = slice(64 * head, 64 * head + 64)
            total = l_ref[head : head + 1]
            ot_ref[at] = ot_ref[at] / total
            lse_ref[head : head + 1] = m_ref[head : head + 1] + jnp.log(total)
        h_buf[...] = ot_ref[...].T.astype(BF)
        heads_copies = []
        for d in steps:
            c = remote(
                h_buf, ho_ref.at[z, k], hs.at[d], hr.at[d], device(y, ring(z, d), k, x)
            )
            c.start()
            heads_copies.append(c)
        c = remote(h_buf, ho_ref.at[z, k], gs.at[0], gr.at[0], sib)
        c.start()
        forward_copies = [c, row_first]
        own_h = pltpu.make_async_copy(h_buf, ho_ref.at[z, k], loc.at[2])
        own_h.start()
        for d in steps:
            row_copies[d - 1].wait_recv()
            src = ring(z, 4 - d)
            c = remote(ro_ref.at[k, src], ro_ref.at[k, src], ds.at[d], dr.at[d], sib)
            c.start()
            forward_copies.append(c)
        for a in steps:

            @pl.when(x == a)
            def _():
                weight_own(a).wait()

            @pl.when(x == (a + 1) % 4)
            def _():
                direct(a, 1, 1).wait_recv()

            @pl.when(x == (a + 3) % 4)
            def _():
                direct(a, 0, 1).wait_recv()

            @pl.when(x == (a + 2) % 4)
            def _():
                direct(a, 0, 1).wait_recv()
                direct(a, 1, 1).wait_recv()

        c = remote(oo_ref.at[k], oo_ref.at[k], os.at[0], orr.at[0], sib)
        c.start()
        forward_copies.append(c)
        for d in steps:
            heads_copies[d - 1].wait_recv()
            src = ring(z, 4 - d)
            c = remote(ho_ref.at[src, k], ho_ref.at[src, k], gs.at[d], gr.at[d], sib)
            c.start()
            forward_copies.append(c)
        for c in forward_copies + token_cross:
            c.wait()
        for c in row_copies + heads_copies + token_copies + [swap]:
            c.wait_send()
        for c in message_q + cross_q + message_r + cross_r:
            c.wait_send()
        for d in steps:

            @pl.when(y + d < 4)
            def _():
                kv_copy(d).wait_send()

            @pl.when(y >= d)
            def _():
                pass_on(d).wait_send()

        for a in steps:

            @pl.when(x == a)
            def _():
                for half_at, d in ((0, 1), (1, 3), (1, 1), (0, 3)):
                    direct(a, half_at, d).wait_send()

            @pl.when(x == (a + 1) % 4)
            def _():
                onward(a, 0, 1).wait_send()

            @pl.when(x == (a + 3) % 4)
            def _():
                onward(a, 1, 3).wait_send()

        @pl.when((x == 3) & (k == z // 2))
        def _():
            for a in range(1, 4):
                p_copy(a).wait_send()

            @pl.when(z != y)
            def _():
                p_copy(0).wait_send()

        @pl.when(x < 3)
        def _():
            for d in steps:
                x_copy(d).wait_send()

        for a in range(3):

            @pl.when(x != a)
            def _():
                pass_q(a).wait_send()

        own_r.wait()
        own_h.wait()

    return comm(
        kernel,
        [
            jax.ShapeDtypeStruct((4, 2, 512, 192), BF),
            jax.ShapeDtypeStruct((192, 512), F32),
            jax.ShapeDtypeStruct((8, 512), F32),
            jax.ShapeDtypeStruct((4, 2, 512, 384), BF),
            jax.ShapeDtypeStruct((2, 4, 128, 768), BF),
            jax.ShapeDtypeStruct((16, 48, 384), BF),
            jax.ShapeDtypeStruct((2, 16, 48, 384), BF),
            jax.ShapeDtypeStruct((2, 192, 768), BF),
            jax.ShapeDtypeStruct((512, 192), BF),
            jax.ShapeDtypeStruct((512, 768), BF),
            jax.ShapeDtypeStruct((512, 768), BF),
            jax.ShapeDtypeStruct((16, 48, 640), BF),
            jax.ShapeDtypeStruct((2, 4, 128, 768), BF),
            jax.ShapeDtypeStruct((16, 768), F32),
        ],
        0,
        (4,) * 8 + (16,) * 4 + (4, 2) + (4,) * 8
        + (4, 4, 4, 4, 4, 4, 4, 4, 8, 8, 4, 1, 1, 4, 4, 4, 4, 3),
        (w_qkv, w_fc, w_out, w_proj, vectors, tokens, cotangent),
        scratch=[
            pltpu.VMEM((16, wide_q), F32),
            pltpu.VMEM((16, wide_r), F32),
            pltpu.VMEM((16, wide_q), BF),
            pltpu.VMEM((16, wide_r), BF),
            pltpu.VMEM((8, 16, wide_q), BF),
            pltpu.VMEM((8, 16, wide_r), BF),
            pltpu.VMEM((48, 3072), F32),
            pltpu.VMEM((48, 2432), F32),
            pltpu.VMEM((48, 768), F32),
            pltpu.VMEM((192, 768), F32),
            pltpu.VMEM((4, 48, 640), BF),
            pltpu.VMEM((8, 48, 384), BF),
            pltpu.VMEM((2, 48, 384), BF),
            pltpu.VMEM((192, 768), BF),
            pltpu.VMEM((16, 48, 384), BF),
            pltpu.VMEM((16, 48, 384), BF),
            pltpu.VMEM((2, 192, 768), BF),
            pltpu.VMEM((1, 640), F32),
            pltpu.VMEM((3, 192, 512), BF),
            pltpu.VMEM((8, 512), F32),
            pltpu.VMEM((8, 512), F32),
            pltpu.VMEM((512, 192), BF),
            pltpu.VMEM((512, 384), BF),
        ],
        spaces=(
            [VMEM] * 6 + [ANY],
            [ANY, VMEM, VMEM, VMEM, ANY, ANY, ANY, ANY] + [VMEM] * 6,
        ),
        name="forward",
    )


def normalize(rows):
    centered = rows - jnp.mean(rows, -1, keepdims=True)
    inverse = lax.rsqrt(jnp.mean(centered * centered, -1, keepdims=True) + EPSILON)
    return centered * inverse, inverse


def normalize_back(normed, inverse, gain, grad):
    scaled = grad * gain
    return inverse * (
        scaled
        - jnp.mean(scaled, -1, keepdims=True)
        - normed * jnp.mean(scaled * normed, -1, keepdims=True)
    )


def feed_body(
    h_ref, x_ref, dy_ref, wo_ref, wf_ref, wp_ref, v_ref,
    base_ref, res_mine, gx_ref, bo_ref, gwf_ref, gwp_ref, gfb_ref, gv_ref,
    a2, act, df, x_two, normed, inverse, norm_other, norm_mine, res_other,
    norm_got, res_got, norm_far, branch,
    cs, cr, es, er, zs, zr, bs, br, everyone,
):
    y, z, k, x = coords()
    sib = device(y, z, 1 - k, x)
    steps = (1, 2, 3)
    out_bias, gain, shift, proj_bias = (v_ref[i : i + 1] for i in range(4, 8))
    fc_bias = jnp.zeros((1, 384), F32)
    for b in range(4):
        row = v_ref[8 + b : 9 + b, pl.ds(pl.multiple_of(384 * k, 128), 384)]
        fc_bias = fc_bias + jnp.where(z == b, row, 0.0)

    def half(kk, norm_ref):
        two = x_ref[kk].reshape(512, 768).astype(F32) + out_bias
        for g in range(4):
            h = h_ref[g, kk]
            at = slice(192 * g, 192 * g + 192)
            part = jnp.concatenate([dot(h, wo_ref[0, at]), dot(h, wo_ref[1, at])], 1)
            two = two + part
        x_two[...] = two
        n, inv = normalize(two)
        normed[...] = n
        inverse[...] = jnp.broadcast_to(inv, (512, 128))
        a = (n * gain + shift).astype(BF)
        a2[kk] = a
        hidden = dot(a, wf_ref[...]) + fc_bias
        square = hidden * hidden
        t = jnp.tanh(0.7978845608028654 * (hidden + 0.044715 * square * hidden))
        act_blk = (0.5 * hidden * (1.0 + t)).astype(BF)
        act[kk] = act_blk
        slope = 0.5 * (1.0 + t) + 0.5 * hidden * (1.0 - t * t) * (
            0.7978845608028654 * (1.0 + 3 * 0.044715 * square)
        )
        dy = dy_ref[kk].reshape(512, 768)
        back = lax.dot_general(
            dy, wp_ref[...], (((1,), (1,)), ((), ())), preferred_element_type=F32
        )
        df_blk = (back * slope).astype(BF)
        df[kk] = df_blk
        norm_part = lax.dot_general(
            df_blk, wf_ref[...], (((1,), (1,)), ((), ())), preferred_element_type=F32
        )
        norm_ref[...] = norm_part.astype(BF).reshape(4, 128, 768)

    def result(kk, res_ref):
        res_ref[...] = dot(act[kk], wp_ref[...]).astype(BF).reshape(4, 128, 768)

    half(1 - k, norm_other)
    everyone()
    swaps = []
    for d in (1, 2, 3, 0):
        b = ring(z, d)
        c = remote(norm_other.at[b], norm_got.at[b], cs.at[d], cr.at[d], sib)
        c.start()
        swaps.append(c)
    half(k, norm_mine)
    sends = []
    for d in steps:
        b = ring(z, d)
        swaps[d - 1].wait_recv()
        norm_mine[b] = (norm_mine[b].astype(F32) + norm_got[b].astype(F32)).astype(BF)
        c = remote(
            norm_mine.at[b], norm_far.at[d - 1], zs.at[d - 1], zr.at[d - 1],
            device(y, b, k, x),
        )
        c.start()
        sends.append(c)
    result(1 - k, res_other)
    for d in (1, 2, 3, 0):
        b = ring(z, d)
        c = remote(res_other.at[b], res_got.at[b], es.at[d], er.at[d], sib)
        c.start()
        swaps.append(c)
    tn = (((0,), (0,)), ((), ()))
    gwf = lax.dot_general(a2[0], df[0], tn, preferred_element_type=F32)
    gwf += lax.dot_general(a2[1], df[1], tn, preferred_element_type=F32)
    gwf_ref[...] = gwf.astype(BF).reshape(4, 4, 48, 384)
    own_rows = pl.ds(pl.multiple_of(128 * z, 128), 128)
    swaps[3].wait_recv()
    for c in sends:
        c.wait_recv()
    da = (
        norm_mine[z].astype(F32)
        + norm_got[z].astype(F32)
        + norm_far[0].astype(F32)
        + norm_far[1].astype(F32)
        + norm_far[2].astype(F32)
    )
    n = normed[own_rows]
    dy = dy_ref[k, z].astype(F32)
    gx = dy + normalize_back(n, inverse[own_rows, 0:1], gain, da)
    gx_ref[...] = gx
    low = gx.astype(BF)
    branch[...] = low
    bo_ref[z] = low
    branches = []
    for d in steps:
        c = remote(
            branch, bo_ref.at[z], bs.at[d - 1], br.at[d - 1], device(y, ring(z, d), k, x)
        )
        c.start()
        branches.append(c)
    result(k, res_mine)
    gwp = lax.dot_general(
        act[0], dy_ref[0].reshape(512, 768), tn, preferred_element_type=F32
    )
    gwp += lax.dot_general(
        act[1], dy_ref[1].reshape(512, 768), tn, preferred_element_type=F32
    )
    gwp_ref[...] = gwp.astype(BF).reshape(2, 4, 48, 768)
    gfb_ref[...] = jnp.sum(df[0].astype(F32), 0, keepdims=True) + jnp.sum(
        df[1].astype(F32), 0, keepdims=True
    )
    gv_ref[0:1] = jnp.sum(low.astype(F32), 0, keepdims=True)
    gv_ref[1:2] = jnp.sum(da * n, 0, keepdims=True)
    gv_ref[2:3] = jnp.sum(da, 0, keepdims=True)
    gv_ref[3:4] = jnp.sum(dy, 0, keepdims=True)
    for c in swaps[4:]:
        c.wait_recv()
    res_mine[...] = (res_mine[...].astype(F32) + res_got[...].astype(F32)).astype(BF)
    base_ref[...] = x_two[own_rows] + proj_bias
    for c in branches:
        c.wait()
    for c in swaps + sends:
        c.wait_send()


def back_body(
    q_ref, b_ref, w_ref, kv_ref, ot_ref, lse_ref, f_ref, p_ref, base_ref, res_ref,
    dq_ref, dkv_ref, fo_ref, po_ref, out_ref,
    qt, gt, qm, gm, delta, dqt, out_buf, keep, got, far, f_far, p_far, r_far,
    f_sum, p_sum, f_all, p_all,
    cs, cr, ys, yr, fs, fr, ps, pr, rs, rr, s4, r4, s6, r6,
):
    y, z, k, x = coords()
    sib = device(y, z, 1 - k, x)
    steps = (1, 2, 3)
    me = y * 4 + z
    results = []
    for d in steps:
        b = ring(z, d)
        c = remote(
            res_ref.at[b], r_far.at[d - 1], rs.at[d - 1], rr.at[d - 1], device(y, b, k, x)
        )
        c.start()
        results.append(c)
    weights = []
    for d in steps:
        b = ring(x, d)
        to = device(y, z, k, b)
        weights.append(
            remote(f_ref.at[:, b], f_far.at[d - 1], fs.at[d - 1], fr.at[d - 1], to)
        )
        weights.append(
            remote(p_ref.at[:, b], p_far.at[d - 1], ps.at[d - 1], pr.at[d - 1], to)
        )
    for c in weights:
        c.start()
    query_blk = q_ref[...]
    q_t = query_blk.T
    for head in range(3):
        qt[head] = head_rows(q_t, head)
        qm[head] = head_cols(query_blk, head)
    dqt[...] = jnp.zeros_like(dqt)
    nt = (((1,), (1,)), ((), ()))
    branch = b_ref[...].reshape(512, 768)
    own_heads = pl.ds(pl.multiple_of(192 * z, 64), 192)
    grad_blk = lax.dot_general(
        branch[:, :384], w_ref[0, own_heads], nt, preferred_element_type=F32
    )
    grad_blk += lax.dot_general(
        branch[:, 384:], w_ref[1, own_heads], nt, preferred_element_type=F32
    )
    grad_blk = grad_blk.astype(BF)
    g_t = grad_blk.T
    for head in range(3):
        at = slice(64 * head, 64 * head + 64)
        gt[head] = head_rows(g_t, head)
        gm[head] = head_cols(grad_blk, head)
        delta[head : head + 1] = jnp.sum(g_t[at].astype(F32) * ot_ref[at], 0, keepdims=True)

    def block(by, bk, masked, to_ref, to):
        keys = kv_ref[by, bk, :, :192]
        values = kv_ref[by, bk, :, 192:]
        keys_t = keys.T
        if masked:
            key_at = place(lax.broadcasted_iota(jnp.int32, (512, 512), 0)) + 128 * bk
            query_at = place(lax.broadcasted_iota(jnp.int32, (512, 512), 1)) + 128 * k
            visible = query_at >= key_at
        dk = dv = None
        for head in range(3):
            s = dot(keys, qt[head])
            p = jnp.exp(s - lse_ref[head : head + 1])
            if masked:
                p = jnp.where(visible, p, 0.0)
            dp = dot(values, gt[head])
            ds = (p * (dp - delta[head : head + 1])).astype(BF)
            pv = dot(p.astype(BF), gm[head])
            pk = dot(ds, qm[head])
            dv = pv if dv is None else dv + pv
            dk = pk if dk is None else dk + pk
            at = slice(64 * head, 64 * head + 64)
            dqt[at] += dot(keys_t[at], ds)
        to_ref[to, :, :192] = dk.astype(BF)
        to_ref[to, :, 192:] = dv.astype(BF)

    def cross(d):
        return remote(out_buf.at[d], got.at[d], cs.at[d], cr.at[d], sib)

    def up(d):
        return remote(keep.at[d], far.at[d], ys.at[d], yr.at[d], device(y - d, z, k, x))

    def earlier(i, carry):
        d = y - i
        block(y - d, 1 - k, False, out_buf, d)
        cross(d).start()
        block(y - d, k, False, keep, d)
        cross(d).wait_recv()
        keep[d] = (keep[d].astype(F32) + got[d].astype(F32)).astype(BF)
        up(d).start()
        return carry

    lax.fori_loop(0, y, earlier, 0)
    block(y, 1 - k, True, out_buf, 0)
    cross(0).start()

    for c in weights:
        c.wait()
    f_sum[...] = (
        f_ref[:, x].astype(F32)
        + f_far[0].astype(F32)
        + f_far[1].astype(F32)
        + f_far[2].astype(F32)
    ).astype(BF)
    p_sum[...] = (
        p_ref[:, x].astype(F32)
        + p_far[0].astype(F32)
        + p_far[1].astype(F32)
        + p_far[2].astype(F32)
    ).astype(BF)

    def f_copy(a):
        return remote(
            f_sum.at[a], f_all.at[me], s4.at[a], r4.at[me], device(a, x, k, x)
        )

    def p_copy(j):
        return remote(
            p_sum.at[j], p_all.at[y], s6.at[j], r6.at[y], device(z, 2 * k + j, k, x)
        )

    f_here = [(a == y) & (z == x) for a in range(4)]
    p_here = [(y == z) & (z == 2 * k + j) for j in range(2)]
    for a in range(4):

        @pl.when(jnp.logical_not(f_here[a]))
        def _():
            f_copy(a).start()

        @pl.when(f_here[a])
        def _():
            f_all[me] = f_sum[a]

    for j in range(2):

        @pl.when(jnp.logical_not(p_here[j]))
        def _():
            p_copy(j).start()

        @pl.when(p_here[j])
        def _():
            p_all[y] = p_sum[j]

    block(y, k, True, keep, 0)
    dq_ref[...] = (dqt[...].T * 0.125).astype(BF)
    cross(0).wait_recv()
    for c in results:
        c.wait()
    out_ref[...] = (
        base_ref[...]
        + res_ref[z].astype(F32)
        + r_far[0].astype(F32)
        + r_far[1].astype(F32)
        + r_far[2].astype(F32)
    )
    dkv_ref[...] = keep[0].astype(F32) + got[0].astype(F32)
    for d in (1, 2, 3):

        @pl.when(y + d < 4)
        def _():
            remote(keep.at[d], far.at[d], ys.at[d], yr.at[d], sib).wait_recv()
            dkv_ref[...] += far[d].astype(F32)

    @pl.when(z == x)
    def _():
        def arrive(i, carry):
            @pl.when(i != me)
            def _():
                remote(f_sum.at[0], f_all.at[i], s4.at[0], r4.at[i], sib).wait_recv()

            return carry

        lax.fori_loop(0, 16, arrive, 0)
        for b in range(4):
            fo_ref[:, 384 * b : 384 * b + 384] = (
                f_all[b].astype(F32)
                + f_all[4 + b].astype(F32)
                + f_all[8 + b].astype(F32)
                + f_all[12 + b].astype(F32)
            )

    for a in range(4):

        @pl.when((k == z // 2) & jnp.logical_not((a == y) & (z == y)))
        def _():
            remote(p_sum.at[0], p_all.at[a], s6.at[0], r6.at[a], sib).wait_recv()

    @pl.when(k == z // 2)
    def _():
        po_ref[...] = (
            p_all[0].astype(F32)
            + p_all[1].astype(F32)
            + p_all[2].astype(F32)
            + p_all[3].astype(F32)
        )

    for a in range(4):

        @pl.when(jnp.logical_not(f_here[a]))
        def _():
            f_copy(a).wait_send()

    for j in range(2):

        @pl.when(jnp.logical_not(p_here[j]))
        def _():
            p_copy(j).wait_send()

    cross(0).wait_send()
    for d in (1, 2, 3):

        @pl.when(y >= d)
        def _():
            cross(d).wait_send()
            up(d).wait_send()


def middle(heads_all, x_group, dy_group, wo, wf, wp, vec_rows, query, kv_all, out_t, lse):
    def kernel(*refs):
        (h_ref, x_ref, dy_ref, wo_ref, wf_ref, wp_ref, v_ref) = refs[:7]
        (q_ref, kv_ref, ot_ref, lse_ref) = refs[7:11]
        (gx_ref, bo_ref, gfb_ref, gv_ref) = refs[11:15]
        back_outs = refs[15:20]
        (base_ref, res_ref, gwf_ref, gwp_ref) = refs[20:24]
        feed_rest = refs[24:45]
        back_rest = refs[45:]
        y, z, k, x = coords()
        everyone = greet(
            [device(y, z, 1 - k, x)]
            + [device(y, z, k, ring(x, d)) for d in (1, 2, 3)]
            + [
                device(ring(y, a), ring(z, b), k, x)
                for a in range(4)
                for b in range(4)
                if (a, b) != (0, 0)
            ]
        )
        feed_body(
            h_ref, x_ref, dy_ref, wo_ref, wf_ref, wp_ref, v_ref,
            base_ref, res_ref, gx_ref, bo_ref, gwf_ref, gwp_ref, gfb_ref, gv_ref,
            *feed_rest, everyone,
        )
        back_body(
            q_ref, bo_ref, wo_ref, kv_ref, ot_ref, lse_ref, gwf_ref, gwp_ref, base_ref, res_ref,
            *back_outs, *back_rest,
        )

    feed_scratch = ([pltpu.VMEM((2, 512, 768), BF),
            pltpu.VMEM((2, 512, 384), BF),
            pltpu.VMEM((2, 512, 384), BF),
            pltpu.VMEM((512, 768), F32),
            pltpu.VMEM((512, 768), F32),
            pltpu.VMEM((512, 128), F32),
        ]
        + [pltpu.VMEM((4, 128, 768), BF)] * 5
        + [pltpu.VMEM((3, 128, 768), BF)]
        + [pltpu.VMEM((128, 768), BF)])
    back_scratch = [
            pltpu.VMEM((3, 192, 512), BF),
            pltpu.VMEM((3, 192, 512), BF),
            pltpu.VMEM((3, 512, 192), BF),
            pltpu.VMEM((3, 512, 192), BF),
            pltpu.VMEM((8, 512), F32),
            pltpu.VMEM((192, 512), F32),
            pltpu.VMEM((4, 512, 384), BF),
            pltpu.VMEM((4, 512, 384), BF),
            pltpu.VMEM((4, 512, 384), BF),
            pltpu.VMEM((4, 512, 384), BF),
            pltpu.VMEM((3, 4, 48, 384), BF),
            pltpu.VMEM((3, 2, 48, 768), BF),
            pltpu.VMEM((3, 128, 768), BF),
            pltpu.VMEM((4, 48, 384), BF),
            pltpu.VMEM((2, 48, 768), BF),
            pltpu.VMEM((16, 48, 384), BF),
            pltpu.VMEM((4, 48, 768), BF),
    ]
    dma = pltpu.SemaphoreType.DMA
    return pl.pallas_call(
        kernel,
        out_shape=[
            jax.ShapeDtypeStruct((128, 768), F32),
            jax.ShapeDtypeStruct((4, 128, 768), BF),
            jax.ShapeDtypeStruct((1, 384), F32),
            jax.ShapeDtypeStruct((4, 768), F32),
            jax.ShapeDtypeStruct((512, 192), BF),
            jax.ShapeDtypeStruct((512, 384), F32),
            jax.ShapeDtypeStruct((48, 1536), F32),
            jax.ShapeDtypeStruct((48, 768), F32),
            jax.ShapeDtypeStruct((128, 768), F32),
        ],
        in_specs=[VMEM] * 11,
        out_specs=[VMEM] * 9,
        scratch_shapes=[
            pltpu.VMEM((128, 768), F32),
            pltpu.VMEM((4, 128, 768), BF),
            pltpu.VMEM((4, 4, 48, 384), BF),
            pltpu.VMEM((2, 4, 48, 768), BF),
        ]
        + feed_scratch
        + [dma((n,)) for n in (4, 4, 4, 4, 3, 3, 3, 3)]
        + back_scratch
        + [dma((n,)) for n in (4, 4, 4, 4, 3, 3, 3, 3, 3, 3, 4, 16, 2, 4)],
        compiler_params=pltpu.CompilerParams(
            collective_id=3, has_side_effects=True, vmem_limit_bytes=LIMIT
        ),
        name="middle",
    )(heads_all, x_group, dy_group, wo, wf, wp, vec_rows, query, kv_all, out_t, lse)


def adam_update(weight, moment_one, moment_two, gradient, rate, decay):
    new_one = BETA_ONE * moment_one + (1.0 - BETA_ONE) * gradient
    new_two = BETA_TWO * moment_two + (1.0 - BETA_TWO) * gradient * gradient
    fix_one = 1.0 - BETA_ONE**STEP
    fix_two = 1.0 - BETA_TWO**STEP
    direction = new_one / fix_one / (jnp.sqrt(new_two / fix_two) + ADAM_EPSILON)
    return (weight - rate * (direction + decay * weight), new_one, new_two)


def shards(
    tokens,
    cotangent,
    w_qkv,
    qkv_m,
    qkv_v,
    w_out,
    out_m,
    out_v,
    w_fc,
    fc_m,
    fc_v,
    w_proj,
    proj_m,
    proj_v,
    vectors,
    vec_m,
    vec_v,
):
    state = (
        w_qkv, qkv_m, qkv_v, w_out, out_m, out_v, w_fc, fc_m, fc_v, w_proj, proj_m, proj_v,
        vectors, vec_m, vec_v,
    )
    (
        heads_all, out_t, lse, kv_all, dy_group, wf, wo, wp, query, act_one, normed_core,
        wq, x_group, vec_rows,
    ) = forward(w_qkv, w_fc, w_out, w_proj, vectors, tokens[0], cotangent[0])
    wq = wq.reshape(768, 640)
    wo = wo.reshape(2, 768, 384)
    (
        grad_x_two, branch_core, grad_fc_bias, vec_sums, grad_query, grad_kv, fc_sum, proj_sum,
        result_sum,
    ) = middle(
        heads_all,
        x_group,
        dy_group,
        wo,
        wf.reshape(768, 384),
        wp.reshape(384, 768),
        vec_rows,
        query,
        kv_all,
        out_t,
        lse,
    )
    branch_core = branch_core.reshape(512, 768)
    grad_one, last_rows, proj_rows, fc_rows = last_sums(
        (
            act_one,
            normed_core,
            heads_all,
            grad_query,
            grad_kv,
            branch_core,
            wq,
            vec_sums,
            grad_fc_bias,
        ),
        fc_sum,
        proj_sum,
    )
    output, grad_inputs, *new_state = finish(
        grad_one, grad_x_two, tokens[0], vec_rows, last_rows, proj_rows, fc_rows, result_sum, state
    )
    return (output[None], grad_inputs[None], *new_state)


def solution(mesh):
    split = P("fsdp", "ctx", None)
    rows = P(("ctx", "fsdp"), None)
    return jax.shard_map(
        shards,
        mesh=mesh,
        in_specs=(split, split) + (rows,) * 15,
        out_specs=(split, split) + (rows,) * 15,
        check_vma=False,
    )
```

```python
import jax
import jax.numpy as jnp
from jax import lax
from jax.experimental import pallas as pl
from jax.experimental.pallas import tpu as pltpu
from jax.sharding import PartitionSpec as P

STEP = 10
EPSILON = 1e-05
BETA_ONE = 0.9
BETA_TWO = 0.999
ADAM_EPSILON = 1e-08
MESH = pl.DeviceIdType.MESH
BF = jnp.bfloat16
F32 = jnp.float32
ANY = pl.BlockSpec(memory_space=pl.ANY)
VMEM = pl.BlockSpec(memory_space=pltpu.VMEM)
LIMIT = 56 * 1024 * 1024


def coords():
    c = lax.axis_index("ctx")
    return c // 8, (c // 2) % 4, c % 2, lax.axis_index("fsdp")


def device(y, z, k, x):
    return ((y * 4 + z) * 2 + k, x)


def ring(v, step):
    return lax.rem(v + step, 4)


def greet(devices):
    barrier = pltpu.get_barrier_semaphore()
    for one in devices:
        pl.semaphore_signal(barrier, inc=1, device_id=one, device_id_type=MESH)
    return lambda: pl.semaphore_wait(barrier, len(devices))


def remote(src, dst, send, recv, to):
    return pltpu.make_async_remote_copy(
        src, dst, send, recv, device_id=to, device_id_type=MESH
    )


def comm(kernel, outs, cid, sems, args, scratch=(), spaces=None, name=None):
    return pl.pallas_call(
        kernel,
        out_shape=outs,
        in_specs=[ANY] * len(args) if spaces is None else spaces[0],
        out_specs=[ANY] * len(outs) if spaces is None else spaces[1],
        scratch_shapes=list(scratch) + [pltpu.SemaphoreType.DMA((n,)) for n in sems],
        compiler_params=pltpu.CompilerParams(
            collective_id=cid, has_side_effects=True, vmem_limit_bytes=LIMIT
        ),
        name=name,
    )(*args)


def last_sums(pieces, fc, proj):
    wide = 1664

    def kernel(*refs):
        (
            act_ref, n_ref, h_ref, gq_ref, gkv_ref, br_ref, wq_ref, vs_ref, fb_ref,
            fc_ref, proj_ref,
        ) = refs[:11]
        one_out, rows_out, proj_out, fc_out = refs[11:15]
        (
            one_far, mix_got, mix_sum, mix_all, vec_all, proj_sum, out_send, fc_send,
            one_ref, mix_other, mix_ref, vec_ref,
            act_t, heads, heads_t, d_ref, right_one, right_two, vec_rows,
        ) = refs[15:34]
        (
        zs, zr, cs, cr, s3, r3, s4, r4, s5, r5, s7, r7, s8, r8, loc,
        ) = refs[34:]
        y, z, k, x = coords()
        me = y * 4 + z
        sib = device(y, z, 1 - k, x)
        steps = (1, 2, 3)
        everyone = greet(
            [sib]
            + [device(y, z, j, ring(x, d)) for d in steps for j in (k, 1 - k)]
            + [
                device(ring(y, a), ring(z, b), k, x)
                for a in range(4)
                for b in range(4)
                if (a, b) != (0, 0)
            ]
        )
        d_ref[:, 0:192] = gq_ref[...]
        d_ref[:, 192:576] = gkv_ref[...].astype(BF)
        d_ref[:, 576:640] = jnp.zeros((512, 64), BF)
        right_one[...] = jnp.zeros_like(right_one)
        right_one[:, 0:288] = d_ref[:, 0:288]
        right_one[:, 384:672] = d_ref[:, 288:576]
        right_two[...] = jnp.zeros_like(right_two)
        vec_rows[...] = jnp.zeros_like(vec_rows)
        sums = jnp.sum(d_ref[...].astype(F32), 0, keepdims=True)
        at_half = pl.ds(pl.multiple_of(384 * k, 128), 384)
        for b in range(4):
            heads[:, 192 * b : 192 * b + 192] = h_ref[b, k]

            @pl.when(z == b)
            def _():
                right_two[:, 288:384] = br_ref[:, 192 * b : 192 * b + 96]
                right_two[:, 672:768] = br_ref[:, 192 * b + 96 : 192 * b + 192]
                vec_rows[2:3, 192 * b : 192 * b + 192] = sums[:, 0:192]
                vec_rows[3:4, 192 * b : 192 * b + 192] = sums[:, 384:576]
                vec_rows[8 + b : 9 + b, at_half] = fb_ref[...]

        vec_rows[4:8] = vs_ref[...]
        act_t[...] = act_ref[...].T
        heads_t[...] = heads[...].T

        def product(h):
            at = pl.ds(pl.multiple_of(384 * h, 128), 384)
            total = dot(act_t[...], right_one[:, at]) + dot(heads_t[...], right_two[:, at])
            return total.reshape(4, 4, 48, 384)

        mix_other[...] = product(1 - k).astype(BF)
        everyone()
        swap = []
        for d in (1, 2, 3, 0):
            b = ring(y, d)
            c = remote(mix_other.at[b], mix_got.at[b], cs.at[d], cr.at[d], sib)
            c.start()
            swap.append(c)
        def proj_last(i):
            return remote(
                proj_sum.at[i], proj_out, s8.at[i], r8.at[0],
                device(y, z, x // 2, lax.rem(2 * x + i, 4)),
            )

        def proj_here(i):
            return (k == x // 2) & (x == lax.rem(2 * x + i, 4))

        holder = k == z // 2

        @pl.when(holder)
        def _():
            for i in range(2):
                proj_sum[i] = proj_ref[24 * i : 24 * i + 24]

                @pl.when(jnp.logical_not(proj_here(i)))
                def _():
                    proj_last(i).start()

                @pl.when(proj_here(i))
                def _():
                    proj_out[...] = proj_sum[i]

        def last_here(i):
            return k * 4 + x == i

        def fc_last(i):
            return remote(
                fc_send.at[i], fc_out.at[k], s4.at[i], r4.at[k], device(y, z, i // 4, i % 4)
            )

        @pl.when(z == x)
        def _():
            for i in range(8):
                fc_send[i, 0:6] = fc_ref[6 * i : 6 * i + 6]
                fc_send[i, 6:8] = jnp.zeros((2, 1536), F32)

                @pl.when(jnp.logical_not(last_here(i)))
                def _():
                    fc_last(i).start()

                @pl.when(last_here(i))
                def _():
                    fc_out[k] = fc_send[i]

        mix_ref[...] = product(k).astype(BF)
        one = lax.dot_general(
            d_ref[...], wq_ref[...], (((1,), (1,)), ((), ())), preferred_element_type=F32
        )
        one_ref[...] = one.astype(BF).reshape(4, 128, 768)
        vec_rows[0:1] = jnp.sum(one * n_ref[...].astype(F32), 0, keepdims=True)
        vec_rows[1:2] = jnp.sum(one, 0, keepdims=True)
        vec_ref[...] = vec_rows[...].T.astype(BF).reshape(4, 4, 48, 128)
        ones = []
        for d in steps:
            c = remote(
                one_ref.at[ring(z, d)], one_far.at[d - 1], zs.at[d - 1], zr.at[d - 1],
                device(y, ring(z, d), k, x),
            )
            c.start()
            ones.append(c)

        def plane(src, dst, send, recv, m):
            ty, tz = ring(y, m // 4), ring(z, m % 4)
            return remote(
                src.at[ty, tz], dst.at[me], send.at[m], recv.at[m], device(ty, tz, k, x)
            )

        def vec_copy(m):
            return plane(vec_ref, vec_all, s5, r5, m)

        def mix_copy(m):
            return plane(mix_sum, mix_all, s3, r3, m)

        def each(copy, what, first, last):
            def step(m, carry):
                what(copy(m))
                return carry

            lax.fori_loop(first, last, step, 0)

        start = lambda c: c.start()
        finish_all = lambda c: c.wait()
        each(vec_copy, start, 1, 16)
        vec_all[me] = vec_ref[y, z]
        for d in (1, 2, 3, 0):
            b = ring(y, d)
            swap[d - 1].wait_recv()
            mix_sum[b] = (mix_ref[b].astype(F32) + mix_got[b].astype(F32)).astype(BF)
            each(mix_copy, start, max(4 * d, 1), 4 * d + 4)
        mix_all[me] = mix_sum[y, z]
        for c in ones:
            c.wait_recv()
        one_out[...] = (
            one_ref[z].astype(F32)
            + one_far[0].astype(F32)
            + one_far[1].astype(F32)
            + one_far[2].astype(F32)
        )

        def last_copy(i):
            return remote(
                out_send.at[i], rows_out.at[k * 4 + x], s7.at[i], r7.at[k * 4 + x],
                device(y, z, i // 4, i % 4),
            )

        each(vec_copy, finish_all, 1, 16)
        each(mix_copy, finish_all, 1, 16)

        def four(ref, b):
            return (
                ref[b].astype(F32)
                + ref[4 + b].astype(F32)
                + ref[8 + b].astype(F32)
                + ref[12 + b].astype(F32)
            )

        for b in range(4):
            m = four(mix_all, b)
            for i in range(8):
                out_send[i, 0:6, 384 * b : 384 * b + 384] = m[6 * i : 6 * i + 6]
        v = four(vec_all, 0) + four(vec_all, 1) + four(vec_all, 2) + four(vec_all, 3)
        for i in range(8):
            out_send[i, 0:6, 1536:1664] = v[6 * i : 6 * i + 6]
            out_send[i, 6:8, :] = jnp.zeros((2, wide), F32)
        for i in range(8):

            @pl.when(jnp.logical_not(last_here(i)))
            def _():
                last_copy(i).start()

            @pl.when(last_here(i))
            def _():
                rows_out[i] = out_send[i]

        for j in range(2):

            @pl.when(jnp.logical_not((z == x) & (k == j)))
            def _():
                remote(fc_send.at[0], fc_out.at[j], s4.at[0], r4.at[j], sib).wait_recv()

        for i in range(8):

            @pl.when(jnp.logical_not(last_here(i)))
            def _():
                remote(out_send.at[0], rows_out.at[i], s7.at[0], r7.at[i], sib).wait_recv()
                last_copy(i).wait_send()

        @pl.when(jnp.logical_not((k == z // 2) & (x == (4 * k + x) // 2)))
        def _():
            remote(proj_sum.at[0], proj_out, s8.at[0], r8.at[0], sib).wait_recv()

        @pl.when(z == x)
        def _():
            for i in range(8):

                @pl.when(jnp.logical_not(last_here(i)))
                def _():
                    fc_last(i).wait_send()

        for i in range(2):

            @pl.when(holder & jnp.logical_not(proj_here(i)))
            def _():
                proj_last(i).wait_send()

        for c in swap + ones:
            c.wait_send()

    return comm(
        kernel,
        [
            jax.ShapeDtypeStruct((128, 768), F32),
            jax.ShapeDtypeStruct((8, 8, wide), F32),
            jax.ShapeDtypeStruct((24, 768), F32),
            jax.ShapeDtypeStruct((2, 8, 1536), F32),
        ],
        6,
        (3, 3, 4, 4, 16, 16, 8, 2, 16, 16, 8, 8, 2, 1, 4),
        (*pieces, fc, proj),
        scratch=[
            pltpu.VMEM((3, 128, 768), BF),
            pltpu.VMEM((4, 4, 48, 384), BF),
            pltpu.VMEM((4, 4, 48, 384), BF),
            pltpu.VMEM((16, 48, 384), BF),
            pltpu.VMEM((16, 48, 128), BF),
            pltpu.VMEM((2, 24, 768), F32),
            pltpu.VMEM((8, 8, wide), F32),
            pltpu.VMEM((8, 8, 1536), F32),
            pltpu.VMEM((4, 128, 768), BF),
            pltpu.VMEM((4, 4, 48, 384), BF),
            pltpu.VMEM((4, 4, 48, 384), BF),
            pltpu.VMEM((4, 4, 48, 128), BF),
            pltpu.VMEM((768, 512), BF),
            pltpu.VMEM((512, 768), BF),
            pltpu.VMEM((768, 512), BF),
            pltpu.VMEM((512, 640), BF),
            pltpu.VMEM((512, 768), BF),
            pltpu.VMEM((512, 768), BF),
            pltpu.VMEM((128, 768), F32),
        ],
        spaces=([VMEM] * 11, [VMEM] * 4),
        name="last_sums",
    )


def finish(grad_one, grad_x_two, tokens, vec_rows, rows, proj_rows, fc_rows, result, state):
    def kernel(*refs):
        one_ref, gx_ref, t_ref, v_ref, rows_ref, p_ref, f_ref, res_ref = refs[:8]
        state_ref = refs[8:23]
        out_ref, gin_ref = refs[23:25]
        new_ref = refs[25:40]
        g_qkv, g_out, g_fc = refs[40:]
        out_ref[...] = res_ref[...]
        normed, inverse = normalize(t_ref[...].astype(F32))
        gin_ref[...] = gx_ref[...] + normalize_back(normed, inverse, v_ref[0:1], one_ref[...])
        for b in range(4):
            at_z = slice(384 * b, 384 * b + 384)
            one_half = jnp.sum(rows_ref[0:4, 0:6, at_z], 0)
            two_half = jnp.sum(rows_ref[4:8, 0:6, at_z], 0)
            q = 192 * b
            g_qkv[:, q : q + 192] = one_half[:, 0:192]
            g_qkv[:, 768 + q : 864 + q] = one_half[:, 192:288]
            g_qkv[:, 864 + q : 960 + q] = two_half[:, 0:96]
            g_qkv[:, 1536 + q : 1728 + q] = two_half[:, 96:288]
            g_out[:, q : q + 96] = one_half[:, 288:384]
            g_out[:, q + 96 : q + 192] = two_half[:, 288:384]
            for j in range(2):
                at = 384 * (2 * b + j)
                g_fc[:, at : at + 384] = f_ref[j, 0:6, 384 * b : 384 * b + 384]
        g_vec = jnp.sum(rows_ref[:, 0:6, 1536:1548], 0)
        for i, (gradient, rate, decay) in enumerate(
            (
                (g_qkv[...], 0.1, 0.1),
                (g_out[...], 0.3, 0.1),
                (g_fc[...], 0.05, 0.1),
                (p_ref[...], 0.03, 0.1),
                (g_vec, 0.5, 0.0),
            )
        ):
            w, m, v = state_ref[3 * i : 3 * i + 3]
            results = adam_update(w[...], m[...], v[...], gradient, rate, decay)
            for j in range(3):
                new_ref[3 * i + j][...] = results[j]

    return pl.pallas_call(
        kernel,
        out_shape=[jax.ShapeDtypeStruct((128, 768), F32)] * 2
        + [jax.ShapeDtypeStruct(one.shape, F32) for one in state],
        in_specs=[VMEM] * 23,
        out_specs=[VMEM] * 17,
        scratch_shapes=[
            pltpu.VMEM((6, 2304), F32),
            pltpu.VMEM((6, 768), F32),
            pltpu.VMEM((6, 3072), F32),
        ],
        compiler_params=pltpu.CompilerParams(vmem_limit_bytes=LIMIT),
        name="finish",
    )(grad_one, grad_x_two, tokens, vec_rows, rows, proj_rows, fc_rows, result, *state)


def head_rows(matrix, head):
    row = lax.broadcasted_iota(jnp.int32, matrix.shape, 0)
    keep = (row >= 64 * head) & (row < 64 * head + 64)
    return jnp.where(keep, matrix, jnp.zeros_like(matrix))


def head_cols(matrix, head):
    col = lax.broadcasted_iota(jnp.int32, matrix.shape, 1)
    keep = (col >= 64 * head) & (col < 64 * head + 64)
    return jnp.where(keep, matrix, jnp.zeros_like(matrix))


def place(index):
    return (index // 128) * 256 + index % 128


def dot(a, b):
    return jnp.dot(a, b, preferred_element_type=F32)


def forward(w_qkv, w_fc, w_out, w_proj, vectors, tokens, cotangent):
    wide_q, wide_r = 1280, 3456

    def kernel(
        wq_ref, wf_ref, wo_ref, wp_ref, wv_ref, t_ref, r_ref,
        ho_ref, ot_ref, lse_ref, vo_ref, ro_ref, fo_ref, oo_ref, po_ref, q_ref, a_ref, n_ref,
        q_out, x_ref, vec_ref,
        wide_one, wide_two, packed_q, packed_r, got_q, got_r,
        fc48, qkv48, out48, proj_wide, q_send, f_send, o_send, p_send, f_mid, o_mid, p_mid,
        bias, qt, m_ref, l_ref, h_buf, v_ref,
        mq_s, mq_r, fq_s, fq_r, mr_s, mr_r, fr_s, fr_r, s1, r1, s2, r2, ps, pr,
        xs_s, xs_r, xf_s, xf_r, ts, tr, us, ur,
        vs, vr, rs, rr, cs, cr, ds, dr, ws, wr, wf, os, orr, hs, hr, gs, gr, loc,
    ):
        y, z, k, x = coords()
        me = y * 4 + z
        t = k * 4 + x
        sib = device(y, z, 1 - k, x)
        steps = (1, 2, 3)
        everyone = greet(
            [sib]
            + [device(y, z, k, ring(x, d)) for d in steps]
            + [
                device(ring(y, a), ring(z, b), k, x)
                for a in range(4)
                for b in range(4)
                if (a, b) != (0, 0)
            ]
        )

        def first(packed, got, send, recv):
            copies = [
                remote(packed, got.at[t], send.at[d], recv.at[d], device(y, z, k, ring(x, d)))
                for d in steps
            ]
            for c in copies:
                c.start()
            return copies

        def crossing(packed, got, copies, send, recv):
            out = [remote(packed, got.at[t], send.at[0], recv.at[0], sib)]
            out[0].start()
            for d in steps:
                copies[d - 1].wait_recv()
                src = k * 4 + ring(x, 4 - d)
                c = remote(got.at[src], got.at[src], send.at[d], recv.at[d], sib)
                c.start()
                out.append(c)
            return out

        wide_one[...] = jnp.zeros_like(wide_one)
        wide_one[0:6, 0:1152] = wq_ref[:, 0:1152]
        wide_one[6:12, 0:1152] = wq_ref[:, 1152:2304]
        wide_one[0:6, 1152:1164] = wv_ref[...]
        packed_q[...] = wide_one[...].astype(BF)
        got_q[t] = packed_q[...]
        everyone()
        message_q = first(packed_q, got_q, mq_s, mq_r)
        token_copies = []
        for d in steps:
            c = remote(
                t_ref, x_ref.at[k, z], ts.at[d], tr.at[d], device(y, ring(z, d), k, x)
            )
            c.start()
            token_copies.append(c)
        token_cross = [remote(t_ref, x_ref.at[k, z], us.at[0], ur.at[0], sib)]
        token_cross[0].start()
        x_ref[k, z] = t_ref[...]
        wide_two[...] = jnp.zeros_like(wide_two)
        wide_two[0:6, 0:1920] = wf_ref[:, 0:1920]
        wide_two[6:12, 0:1152] = wf_ref[:, 1920:3072]
        wide_two[6:12, 1152:1920] = wo_ref[...]
        wide_two[0:12, 1920:2688] = wp_ref[0:12]
        wide_two[0:12, 2688:3456] = wp_ref[12:24]
        packed_r[...] = wide_two[...].astype(BF)
        got_r[t] = packed_r[...]
        cross_q = crossing(packed_q, got_q, message_q, fq_s, fq_r)
        message_r = first(packed_r, got_r, mr_s, mr_r)
        for c in cross_q:
            c.wait_recv()
        for i in range(8):
            piece = got_q[i].astype(F32)
            at = slice(6 * i, 6 * i + 6)
            qkv48[at, 0:1152] = piece[0:6, 0:1152]
            qkv48[at, 1152:2304] = piece[6:12, 0:1152]
            qkv48[at, 2304:2432] = piece[0:6, 1152:1280]
        for j in range(4):
            q_send[j, :, 0:192] = qkv48[:, 192 * j : 192 * j + 192].astype(BF)
            q_send[j, :, 192:384] = qkv48[:, 768 + 192 * j : 960 + 192 * j].astype(BF)
            q_send[j, :, 384:576] = qkv48[:, 1536 + 192 * j : 1728 + 192 * j].astype(BF)
            q_send[j, :, 576:640] = qkv48[:, 2304:2368].astype(BF)

        group = pl.ds(pl.multiple_of(16 * jnp.minimum(x, 2), 16), 16)

        def to_of(m):
            return ring(y, m // 4), ring(z, m % 4)

        def q_copy(m):
            ty, tz = to_of(m)
            return remote(
                q_send.at[tz, group], q_out.at[me, group], s1.at[m], r1.at[m],
                device(ty, tz, k, x),
            )

        def f_copy(m):
            ty, tz = to_of(m)
            return remote(
                f_send.at[tz * 2 + k], f_mid.at[me], s2.at[m], r2.at[m], device(ty, tz, k, x)
            )

        def o_copy(m):
            ty, tz = to_of(m)
            return remote(o_send.at[k], o_mid.at[me], s2.at[m], r2.at[m], device(ty, tz, k, x))

        def p_copy(a):
            return remote(
                p_send, p_mid.at[z % 2], ps.at[a], pr.at[z % 2], device(ring(y, a), y, k, x)
            )

        def each(copy, what):
            def step(m, carry):
                what(copy(m))
                return carry

            lax.fori_loop(1, 16, step, 0)

        start = lambda c: c.start()
        finish = lambda c: c.wait()

        @pl.when(x < 3)
        def _():
            each(q_copy, start)
            q_out[me, group] = q_send[z, group]

        half = pl.ds(8 * k, 8)
        other_half = pl.ds(8 * (1 - k), 8)

        def rows_of(plane):
            return pl.ds(pl.multiple_of(16 * plane, 16), 16)

        def x_copy(d):
            return remote(
                q_out.at[half, group], q_out.at[half, group], xs_s.at[d], xs_r.at[x],
                device(y, z, k, ring(x, d)),
            )

        @pl.when(x < 3)
        def _():
            each(q_copy, finish)
            for d in steps:
                x_copy(d).start()

        cross_r = crossing(packed_r, got_r, message_r, fr_s, fr_r)
        for c in cross_r:
            c.wait_recv()
        for i in range(8):
            piece = got_r[i].astype(F32)
            at = slice(6 * i, 6 * i + 6)
            fc48[at, 0:1920] = piece[0:6, 0:1920]
            fc48[at, 1920:3072] = piece[6:12, 0:1152]
            out48[at] = piece[6:12, 1152:1920]
            proj_wide[24 * i : 24 * i + 12] = piece[0:12, 1920:2688]
            proj_wide[24 * i + 12 : 24 * i + 24] = piece[0:12, 2688:3456]
        for j in range(8):
            f_send[j] = fc48[:, 384 * j : 384 * j + 384].astype(BF)
        o_send[0] = out48[:, 0:384].astype(BF)
        o_send[1] = out48[:, 384:768].astype(BF)
        p_send[...] = proj_wide[...].astype(BF)

        @pl.when(x == 1)
        def _():
            each(f_copy, start)
            f_mid[me] = f_send[z * 2 + k]

        @pl.when(x == 2)
        def _():
            each(o_copy, start)
            o_mid[me] = o_send[k]

        @pl.when((x == 3) & (k == z // 2))
        def _():
            for a in range(1, 4):
                p_copy(a).start()

            @pl.when(z != y)
            def _():
                p_copy(0).start()

            @pl.when(z == y)
            def _():
                p_mid[z % 2] = p_send[...]

        def pass_q(a):
            return remote(
                q_out.at[half, rows_of(a)], q_out.at[half, rows_of(a)], xf_s.at[a], xf_r.at[a], sib
            )

        for a in range(3):

            @pl.when(x != a)
            def _():
                remote(
                    q_out.at[half, rows_of(a)], q_out.at[half, rows_of(a)], xs_s.at[0],
                    xs_r.at[a], sib,
                ).wait_recv()
                pass_q(a).start()

        for d in steps:
            token_copies[d - 1].wait_recv()
            src = ring(z, 4 - d)
            c = remote(x_ref.at[k, src], x_ref.at[k, src], us.at[d], ur.at[d], sib)
            c.start()
            token_cross.append(c)
        normed, _ = normalize(x_ref[k].reshape(512, 768).astype(F32))
        n_ref[...] = normed.astype(BF)

        weights = ((1, f_mid, fo_ref, 8), (2, o_mid, oo_ref, 8), (3, p_mid, po_ref, 1))

        def ends(a, half):
            _, src, dst, n = weights[a - 1]
            at = pl.ds(n * half, n)
            return src.at[at], (dst.at[k, at] if a == 2 else dst.at[at])

        def direct(a, half, d):
            src, dst = ends(a, half)
            return remote(
                src, dst, ws.at[4 * half + d], wr.at[2 * a + half], device(y, z, k, ring(x, d))
            )

        def onward(a, half, d):
            _, dst = ends(a, half)
            return remote(
                dst, dst, wf.at[a], wr.at[2 * a + half], device(y, z, k, ring(x, d))
            )

        def weight_own(a):
            _, src, dst, _ = weights[a - 1]
            return pltpu.make_async_copy(src, dst.at[k] if a == 2 else dst, loc.at[1])

        @pl.when(x == 1)
        def _():
            each(f_copy, finish)

        @pl.when(x == 2)
        def _():
            each(o_copy, finish)

        for i in range(2):
            @pl.when((x == 3) & jnp.logical_not((y == z) & (z == 2 * k + i)))
            def _():
                remote(p_send, p_mid.at[i], ps.at[0], pr.at[i], sib).wait_recv()

        for a in steps:

            @pl.when(x == a)
            def _():
                for half_at, d in ((0, 1), (1, 3), (1, 1), (0, 3)):
                    direct(a, half_at, d).start()
                weight_own(a).start()

        def move_on():
            for a in steps:

                @pl.when(x == (a + 1) % 4)
                def _():
                    direct(a, 0, 1).wait_recv()
                    onward(a, 0, 1).start()

                @pl.when(x == (a + 3) % 4)
                def _():
                    direct(a, 1, 1).wait_recv()
                    onward(a, 1, 3).start()

        for a in range(3):

            @pl.when(x != a)
            def _():
                remote(
                    q_out.at[other_half, rows_of(a)], q_out.at[other_half, rows_of(a)],
                    xf_s.at[a], xf_r.at[a], sib,
                ).wait_recv()

        vec_ref[...] = q_out[:, :, 512:640].reshape(768, 128).astype(F32).T[64:80]
        bias[...] = jnp.zeros_like(bias)
        for b in range(4):

            @pl.when(z == b)
            def _():
                bias[:, 0:192] = vec_ref[2:3, 192 * b : 192 * b + 192]
                bias[:, 384:576] = vec_ref[3:4, 192 * b : 192 * b + 192]

        act = (normed * vec_ref[0:1] + vec_ref[1:2]).astype(BF)
        a_ref[...] = act
        mixed = dot(act, q_out[...].reshape(768, 640)) + bias[...]
        v_ref[...] = mixed[:, 192:576].astype(BF)

        def kv_copy(d):
            return remote(
                v_ref, vo_ref.at[y, k], vs.at[d], vr.at[d], device(ring(y, d), z, k, x)
            )

        for d in steps:

            @pl.when(y + d < 4)
            def _():
                kv_copy(d).start()

        swap = remote(v_ref, vo_ref.at[y, k], cs.at[0], cr.at[0], sib)
        swap.start()
        vo_ref[y, k] = v_ref[...]
        own_r = pltpu.make_async_copy(r_ref, ro_ref.at[k, z], loc.at[0])
        own_r.start()
        row_copies = []
        for d in steps:
            c = remote(
                r_ref, ro_ref.at[k, z], rs.at[d], rr.at[d], device(y, ring(z, d), k, x)
            )
            c.start()
            row_copies.append(c)
        row_first = remote(r_ref, ro_ref.at[k, z], ds.at[0], dr.at[0], sib)
        row_first.start()
        query = mixed[:, :192].astype(BF) * jnp.asarray(0.125, BF)
        q_ref[...] = query
        q_t = query.T
        for head in range(3):
            qt[head] = head_rows(q_t, head)
        m_ref[...] = jnp.full_like(m_ref, -1e30)
        l_ref[...] = jnp.zeros_like(l_ref)
        ot_ref[...] = jnp.zeros_like(ot_ref)

        def block(by, bk, masked):
            keys = vo_ref[by, bk, :, :192]
            values_t = vo_ref[by, bk, :, 192:].T
            if masked:
                key_at = place(lax.broadcasted_iota(jnp.int32, (512, 512), 0)) + 128 * bk
                query_at = place(lax.broadcasted_iota(jnp.int32, (512, 512), 1)) + 128 * k
                visible = query_at >= key_at
            for head in range(3):
                s = dot(keys, qt[head])
                if masked:
                    s = jnp.where(visible, s, -1e9)
                old = m_ref[head : head + 1]
                new = jnp.maximum(old, jnp.max(s, 0, keepdims=True))
                e = jnp.exp(s - new)
                scale = jnp.exp(old - new)
                m_ref[head : head + 1] = new
                l_ref[head : head + 1] = l_ref[head : head + 1] * scale + jnp.sum(
                    e, 0, keepdims=True
                )
                at = slice(64 * head, 64 * head + 64)
                ot_ref[at] = ot_ref[at] * scale + dot(values_t[at], e.astype(BF))

        def diagonal(j, carry):
            @pl.when(j == 1)
            def _():
                remote(v_ref, vo_ref.at[y, 1 - k], cs.at[0], cr.at[0], sib).wait_recv()

            block(y, lax.rem(k + j, 2), True)

            return carry

        lax.fori_loop(0, 2, diagonal, 0)

        def pass_on(d):
            return remote(
                vo_ref.at[y - d, k], vo_ref.at[y - d, k], cs.at[d], cr.at[d], sib
            )

        def earlier(i, carry):
            d, j = i // 2 + 1, i % 2

            @pl.when(j == 0)
            def _():
                remote(v_ref, vo_ref.at[y - d, k], vs.at[d], vr.at[d], sib).wait_recv()
                pass_on(d).start()

            @pl.when(j == 1)
            def _():
                remote(v_ref, vo_ref.at[y - d, 1 - k], cs.at[d], cr.at[d], sib).wait_recv()

            block(y - d, lax.rem(k + j, 2), False)

            @pl.when(i == jnp.minimum(2, 2 * y - 1))
            def _():
                move_on()

            return carry

        @pl.when(y == 0)
        def _():
            move_on()

        lax.fori_loop(0, 2 * y, earlier, 0)
        for head in range(3):
            at = slice(64 * head, 64 * head + 64)
            total = l_ref[head : head + 1]
            ot_ref[at] = ot_ref[at] / total
            lse_ref[head : head + 1] = m_ref[head : head + 1] + jnp.log(total)
        h_buf[...] = ot_ref[...].T.astype(BF)
        heads_copies = []
        for d in steps:
            c = remote(
                h_buf, ho_ref.at[z, k], hs.at[d], hr.at[d], device(y, ring(z, d), k, x)
            )
            c.start()
            heads_copies.append(c)
        c = remote(h_buf, ho_ref.at[z, k], gs.at[0], gr.at[0], sib)
        c.start()
        forward_copies = [c, row_first]
        own_h = pltpu.make_async_copy(h_buf, ho_ref.at[z, k], loc.at[2])
        own_h.start()
        for d in steps:
            row_copies[d - 1].wait_recv()
            src = ring(z, 4 - d)
            c = remote(ro_ref.at[k, src], ro_ref.at[k, src], ds.at[d], dr.at[d], sib)
            c.start()
            forward_copies.append(c)
        for a in steps:

            @pl.when(x == a)
            def _():
                weight_own(a).wait()

            @pl.when(x == (a + 1) % 4)
            def _():
                direct(a, 1, 1).wait_recv()

            @pl.when(x == (a + 3) % 4)
            def _():
                direct(a, 0, 1).wait_recv()

            @pl.when(x == (a + 2) % 4)
            def _():
                direct(a, 0, 1).wait_recv()
                direct(a, 1, 1).wait_recv()

        c = remote(oo_ref.at[k], oo_ref.at[k], os.at[0], orr.at[0], sib)
        c.start()
        forward_copies.append(c)
        for d in steps:
            heads_copies[d - 1].wait_recv()
            src = ring(z, 4 - d)
            c = remote(ho_ref.at[src, k], ho_ref.at[src, k], gs.at[d], gr.at[d], sib)
            c.start()
            forward_copies.append(c)
        for c in forward_copies + token_cross:
            c.wait()
        for c in row_copies + heads_copies + token_copies + [swap]:
            c.wait_send()
        for c in message_q + cross_q + message_r + cross_r:
            c.wait_send()
        for d in steps:

            @pl.when(y + d < 4)
            def _():
                kv_copy(d).wait_send()

            @pl.when(y >= d)
            def _():
                pass_on(d).wait_send()

        for a in steps:

            @pl.when(x == a)
            def _():
                for half_at, d in ((0, 1), (1, 3), (1, 1), (0, 3)):
                    direct(a, half_at, d).wait_send()

            @pl.when(x == (a + 1) % 4)
            def _():
                onward(a, 0, 1).wait_send()

            @pl.when(x == (a + 3) % 4)
            def _():
                onward(a, 1, 3).wait_send()

        @pl.when((x == 3) & (k == z // 2))
        def _():
            for a in range(1, 4):
                p_copy(a).wait_send()

            @pl.when(z != y)
            def _():
                p_copy(0).wait_send()

        @pl.when(x < 3)
        def _():
            for d in steps:
                x_copy(d).wait_send()

        for a in range(3):

            @pl.when(x != a)
            def _():
                pass_q(a).wait_send()

        own_r.wait()
        own_h.wait()

    return comm(
        kernel,
        [
            jax.ShapeDtypeStruct((4, 2, 512, 192), BF),
            jax.ShapeDtypeStruct((192, 512), F32),
            jax.ShapeDtypeStruct((8, 512), F32),
            jax.ShapeDtypeStruct((4, 2, 512, 384), BF),
            jax.ShapeDtypeStruct((2, 4, 128, 768), BF),
            jax.ShapeDtypeStruct((16, 48, 384), BF),
            jax.ShapeDtypeStruct((2, 16, 48, 384), BF),
            jax.ShapeDtypeStruct((2, 192, 768), BF),
            jax.ShapeDtypeStruct((512, 192), BF),
            jax.ShapeDtypeStruct((512, 768), BF),
            jax.ShapeDtypeStruct((512, 768), BF),
            jax.ShapeDtypeStruct((16, 48, 640), BF),
            jax.ShapeDtypeStruct((2, 4, 128, 768), BF),
            jax.ShapeDtypeStruct((16, 768), F32),
        ],
        0,
        (4,) * 8 + (16,) * 4 + (4, 2) + (4,) * 8
        + (4, 4, 4, 4, 4, 4, 4, 4, 8, 8, 4, 1, 1, 4, 4, 4, 4, 3),
        (w_qkv, w_fc, w_out, w_proj, vectors, tokens, cotangent),
        scratch=[
            pltpu.VMEM((16, wide_q), F32),
            pltpu.VMEM((16, wide_r), F32),
            pltpu.VMEM((16, wide_q), BF),
            pltpu.VMEM((16, wide_r), BF),
            pltpu.VMEM((8, 16, wide_q), BF),
            pltpu.VMEM((8, 16, wide_r), BF),
            pltpu.VMEM((48, 3072), F32),
            pltpu.VMEM((48, 2432), F32),
            pltpu.VMEM((48, 768), F32),
            pltpu.VMEM((192, 768), F32),
            pltpu.VMEM((4, 48, 640), BF),
            pltpu.VMEM((8, 48, 384), BF),
            pltpu.VMEM((2, 48, 384), BF),
            pltpu.VMEM((192, 768), BF),
            pltpu.VMEM((16, 48, 384), BF),
            pltpu.VMEM((16, 48, 384), BF),
            pltpu.VMEM((2, 192, 768), BF),
            pltpu.VMEM((1, 640), F32),
            pltpu.VMEM((3, 192, 512), BF),
            pltpu.VMEM((8, 512), F32),
            pltpu.VMEM((8, 512), F32),
            pltpu.VMEM((512, 192), BF),
            pltpu.VMEM((512, 384), BF),
        ],
        spaces=(
            [VMEM] * 6 + [ANY],
            [ANY, VMEM, VMEM, VMEM, ANY, ANY, ANY, ANY] + [VMEM] * 6,
        ),
        name="forward",
    )


def normalize(rows):
    centered = rows - jnp.mean(rows, -1, keepdims=True)
    inverse = lax.rsqrt(jnp.mean(centered * centered, -1, keepdims=True) + EPSILON)
    return centered * inverse, inverse


def normalize_back(normed, inverse, gain, grad):
    scaled = grad * gain
    return inverse * (
        scaled
        - jnp.mean(scaled, -1, keepdims=True)
        - normed * jnp.mean(scaled * normed, -1, keepdims=True)
    )


def feed_body(
    h_ref, x_ref, dy_ref, wo_ref, wf_ref, wp_ref, v_ref,
    base_ref, res_mine, gx_ref, bo_ref, gwf_ref, gwp_ref, gfb_ref, gv_ref,
    a2, act, df, x_two, normed, inverse, norm_other, norm_mine, res_other,
    norm_got, res_got, norm_far, branch,
    cs, cr, es, er, zs, zr, bs, br, everyone, gradients_done,
):
    y, z, k, x = coords()
    sib = device(y, z, 1 - k, x)
    steps = (1, 2, 3)
    out_bias, gain, shift, proj_bias = (v_ref[i : i + 1] for i in range(4, 8))
    fc_bias = jnp.zeros((1, 384), F32)
    for b in range(4):
        row = v_ref[8 + b : 9 + b, pl.ds(pl.multiple_of(384 * k, 128), 384)]
        fc_bias = fc_bias + jnp.where(z == b, row, 0.0)

    def half(kk, norm_ref):
        two = x_ref[kk].reshape(512, 768).astype(F32) + out_bias
        for g in range(4):
            h = h_ref[g, kk]
            at = slice(192 * g, 192 * g + 192)
            part = jnp.concatenate([dot(h, wo_ref[0, at]), dot(h, wo_ref[1, at])], 1)
            two = two + part
        x_two[...] = two
        n, inv = normalize(two)
        normed[...] = n
        inverse[...] = jnp.broadcast_to(inv, (512, 128))
        a = (n * gain + shift).astype(BF)
        a2[kk] = a
        hidden = dot(a, wf_ref[...]) + fc_bias
        square = hidden * hidden
        t = jnp.tanh(0.7978845608028654 * (hidden + 0.044715 * square * hidden))
        act_blk = (0.5 * hidden * (1.0 + t)).astype(BF)
        act[kk] = act_blk
        slope = 0.5 * (1.0 + t) + 0.5 * hidden * (1.0 - t * t) * (
            0.7978845608028654 * (1.0 + 3 * 0.044715 * square)
        )
        dy = dy_ref[kk].reshape(512, 768)
        back = lax.dot_general(
            dy, wp_ref[...], (((1,), (1,)), ((), ())), preferred_element_type=F32
        )
        df_blk = (back * slope).astype(BF)
        df[kk] = df_blk
        norm_part = lax.dot_general(
            df_blk, wf_ref[...], (((1,), (1,)), ((), ())), preferred_element_type=F32
        )
        norm_ref[...] = norm_part.astype(BF).reshape(4, 128, 768)

    def result(kk, res_ref):
        res_ref[...] = dot(act[kk], wp_ref[...]).astype(BF).reshape(4, 128, 768)

    half(1 - k, norm_other)
    everyone()
    swaps = []
    for d in (1, 2, 3, 0):
        b = ring(z, d)
        c = remote(norm_other.at[b], norm_got.at[b], cs.at[d], cr.at[d], sib)
        c.start()
        swaps.append(c)
    half(k, norm_mine)
    sends = []
    for d in steps:
        b = ring(z, d)
        swaps[d - 1].wait_recv()
        norm_mine[b] = (norm_mine[b].astype(F32) + norm_got[b].astype(F32)).astype(BF)
        c = remote(
            norm_mine.at[b], norm_far.at[d - 1], zs.at[d - 1], zr.at[d - 1],
            device(y, b, k, x),
        )
        c.start()
        sends.append(c)
    result(1 - k, res_other)
    for d in (1, 2, 3, 0):
        b = ring(z, d)
        c = remote(res_other.at[b], res_got.at[b], es.at[d], er.at[d], sib)
        c.start()
        swaps.append(c)
    tn = (((0,), (0,)), ((), ()))
    gwf = lax.dot_general(a2[0], df[0], tn, preferred_element_type=F32)
    gwf += lax.dot_general(a2[1], df[1], tn, preferred_element_type=F32)
    gwf_ref[...] = gwf.astype(BF).reshape(4, 4, 48, 384)
    own_rows = pl.ds(pl.multiple_of(128 * z, 128), 128)
    swaps[3].wait_recv()
    for c in sends:
        c.wait_recv()
    da = (
        norm_mine[z].astype(F32)
        + norm_got[z].astype(F32)
        + norm_far[0].astype(F32)
        + norm_far[1].astype(F32)
        + norm_far[2].astype(F32)
    )
    n = normed[own_rows]
    dy = dy_ref[k, z].astype(F32)
    gx = dy + normalize_back(n, inverse[own_rows, 0:1], gain, da)
    gx_ref[...] = gx
    low = gx.astype(BF)
    branch[...] = low
    bo_ref[z] = low
    branches = []
    for d in steps:
        c = remote(
            branch, bo_ref.at[z], bs.at[d - 1], br.at[d - 1], device(y, ring(z, d), k, x)
        )
        c.start()
        branches.append(c)
    result(k, res_mine)
    gwp = lax.dot_general(
        act[0], dy_ref[0].reshape(512, 768), tn, preferred_element_type=F32
    )
    gwp += lax.dot_general(
        act[1], dy_ref[1].reshape(512, 768), tn, preferred_element_type=F32
    )
    gwp_ref[...] = gwp.astype(BF).reshape(2, 4, 48, 768)
    gradients_done()
    gfb_ref[...] = jnp.sum(df[0].astype(F32), 0, keepdims=True) + jnp.sum(
        df[1].astype(F32), 0, keepdims=True
    )
    gv_ref[0:1] = jnp.sum(low.astype(F32), 0, keepdims=True)
    gv_ref[1:2] = jnp.sum(da * n, 0, keepdims=True)
    gv_ref[2:3] = jnp.sum(da, 0, keepdims=True)
    gv_ref[3:4] = jnp.sum(dy, 0, keepdims=True)
    for c in swaps[4:]:
        c.wait_recv()
    res_mine[...] = (res_mine[...].astype(F32) + res_got[...].astype(F32)).astype(BF)
    base_ref[...] = x_two[own_rows] + proj_bias
    for c in branches:
        c.wait()
    for c in swaps + sends:
        c.wait_send()


def back_body(
    q_ref, b_ref, w_ref, kv_ref, ot_ref, lse_ref, f_ref, p_ref, base_ref, res_ref,
    dq_ref, dkv_ref, fo_ref, po_ref, out_ref,
    qt, gt, qm, gm, delta, dqt, out_buf, keep, got, far, f_far, p_far, r_far,
    f_sum, p_sum, f_all, p_all,
    cs, cr, ys, yr, fs, fr, ps, pr, rs, rr, s4, r4, s6, r6, weights,
):
    y, z, k, x = coords()
    sib = device(y, z, 1 - k, x)
    steps = (1, 2, 3)
    me = y * 4 + z
    results = []
    for d in steps:
        b = ring(z, d)
        c = remote(
            res_ref.at[b], r_far.at[d - 1], rs.at[d - 1], rr.at[d - 1], device(y, b, k, x)
        )
        c.start()
        results.append(c)
    query_blk = q_ref[...]
    q_t = query_blk.T
    for head in range(3):
        qt[head] = head_rows(q_t, head)
        qm[head] = head_cols(query_blk, head)
    dqt[...] = jnp.zeros_like(dqt)
    nt = (((1,), (1,)), ((), ()))
    branch = b_ref[...].reshape(512, 768)
    own_heads = pl.ds(pl.multiple_of(192 * z, 64), 192)
    grad_blk = lax.dot_general(
        branch[:, :384], w_ref[0, own_heads], nt, preferred_element_type=F32
    )
    grad_blk += lax.dot_general(
        branch[:, 384:], w_ref[1, own_heads], nt, preferred_element_type=F32
    )
    grad_blk = grad_blk.astype(BF)
    g_t = grad_blk.T
    for head in range(3):
        at = slice(64 * head, 64 * head + 64)
        gt[head] = head_rows(g_t, head)
        gm[head] = head_cols(grad_blk, head)
        delta[head : head + 1] = jnp.sum(g_t[at].astype(F32) * ot_ref[at], 0, keepdims=True)

    def block(by, bk, masked, to_ref, to):
        keys = kv_ref[by, bk, :, :192]
        values = kv_ref[by, bk, :, 192:]
        keys_t = keys.T
        if masked:
            key_at = place(lax.broadcasted_iota(jnp.int32, (512, 512), 0)) + 128 * bk
            query_at = place(lax.broadcasted_iota(jnp.int32, (512, 512), 1)) + 128 * k
            visible = query_at >= key_at
        dk = dv = None
        for head in range(3):
            s = dot(keys, qt[head])
            p = jnp.exp(s - lse_ref[head : head + 1])
            if masked:
                p = jnp.where(visible, p, 0.0)
            dp = dot(values, gt[head])
            ds = (p * (dp - delta[head : head + 1])).astype(BF)
            pv = dot(p.astype(BF), gm[head])
            pk = dot(ds, qm[head])
            dv = pv if dv is None else dv + pv
            dk = pk if dk is None else dk + pk
            at = slice(64 * head, 64 * head + 64)
            dqt[at] += dot(keys_t[at], ds)
        to_ref[to, :, :192] = dk.astype(BF)
        to_ref[to, :, 192:] = dv.astype(BF)

    def cross(d):
        return remote(out_buf.at[d], got.at[d], cs.at[d], cr.at[d], sib)

    def up(d):
        return remote(keep.at[d], far.at[d], ys.at[d], yr.at[d], device(y - d, z, k, x))

    def f_copy(a):
        return remote(
            f_sum.at[a], f_all.at[me], s4.at[a], r4.at[me], device(a, x, k, x)
        )

    def p_copy(j):
        return remote(
            p_sum.at[j], p_all.at[y], s6.at[j], r6.at[y], device(z, 2 * k + j, k, x)
        )

    f_here = [(a == y) & (z == x) for a in range(4)]
    p_here = [(y == z) & (z == 2 * k + j) for j in range(2)]
    def over_plane():
        for c in weights:
            c.wait()
        f_sum[...] = (
            f_ref[:, x].astype(F32)
            + f_far[0].astype(F32)
            + f_far[1].astype(F32)
            + f_far[2].astype(F32)
        ).astype(BF)
        p_sum[...] = (
            p_ref[:, x].astype(F32)
            + p_far[0].astype(F32)
            + p_far[1].astype(F32)
            + p_far[2].astype(F32)
        ).astype(BF)

        for a in range(4):

            @pl.when(jnp.logical_not(f_here[a]))
            def _():
                f_copy(a).start()

            @pl.when(f_here[a])
            def _():
                f_all[me] = f_sum[a]

        for j in range(2):

            @pl.when(jnp.logical_not(p_here[j]))
            def _():
                p_copy(j).start()

            @pl.when(p_here[j])
            def _():
                p_all[y] = p_sum[j]

    def earlier(i, carry):
        d = y - i
        block(y - d, 1 - k, False, out_buf, d)
        cross(d).start()

        @pl.when(i == 0)
        def _():
            over_plane()

        block(y - d, k, False, keep, d)
        cross(d).wait_recv()
        keep[d] = (keep[d].astype(F32) + got[d].astype(F32)).astype(BF)
        up(d).start()
        return carry

    lax.fori_loop(0, y, earlier, 0)
    block(y, 1 - k, True, out_buf, 0)
    cross(0).start()

    @pl.when(y == 0)
    def _():
        over_plane()


    block(y, k, True, keep, 0)
    dq_ref[...] = (dqt[...].T * 0.125).astype(BF)
    cross(0).wait_recv()
    for c in results:
        c.wait()
    out_ref[...] = (
        base_ref[...]
        + res_ref[z].astype(F32)
        + r_far[0].astype(F32)
        + r_far[1].astype(F32)
        + r_far[2].astype(F32)
    )
    dkv_ref[...] = keep[0].astype(F32) + got[0].astype(F32)
    for d in (1, 2, 3):

        @pl.when(y + d < 4)
        def _():
            remote(keep.at[d], far.at[d], ys.at[d], yr.at[d], sib).wait_recv()
            dkv_ref[...] += far[d].astype(F32)

    @pl.when(z == x)
    def _():
        def arrive(i, carry):
            @pl.when(i != me)
            def _():
                remote(f_sum.at[0], f_all.at[i], s4.at[0], r4.at[i], sib).wait_recv()

            return carry

        lax.fori_loop(0, 16, arrive, 0)
        for b in range(4):
            fo_ref[:, 384 * b : 384 * b + 384] = (
                f_all[b].astype(F32)
                + f_all[4 + b].astype(F32)
                + f_all[8 + b].astype(F32)
                + f_all[12 + b].astype(F32)
            )

    for a in range(4):

        @pl.when((k == z // 2) & jnp.logical_not((a == y) & (z == y)))
        def _():
            remote(p_sum.at[0], p_all.at[a], s6.at[0], r6.at[a], sib).wait_recv()

    @pl.when(k == z // 2)
    def _():
        po_ref[...] = (
            p_all[0].astype(F32)
            + p_all[1].astype(F32)
            + p_all[2].astype(F32)
            + p_all[3].astype(F32)
        )

    for a in range(4):

        @pl.when(jnp.logical_not(f_here[a]))
        def _():
            f_copy(a).wait_send()

    for j in range(2):

        @pl.when(jnp.logical_not(p_here[j]))
        def _():
            p_copy(j).wait_send()

    cross(0).wait_send()
    for d in (1, 2, 3):

        @pl.when(y >= d)
        def _():
            cross(d).wait_send()
            up(d).wait_send()


def middle(heads_all, x_group, dy_group, wo, wf, wp, vec_rows, query, kv_all, out_t, lse):
    def kernel(*refs):
        (h_ref, x_ref, dy_ref, wo_ref, wf_ref, wp_ref, v_ref) = refs[:7]
        (q_ref, kv_ref, ot_ref, lse_ref) = refs[7:11]
        (gx_ref, bo_ref, gfb_ref, gv_ref) = refs[11:15]
        back_outs = refs[15:20]
        (base_ref, res_ref, gwf_ref, gwp_ref) = refs[20:24]
        feed_rest = refs[24:45]
        back_rest = refs[45:]
        y, z, k, x = coords()
        everyone = greet(
            [device(y, z, 1 - k, x)]
            + [device(y, z, k, ring(x, d)) for d in (1, 2, 3)]
            + [
                device(ring(y, a), ring(z, b), k, x)
                for a in range(4)
                for b in range(4)
                if (a, b) != (0, 0)
            ]
        )
        f_far, p_far = back_rest[10], back_rest[11]
        fs, fr, ps, pr = back_rest[21:25]
        steps = (1, 2, 3)
        weights = []
        for d in steps:
            b = ring(x, d)
            to = device(y, z, k, b)
            weights.append(
                remote(gwf_ref.at[:, b], f_far.at[d - 1], fs.at[d - 1], fr.at[d - 1], to)
            )
            weights.append(
                remote(gwp_ref.at[:, b], p_far.at[d - 1], ps.at[d - 1], pr.at[d - 1], to)
            )
        feed_body(
            h_ref, x_ref, dy_ref, wo_ref, wf_ref, wp_ref, v_ref,
            base_ref, res_ref, gx_ref, bo_ref, gwf_ref, gwp_ref, gfb_ref, gv_ref,
            *feed_rest, everyone, lambda: [c.start() for c in weights],
        )
        back_body(
            q_ref, bo_ref, wo_ref, kv_ref, ot_ref, lse_ref, gwf_ref, gwp_ref, base_ref, res_ref,
            *back_outs, *back_rest, weights,
        )

    feed_scratch = ([pltpu.VMEM((2, 512, 768), BF),
            pltpu.VMEM((2, 512, 384), BF),
            pltpu.VMEM((2, 512, 384), BF),
            pltpu.VMEM((512, 768), F32),
            pltpu.VMEM((512, 768), F32),
            pltpu.VMEM((512, 128), F32),
        ]
        + [pltpu.VMEM((4, 128, 768), BF)] * 5
        + [pltpu.VMEM((3, 128, 768), BF)]
        + [pltpu.VMEM((128, 768), BF)])
    back_scratch = [
            pltpu.VMEM((3, 192, 512), BF),
            pltpu.VMEM((3, 192, 512), BF),
            pltpu.VMEM((3, 512, 192), BF),
            pltpu.VMEM((3, 512, 192), BF),
            pltpu.VMEM((8, 512), F32),
            pltpu.VMEM((192, 512), F32),
            pltpu.VMEM((4, 512, 384), BF),
            pltpu.VMEM((4, 512, 384), BF),
            pltpu.VMEM((4, 512, 384), BF),
            pltpu.VMEM((4, 512, 384), BF),
            pltpu.VMEM((3, 4, 48, 384), BF),
            pltpu.VMEM((3, 2, 48, 768), BF),
            pltpu.VMEM((3, 128, 768), BF),
            pltpu.VMEM((4, 48, 384), BF),
            pltpu.VMEM((2, 48, 768), BF),
            pltpu.VMEM((16, 48, 384), BF),
            pltpu.VMEM((4, 48, 768), BF),
    ]
    dma = pltpu.SemaphoreType.DMA
    return pl.pallas_call(
        kernel,
        out_shape=[
            jax.ShapeDtypeStruct((128, 768), F32),
            jax.ShapeDtypeStruct((4, 128, 768), BF),
            jax.ShapeDtypeStruct((1, 384), F32),
            jax.ShapeDtypeStruct((4, 768), F32),
            jax.ShapeDtypeStruct((512, 192), BF),
            jax.ShapeDtypeStruct((512, 384), F32),
            jax.ShapeDtypeStruct((48, 1536), F32),
            jax.ShapeDtypeStruct((48, 768), F32),
            jax.ShapeDtypeStruct((128, 768), F32),
        ],
        in_specs=[VMEM] * 11,
        out_specs=[VMEM] * 9,
        scratch_shapes=[
            pltpu.VMEM((128, 768), F32),
            pltpu.VMEM((4, 128, 768), BF),
            pltpu.VMEM((4, 4, 48, 384), BF),
            pltpu.VMEM((2, 4, 48, 768), BF),
        ]
        + feed_scratch
        + [dma((n,)) for n in (4, 4, 4, 4, 3, 3, 3, 3)]
        + back_scratch
        + [dma((n,)) for n in (4, 4, 4, 4, 3, 3, 3, 3, 3, 3, 4, 16, 2, 4)],
        compiler_params=pltpu.CompilerParams(
            collective_id=3, has_side_effects=True, vmem_limit_bytes=LIMIT
        ),
        name="middle",
    )(heads_all, x_group, dy_group, wo, wf, wp, vec_rows, query, kv_all, out_t, lse)


def adam_update(weight, moment_one, moment_two, gradient, rate, decay):
    new_one = BETA_ONE * moment_one + (1.0 - BETA_ONE) * gradient
    new_two = BETA_TWO * moment_two + (1.0 - BETA_TWO) * gradient * gradient
    fix_one = 1.0 - BETA_ONE**STEP
    fix_two = 1.0 - BETA_TWO**STEP
    direction = new_one / fix_one / (jnp.sqrt(new_two / fix_two) + ADAM_EPSILON)
    return (weight - rate * (direction + decay * weight), new_one, new_two)


def shards(
    tokens,
    cotangent,
    w_qkv,
    qkv_m,
    qkv_v,
    w_out,
    out_m,
    out_v,
    w_fc,
    fc_m,
    fc_v,
    w_proj,
    proj_m,
    proj_v,
    vectors,
    vec_m,
    vec_v,
):
    state = (
        w_qkv, qkv_m, qkv_v, w_out, out_m, out_v, w_fc, fc_m, fc_v, w_proj, proj_m, proj_v,
        vectors, vec_m, vec_v,
    )
    (
        heads_all, out_t, lse, kv_all, dy_group, wf, wo, wp, query, act_one, normed_core,
        wq, x_group, vec_rows,
    ) = forward(w_qkv, w_fc, w_out, w_proj, vectors, tokens[0], cotangent[0])
    wq = wq.reshape(768, 640)
    wo = wo.reshape(2, 768, 384)
    (
        grad_x_two, branch_core, grad_fc_bias, vec_sums, grad_query, grad_kv, fc_sum, proj_sum,
        result_sum,
    ) = middle(
        heads_all,
        x_group,
        dy_group,
        wo,
        wf.reshape(768, 384),
        wp.reshape(384, 768),
        vec_rows,
        query,
        kv_all,
        out_t,
        lse,
    )
    branch_core = branch_core.reshape(512, 768)
    grad_one, last_rows, proj_rows, fc_rows = last_sums(
        (
            act_one,
            normed_core,
            heads_all,
            grad_query,
            grad_kv,
            branch_core,
            wq,
            vec_sums,
            grad_fc_bias,
        ),
        fc_sum,
        proj_sum,
    )
    output, grad_inputs, *new_state = finish(
        grad_one, grad_x_two, tokens[0], vec_rows, last_rows, proj_rows, fc_rows, result_sum, state
    )
    return (output[None], grad_inputs[None], *new_state)


def solution(mesh):
    split = P("fsdp", "ctx", None)
    rows = P(("ctx", "fsdp"), None)
    return jax.shard_map(
        shards,
        mesh=mesh,
        in_specs=(split, split) + (rows,) * 15,
        out_specs=(split, split) + (rows,) * 15,
        check_vma=False,
    )
```
